32 devices in a mesh: seq: 8 (over z, x), batch: 4 (over y, core).
Axes of the slice: x: 2, y: 2, z: 4, core: 2. Of those that a mesh axis runs over, the one named last changes fastest.
Arguments:
- layer_input: bfloat16 [4, 2048, 1024], P('batch', 'seq'), may hold values from -6 to 6
- seq_lengths: int32 [4, 3], P('batch'), may hold values from 43 to 1962, as said below
- w_attn: bfloat16 [1024, 768], P(('seq', 'batch')), may hold values from -0.1875 to 0.1875
- w_ssm_in: bfloat16 [1024, 3328], P(('seq', 'batch')), may hold values from -0.1875 to 0.1875
- w_dt: bfloat16 [1024, 24], P(('seq', 'batch')), may hold values from -0.1875 to 0.1875
- w_out: bfloat16 [2048, 1024], P(None, ('seq', 'batch')), may hold values from -0.125 to 0.125
- w_gate_up: bfloat16 [1024, 4096], P(('seq', 'batch')), may hold values from -0.1875 to 0.1875
- w_down: bfloat16 [2048, 1024], P(None, ('seq', 'batch')), may hold values from -0.125 to 0.125
- norm_gain: float32 [1024], replicated, may hold values from 0.5 to 1.5
- mlp_gain: float32 [1024], replicated, may hold values from 0.5 to 1.5
- ssm_gain: float32 [1536], replicated, may hold values from 0.5 to 1.5
- conv_w: float32 [4, 1792], replicated, may hold values from -3 to 3
- conv_b: float32 [1792], replicated, may hold values from -2 to 2
- a_log: float32 [24], replicated, may hold values from -9 to 0
- dt_bias: float32 [24], replicated, may hold values from -4 to -1
- d_skip: float32 [24], replicated, may hold values from 0.5 to 1.5
- out_grad: bfloat16 [4, 2048, 1024], P('batch', 'seq'), may hold values from -6 to 6
Outputs:
- layer_out: bfloat16 [4, 2048, 1024], P('batch', 'seq')
- input_grad: float32 [4, 2048, 1024], P('batch', 'seq')
- grad_w_attn: float32 [1024, 768], P(('seq', 'batch'))
- grad_w_ssm_in: float32 [1024, 3328], P(('seq', 'batch'))
- grad_w_dt: float32 [1024, 24], P(('seq', 'batch'))
- grad_w_out: float32 [2048, 1024], P(None, ('seq', 'batch'))
- grad_w_gate_up: float32 [1024, 4096], P(('seq', 'batch'))
- grad_w_down: float32 [2048, 1024], P(None, ('seq', 'batch'))
- grad_norm_gain: float32 [1024], replicated
- grad_mlp_gain: float32 [1024], replicated
- grad_ssm_gain: float32 [1536], replicated
- grad_conv_w: float32 [4, 1792], replicated
- grad_conv_b: float32 [1792], replicated
- grad_a_log: float32 [24], replicated
- grad_dt_bias: float32 [24], replicated
- grad_d_skip: float32 [24], replicated
The draws below stay inside these ranges and needn't reach their ends.
Inputs may be any that keep to these rules, and one draw needn't show every extreme that they name: Each row of seq_lengths sums to 2048. One sequence of each row, at a place drawn from the seed, begins among the first 256 tokens and ends among the last 256; every other length lies between 43 and 85.
All inputs are finite; a program needn't handle non-finite values.
Results may differ from the reference program's by a relative error of at most 0.019.
Values may be sent and summed in bfloat16 or wider, within the bound.
A program may use at most 384 MiB of HBM per device.

```python
import math
import jax
import jax.numpy as jnp
from jax import lax

D = 1024
QUERY_HEADS = 8
KEY_VALUE_HEADS = 2
HEAD_SIZE = 64
MH = 24
MP = 64
NS = 128
FF = 2048
CONV = 4
SPAN = 128
TOK_DEV = 256
NSEQ = 3
QW = 512
KW = 128
SW = 1536
XW = 1792
GROUPS = 4
SEQ_TOK = 2048


def draw_seq_lengths(key, part):
    splits = jax.random.split(key, 2)
    low_len = TOK_DEV // (2 * NSEQ) + 1
    high_len = TOK_DEV // NSEQ + 1
    short_lens = jax.random.randint(splits[0], (GROUPS, NSEQ), low_len, high_len, dtype=jnp.int32)
    chosen_idx = jax.random.randint(splits[1], (GROUPS, 1), 0, NSEQ, dtype=jnp.int32)
    chosen = jnp.arange(NSEQ, dtype=jnp.int32)[None, :] == chosen_idx
    others = jnp.sum(jnp.where(chosen, 0, short_lens), axis=1, keepdims=True)
    return jnp.where(chosen, SEQ_TOK - others, short_lens).astype(jnp.int32)


def block_levels(stream_key, shape, cuts, smallest, high):
    def one(dim, parts):
        draws = jax.random.uniform(jax.random.fold_in(jax.random.fold_in(stream_key, 6), dim), (parts,), jnp.float32, smallest / len(cuts), high / len(cuts))
        return jnp.repeat(jnp.exp(draws), shape[dim] // parts).reshape((-1,) + (1,) * (len(shape) - dim - 1))

    level = one(*cuts[0])
    for cut in cuts[1:]:
        level = level * one(*cut)
    return level


def centred(key, dims, scale, most, cuts=(), held_as=jnp.bfloat16):
    level = block_levels(key, dims, cuts, -0.22, 0.18) if cuts else 1.0
    values = jax.random.normal(key, dims, jnp.float32) * scale * level
    return jnp.minimum(jnp.maximum(values, -most), most).astype(held_as)


def setup_inputs(seed: int = 0) -> dict:
    arg_keys = jax.random.split(jax.random.key(seed), 18)
    return {
        "layer_input": centred(arg_keys[0], (GROUPS, SEQ_TOK, D), 1.0, 6.0, ((0, 4), (1, 8))),
        "seq_lengths": draw_seq_lengths(jax.random.fold_in(arg_keys[17], 71), 0),
        "w_attn": centred(arg_keys[2], (D, QW + 2 * KW), D ** -0.5, 0.1875, ((0, 32),)),
        "w_ssm_in": centred(arg_keys[3], (D, SW + XW), D ** -0.5, 0.1875, ((0, 32),)),
        "w_dt": centred(arg_keys[4], (D, MH), D ** -0.5, 0.1875, ((0, 32),)),
        "w_out": centred(arg_keys[5], (QW + SW, D), (QW + SW) ** -0.5, 0.125, ((1, 32),)),
        "w_gate_up": centred(arg_keys[6], (D, 2 * FF), D ** -0.5, 0.1875, ((0, 32),)),
        "w_down": centred(arg_keys[7], (FF, D), FF ** -0.5, 0.125, ((1, 32),)),
        "norm_gain": jnp.clip(1.0 + 0.1 * jax.random.normal(arg_keys[8], (D,), jnp.float32), 0.5, 1.5),
        "mlp_gain": jnp.clip(1.0 + 0.1 * jax.random.normal(arg_keys[9], (D,), jnp.float32), 0.5, 1.5),
        "ssm_gain": jnp.clip(1.0 + 0.1 * jax.random.normal(arg_keys[10], (SW,), jnp.float32), 0.5, 1.5),
        "conv_w": centred(arg_keys[11], (CONV, XW), 0.5, 3.0, (), jnp.float32),
        "conv_b": centred(arg_keys[12], (XW,), 0.3, 2.0, (), jnp.float32),
        "a_log": jnp.clip(jax.random.uniform(arg_keys[13], (MH,), jnp.float32, -9.0, 0.0), -9.0, 0.0),
        "dt_bias": jnp.clip(jax.random.uniform(arg_keys[14], (MH,), jnp.float32, -4.0, -1.0), -4.0, -1.0),
        "d_skip": jnp.clip(jax.random.uniform(arg_keys[15], (MH,), jnp.float32, 0.5, 1.5), 0.5, 1.5),
        "out_grad": centred(arg_keys[16], (GROUPS, SEQ_TOK, D), 1.0, 6.0, ((0, 4), (1, 8))),
    }


@jax.custom_vjp
def lower_bound(v):
    return lax.optimization_barrier(v.astype(jnp.bfloat16)).astype(jnp.float32)

@jax.custom_vjp
def low_back(v):
    return v

def low_keep(v):
    return (lower_bound(v), None)

def low_pass(kept, grad):
    return (grad,)

def back_keep(v):
    return (v, None)

def back_low(kept, grad):
    return (lower_bound(grad),)
lower_bound.defvjp(low_keep, low_pass)
low_back.defvjp(back_keep, back_low)
HIGHEST = lax.Precision.HIGHEST
NEGATIVE_FILL = -1e+30
ROPE_BASE = 10000.0
NORM_EPS = 1e-06

def rms_scale(value_rows):
    return lax.rsqrt(lax.optimization_barrier(jnp.mean(value_rows * value_rows, axis=-1, keepdims=True)) + NORM_EPS)

def rotary_embed(value_rows, device_places, direction):
    half_dim = value_rows.shape[-1] // 2
    freqs = ROPE_BASE ** (-jnp.arange(half_dim, dtype=jnp.float32) / half_dim)
    angles = direction * device_places.astype(jnp.float32)[:, None] * freqs[None, :]
    cosine = jnp.cos(angles)[:, None, :]
    sine = jnp.sin(angles)[:, None, :]
    first_half = value_rows[..., :half_dim]
    second_half = value_rows[..., half_dim:]
    return jnp.concatenate([first_half * cosine - second_half * sine, second_half * cosine + first_half * sine], axis=-1)

def segments(lengths, positions):
    ends = jnp.cumsum(lengths).astype(jnp.int32)
    passed = ends[None, :] <= positions[:, None]
    segment = lax.optimization_barrier(jnp.sum(passed.astype(jnp.int32), axis=1)).astype(jnp.int32)
    device_places = (positions - lax.optimization_barrier(jnp.sum(jnp.where(passed, lengths[None, :], 0), axis=1))).astype(jnp.int32)
    return (segment, device_places)

def conv_mix(extended, ext_segment, conv_weight, conv_bias):
    row_count = extended.shape[0] - (CONV - 1)
    summed = conv_bias[None, :]
    for lagged in range(CONV):
        same_seq = (ext_segment[lagged:lagged + row_count] == ext_segment[CONV - 1:]).astype(extended.dtype)
        summed = summed + conv_weight[lagged][None, :] * extended[lagged:lagged + row_count] * same_seq[:, None]
    return jax.nn.silu(summed)

def ssd_blocks(inputs_x, inputs_b, inputs_c, steps_dt, log_rates, skip_gain, segment, segment_before, state_in, rounder):
    total_rows = inputs_x.shape[0]
    count_of_blocks = total_rows // SPAN
    decay_rates = jnp.exp(log_rates)
    offsets = jnp.arange(SPAN)
    causal = offsets[:, None] >= offsets[None, :]

    def advance(carry_in, pieces):
        carried, previous = carry_in
        block_x, block_b, block_c, block_dt, block_seg = pieces
        log_decay = jnp.cumsum(-block_dt * decay_rates[None, :], axis=0)
        allowed = (block_seg[:, None] == block_seg[None, :]) & causal
        spread = log_decay[:, None, :] - log_decay[None, :, :]
        decays = jnp.exp(jnp.where(allowed[:, :, None], spread, NEGATIVE_FILL))
        inner_cb = jnp.dot(block_c, block_b.T, precision=HIGHEST)
        mixing = rounder(inner_cb[:, :, None] * decays * block_dt[None, :, :])
        result = jnp.einsum('tsh,shp->thp', mixing, block_x, precision=HIGHEST)
        linked = (block_seg == previous).astype(block_x.dtype)
        entering = jnp.exp(log_decay) * linked[:, None]
        result = result + entering[:, :, None] * jnp.einsum('hpn,tn->thp', carried, block_c, precision=HIGHEST)
        result = result + skip_gain[None, :, None] * block_x
        same_last = (block_seg == block_seg[-1]).astype(block_x.dtype)
        leaving = jnp.exp(log_decay[-1][None, :] - log_decay) * same_last[:, None] * block_dt
        carried = entering[-1][:, None, None] * carried + jnp.einsum('th,thp,tn->hpn', leaving, block_x, block_b, precision=HIGHEST)
        return ((carried, block_seg[-1]), result)
    blocks = (inputs_x.reshape(count_of_blocks, SPAN, MH, MP), inputs_b.reshape(count_of_blocks, SPAN, NS), inputs_c.reshape(count_of_blocks, SPAN, NS), steps_dt.reshape(count_of_blocks, SPAN, MH), segment.reshape(count_of_blocks, SPAN))
    (carried, last_seg), results = lax.scan(jax.checkpoint(advance), (state_in, segment_before), blocks)
    return (results.reshape(inputs_x.shape), carried)

def attention(query_rows, key_rows, value_rows, segment, positions):
    sequence_length = query_rows.shape[0]
    rows_per_block = math.gcd(sequence_length, 512)
    query_group_width = QUERY_HEADS // KEY_VALUE_HEADS
    score_scale = HEAD_SIZE ** (-0.5)

    def one_block(inputs):
        query_block_rows, block_seg, block_pos = inputs
        heads_grouped = query_block_rows.reshape(rows_per_block, KEY_VALUE_HEADS, query_group_width, HEAD_SIZE)
        scores = low_back(jnp.einsum('qkgd,skd->kgqs', heads_grouped, key_rows, precision=HIGHEST) * score_scale)
        visible = (block_seg[:, None] == segment[None, :]) & (block_pos[:, None] >= positions[None, :])
        scores = jnp.where(visible[None, None], scores, NEGATIVE_FILL)
        prob_all = jax.nn.softmax(scores, axis=-1)
        mixed = jnp.einsum('kgqs,skd->qkgd', lower_bound(prob_all), value_rows, precision=HIGHEST)
        return mixed.reshape(rows_per_block, QUERY_HEADS * HEAD_SIZE)
    count_of_blocks = sequence_length // rows_per_block
    outputs = lax.map(jax.checkpoint(one_block), (query_rows.reshape(count_of_blocks, rows_per_block, QUERY_HEADS, HEAD_SIZE), segment.reshape(count_of_blocks, rows_per_block), positions.reshape(count_of_blocks, rows_per_block)))
    return outputs.reshape(sequence_length, QUERY_HEADS * HEAD_SIZE)

def layer_forward(x_rows, segment, device_places, positions, params):
    w_attn, w_ssm_in, w_dt, w_out, w_gate_up, w_down, norm_gain, mlp_gain, ssm_gain, conv_w, conv_b, a_log, dt_bias, d_skip = params
    sequence_length = x_rows.shape[0]
    query_width = QUERY_HEADS * HEAD_SIZE
    key_value_width = KEY_VALUE_HEADS * HEAD_SIZE
    ssm_width = MH * MP
    normed = lower_bound(x_rows * rms_scale(x_rows) * norm_gain)
    attention_projected = low_back(jnp.dot(normed, w_attn, precision=HIGHEST))
    ssm_proj = low_back(jnp.dot(normed, w_ssm_in, precision=HIGHEST))
    step_proj = low_back(jnp.dot(normed, w_dt, precision=HIGHEST))
    query_rows = lower_bound(rotary_embed(attention_projected[:, :query_width].reshape(sequence_length, QUERY_HEADS, HEAD_SIZE), device_places, 1.0))
    key_rows = lower_bound(rotary_embed(attention_projected[:, query_width:query_width + key_value_width].reshape(sequence_length, KEY_VALUE_HEADS, HEAD_SIZE), device_places, 1.0))
    value_rows = lower_bound(attention_projected[:, query_width + key_value_width:].reshape(sequence_length, KEY_VALUE_HEADS, HEAD_SIZE))
    attended = attention(query_rows, key_rows, value_rows, segment, positions)
    gate_z = ssm_proj[:, :ssm_width]
    raw_xbc = ssm_proj[:, ssm_width:]
    extended = jnp.concatenate([jnp.zeros((CONV - 1, raw_xbc.shape[1]), jnp.float32), raw_xbc], axis=0)
    ext_segment = jnp.concatenate([jnp.full((CONV - 1,), -1, jnp.int32), segment])
    conv_out = conv_mix(extended, ext_segment, conv_w, conv_b)
    inputs_x = lower_bound(conv_out[:, :ssm_width]).reshape(sequence_length, MH, MP)
    inputs_b = lower_bound(conv_out[:, ssm_width:ssm_width + NS])
    inputs_c = lower_bound(conv_out[:, ssm_width + NS:])
    steps_dt = jax.nn.softplus(step_proj + dt_bias)
    ssm_out, final_state = ssd_blocks(inputs_x, inputs_b, inputs_c, steps_dt, a_log, d_skip, segment, jnp.array(-1, jnp.int32), jnp.zeros((MH, MP, NS), jnp.float32), lower_bound)
    gated = ssm_out.reshape(sequence_length, ssm_width) * jax.nn.silu(gate_z)
    ssm_normed = gated * rms_scale(gated) * ssm_gain
    joined = jnp.concatenate([lower_bound(low_back(attended)), lower_bound(ssm_normed)], axis=1)
    middle = x_rows + low_back(jnp.dot(joined, w_out, precision=HIGHEST))
    normed_two = lower_bound(middle * rms_scale(middle) * mlp_gain)
    gate_up = low_back(jnp.dot(normed_two, w_gate_up, precision=HIGHEST))
    hidden = lower_bound(jax.nn.silu(gate_up[:, :FF]) * gate_up[:, FF:])
    return middle + jnp.dot(hidden, w_down, precision=HIGHEST)

def reference(layer_input, seq_lengths, w_attn, w_ssm_in, w_dt, w_out, w_gate_up, w_down, norm_gain, mlp_gain, ssm_gain, conv_w, conv_b, a_log, dt_bias, d_skip, out_grad):
    positions = jnp.arange(SEQ_TOK, dtype=jnp.int32)
    params = tuple((weight_arr.astype(jnp.float32) for weight_arr in (w_attn, w_ssm_in, w_dt, w_out, w_gate_up, w_down, norm_gain, mlp_gain, ssm_gain, conv_w, conv_b, a_log, dt_bias, d_skip)))
    x_float = layer_input.astype(jnp.float32)

    def forward(x_all, *param_list):
        results = []
        for group_idx in range(GROUPS):
            segment, device_places = segments(seq_lengths[group_idx], positions)
            results.append(layer_forward(x_all[group_idx], segment, device_places, positions, param_list))
        return jnp.stack(results)
    out_full, pullback = jax.vjp(forward, x_float, *params)
    grads = pullback(out_grad.astype(jnp.float32))
    return (out_full.astype(jnp.bfloat16), grads[0], grads[1], grads[2], grads[3], grads[4], grads[5], grads[6], grads[7], grads[8], grads[9], grads[10], grads[11], grads[12], grads[13], grads[14])
```

```python
import math

import jax
import jax.numpy as jnp
from jax import lax
from jax.sharding import PartitionSpec as P

QUERY_HEADS = 8
KEY_VALUE_HEADS = 2
HEAD_SIZE = 64
MH = 24
MP = 64
NS = 128
FF = 2048
CONV = 4
SPAN = 128


HIGHEST = lax.Precision.HIGHEST
NEGATIVE_FILL = -1e30
ROPE_BASE = 10000.0
NORM_EPS = 1e-06
block_limit = 512


def shifted(block, axis, distance):
    devices = range(lax.axis_size(axis))
    route = [(i - distance, i) for i in devices if i - distance in devices]
    return lax.ppermute(block, axis, route)


def prefix(array, axis, combine, identity):
    peers, place = (lax.axis_size(axis), lax.axis_index(axis))
    everything = jax.tree.map(
        lambda part, kind: lax.all_gather(part.astype(kind), axis),
        array,
        (jnp.bfloat16, jnp.bfloat16),
    )
    start = jax.tree.map(
        lambda part, zero: jnp.broadcast_to(jnp.asarray(zero, part.dtype), part.shape),
        array,
        identity,
    )

    def step(k, before):
        reached = k < place
        new = combine(
            before, jax.tree.map(lambda part, own: part[k].astype(own.dtype), everything, array)
        )
        return jax.tree.map(lambda a, b: jnp.where(reached, a, b), new, before)

    return lax.fori_loop(0, peers, step, start)


def entering_2(array, axis, join, neutral):
    count = lax.axis_size(axis)
    place = lax.axis_index(axis)
    ahead = count - 1 - place
    gathered = jax.tree.map(
        lambda a, kind: lax.all_gather(a.astype(kind), axis),
        array,
        jax.tree.map(lambda a: jnp.bfloat16 if a.dtype == jnp.float32 else a.dtype, array),
    )
    state = jax.tree.map(lambda a, e: jnp.zeros_like(a) + jnp.asarray(e, a.dtype), array, neutral)

    def one(step, state):
        source = count - 1 - step
        return join(
            state,
            jax.tree.map(
                lambda a, own: lax.dynamic_index_in_dim(a, source, 0, False).astype(own.dtype),
                gathered,
                array,
            ),
        )

    return lax.fori_loop(0, ahead, one, state)


def is_fast(width):
    return lax.axis_size("seq") == 8 and lax.axis_size("batch") == 4 and width % (32 * 32) == 0


def swap(value, axis, bit):
    route = [(i, i ^ bit) for i in range(lax.axis_size(axis))]
    return lax.ppermute(value, axis, route)


def gather_stages(shard, x_first):
    rows = jnp.concatenate([shard, swap(shard, "seq", 4)], axis=0)
    rows = jnp.concatenate([rows, swap(rows, "seq", 2)], axis=0)
    along_z = rows
    if x_first:
        rows = jnp.concatenate([rows, swap(rows, "seq", 1)], axis=0)
        rows = jnp.concatenate([rows, swap(rows, "batch", 2)], axis=0)
    else:
        rows = jnp.stack([rows, swap(rows, "batch", 2)], axis=0)
        rows = jnp.stack([rows, swap(rows, "seq", 1)], axis=1)
        rows = rows.reshape(-1, rows.shape[-1])
    return along_z, jnp.concatenate([rows, swap(rows, "batch", 1)], axis=0)


def add_narrow(own, other):
    return (own.astype(jnp.float32) + other.astype(jnp.float32)).astype(jnp.bfloat16)


def scatter_stages(rows, y_first):
    size, cols = rows.shape
    if y_first:
        half = size // 2
        rows = add_narrow(rows[:half], swap(rows[half:], "batch", 2))
        half = half // 2
        rows = add_narrow(rows[:half], swap(rows[half:], "seq", 1))
    else:
        split = rows.reshape(2, 2, size // 4, cols)
        split = add_narrow(split[:, 0], swap(split[:, 1], "seq", 1))
        rows = add_narrow(split[0], swap(split[1], "batch", 2))
    half = rows.shape[0] // 2
    rows = add_narrow(rows[:half], swap(rows[half:], "seq", 2))
    half = half // 2
    return rows[:half].astype(jnp.float32) + swap(rows[half:], "seq", 4).astype(jnp.float32)


def weight_grad(left, right, fast, y_first):
    if not fast:
        full = jnp.einsum("td,tc->dc", left, right, preferred_element_type=jnp.float32)
        return lax.psum_scatter(full, ("seq", "batch"), scatter_dimension=0, tiled=True)
    half = left.shape[1] // 2
    lefts = jnp.concatenate([left[:, :half], swap(left[:, half:], "batch", 1)], axis=0)
    rights = jnp.concatenate([right, swap(right, "batch", 1)], axis=0)
    partial = jnp.einsum("td,tc->dc", lefts, rights, preferred_element_type=jnp.float32)
    return scatter_stages(partial.astype(jnp.bfloat16), y_first)


def total_small(arrays, fast):
    flat = jnp.concatenate([a.reshape(-1) for a in arrays])
    size = flat.shape[0]
    flat = jnp.pad(flat, (0, -size % 1024)).reshape(-1, 128)
    if fast:
        for axis, bit in (("batch", 1), ("batch", 2), ("seq", 1), ("seq", 2), ("seq", 4)):
            flat = flat + swap(flat, axis, bit)
    else:
        flat = lax.psum(flat, ("seq", "batch"))
    flat = flat.reshape(-1)
    out, start = [], 0
    for a in arrays:
        out.append(flat[start : start + a.size].reshape(a.shape))
        start += a.size
    return out


def own_order(width, fast):
    blocks = 32
    per = width // blocks
    row = lax.broadcasted_iota(jnp.int32, (width, width), 0)
    col = lax.broadcasted_iota(jnp.int32, (width, width), 1)
    if not fast:
        return (row == col).astype(jnp.bfloat16)
    me = lax.axis_index("seq") * 4 + lax.axis_index("batch")
    j = col // per
    flipped = (j & 1) * 16 + (j & 2) * 4 + (j & 4) + (j & 8) // 4 + (j & 16) // 16
    source = (flipped ^ me) * per + col % per
    return (row == source).astype(jnp.bfloat16)


def rms_scale(value_rows):
    return lax.rsqrt(jnp.mean(value_rows * value_rows, axis=-1, keepdims=True) + NORM_EPS)


def norm_back(value_rows, scales, gains, grads):
    gain_grad = jnp.sum(grads * value_rows * scales, axis=0)
    inner = grads * gains
    coeff = jnp.mean(inner * value_rows, axis=-1, keepdims=True)
    return (scales * (inner - value_rows * scales * scales * coeff), gain_grad)


def rotary_embed(value_rows, device_places, direction):
    half_dim = value_rows.shape[-1] // 2
    freqs = ROPE_BASE ** (-jnp.arange(half_dim, dtype=jnp.float32) / half_dim)
    angles = direction * device_places.astype(jnp.float32)[:, None] * freqs[None, :]
    cosine = jnp.cos(angles)[:, None, :]
    sine = jnp.sin(angles)[:, None, :]
    first_half = value_rows[..., :half_dim]
    second_half = value_rows[..., half_dim:]
    return jnp.concatenate(
        [first_half * cosine - second_half * sine, second_half * cosine + first_half * sine],
        axis=-1,
    )


def segments(lengths, positions):
    ends = jnp.cumsum(lengths)
    passed = ends[None, :] <= positions[:, None]
    segment = jnp.sum(passed.astype(jnp.int32), axis=1)
    device_places = positions - jnp.sum(jnp.where(passed, lengths[None, :], 0), axis=1)
    return (segment, device_places)


def rounded(value_rows):
    narrow = lax.optimization_barrier(value_rows.astype(jnp.bfloat16)).astype(jnp.float32)
    return value_rows + lax.stop_gradient(narrow - value_rows)


def keep_same(running_total):
    return running_total


def conv_mix(extended, ext_segment, conv_weight, conv_bias):
    row_count = extended.shape[0] - (CONV - 1)
    summed = conv_bias[None, :]
    for lagged in range(CONV):
        same_seq = (ext_segment[lagged : lagged + row_count] == ext_segment[CONV - 1 :]).astype(
            extended.dtype
        )
        summed = (
            summed
            + conv_weight[lagged][None, :]
            * extended[lagged : lagged + row_count]
            * same_seq[:, None]
        )
    return jax.nn.silu(summed)


def ssd_blocks(
    inputs_x,
    inputs_b,
    inputs_c,
    inner_all,
    steps_dt,
    log_rates,
    skip_gain,
    segment,
    segment_before,
    state_in,
    rounder,
):
    total_rows = inputs_x.shape[0]
    count_of_blocks = total_rows // SPAN
    decay_rates = jnp.exp(log_rates)
    offsets = jnp.arange(SPAN)
    causal = offsets[:, None] >= offsets[None, :]

    def ssd_advance(carry_in, pieces):
        carried, previous = carry_in
        block_x, block_b, block_c, inner_cb, block_dt, block_seg = pieces
        log_decay = jnp.cumsum(-block_dt * decay_rates[None, :], axis=0)
        allowed = (block_seg[:, None] == block_seg[None, :]) & causal
        spread = log_decay[:, None, :] - log_decay[None, :, :]
        decays = jnp.exp(jnp.where(allowed[:, :, None], spread, NEGATIVE_FILL))
        mixing = rounder(inner_cb[:, :, None] * decays * block_dt[None, :, :])
        result = jnp.einsum("tsh,shp->thp", mixing, block_x, precision=HIGHEST)
        linked = (block_seg == previous).astype(block_x.dtype)
        entering = jnp.exp(log_decay) * linked[:, None]
        result = result + entering[:, :, None] * jnp.einsum(
            "hpn,tn->thp", carried, block_c, precision=HIGHEST
        )
        result = result + skip_gain[None, :, None] * block_x
        same_last = (block_seg == block_seg[-1]).astype(block_x.dtype)
        leaving = jnp.exp(log_decay[-1][None, :] - log_decay) * same_last[:, None] * block_dt
        carried = entering[-1][:, None, None] * carried + jnp.einsum(
            "th,thp,tn->hpn", leaving, block_x, block_b, precision=HIGHEST
        )
        return ((carried, block_seg[-1]), result)

    blocks = (
        inputs_x.reshape(count_of_blocks, SPAN, MH, MP),
        inputs_b.reshape(count_of_blocks, SPAN, NS),
        inputs_c.reshape(count_of_blocks, SPAN, NS),
        inner_all,
        steps_dt.reshape(count_of_blocks, SPAN, MH),
        segment.reshape(count_of_blocks, SPAN),
    )
    (carried, last_seg), results = lax.scan(ssd_advance, (state_in, segment_before), blocks)
    return (results.reshape(inputs_x.shape), carried)


def chain(earlier, later):
    return (earlier[0] * later[0], later[0][:, None, None] * earlier[1] + later[1])


def on_device(
    layer_input,
    seq_lengths,
    w_attn,
    w_ssm_in,
    w_dt,
    w_out,
    w_gate_up,
    w_down,
    norm_gain,
    mlp_gain,
    ssm_gain,
    conv_w,
    conv_b,
    a_log,
    dt_bias,
    d_skip,
    out_grad,
):
    token_rows = layer_input.shape[1]
    query_width = QUERY_HEADS * HEAD_SIZE
    key_value_width = KEY_VALUE_HEADS * HEAD_SIZE
    ssm_width = MH * MP
    xbc_width = ssm_width + 2 * NS
    query_group_width = QUERY_HEADS // KEY_VALUE_HEADS
    score_scale = HEAD_SIZE ** (-0.5)
    seq_lens = seq_lengths[0]
    first_pos = lax.axis_index("seq") * token_rows
    positions = first_pos + jnp.arange(token_rows, dtype=jnp.int32)
    segment, device_places = segments(seq_lens, positions)
    segment_before = segments(seq_lens, positions[:1] - 1)[0][0]
    width = layer_input.shape[2]
    fast = is_fast(width)
    order = own_order(width, fast)

    def to_own(value):
        if not fast:
            return value
        return jnp.dot(value, order, preferred_element_type=jnp.float32).astype(value.dtype)

    def to_plain(value):
        if not fast:
            return value
        return jnp.einsum("tc,dc->td", value, order, preferred_element_type=jnp.float32)

    def to_plain_wide(value):
        if not fast:
            return value
        return jnp.einsum("tc,dc->td", value, order.astype(jnp.float32), precision=HIGHEST)

    def gain_own(value):
        if not fast:
            return value
        return jnp.dot(value[None], order.astype(jnp.float32), precision=HIGHEST)[0]

    norm_gain, mlp_gain = gain_own(norm_gain), gain_own(mlp_gain)
    x_rows = to_own(layer_input[0]).astype(jnp.float32)
    grad_rows = to_own(out_grad[0])
    step_pad = jnp.pad(w_dt, ((0, 0), (0, 128 - MH)))
    shards = (
        jnp.concatenate([w_ssm_in[:, ssm_width:], step_pad], axis=1),
        jnp.concatenate([w_attn, w_ssm_in[:, :ssm_width]], axis=1),
        w_out.T[:, : w_out.shape[0] // 2],
        w_out.T[:, w_out.shape[0] // 2 :],
        w_gate_up[:, :FF],
        w_gate_up[:, FF:],
        w_down.T[:, : FF // 2],
        w_down.T[:, FF // 2 :],
    )
    full = []
    ahead = None
    for i in range(0, 8, 2):
        pair = shards[i : i + 2]
        if fast:
            if ahead is not None:
                pair, ahead = lax.optimization_barrier((pair, ahead))
            za, fa = gather_stages(pair[0], True)
            zb, fb = gather_stages(pair[1], False)
            ahead = (za, zb)
            full += [fa, fb]
        else:
            full += [lax.all_gather(p, ("seq", "batch"), axis=0, tiled=True) for p in pair]
    full_conv, full_mix, out_a, out_b, full_gate, full_up, down_a, down_b = full
    scale_one = rms_scale(x_rows)
    normed = (x_rows * scale_one * norm_gain).astype(jnp.bfloat16)
    conv_proj = jnp.dot(normed, full_conv, preferred_element_type=jnp.float32)
    mix_proj = jnp.dot(normed, full_mix, preferred_element_type=jnp.float32)
    attn_width = query_width + 2 * key_value_width
    attention_projected = mix_proj[:, :attn_width]
    step_proj = conv_proj[:, xbc_width : xbc_width + MH]
    query_rows = rotary_embed(
        attention_projected[:, :query_width].reshape(token_rows, QUERY_HEADS, HEAD_SIZE),
        device_places,
        1.0,
    ).astype(jnp.bfloat16)
    flattened_keys = (
        rotary_embed(
            attention_projected[:, query_width : query_width + key_value_width].reshape(
                token_rows, KEY_VALUE_HEADS, HEAD_SIZE
            ),
            device_places,
            1.0,
        )
        .astype(jnp.bfloat16)
        .reshape(token_rows, key_value_width)
    )
    flattened_values = attention_projected[:, query_width + key_value_width :].astype(jnp.bfloat16)
    heads_of_queries = query_rows.reshape(token_rows, KEY_VALUE_HEADS, query_group_width, HEAD_SIZE)

    def visible(query_pos, query_seg, key_pos, key_seg):
        return (query_seg[:, None] == key_seg[None, :]) & (query_pos[:, None] >= key_pos[None, :])

    def key_blocks(piece_in):
        incoming_keys, incoming_values = piece_in
        piece_rows = incoming_keys.shape[0]
        rows_per_block = math.gcd(piece_rows, block_limit)
        count_of_blocks = piece_rows // rows_per_block
        starts = jnp.arange(count_of_blocks, dtype=jnp.int32) * rows_per_block
        return (
            (
                incoming_keys.reshape(count_of_blocks, rows_per_block, KEY_VALUE_HEADS, HEAD_SIZE),
                incoming_values.reshape(
                    count_of_blocks, rows_per_block, KEY_VALUE_HEADS, HEAD_SIZE
                ),
                starts,
            ),
            rows_per_block,
        )

    start_state = (
        jnp.full((KEY_VALUE_HEADS, query_group_width, token_rows), NEGATIVE_FILL, jnp.float32),
        jnp.zeros((KEY_VALUE_HEADS, query_group_width, token_rows), jnp.float32),
        jnp.zeros((KEY_VALUE_HEADS, query_group_width, token_rows, HEAD_SIZE), jnp.float32),
    )
    running_total = start_state
    all_pairs = lax.all_gather(
        jnp.concatenate([flattened_keys, flattened_values], axis=1), "seq", axis=0, tiled=True
    )
    all_keys, all_values = all_pairs[:, :key_value_width], all_pairs[:, key_value_width:]
    blocks, rows_per_block = key_blocks((all_keys, all_values))

    def attend_advance(state_now, pieces):
        key_blk, value_blk, key_first = pieces
        key_pos = key_first + jnp.arange(rows_per_block, dtype=jnp.int32)
        key_seg = segments(seq_lens, key_pos)[0]
        needed = (key_first <= positions[-1]) & (key_seg[-1] >= segment[0])

        def attend_update(state_in):
            row_max, weight_sum, accumulated = state_in
            scores = (
                jnp.einsum(
                    "qkgd,skd->kgqs", heads_of_queries, key_blk, preferred_element_type=jnp.float32
                )
                * score_scale
            )
            allowed = visible(positions, segment, key_pos, key_seg)[None, None]
            scores = jnp.where(allowed, scores, NEGATIVE_FILL)
            new_max = jnp.maximum(row_max, jnp.max(scores, axis=-1))
            shrink = jnp.exp(row_max - new_max)
            prob_blk = jnp.where(allowed, jnp.exp(scores - new_max[..., None]), 0.0)
            weight_sum = weight_sum * shrink + jnp.sum(prob_blk, axis=-1)
            accumulated = accumulated * shrink[..., None] + jnp.einsum(
                "kgqs,skd->kgqd",
                prob_blk.astype(jnp.bfloat16),
                value_blk,
                preferred_element_type=jnp.float32,
            )
            return (new_max, weight_sum, accumulated)

        return (lax.cond(needed, attend_update, keep_same, state_now), None)

    running_total, unused_out = lax.scan(attend_advance, running_total, blocks)
    row_max, weight_sum, accumulated = running_total
    attn_heads = accumulated / weight_sum[..., None]
    log_total = row_max + jnp.log(weight_sum)
    attended = (
        attn_heads.transpose(2, 0, 1, 3).reshape(token_rows, query_width).astype(jnp.bfloat16)
    )
    gate_z = mix_proj[:, attn_width:]
    raw_xbc = conv_proj[:, :xbc_width]
    rim_rows = shifted(raw_xbc[token_rows - (CONV - 1) :], "seq", 1)
    extended = jnp.concatenate([rim_rows, raw_xbc], axis=0)
    ext_pos = first_pos - (CONV - 1) + jnp.arange(token_rows + CONV - 1, dtype=jnp.int32)
    ext_segment = segments(seq_lens, ext_pos)[0]

    def conv_local(ext_rows, conv_weight, conv_bias):
        return conv_mix(ext_rows, ext_segment, conv_weight, conv_bias)

    conv_out, conv_pullback = jax.vjp(conv_local, extended, conv_w, conv_b)
    block_total = token_rows // SPAN
    narrow_b = conv_out[:, ssm_width : ssm_width + NS].astype(jnp.bfloat16)
    narrow_c = conv_out[:, ssm_width + NS :].astype(jnp.bfloat16)
    inputs_x = (
        conv_out[:, :ssm_width].astype(jnp.bfloat16).astype(jnp.float32).reshape(token_rows, MH, MP)
    )
    inputs_b = narrow_b.astype(jnp.float32)
    inputs_c = narrow_c.astype(jnp.float32)
    inner_all = jnp.einsum(
        "btn,bsn->bts",
        narrow_c.reshape(block_total, SPAN, NS),
        narrow_b.reshape(block_total, SPAN, NS),
        preferred_element_type=jnp.float32,
    )
    steps_dt = jax.nn.softplus(step_proj + dt_bias)

    def ssd_local(block_x, block_b, block_c, inner_in, block_dt, log_rates, skip_gain, carried_in):
        return ssd_blocks(
            block_x,
            block_b,
            block_c,
            inner_in,
            block_dt,
            log_rates,
            skip_gain,
            segment,
            segment_before,
            carried_in,
            rounded,
        )

    zero_state = jnp.zeros((MH, MP, NS), jnp.float32)
    ssm_local, state_local = ssd_local(
        inputs_x, inputs_b, inputs_c, inner_all, steps_dt, a_log, d_skip, zero_state
    )
    running_decay = jnp.cumsum(-steps_dt * jnp.exp(a_log)[None, :], axis=0)
    linked = (segment == segment_before).astype(jnp.float32)
    entering = jnp.exp(running_decay) * linked[:, None]
    through = entering[-1]
    chain_identity = (jnp.ones((MH,), jnp.float32), zero_state)
    unused_rate, state_in = prefix((through, state_local), "seq", chain, chain_identity)
    ssm_out = ssm_local + entering[:, :, None] * jnp.einsum(
        "hpn,tn->thp", state_in, inputs_c, precision=HIGHEST
    )
    ssm_flat = ssm_out.reshape(token_rows, ssm_width)
    silu_z = jax.nn.silu(gate_z)
    gated = ssm_flat * silu_z
    scale_gated = rms_scale(gated)
    ssm_normed = gated * scale_gated * ssm_gain
    joined = jnp.concatenate([attended, ssm_normed.astype(jnp.bfloat16)], axis=1)
    half_in = joined.shape[1] // 2

    def narrow_out(left, parts):
        cut = left.shape[1] // 2
        return jnp.einsum(
            "tc,dc->td", left[:, :cut], parts[0], preferred_element_type=jnp.float32
        ) + jnp.einsum("tc,dc->td", left[:, cut:], parts[1], preferred_element_type=jnp.float32)

    middle = x_rows + narrow_out(joined, (out_a, out_b))
    scale_two = rms_scale(middle)
    normed_two = (middle * scale_two * mlp_gain).astype(jnp.bfloat16)
    gate_part = jnp.dot(normed_two, full_gate, preferred_element_type=jnp.float32)
    up_part = jnp.dot(normed_two, full_up, preferred_element_type=jnp.float32)
    hidden = (jax.nn.silu(gate_part) * up_part).astype(jnp.bfloat16)
    layer_out = middle + narrow_out(hidden, (down_a, down_b))
    g_down = [
        weight_grad(grad_rows, hidden[:, : FF // 2], fast, True),
        weight_grad(grad_rows, hidden[:, FF // 2 :], fast, False),
    ]
    d_hidden = jnp.concatenate(
        [
            jnp.dot(grad_rows, down_a, preferred_element_type=jnp.float32),
            jnp.dot(grad_rows, down_b, preferred_element_type=jnp.float32),
        ],
        axis=1,
    )
    sig_gate = jax.nn.sigmoid(gate_part)
    d_gate = d_hidden * up_part * (sig_gate * (1.0 + gate_part * (1.0 - sig_gate)))
    d_up = d_hidden * gate_part * sig_gate
    d_gate, d_up = d_gate.astype(jnp.bfloat16), d_up.astype(jnp.bfloat16)
    g_gate_up = [
        weight_grad(normed_two, d_gate, fast, True),
        weight_grad(normed_two, d_up, fast, False),
    ]
    d_normed_two = narrow_out(
        jnp.concatenate([d_gate, d_up], axis=1), (full_gate, full_up)
    )
    d_middle_norm, g_mlp_gain = norm_back(middle, scale_two, mlp_gain, d_normed_two)
    d_middle = grad_rows.astype(jnp.float32) + d_middle_norm
    d_mixer = d_middle.astype(jnp.bfloat16)
    g_out = [
        weight_grad(d_mixer, joined[:, :half_in], fast, True),
        weight_grad(d_mixer, joined[:, half_in:], fast, False),
    ]
    d_joined = jnp.concatenate(
        [
            jnp.dot(d_mixer, out_a, preferred_element_type=jnp.float32),
            jnp.dot(d_mixer, out_b, preferred_element_type=jnp.float32),
        ],
        axis=1,
    )
    attended_gradient = d_joined[:, :query_width].astype(jnp.bfloat16)
    d_ssm_normed = d_joined[:, query_width:]
    d_gated, g_ssm_gain = norm_back(gated, scale_gated, ssm_gain, d_ssm_normed)
    d_ssm_out = (d_gated * silu_z).reshape(token_rows, MH, MP)
    sig_z = jax.nn.sigmoid(gate_z)
    d_gate_z = d_gated * ssm_flat * (sig_z * (1.0 + gate_z * (1.0 - sig_z)))
    pull_state = jnp.einsum("th,thp,tn->hpn", entering, d_ssm_out, inputs_c, precision=HIGHEST)
    unused_rate, d_state_out = entering_2((through, pull_state), "seq", chain, chain_identity)
    unused_out, ssd_pullback = jax.vjp(
        ssd_local, inputs_x, inputs_b, inputs_c, inner_all, steps_dt, a_log, d_skip, state_in
    )
    g_inputs_x, g_part_b, g_part_c, g_inner, g_steps, g_a_log, g_d_skip, unused_state = (
        ssd_pullback((d_ssm_out, d_state_out))
    )
    block_b = inputs_b.reshape(block_total, SPAN, NS)
    block_c = inputs_c.reshape(block_total, SPAN, NS)
    g_inputs_c = g_part_c + jnp.einsum("bts,bsn->btn", g_inner, block_b, precision=HIGHEST).reshape(
        token_rows, NS
    )
    g_inputs_b = g_part_b + jnp.einsum("bts,btn->bsn", g_inner, block_c, precision=HIGHEST).reshape(
        token_rows, NS
    )
    d_step_pre = g_steps * jax.nn.sigmoid(step_proj + dt_bias)
    g_dt_bias = jnp.sum(d_step_pre, axis=0)
    d_step_proj = d_step_pre.astype(jnp.bfloat16)
    d_conv_out = jnp.concatenate(
        [g_inputs_x.reshape(token_rows, ssm_width), g_inputs_b, g_inputs_c], axis=1
    )
    g_extended, g_conv_w, g_conv_b = conv_pullback(d_conv_out)
    back_rim = shifted(g_extended[: CONV - 1], "seq", -1)
    d_raw = g_extended[CONV - 1 :] + jnp.concatenate(
        [jnp.zeros((token_rows - (CONV - 1), xbc_width), jnp.float32), back_rim], axis=0
    )
    d_step_pad = jnp.pad(d_step_proj, ((0, 0), (0, 128 - MH)))
    d_conv_proj = jnp.concatenate([d_raw.astype(jnp.bfloat16), d_step_pad], axis=1)
    head_gradients = attended_gradient.reshape(
        token_rows, KEY_VALUE_HEADS, query_group_width, HEAD_SIZE
    )
    delta = jnp.einsum("qkgd,kgqd->kgq", head_gradients.astype(jnp.float32), attn_heads)
    running_total = jnp.zeros(
        (KEY_VALUE_HEADS, query_group_width, token_rows, HEAD_SIZE), jnp.float32
    )
    blocks, query_rows_per_block = key_blocks((all_keys, all_values))

    def query_advance(grad_now, pieces):
        key_blk, value_blk, key_first = pieces
        key_pos = key_first + jnp.arange(query_rows_per_block, dtype=jnp.int32)
        key_seg = segments(seq_lens, key_pos)[0]
        needed = (key_first <= positions[-1]) & (key_seg[-1] >= segment[0])

        def query_update(grad_in):
            scores = (
                jnp.einsum(
                    "qkgd,skd->kgqs", heads_of_queries, key_blk, preferred_element_type=jnp.float32
                )
                * score_scale
            )
            allowed = visible(positions, segment, key_pos, key_seg)[None, None]
            prob_blk = jnp.where(allowed, jnp.exp(scores - log_total[..., None]), 0.0)
            d_prob = jnp.einsum(
                "qkgd,skd->kgqs", head_gradients, value_blk, preferred_element_type=jnp.float32
            )
            d_score = (prob_blk * (d_prob - delta[..., None])).astype(jnp.bfloat16)
            return (
                grad_in
                + jnp.einsum("kgqs,skd->kgqd", d_score, key_blk, preferred_element_type=jnp.float32)
                * score_scale
            )

        return (lax.cond(needed, query_update, keep_same, grad_now), None)

    running_total, unused_out = lax.scan(query_advance, running_total, blocks)
    d_queries = running_total
    all_lse, all_delta = (
        lax.all_gather(log_total.reshape(QUERY_HEADS, token_rows), "seq", axis=1, tiled=True),
        lax.all_gather(delta.reshape(QUERY_HEADS, token_rows), "seq", axis=1, tiled=True),
    )
    heads_of_keys = flattened_keys.reshape(token_rows, KEY_VALUE_HEADS, HEAD_SIZE)
    heads_of_values = flattened_values.reshape(token_rows, KEY_VALUE_HEADS, HEAD_SIZE)
    zeroed_key_value = jnp.zeros((token_rows, KEY_VALUE_HEADS, HEAD_SIZE), jnp.float32)
    running_total = (zeroed_key_value, zeroed_key_value)
    incoming_query = lax.all_gather(
        query_rows.reshape(token_rows, query_width), "seq", axis=0, tiled=True
    )
    input_gradient_rows = lax.all_gather(attended_gradient, "seq", axis=0, tiled=True)
    piece_rows = incoming_query.shape[0]
    key_rows_per_block = math.gcd(piece_rows, block_limit)
    count_of_blocks = piece_rows // key_rows_per_block
    blocks = (
        incoming_query.reshape(
            count_of_blocks, key_rows_per_block, KEY_VALUE_HEADS, query_group_width, HEAD_SIZE
        ),
        input_gradient_rows.reshape(
            count_of_blocks, key_rows_per_block, KEY_VALUE_HEADS, query_group_width, HEAD_SIZE
        ),
        jnp.arange(count_of_blocks, dtype=jnp.int32) * key_rows_per_block,
    )

    def key_advance(grad_now, pieces):
        query_blk, dgrad_blk, query_first = pieces
        query_pos = query_first + jnp.arange(key_rows_per_block, dtype=jnp.int32)
        query_seg = segments(seq_lens, query_pos)[0]
        needed = (query_pos[-1] >= positions[0]) & (query_seg[0] <= segment[-1])

        def key_update(grad_in):
            key_grad, value_grad = grad_in
            blk_lse = lax.dynamic_slice_in_dim(all_lse, query_first, key_rows_per_block, 1).reshape(
                KEY_VALUE_HEADS, query_group_width, key_rows_per_block
            )
            blk_delta = lax.dynamic_slice_in_dim(
                all_delta, query_first, key_rows_per_block, 1
            ).reshape(KEY_VALUE_HEADS, query_group_width, key_rows_per_block)
            scores = (
                jnp.einsum(
                    "qkgd,skd->kgqs", query_blk, heads_of_keys, preferred_element_type=jnp.float32
                )
                * score_scale
            )
            allowed = visible(query_pos, query_seg, positions, segment)[None, None]
            prob_blk = jnp.where(allowed, jnp.exp(scores - blk_lse[..., None]), 0.0)
            d_prob = jnp.einsum(
                "qkgd,skd->kgqs", dgrad_blk, heads_of_values, preferred_element_type=jnp.float32
            )
            d_score = (prob_blk * (d_prob - blk_delta[..., None])).astype(jnp.bfloat16)
            value_grad = value_grad + jnp.einsum(
                "kgqs,qkgd->skd",
                prob_blk.astype(jnp.bfloat16),
                dgrad_blk,
                preferred_element_type=jnp.float32,
            )
            key_grad = (
                key_grad
                + jnp.einsum(
                    "kgqs,qkgd->skd", d_score, query_blk, preferred_element_type=jnp.float32
                )
                * score_scale
            )
            return (key_grad, value_grad)

        return (lax.cond(needed, key_update, keep_same, grad_now), None)

    running_total, unused_out = lax.scan(key_advance, running_total, blocks)
    d_keys, d_values = running_total
    d_query_flat = rotary_embed(
        d_queries.transpose(2, 0, 1, 3).reshape(token_rows, QUERY_HEADS, HEAD_SIZE),
        device_places,
        -1.0,
    ).reshape(token_rows, query_width)
    d_key_flat = rotary_embed(d_keys, device_places, -1.0).reshape(token_rows, key_value_width)
    d_attn_proj = jnp.concatenate(
        [d_query_flat, d_key_flat, d_values.reshape(token_rows, key_value_width)], axis=1
    ).astype(jnp.bfloat16)
    d_mix_proj = jnp.concatenate([d_attn_proj, d_gate_z.astype(jnp.bfloat16)], axis=1)
    g_conv_in = weight_grad(normed, d_conv_proj, fast, True)
    g_mix_in = weight_grad(normed, d_mix_proj, fast, False)
    d_normed = jnp.einsum(
        "tc,dc->td", d_conv_proj, full_conv, preferred_element_type=jnp.float32
    ) + jnp.einsum("tc,dc->td", d_mix_proj, full_mix, preferred_element_type=jnp.float32)
    d_input_norm, g_norm_gain = norm_back(x_rows, scale_one, norm_gain, d_normed)
    input_grad = d_middle + d_input_norm
    grad_attn = g_mix_in[:, :attn_width]
    grad_ssm_in = jnp.concatenate([g_mix_in[:, attn_width:], g_conv_in[:, :xbc_width]], axis=1)
    grad_dt = g_conv_in[:, xbc_width : xbc_width + MH]
    grad_out = jnp.concatenate(g_out, axis=1).T
    grad_gate_up = jnp.concatenate(g_gate_up, axis=1)
    grad_down = jnp.concatenate(g_down, axis=1).T
    gains = to_plain_wide(jnp.stack([g_norm_gain, g_mlp_gain]))
    small_sums = total_small(
        (gains[0], gains[1], g_ssm_gain, g_conv_w, g_conv_b, g_a_log, g_dt_bias, g_d_skip), fast
    )
    return (
        to_plain(layer_out.astype(jnp.bfloat16)).astype(jnp.bfloat16)[None],
        to_plain_wide(input_grad)[None],
        grad_attn,
        grad_ssm_in,
        grad_dt,
        grad_out,
        grad_gate_up,
        grad_down,
        small_sums[0],
        small_sums[1],
        small_sums[2],
        small_sums[3],
        small_sums[4],
        small_sums[5],
        small_sums[6],
        small_sums[7],
    )


def solution(mesh):
    return jax.shard_map(
        on_device,
        mesh=mesh,
        in_specs=(
            P("batch", "seq", None),
            P("batch", None),
            P(("seq", "batch"), None),
            P(("seq", "batch"), None),
            P(("seq", "batch"), None),
            P(None, ("seq", "batch")),
            P(("seq", "batch"), None),
            P(None, ("seq", "batch")),
            P(),
            P(),
            P(),
            P(),
            P(),
            P(),
            P(),
            P(),
            P("batch", "seq", None),
        ),
        out_specs=(
            P("batch", "seq", None),
            P("batch", "seq", None),
            P(("seq", "batch"), None),
            P(("seq", "batch"), None),
            P(("seq", "batch"), None),
            P(None, ("seq", "batch")),
            P(("seq", "batch"), None),
            P(None, ("seq", "batch")),
            P(),
            P(),
            P(),
            P(),
            P(),
            P(),
            P(),
            P(),
        ),
        check_vma=False,
    )
```

```python
import jax
import jax.numpy as jnp
from jax import lax
from jax.experimental import pallas as pl
from jax.experimental.pallas import tpu as pltpu
from jax.sharding import PartitionSpec as P

QUERY_HEADS = 8
KEY_VALUE_HEADS = 2
HEAD_SIZE = 64
MH = 24
MP = 64
NS = 128
FF = 2048
CONV = 4
SPAN = 128


HIGHEST = lax.Precision.HIGHEST
NEGATIVE_FILL = -1e30
ROPE_BASE = 10000.0
NORM_EPS = 1e-06


def shifted(block, axis, distance):
    devices = range(lax.axis_size(axis))
    route = [(i - distance, i) for i in devices if i - distance in devices]
    return lax.ppermute(block, axis, route)


def is_fast(width):
    return lax.axis_size("seq") == 8 and lax.axis_size("batch") == 4 and width % (32 * 32) == 0


def swap(value, axis, bit):
    route = [(i, i ^ bit) for i in range(lax.axis_size(axis))]
    return lax.ppermute(value, axis, route)


def gather_stages(shard, x_first):
    rows = jnp.concatenate([shard, swap(shard, "seq", 4)], axis=0)
    rows = jnp.concatenate([rows, swap(rows, "seq", 2)], axis=0)
    along_z = rows
    if x_first:
        rows = jnp.concatenate([rows, swap(rows, "seq", 1)], axis=0)
        rows = jnp.concatenate([rows, swap(rows, "batch", 2)], axis=0)
    else:
        rows = jnp.stack([rows, swap(rows, "batch", 2)], axis=0)
        rows = jnp.stack([rows, swap(rows, "seq", 1)], axis=1)
        rows = rows.reshape(-1, rows.shape[-1])
    return along_z, jnp.concatenate([rows, swap(rows, "batch", 1)], axis=0)


def add_narrow(own, other):
    return (own.astype(jnp.float32) + other.astype(jnp.float32)).astype(jnp.bfloat16)


def scatter_stages(rows, y_first):
    size, cols = rows.shape
    if y_first:
        half = size // 2
        rows = add_narrow(rows[:half], swap(rows[half:], "batch", 2))
        half = half // 2
        rows = add_narrow(rows[:half], swap(rows[half:], "seq", 1))
    else:
        split = rows.reshape(2, 2, size // 4, cols)
        split = add_narrow(split[:, 0], swap(split[:, 1], "seq", 1))
        rows = add_narrow(split[0], swap(split[1], "batch", 2))
    half = rows.shape[0] // 2
    rows = add_narrow(rows[:half], swap(rows[half:], "seq", 2))
    half = half // 2
    return rows[:half].astype(jnp.float32) + swap(rows[half:], "seq", 4).astype(jnp.float32)


def weight_grad(left, right, fast, y_first):
    if not fast:
        full = jnp.einsum("td,tc->dc", left, right, preferred_element_type=jnp.float32)
        return lax.psum_scatter(full, ("seq", "batch"), scatter_dimension=0, tiled=True)
    half = left.shape[1] // 2
    lefts = jnp.concatenate([left[:, :half], swap(left[:, half:], "batch", 1)], axis=0)
    rights = jnp.concatenate([right, swap(right, "batch", 1)], axis=0)
    partial = jnp.einsum("td,tc->dc", lefts, rights, preferred_element_type=jnp.float32)
    return scatter_stages(partial.astype(jnp.bfloat16), y_first)


def total_small(arrays, fast):
    flat = jnp.concatenate([a.reshape(-1) for a in arrays])
    size = flat.shape[0]
    flat = jnp.pad(flat, (0, -size % 1024)).reshape(-1, 128)
    if fast:
        for axis, bit in (("batch", 1), ("batch", 2), ("seq", 1), ("seq", 2), ("seq", 4)):
            flat = flat + swap(flat, axis, bit)
    else:
        flat = lax.psum(flat, ("seq", "batch"))
    flat = flat.reshape(-1)
    out, start = [], 0
    for a in arrays:
        out.append(flat[start : start + a.size].reshape(a.shape))
        start += a.size
    return out


def own_order(width, fast):
    blocks = 32
    per = width // blocks
    row = lax.broadcasted_iota(jnp.int32, (width, width), 0)
    col = lax.broadcasted_iota(jnp.int32, (width, width), 1)
    if not fast:
        return (row == col).astype(jnp.bfloat16)
    me = lax.axis_index("seq") * 4 + lax.axis_index("batch")
    j = col // per
    flipped = (j & 1) * 16 + (j & 2) * 4 + (j & 4) + (j & 8) // 4 + (j & 16) // 16
    source = (flipped ^ me) * per + col % per
    return (row == source).astype(jnp.bfloat16)


def rms_scale(value_rows):
    return lax.rsqrt(jnp.mean(value_rows * value_rows, axis=-1, keepdims=True) + NORM_EPS)


def norm_back(value_rows, scales, gains, grads):
    gain_grad = jnp.sum(grads * value_rows * scales, axis=0)
    inner = grads * gains
    coeff = jnp.mean(inner * value_rows, axis=-1, keepdims=True)
    return (scales * (inner - value_rows * scales * scales * coeff), gain_grad)


def segments(lengths, positions):
    ends = jnp.cumsum(lengths)
    passed = ends[None, :] <= positions[:, None]
    segment = jnp.sum(passed.astype(jnp.int32), axis=1)
    device_places = positions - jnp.sum(jnp.where(passed, lengths[None, :], 0), axis=1)
    return (segment, device_places)


def conv_mix(extended, ext_segment, conv_weight, conv_bias):
    row_count = extended.shape[0] - (CONV - 1)
    summed = conv_bias[None, :]
    for lagged in range(CONV):
        same_seq = (ext_segment[lagged : lagged + row_count] == ext_segment[CONV - 1 :]).astype(
            extended.dtype
        )
        summed = (
            summed
            + conv_weight[lagged][None, :]
            * extended[lagged : lagged + row_count]
            * same_seq[:, None]
        )
    return jax.nn.silu(summed)


TILE = 128
PAIRS = QUERY_HEADS // 2
CHUNK = 256


def dot(left, right):
    return jnp.dot(left, right, preferred_element_type=jnp.float32)


def dot_nt(left, right):
    return lax.dot_general(
        left, right, (((1,), (1,)), ((), ())), preferred_element_type=jnp.float32
    )


def dot_tn(left, right):
    return lax.dot_general(
        left, right, (((0,), (0,)), ((), ())), preferred_element_type=jnp.float32
    )


def exact(left, right):
    return jnp.dot(left, right, precision=HIGHEST, preferred_element_type=jnp.float32)


def two_part(left, right):
    high = left.astype(jnp.bfloat16)
    low = (left - high.astype(jnp.float32)).astype(jnp.bfloat16)
    return dot(high, right) + dot(low, right)


def seg_start(where_at, info):
    start = jnp.zeros_like(where_at)
    for k in range(1, 4):
        start = jnp.where(where_at >= info[k], jnp.maximum(start, info[k]), start)
    return start


def big_call(kernel, outs, *args, scratch=(), flops=0, smem=0, limit=48):
    specs = [pl.BlockSpec(memory_space=pltpu.SMEM)] * smem
    specs += [pl.BlockSpec(memory_space=pltpu.VMEM)] * (len(args) - smem)
    moved = sum(a.size * a.dtype.itemsize for a in args)
    moved += sum(o.size * o.dtype.itemsize for o in outs)
    return pl.pallas_call(
        kernel,
        out_shape=list(outs),
        in_specs=specs,
        out_specs=[pl.BlockSpec(memory_space=pltpu.VMEM)] * len(outs),
        scratch_shapes=list(scratch),
        cost_estimate=pl.CostEstimate(flops=flops, bytes_accessed=moved, transcendentals=0),
        compiler_params=pltpu.CompilerParams(vmem_limit_bytes=limit * 1024 * 1024),
    )(*args)


def shape_of(shape, dtype):
    return jax.ShapeDtypeStruct(shape, dtype)


def turn(value, cosine, sine):
    lane = lax.broadcasted_iota(jnp.int32, value.shape, 1) % HEAD_SIZE
    mixed = jnp.where(
        lane < HEAD_SIZE // 2,
        -pltpu.roll(value, TILE - HEAD_SIZE // 2, 1),
        pltpu.roll(value, HEAD_SIZE // 2, 1),
    )
    return value * cosine + mixed * sine


def rope_kernel(proj, cosine, sine, q_out, kv_out):
    cos, sin = cosine[...], sine[...]
    for i in range(PAIRS):
        cols = pl.ds(i * TILE, TILE)
        turned = turn(proj[:, cols], cos, sin).astype(jnp.bfloat16)
        q_out[:, cols] = (turned.astype(jnp.float32) * HEAD_SIZE**-0.5).astype(jnp.bfloat16)
    base = PAIRS * TILE
    kv_out[:, :TILE] = turn(proj[:, base : base + TILE], cos, sin).astype(jnp.bfloat16)
    kv_out[:, TILE:] = proj[:, base + TILE : base + 2 * TILE].astype(jnp.bfloat16)


def halves_of(value):
    lane = lax.broadcasted_iota(jnp.int32, value.shape, 1)
    wide = value.astype(jnp.float32)
    first = jnp.where(lane < HEAD_SIZE, wide, 0.0).astype(value.dtype)
    return first, jnp.where(lane < HEAD_SIZE, 0.0, wide).astype(value.dtype)


def block_range(info):
    first = info[0]
    low = seg_start(first, info) // CHUNK
    return low, first // CHUNK - low + 1


def attn_mask(info, block):
    rows = lax.broadcasted_iota(jnp.int32, (CHUNK, CHUNK), 0) + block * CHUNK
    at = lax.broadcasted_iota(jnp.int32, (1, CHUNK), 1) + info[0]
    return (rows <= at) & (rows >= seg_start(at, info))


def attn_forward_kernel(info, q, kv, out, out_t, lse, heads, acc, top, total):
    for i in range(PAIRS):
        heads[2 * i], heads[2 * i + 1] = halves_of(q[:, i * TILE : (i + 1) * TILE])
    acc[...] = jnp.zeros_like(acc)
    total[...] = jnp.zeros_like(total)
    top[...] = jnp.full(top.shape, NEGATIVE_FILL, jnp.float32)
    low, count = block_range(info)

    def step(j, carry):
        block = low + j
        place = pl.ds(pl.multiple_of((block ^ info[4]) * CHUNK, CHUNK), CHUNK)
        keys = kv[place, :TILE]
        values_t = kv[place, TILE:].astype(jnp.float32).T.astype(jnp.bfloat16)
        allowed = attn_mask(info, block)
        for h in range(QUERY_HEADS):
            scores = jnp.where(allowed, dot_nt(keys, heads[h]), NEGATIVE_FILL)
            old = top[h : h + 1]
            new = jnp.maximum(old, jnp.max(scores, axis=0, keepdims=True))
            probs = jnp.where(allowed, jnp.exp(scores - new), 0.0)
            shrink = jnp.exp(old - new)
            top[h : h + 1] = new
            total[h : h + 1] = total[h : h + 1] * shrink + jnp.sum(probs, axis=0, keepdims=True)
            side = (h % 2) * HEAD_SIZE
            acc[h] = acc[h] * shrink + dot(
                values_t[side : side + HEAD_SIZE], probs.astype(jnp.bfloat16)
            )
        return carry

    lax.fori_loop(0, count, step, 0)
    lse[...] = top[...] + jnp.log(total[...])
    for i in range(PAIRS):
        pair = jnp.concatenate(
            [acc[2 * i] / total[2 * i : 2 * i + 1], acc[2 * i + 1] / total[2 * i + 1 : 2 * i + 2]],
            axis=0,
        )
        out_t[i * TILE : (i + 1) * TILE] = pair
        out[:, i * TILE : (i + 1) * TILE] = pair.T.astype(jnp.bfloat16)


def attn_forward(info, q, kv):
    rows = q.shape[0]
    f32 = jnp.float32
    return big_call(
        attn_forward_kernel,
        (
            shape_of(q.shape, jnp.bfloat16),
            shape_of(q.shape[::-1], f32),
            shape_of((QUERY_HEADS, rows), f32),
        ),
        info,
        q,
        kv,
        smem=1,
        scratch=(
            pltpu.VMEM((QUERY_HEADS, rows, TILE), jnp.bfloat16),
            pltpu.VMEM((QUERY_HEADS, HEAD_SIZE, rows), f32),
            pltpu.VMEM((QUERY_HEADS, rows), f32),
            pltpu.VMEM((QUERY_HEADS, rows), f32),
        ),
        flops=4 * rows * kv.shape[0] * q.shape[1],
    )


def attn_backward_kernel(info, q, kv, grad, out_t, lse, dq, dkv, heads, grads, delta, acc):
    for i in range(PAIRS):
        cols = slice(i * TILE, (i + 1) * TILE)
        heads[2 * i], heads[2 * i + 1] = halves_of(q[:, cols])
        grads[2 * i], grads[2 * i + 1] = halves_of(grad[:, cols])
        both = grad[:, cols].astype(jnp.float32).T * out_t[cols]
        delta[2 * i : 2 * i + 1] = jnp.sum(both[:HEAD_SIZE], axis=0, keepdims=True)
        delta[2 * i + 1 : 2 * i + 2] = jnp.sum(both[HEAD_SIZE:], axis=0, keepdims=True)
    acc[...] = jnp.zeros_like(acc)
    dkv[...] = jnp.zeros_like(dkv)
    low, count = block_range(info)

    def step(j, carry):
        block = low + j
        place = pl.ds(pl.multiple_of((block ^ info[4]) * CHUNK, CHUNK), CHUNK)
        keys = kv[place, :TILE]
        values = kv[place, TILE:]
        keys_t = keys.astype(jnp.float32).T.astype(jnp.bfloat16)
        allowed = attn_mask(info, block)
        d_keys = jnp.zeros((CHUNK, TILE), jnp.float32)
        d_values = jnp.zeros((CHUNK, TILE), jnp.float32)
        for h in range(QUERY_HEADS):
            scores = dot_nt(keys, heads[h])
            probs = jnp.where(allowed, jnp.exp(scores - lse[h : h + 1]), 0.0)
            d_probs = dot_nt(values, grads[h])
            d_scores = (probs * (d_probs - delta[h : h + 1])).astype(jnp.bfloat16)
            d_values = d_values + dot(probs.astype(jnp.bfloat16), grads[h])
            d_keys = d_keys + dot(d_scores, heads[h])
            side = (h % 2) * HEAD_SIZE
            acc[h] = acc[h] + dot(keys_t[side : side + HEAD_SIZE], d_scores)
        dkv[place, :TILE] = d_keys.astype(jnp.bfloat16)
        dkv[place, TILE:] = d_values.astype(jnp.bfloat16)
        return carry

    lax.fori_loop(0, count, step, 0)
    for i in range(PAIRS):
        pair = jnp.concatenate([acc[2 * i], acc[2 * i + 1]], axis=0)
        dq[:, i * TILE : (i + 1) * TILE] = pair.T * HEAD_SIZE**-0.5


def attn_backward(info, q, kv, grad, out_t, lse):
    rows = q.shape[0]
    f32 = jnp.float32
    return big_call(
        attn_backward_kernel,
        (shape_of(q.shape, f32), shape_of(kv.shape, jnp.bfloat16)),
        info,
        q,
        kv,
        grad,
        out_t,
        lse,
        smem=1,
        scratch=(
            pltpu.VMEM((QUERY_HEADS, rows, TILE), jnp.bfloat16),
            pltpu.VMEM((QUERY_HEADS, rows, TILE), jnp.bfloat16),
            pltpu.VMEM((QUERY_HEADS, rows), f32),
            pltpu.VMEM((QUERY_HEADS, HEAD_SIZE, rows), f32),
        ),
        flops=10 * rows * kv.shape[0] * q.shape[1],
    )


def rope_back_kernel(dq, dkv, cosine, sine, out):
    cos, sin = cosine[...], -sine[...]
    for i in range(PAIRS):
        cols = slice(i * TILE, (i + 1) * TILE)
        out[:, cols] = turn(dq[:, cols], cos, sin).astype(jnp.bfloat16)
    base = PAIRS * TILE
    out[:, base : base + TILE] = turn(dkv[:, :TILE], cos, sin).astype(jnp.bfloat16)
    out[:, base + TILE :] = dkv[:, TILE:].astype(jnp.bfloat16)


STATE_ROWS = NS + 16


def lane_pick(value, first):
    rows = value.shape[0]
    lane = lax.broadcasted_iota(jnp.int32, (rows, TILE), 1)
    return jnp.where(lane < MP, value[:, first : first + 1], value[:, first + 1 : first + 2])


def spread_heads(width):
    head = lax.broadcasted_iota(jnp.int32, (TILE, width), 0)
    col = lax.broadcasted_iota(jnp.int32, (TILE, width), 1)
    return jnp.where(head == col // MP, 1.0, 0.0).astype(jnp.bfloat16)


def gather_heads(width):
    head = lax.broadcasted_iota(jnp.int32, (width, TILE), 1)
    col = lax.broadcasted_iota(jnp.int32, (width, TILE), 0)
    return jnp.where(head == col // MP, 1.0, 0.0).astype(jnp.bfloat16)


def head_lanes(rows):
    return lax.broadcasted_iota(jnp.int32, (rows, TILE), 1) < MH


def chunk_places(info, rows):
    at = lax.broadcasted_iota(jnp.int32, (rows, 1), 0) + info[0]
    return seg_start(at, info) - info[0]


def ssm_forward_kernel(info, x, bc, step_in, head_params, y, state, dt_out, cum_out, dt_t, cum_t):
    rows = x.shape[0]
    bias, rate, skip = head_params[0:1], head_params[1:2], head_params[2:3]
    raw = step_in[...] + bias
    dt = jnp.maximum(raw, 0.0) + jnp.log1p(jnp.exp(-jnp.abs(raw)))
    dt = jnp.where(head_lanes(rows), dt, 0.0)
    row = lax.broadcasted_iota(jnp.int32, (rows, rows), 0)
    col = lax.broadcasted_iota(jnp.int32, (rows, rows), 1)
    lower = jnp.where(row >= col, 1.0, 0.0)
    cum = exact(lower, -dt * rate)
    dt_out[...] = dt
    cum_out[...] = cum
    dt_t[...] = dt.T
    cum_t[...] = cum.T
    starts = chunk_places(info, rows)
    last_start = seg_start(info[0] + rows - 1, info) - info[0]
    place = lax.broadcasted_iota(jnp.int32, (rows, 1), 0)
    end = cum[rows - 1 : rows]
    leave = jnp.where(place >= last_start, jnp.exp(jnp.minimum(end - cum, 0.0)) * dt, 0.0)
    narrow_b, narrow_c = bc[:, :NS], bc[:, NS:]
    b_t = narrow_b.astype(jnp.float32).T.astype(jnp.bfloat16)
    products = dot_nt(narrow_c, narrow_b)
    through = jnp.where(last_start < 0, jnp.exp(end), 0.0)
    high = through.astype(jnp.bfloat16).astype(jnp.float32)
    line = lax.broadcasted_iota(jnp.int32, (16, TILE), 0)
    both = jnp.where(line == 0, high, jnp.where(line == 1, through - high, 0.0))
    spread = spread_heads(x.shape[1])
    state[NS:] = dot(both.astype(jnp.bfloat16), spread).astype(jnp.bfloat16)
    skips = jnp.broadcast_to(skip, (8, TILE))
    skip_row = two_part(skips, spread)[:1]
    lane = lax.broadcasted_iota(jnp.int32, (SPAN, TILE), 1)
    for i in range(MH // 2):
        cols = slice(i * TILE, (i + 1) * TILE)
        tile = x[:, cols]
        state[:NS, cols] = dot(
            b_t, (tile.astype(jnp.float32) * lane_pick(leave, 2 * i)).astype(jnp.bfloat16)
        ).astype(jnp.bfloat16)
        for part in range(rows // SPAN):
            here = slice(part * SPAN, (part + 1) * SPAN)
            upto = (part + 1) * SPAN
            allowed = (row[here, :upto] >= col[here, :upto]) & (col[here, :upto] >= starts[here])
            sides = []
            for h in (2 * i, 2 * i + 1):
                spread_log = cum[here, h : h + 1] - cum_t[h : h + 1, :upto]
                decay = jnp.exp(jnp.where(allowed, spread_log, NEGATIVE_FILL))
                mixing = products[here, :upto] * decay * dt_t[h : h + 1, :upto]
                sides.append(dot(mixing.astype(jnp.bfloat16), tile[:upto]))
            own = skip_row[:, cols] * tile[here].astype(jnp.float32)
            y[here, cols] = jnp.where(lane < MP, sides[0], sides[1]) + own


def ssm_forward(info, x, bc, step_in, head_params):
    rows, width = x.shape
    f32 = jnp.float32
    return big_call(
        ssm_forward_kernel,
        (
            shape_of((rows, width), f32),
            shape_of((STATE_ROWS, width), jnp.bfloat16),
            shape_of((rows, TILE), f32),
            shape_of((rows, TILE), f32),
        ),
        info,
        x,
        bc,
        step_in,
        head_params,
        smem=1,
        scratch=(pltpu.VMEM((TILE, rows), f32), pltpu.VMEM((TILE, rows), f32)),
        flops=4 * rows * rows * width,
    )


def entering_of(info, cum):
    rows = cum.shape[0]
    return jnp.where(chunk_places(info, rows) < 0, jnp.exp(jnp.minimum(cum, 0.0)), 0.0)


def ssm_finish_kernel(info, y, bc, cum, state_in, z, gain, ssm_out, normed, scale):
    rows = y.shape[0]
    enter = entering_of(info, cum[...])
    narrow_c = bc[:, NS:]
    squares = jnp.zeros((rows, TILE), jnp.float32)
    tiles = MH // 2
    for i in range(tiles):
        cols = slice(i * TILE, (i + 1) * TILE)
        out = y[:, cols] + lane_pick(enter, 2 * i) * dot(narrow_c, state_in[:, cols])
        ssm_out[:, cols] = out
        gate = z[:, cols]
        gated = out * (gate * jax.nn.sigmoid(gate))
        squares = squares + gated * gated
    mean = jnp.sum(squares, axis=1, keepdims=True) * (1.0 / (tiles * TILE))
    r = lax.rsqrt(mean + NORM_EPS)
    scale[...] = jnp.broadcast_to(r, scale.shape)
    for i in range(tiles):
        cols = slice(i * TILE, (i + 1) * TILE)
        gate = z[:, cols]
        gated = ssm_out[:, cols] * (gate * jax.nn.sigmoid(gate))
        normed[:, cols] = (gated * r * gain[:, cols]).astype(jnp.bfloat16)


def ssm_finish(info, y, bc, cum, state_in, z, gain):
    rows, width = y.shape
    return big_call(
        ssm_finish_kernel,
        (
            shape_of((rows, width), jnp.float32),
            shape_of((rows, width), jnp.bfloat16),
            shape_of((rows, TILE), jnp.float32),
        ),
        info,
        y,
        bc,
        cum,
        state_in,
        z,
        gain,
        smem=1,
        flops=2 * rows * NS * width,
    )


def gate_back_kernel(info, dy, ssm_out, z, scale, gain, cum, bc, d_out, d_z, pull, g_gain):
    rows = dy.shape[0]
    tiles = MH // 2
    r = scale[:, :1]
    enter = entering_of(info, cum[...])
    c_t = bc[:, NS:].astype(jnp.float32).T.astype(jnp.bfloat16)
    inner = jnp.zeros((rows, TILE), jnp.float32)
    for i in range(tiles):
        cols = slice(i * TILE, (i + 1) * TILE)
        gate = z[:, cols]
        gated = ssm_out[:, cols] * (gate * jax.nn.sigmoid(gate))
        product = dy[:, cols] * gated
        g_gain[:, cols] = jnp.sum(product * r, axis=0, keepdims=True)
        inner = inner + product * gain[:, cols]
    coeff = jnp.sum(inner, axis=1, keepdims=True) * (1.0 / (tiles * TILE))
    for i in range(tiles):
        cols = slice(i * TILE, (i + 1) * TILE)
        gate = z[:, cols]
        sig = jax.nn.sigmoid(gate)
        silu = gate * sig
        out = ssm_out[:, cols]
        d_gated = r * (dy[:, cols] * gain[:, cols] - out * silu * (r * r * coeff))
        d_ssm = d_gated * silu
        d_out[:, cols] = d_ssm
        d_z[:, cols] = (d_gated * out * (sig * (1.0 + gate * (1.0 - sig)))).astype(jnp.bfloat16)
        pull[:, cols] = dot(c_t, (d_ssm * lane_pick(enter, 2 * i)).astype(jnp.bfloat16)).astype(
            jnp.bfloat16
        )


def gate_back(info, dy, ssm_out, z, scale, gain, cum, bc):
    rows, width = dy.shape
    return big_call(
        gate_back_kernel,
        (
            shape_of((rows, width), jnp.float32),
            shape_of((rows, width), jnp.bfloat16),
            shape_of((NS, width), jnp.bfloat16),
            shape_of((1, width), jnp.float32),
        ),
        info,
        dy,
        ssm_out,
        z,
        scale,
        gain,
        cum,
        bc,
        smem=1,
        flops=2 * rows * NS * width,
    )


def ssm_back_kernel(info, x, bc, dt, cum, grad, head_params, dx, d_bc, d_cum, d_dt, g_skip, cols_t, d_rows):
    rows, width = x.shape
    skip = head_params[2:3]
    cols_t[...] = cum[...].T
    row = lax.broadcasted_iota(jnp.int32, (rows, rows), 0)
    col = lax.broadcasted_iota(jnp.int32, (rows, rows), 1)
    at = lax.broadcasted_iota(jnp.int32, (1, rows), 1) + info[0]
    starts = seg_start(at, info) - info[0]
    narrow_b, narrow_c = bc[:, :NS], bc[:, NS:]
    products = dot_nt(narrow_b, narrow_c)
    skip_row = two_part(jnp.broadcast_to(skip, (8, TILE)), spread_heads(width))[:1]
    lane = lax.broadcasted_iota(jnp.int32, (SPAN, TILE), 1)
    parts = rows // SPAN
    d_products = [jnp.zeros((SPAN, rows - p * SPAN), jnp.float32) for p in range(parts)]
    d_rows[...] = jnp.zeros_like(d_rows)
    step_sums = [jnp.zeros((SPAN, TILE), jnp.float32) for p in range(parts)]
    skip_sums = []
    for i in range(MH // 2):
        cols = slice(i * TILE, (i + 1) * TILE)
        tile = x[:, cols]
        wide = grad[:, cols]
        narrow = wide.astype(jnp.bfloat16)
        skip_sums.append(jnp.sum(wide * tile.astype(jnp.float32), axis=0, keepdims=True))
        tile_sides = halves_of(tile)
        for part in range(parts):
            here = slice(part * SPAN, (part + 1) * SPAN)
            since = part * SPAN
            allowed = (row[here, since:] <= col[here, since:]) & (
                row[here, since:] >= starts[:, since:]
            )
            sides = []
            for side in range(2):
                h = 2 * i + side
                spread_log = cols_t[h : h + 1, since:] - cum[here, h : h + 1]
                decay = jnp.exp(jnp.where(allowed, spread_log, NEGATIVE_FILL))
                decay_dt = decay * dt[here, h : h + 1]
                mixing = products[here, since:] * decay_dt
                sides.append(dot(mixing.astype(jnp.bfloat16), narrow[since:]))
                d_mixing = dot_nt(tile_sides[side][here], narrow[since:])
                d_products[part] = d_products[part] + d_mixing * decay_dt
                whole = d_mixing * mixing
                d_rows[h : h + 1, since:] += jnp.sum(whole, axis=0, keepdims=True)
                weighed = d_mixing * (products[here, since:] * decay)
                step_sums[part] = jnp.where(
                    lane == h, jnp.sum(weighed, axis=1, keepdims=True), step_sums[part]
                )
            dx[here, cols] = (
                jnp.where(lane < MP, sides[0], sides[1]) + skip_row[:, cols] * wide[here]
            )
    all_steps = jnp.concatenate(step_sums, axis=0)
    d_dt[...] = all_steps
    d_cum[...] = d_rows[...].T - all_steps * dt[...]
    g_skip[...] = jnp.broadcast_to(
        two_part(
            jnp.broadcast_to(jnp.concatenate(skip_sums, axis=1), (8, width)), gather_heads(width)
        ),
        g_skip.shape,
    )
    full = jnp.concatenate(
        [
            d
            if p == 0
            else jnp.concatenate([jnp.zeros((SPAN, p * SPAN), jnp.float32), d], axis=1)
            for p, d in enumerate(d_products)
        ],
        axis=0,
    ).astype(jnp.bfloat16)
    d_bc[:, :NS] = dot(full, narrow_c)
    d_bc[:, NS:] = dot_tn(full, narrow_b)


def ssm_back(info, x, bc, dt, cum, grad, head_params):
    rows, width = x.shape
    f32 = jnp.float32
    return big_call(
        ssm_back_kernel,
        (
            shape_of((rows, width), f32),
            shape_of((rows, 2 * NS), f32),
            shape_of((rows, TILE), f32),
            shape_of((rows, TILE), f32),
            shape_of((8, TILE), f32),
        ),
        info,
        x,
        bc,
        dt,
        cum,
        grad,
        head_params,
        smem=1,
        scratch=(pltpu.VMEM((TILE, rows), f32), pltpu.VMEM((TILE, rows), f32)),
        flops=8 * rows * rows * width,
    )


def state_back_kernel(
    info, x, bc, dt, cum, grad, head_params, step_in, state_in, d_state, dx_in, d_bc_in, d_cum_in,
    d_dt_in, dx, d_bc, d_step, sums,
):
    rows, width = x.shape
    bias, rate = head_params[0:1], head_params[1:2]
    cums, steps = cum[...], dt[...]
    enter = entering_of(info, cums)
    last_start = seg_start(info[0] + rows - 1, info) - info[0]
    place = lax.broadcasted_iota(jnp.int32, (rows, 1), 0)
    end = cums[rows - 1 : rows]
    fade = jnp.where(place >= last_start, jnp.exp(jnp.minimum(end - cums, 0.0)), 0.0)
    leave = fade * steps
    through = jnp.where(last_start < 0, jnp.exp(end), 0.0)
    narrow_b, narrow_c = bc[:, :NS], bc[:, NS:]
    pick = gather_heads(width)
    d_leave = jnp.zeros((rows, TILE), jnp.float32)
    d_enter = jnp.zeros((rows, TILE), jnp.float32)
    d_b = d_bc_in[:, :NS]
    d_c = d_bc_in[:, NS:]
    link = jnp.zeros((8, TILE), jnp.float32)
    for i in range(MH // 2):
        cols = slice(i * TILE, (i + 1) * TILE)
        tile = x[:, cols].astype(jnp.float32)
        wide = grad[:, cols]
        pulled = d_state[:, cols]
        held = state_in[:, cols]
        from_b = dot(narrow_b, pulled)
        leave_tile = lane_pick(leave, 2 * i)
        dx[:, cols] = dx_in[:, cols] + leave_tile * from_b
        d_leave = d_leave + two_part(tile * from_b, pick[cols])
        d_enter = d_enter + two_part(wide * dot(narrow_c, held), pick[cols])
        d_b = d_b + dot_nt((tile * leave_tile).astype(jnp.bfloat16), pulled)
        d_c = d_c + dot_nt((wide * lane_pick(enter, 2 * i)).astype(jnp.bfloat16), held)
        meet = jnp.sum(
            pulled.astype(jnp.float32) * held.astype(jnp.float32), axis=0, keepdims=True
        )
        link = link + two_part(jnp.broadcast_to(meet, (8, TILE)), pick[cols])
    d_bc[:, :NS] = d_b
    d_bc[:, NS:] = d_c
    left = leave * d_leave
    d_cum = d_cum_in[...] + enter * d_enter - left
    at_end = jnp.sum(left, axis=0, keepdims=True) + through * link[:1]
    d_cum = d_cum + jnp.where(place == rows - 1, at_end, 0.0)
    row = lax.broadcasted_iota(jnp.int32, (rows, rows), 0)
    col = lax.broadcasted_iota(jnp.int32, (rows, rows), 1)
    d_log = exact(jnp.where(row <= col, 1.0, 0.0), d_cum)
    d_steps = d_dt_in[...] + fade * d_leave - d_log * rate
    d_pre = d_steps * jax.nn.sigmoid(step_in[...] + bias)
    d_pre = jnp.where(head_lanes(rows), d_pre, 0.0)
    d_step[...] = d_pre.astype(jnp.bfloat16)
    g_rate = jnp.sum(d_log * (-steps * rate), axis=0, keepdims=True)
    g_bias = jnp.sum(d_pre, axis=0, keepdims=True)
    line = lax.broadcasted_iota(jnp.int32, (8, TILE), 0)
    sums[...] = jnp.where(line == 0, g_rate, jnp.where(line == 1, g_bias, 0.0))


def state_back(info, *args):
    rows, width = args[0].shape
    f32 = jnp.float32
    return big_call(
        state_back_kernel,
        (
            shape_of((rows, width), f32),
            shape_of((rows, 2 * NS), f32),
            shape_of((rows, TILE), jnp.bfloat16),
            shape_of((8, TILE), f32),
        ),
        info,
        *args,
        smem=1,
        flops=12 * rows * NS * width,
    )


def join_states(earlier, later):
    decay = later[NS : NS + 1].astype(jnp.float32) + later[NS + 1 : NS + 2].astype(jnp.float32)
    before = earlier[NS : NS + 1].astype(jnp.float32) + earlier[NS + 1 : NS + 2].astype(jnp.float32)
    state = decay * earlier[:NS].astype(jnp.float32) + later[:NS].astype(jnp.float32)
    both = decay * before
    high = both.astype(jnp.bfloat16)
    low = (both - high.astype(jnp.float32)).astype(jnp.bfloat16)
    rest = jnp.zeros((STATE_ROWS - NS - 2, state.shape[1]), jnp.bfloat16)
    return jnp.concatenate([state.astype(jnp.bfloat16), high, low, rest], axis=0)


def scan_states(own, fast, forward):
    place = lax.axis_index("seq")
    count = lax.axis_size("seq")
    nothing = jnp.concatenate(
        [
            jnp.zeros((NS, own.shape[1]), own.dtype),
            jnp.ones((1, own.shape[1]), own.dtype),
            jnp.zeros((STATE_ROWS - NS - 1, own.shape[1]), own.dtype),
        ],
        axis=0,
    )
    if fast:
        reach, before = own, nothing
        for bit in (1, 2, 4):
            other = swap(reach, "seq", bit)
            second = ((place & bit) != 0) == forward
            before = jnp.where(second, join_states(other, before), before)
            if bit != 4:
                reach = jnp.where(second, join_states(other, reach), join_states(reach, other))
        return before[:NS]
    everything = lax.all_gather(own, "seq")

    def step(k, before):
        index = k if forward else count - 1 - k
        reached = index < place if forward else index > place
        part = lax.dynamic_index_in_dim(everything, index, 0, False)
        return jnp.where(reached, join_states(before, part), before)

    return lax.fori_loop(0, count, step, nothing)[:NS]


def seq_gather(value, fast):
    if not fast:
        return lax.all_gather(value, "seq", axis=0, tiled=True)
    rows = jnp.stack([value, swap(value, "seq", 4)], axis=0)
    rows = jnp.stack([rows, swap(rows, "seq", 2)], axis=1)
    rows = jnp.stack([rows, swap(rows, "seq", 1)], axis=2)
    return rows.reshape(-1, value.shape[1])


def seq_scatter(value, fast):
    if not fast:
        return lax.psum_scatter(
            value.astype(jnp.float32), "seq", scatter_dimension=0, tiled=True
        )
    size, cols = value.shape
    parts = value.reshape(4, 2, size // 8, cols)
    parts = add_narrow(parts[:, 0], swap(parts[:, 1], "seq", 1))
    parts = add_narrow(parts[:2], swap(parts[2:], "seq", 4))
    return parts[0].astype(jnp.float32) + swap(parts[1], "seq", 2).astype(jnp.float32)


def pair_heads(value, back=False):
    rows = value.shape[0]
    group = QUERY_HEADS // KEY_VALUE_HEADS
    width = QUERY_HEADS * HEAD_SIZE
    shape = (group, KEY_VALUE_HEADS) if back else (KEY_VALUE_HEADS, group)
    moved = value[:, :width].reshape(rows, *shape, HEAD_SIZE).transpose(0, 2, 1, 3)
    return jnp.concatenate([moved.reshape(rows, width), value[:, width:]], axis=1)


def on_device(
    layer_input,
    seq_lengths,
    w_attn,
    w_ssm_in,
    w_dt,
    w_out,
    w_gate_up,
    w_down,
    norm_gain,
    mlp_gain,
    ssm_gain,
    conv_w,
    conv_b,
    a_log,
    dt_bias,
    d_skip,
    out_grad,
):
    token_rows = layer_input.shape[1]
    query_width = QUERY_HEADS * HEAD_SIZE
    key_value_width = KEY_VALUE_HEADS * HEAD_SIZE
    attn_width = query_width + 2 * key_value_width
    ssm_width = MH * MP
    xbc_width = ssm_width + 2 * NS
    width = layer_input.shape[2]
    fast = is_fast(width)
    seq_lens = seq_lengths[0]
    first_pos = lax.axis_index("seq") * token_rows
    positions = first_pos + jnp.arange(token_rows, dtype=jnp.int32)
    segment, device_places = segments(seq_lens, positions)
    mask = lax.axis_index("seq") if fast else 0
    ends = jnp.cumsum(seq_lens)
    info = jnp.stack([first_pos, ends[0], ends[1], ends[2], mask]).astype(jnp.int32)
    half = HEAD_SIZE // 2
    freqs = ROPE_BASE ** (-jnp.arange(half, dtype=jnp.float32) / half)
    angles = device_places.astype(jnp.float32)[:, None] * jnp.tile(freqs, TILE // half)[None, :]
    cosine, sine = jnp.cos(angles), jnp.sin(angles)
    order = own_order(width, fast)
    wide_order = order.astype(jnp.float32)

    def to_own(value):
        if not fast:
            return value
        return jnp.dot(value, order, preferred_element_type=jnp.float32).astype(value.dtype)

    def to_plain(value):
        if not fast:
            return value
        return jnp.einsum("tc,dc->td", value, order, preferred_element_type=jnp.float32)

    def to_plain_wide(value):
        if not fast:
            return value
        return jnp.einsum("tc,dc->td", value, wide_order, precision=HIGHEST)

    def gain_own(value):
        if not fast:
            return value
        return jnp.dot(value, wide_order, precision=HIGHEST)

    gains = gain_own(jnp.stack([norm_gain, mlp_gain]))
    norm_gain, mlp_gain = gains[0], gains[1]
    x_rows = to_own(layer_input[0]).astype(jnp.float32)
    grad_rows = to_own(out_grad[0])
    head_params = jnp.pad(
        jnp.stack([dt_bias, jnp.exp(a_log), d_skip]), ((0, 5), (0, TILE - MH))
    )
    step_pad = jnp.pad(w_dt, ((0, 0), (0, TILE - MH)))
    out_shard = pair_heads(w_out.T)
    down_shard = w_down.T
    shards = (
        jnp.concatenate([w_ssm_in[:, ssm_width:], step_pad], axis=1),
        jnp.concatenate([pair_heads(w_attn), w_ssm_in[:, :ssm_width]], axis=1),
        out_shard[:, : w_out.shape[0] // 2],
        out_shard[:, w_out.shape[0] // 2 :],
        w_gate_up[:, :FF],
        w_gate_up[:, FF:],
        down_shard[:, : FF // 2],
        down_shard[:, FF // 2 :],
    )
    full = []
    ahead = None
    for i in range(0, 8, 2):
        pair = shards[i : i + 2]
        if fast:
            if ahead is not None:
                pair, ahead = lax.optimization_barrier((pair, ahead))
            za, fa = gather_stages(pair[0], True)
            zb, fb = gather_stages(pair[1], False)
            ahead = (za, zb)
            full += [fa, fb]
        else:
            full += [lax.all_gather(p, ("seq", "batch"), axis=0, tiled=True) for p in pair]
    full_conv, full_mix, out_a, out_b, full_gate, full_up, down_a, down_b = full
    scale_one = rms_scale(x_rows)
    normed = (x_rows * scale_one * norm_gain).astype(jnp.bfloat16)
    conv_proj = jnp.dot(normed, full_conv, preferred_element_type=jnp.float32)
    mix_proj = jnp.dot(normed, full_mix, preferred_element_type=jnp.float32)
    queries, own_pairs = big_call(
        rope_kernel,
        (
            shape_of((token_rows, query_width), jnp.bfloat16),
            shape_of((token_rows, 2 * key_value_width), jnp.bfloat16),
        ),
        mix_proj[:, :attn_width],
        cosine,
        sine,
    )
    all_pairs = seq_gather(own_pairs, fast)
    gate_z = mix_proj[:, attn_width:]
    raw_xbc = conv_proj[:, :xbc_width]
    step_proj = conv_proj[:, xbc_width:]
    rim_rows = shifted(raw_xbc[token_rows - (CONV - 1) :], "seq", 1)
    extended = jnp.concatenate([rim_rows, raw_xbc], axis=0)
    ext_pos = first_pos - (CONV - 1) + jnp.arange(token_rows + CONV - 1, dtype=jnp.int32)
    ext_segment = segments(seq_lens, ext_pos)[0]

    def conv_local(ext_rows, conv_weight, conv_bias):
        return conv_mix(ext_rows, ext_segment, conv_weight, conv_bias)

    conv_out, conv_pullback = jax.vjp(conv_local, extended, conv_w, conv_b)
    conv_narrow = conv_out.astype(jnp.bfloat16)
    inputs_x, inputs_bc = conv_narrow[:, :ssm_width], conv_narrow[:, ssm_width:]
    ssm_local, state_own, steps_dt, running_decay = ssm_forward(
        info, inputs_x, inputs_bc, step_proj, head_params
    )
    state_in = scan_states(state_own, fast, True)
    attended, attended_t, log_total = attn_forward(info, queries, all_pairs)
    ssm_flat, ssm_normed, scale_gated = ssm_finish(
        info, ssm_local, inputs_bc, running_decay, state_in, gate_z, ssm_gain[None]
    )
    joined = jnp.concatenate([attended, ssm_normed], axis=1)
    half_in = joined.shape[1] // 2

    def narrow_out(left, parts):
        cut = left.shape[1] // 2
        return jnp.einsum(
            "tc,dc->td", left[:, :cut], parts[0], preferred_element_type=jnp.float32
        ) + jnp.einsum("tc,dc->td", left[:, cut:], parts[1], preferred_element_type=jnp.float32)

    middle = x_rows + narrow_out(joined, (out_a, out_b))
    scale_two = rms_scale(middle)
    normed_two = (middle * scale_two * mlp_gain).astype(jnp.bfloat16)
    gate_part = jnp.dot(normed_two, full_gate, preferred_element_type=jnp.float32)
    up_part = jnp.dot(normed_two, full_up, preferred_element_type=jnp.float32)
    hidden = (jax.nn.silu(gate_part) * up_part).astype(jnp.bfloat16)
    layer_out = middle + narrow_out(hidden, (down_a, down_b))
    g_down = [
        weight_grad(grad_rows, hidden[:, : FF // 2], fast, True),
        weight_grad(grad_rows, hidden[:, FF // 2 :], fast, False),
    ]
    d_hidden = jnp.concatenate(
        [
            jnp.dot(grad_rows, down_a, preferred_element_type=jnp.float32),
            jnp.dot(grad_rows, down_b, preferred_element_type=jnp.float32),
        ],
        axis=1,
    )
    sig_gate = jax.nn.sigmoid(gate_part)
    d_gate = (d_hidden * up_part * (sig_gate * (1.0 + gate_part * (1.0 - sig_gate)))).astype(
        jnp.bfloat16
    )
    d_up = (d_hidden * gate_part * sig_gate).astype(jnp.bfloat16)
    g_gate_up = [
        weight_grad(normed_two, d_gate, fast, True),
        weight_grad(normed_two, d_up, fast, False),
    ]
    d_normed_two = narrow_out(jnp.concatenate([d_gate, d_up], axis=1), (full_gate, full_up))
    d_middle_norm, g_mlp_gain = norm_back(middle, scale_two, mlp_gain, d_normed_two)
    d_middle = grad_rows.astype(jnp.float32) + d_middle_norm
    d_mixer = d_middle.astype(jnp.bfloat16)
    g_out = [
        weight_grad(d_mixer, joined[:, :half_in], fast, True),
        weight_grad(d_mixer, joined[:, half_in:], fast, False),
    ]
    d_joined = jnp.concatenate(
        [
            jnp.dot(d_mixer, out_a, preferred_element_type=jnp.float32),
            jnp.dot(d_mixer, out_b, preferred_element_type=jnp.float32),
        ],
        axis=1,
    )
    attended_gradient = d_joined[:, :query_width].astype(jnp.bfloat16)
    d_ssm_out, d_gate_z, pull, g_ssm_gain = gate_back(
        info,
        d_joined[:, query_width:],
        ssm_flat,
        gate_z,
        scale_gated,
        ssm_gain[None],
        running_decay,
        inputs_bc,
    )
    d_state = scan_states(jnp.concatenate([pull, state_own[NS:]], axis=0), fast, False)
    d_queries, d_pairs = attn_backward(
        info, queries, all_pairs, attended_gradient, attended_t, log_total
    )
    own_d_pairs = seq_scatter(d_pairs, fast)
    dx_part, d_bc_part, d_cum_part, d_dt_part, g_skip_rows = ssm_back(
        info, inputs_x, inputs_bc, steps_dt, running_decay, d_ssm_out, head_params
    )
    g_inputs_x, g_inputs_bc, d_step_pad, head_sums = state_back(
        info,
        inputs_x,
        inputs_bc,
        steps_dt,
        running_decay,
        d_ssm_out,
        head_params,
        step_proj,
        state_in,
        d_state,
        dx_part,
        d_bc_part,
        d_cum_part,
        d_dt_part,
    )
    g_a_log, g_dt_bias, g_d_skip = head_sums[0, :MH], head_sums[1, :MH], g_skip_rows[0, :MH]
    d_conv_out = jnp.concatenate([g_inputs_x, g_inputs_bc], axis=1)
    g_extended, g_conv_w, g_conv_b = conv_pullback(d_conv_out)
    back_rim = shifted(g_extended[: CONV - 1], "seq", -1)
    d_raw = g_extended[CONV - 1 :] + jnp.concatenate(
        [jnp.zeros((token_rows - (CONV - 1), xbc_width), jnp.float32), back_rim], axis=0
    )
    d_conv_proj = jnp.concatenate([d_raw.astype(jnp.bfloat16), d_step_pad], axis=1)
    (d_attn_proj,) = big_call(
        rope_back_kernel,
        (shape_of((token_rows, attn_width), jnp.bfloat16),),
        d_queries,
        own_d_pairs,
        cosine,
        sine,
    )
    d_mix_proj = jnp.concatenate([d_attn_proj, d_gate_z], axis=1)
    g_conv_in = weight_grad(normed, d_conv_proj, fast, True)
    g_mix_in = weight_grad(normed, d_mix_proj, fast, False)
    d_normed = jnp.einsum(
        "tc,dc->td", d_conv_proj, full_conv, preferred_element_type=jnp.float32
    ) + jnp.einsum("tc,dc->td", d_mix_proj, full_mix, preferred_element_type=jnp.float32)
    d_input_norm, g_norm_gain = norm_back(x_rows, scale_one, norm_gain, d_normed)
    input_grad = d_middle + d_input_norm
    grad_attn = pair_heads(g_mix_in[:, :attn_width], True)
    grad_ssm_in = jnp.concatenate([g_mix_in[:, attn_width:], g_conv_in[:, :xbc_width]], axis=1)
    grad_dt = g_conv_in[:, xbc_width : xbc_width + MH]
    grad_out = pair_heads(jnp.concatenate(g_out, axis=1), True).T
    grad_gate_up = jnp.concatenate(g_gate_up, axis=1)
    grad_down = jnp.concatenate(g_down, axis=1).T
    gain_grads = to_plain_wide(jnp.stack([g_norm_gain, g_mlp_gain]))
    small_sums = total_small(
        (
            gain_grads[0],
            gain_grads[1],
            g_ssm_gain[0],
            g_conv_w,
            g_conv_b,
            g_a_log,
            g_dt_bias,
            g_d_skip,
        ),
        fast,
    )
    return (
        to_plain(layer_out.astype(jnp.bfloat16)).astype(jnp.bfloat16)[None],
        to_plain_wide(input_grad)[None],
        grad_attn,
        grad_ssm_in,
        grad_dt,
        grad_out,
        grad_gate_up,
        grad_down,
        *small_sums,
    )


def solution(mesh):
    return jax.shard_map(
        on_device,
        mesh=mesh,
        in_specs=(
            P("batch", "seq", None),
            P("batch", None),
            P(("seq", "batch"), None),
            P(("seq", "batch"), None),
            P(("seq", "batch"), None),
            P(None, ("seq", "batch")),
            P(("seq", "batch"), None),
            P(None, ("seq", "batch")),
            P(),
            P(),
            P(),
            P(),
            P(),
            P(),
            P(),
            P(),
            P("batch", "seq", None),
        ),
        out_specs=(
            P("batch", "seq", None),
            P("batch", "seq", None),
            P(("seq", "batch"), None),
            P(("seq", "batch"), None),
            P(("seq", "batch"), None),
            P(None, ("seq", "batch")),
            P(("seq", "batch"), None),
            P(None, ("seq", "batch")),
            P(),
            P(),
            P(),
            P(),
            P(),
            P(),
            P(),
            P(),
        ),
        check_vma=False,
    )
```

```python
import jax
import jax.numpy as jnp
from jax import lax
from jax.experimental import pallas as pl
from jax.experimental.pallas import tpu as pltpu
from jax.sharding import PartitionSpec as P

QUERY_HEADS = 8
KEY_VALUE_HEADS = 2
HEAD_SIZE = 64
MH = 24
MP = 64
NS = 128
FF = 2048
CONV = 4
SPAN = 128


HIGHEST = lax.Precision.HIGHEST
NEGATIVE_FILL = -1e30
ROPE_BASE = 10000.0
NORM_EPS = 1e-06


def shifted(block, axis, distance):
    devices = range(lax.axis_size(axis))
    route = [(i - distance, i) for i in devices if i - distance in devices]
    return lax.ppermute(block, axis, route)


def is_fast(width):
    return lax.axis_size("seq") == 8 and lax.axis_size("batch") == 4 and width % (32 * 32) == 0


def pack_small(arrays):
    flat = jnp.concatenate([a.reshape(-1) for a in arrays])
    return jnp.pad(flat, (0, -flat.shape[0] % 1024)).reshape(-1, 128)


def unpack_small(flat, arrays):
    flat = flat.reshape(-1)
    out, start = [], 0
    for a in arrays:
        out.append(flat[start : start + a.size].reshape(a.shape))
        start += a.size
    return out


def own_order(width, fast):
    blocks = 32
    per = width // blocks
    row = lax.broadcasted_iota(jnp.int32, (width, width), 0)
    col = lax.broadcasted_iota(jnp.int32, (width, width), 1)
    if not fast:
        return (row == col).astype(jnp.bfloat16)
    me = lax.axis_index("seq") * 4 + lax.axis_index("batch")
    j = col // per
    flipped = (j & 1) * 16 + (j & 2) * 4 + (j & 4) + (j & 8) // 4 + (j & 16) // 16
    source = (flipped ^ me) * per + col % per
    return (row == source).astype(jnp.bfloat16)


def rms_scale(value_rows):
    return lax.rsqrt(jnp.mean(value_rows * value_rows, axis=-1, keepdims=True) + NORM_EPS)


def norm_back(value_rows, scales, gains, grads):
    gain_grad = jnp.sum(grads * value_rows * scales, axis=0)
    inner = grads * gains
    coeff = jnp.mean(inner * value_rows, axis=-1, keepdims=True)
    return (scales * (inner - value_rows * scales * scales * coeff), gain_grad)


def segments(lengths, positions):
    ends = jnp.cumsum(lengths)
    passed = ends[None, :] <= positions[:, None]
    segment = jnp.sum(passed.astype(jnp.int32), axis=1)
    device_places = positions - jnp.sum(jnp.where(passed, lengths[None, :], 0), axis=1)
    return (segment, device_places)


def conv_mix(extended, ext_segment, conv_weight, conv_bias):
    row_count = extended.shape[0] - (CONV - 1)
    summed = conv_bias[None, :]
    for lagged in range(CONV):
        same_seq = (ext_segment[lagged : lagged + row_count] == ext_segment[CONV - 1 :]).astype(
            extended.dtype
        )
        summed = (
            summed
            + conv_weight[lagged][None, :]
            * extended[lagged : lagged + row_count]
            * same_seq[:, None]
        )
    return jax.nn.silu(summed)


TILE = 128
PAIRS = QUERY_HEADS // 2
CHUNK = 256


def dot(left, right):
    return jnp.dot(left, right, preferred_element_type=jnp.float32)


def dot_nt(left, right):
    return lax.dot_general(
        left, right, (((1,), (1,)), ((), ())), preferred_element_type=jnp.float32
    )


def dot_tn(left, right):
    return lax.dot_general(
        left, right, (((0,), (0,)), ((), ())), preferred_element_type=jnp.float32
    )


def exact(left, right):
    return jnp.dot(left, right, precision=HIGHEST, preferred_element_type=jnp.float32)


def two_part(left, right):
    high = left.astype(jnp.bfloat16)
    low = (left - high.astype(jnp.float32)).astype(jnp.bfloat16)
    return dot(high, right) + dot(low, right)


def seg_start(where_at, info):
    start = jnp.zeros_like(where_at)
    for k in range(1, 4):
        start = jnp.where(where_at >= info[k], jnp.maximum(start, info[k]), start)
    return start


def big_call(kernel, outs, *args, scratch=(), flops=0, smem=0, limit=48):
    specs = [pl.BlockSpec(memory_space=pltpu.SMEM)] * smem
    specs += [pl.BlockSpec(memory_space=pltpu.VMEM)] * (len(args) - smem)
    moved = sum(a.size * a.dtype.itemsize for a in args)
    moved += sum(o.size * o.dtype.itemsize for o in outs)
    return pl.pallas_call(
        kernel,
        out_shape=list(outs),
        in_specs=specs,
        out_specs=[pl.BlockSpec(memory_space=pltpu.VMEM)] * len(outs),
        scratch_shapes=list(scratch),
        cost_estimate=pl.CostEstimate(flops=flops, bytes_accessed=moved, transcendentals=0),
        compiler_params=pltpu.CompilerParams(vmem_limit_bytes=limit * 1024 * 1024),
    )(*args)


def shape_of(shape, dtype):
    return jax.ShapeDtypeStruct(shape, dtype)


def turn(value, cosine, sine):
    lane = lax.broadcasted_iota(jnp.int32, value.shape, 1) % HEAD_SIZE
    mixed = jnp.where(
        lane < HEAD_SIZE // 2,
        -pltpu.roll(value, TILE - HEAD_SIZE // 2, 1),
        pltpu.roll(value, HEAD_SIZE // 2, 1),
    )
    return value * cosine + mixed * sine


def rope_kernel(proj, cosine, sine, q_out, kv_out):
    cos, sin = cosine[...], sine[...]
    for i in range(PAIRS):
        cols = pl.ds(i * TILE, TILE)
        turned = turn(proj[:, cols], cos, sin).astype(jnp.bfloat16)
        q_out[:, cols] = (turned.astype(jnp.float32) * HEAD_SIZE**-0.5).astype(jnp.bfloat16)
    base = PAIRS * TILE
    kv_out[:, :TILE] = turn(proj[:, base : base + TILE], cos, sin).astype(jnp.bfloat16)
    kv_out[:, TILE:] = proj[:, base + TILE : base + 2 * TILE].astype(jnp.bfloat16)


def halves_of(value):
    lane = lax.broadcasted_iota(jnp.int32, value.shape, 1)
    wide = value.astype(jnp.float32)
    first = jnp.where(lane < HEAD_SIZE, wide, 0.0).astype(value.dtype)
    return first, jnp.where(lane < HEAD_SIZE, 0.0, wide).astype(value.dtype)


def block_range(info):
    first = info[0]
    low = seg_start(first, info) // CHUNK
    return low, first // CHUNK - low + 1


def attn_mask(info, block):
    rows = lax.broadcasted_iota(jnp.int32, (CHUNK, CHUNK), 0) + block * CHUNK
    at = lax.broadcasted_iota(jnp.int32, (1, CHUNK), 1) + info[0]
    return (rows <= at) & (rows >= seg_start(at, info))


def attend_block(info, block, keys, values_t, heads, acc, top, total):
    allowed = attn_mask(info, block)
    for h in range(QUERY_HEADS):
        scores = jnp.where(allowed, dot_nt(keys, heads[h]), NEGATIVE_FILL)
        old = top[h : h + 1]
        new = jnp.maximum(old, jnp.max(scores, axis=0, keepdims=True))
        probs = jnp.where(allowed, jnp.exp(scores - new), 0.0)
        shrink = jnp.exp(old - new)
        top[h : h + 1] = new
        total[h : h + 1] = total[h : h + 1] * shrink + jnp.sum(probs, axis=0, keepdims=True)
        side = (h % 2) * HEAD_SIZE
        acc[h] = acc[h] * shrink + dot(
            values_t[side : side + HEAD_SIZE], probs.astype(jnp.bfloat16)
        )


def attend_write(acc, total, out, out_t):
    for i in range(PAIRS):
        pair = jnp.concatenate(
            [acc[2 * i] / total[2 * i : 2 * i + 1], acc[2 * i + 1] / total[2 * i + 1 : 2 * i + 2]],
            axis=0,
        )
        out_t[i * TILE : (i + 1) * TILE] = pair
        out[:, i * TILE : (i + 1) * TILE] = pair.T.astype(jnp.bfloat16)


def attn_forward_kernel(info, q, kv, out, out_t, lse, heads, acc, top, total):
    for i in range(PAIRS):
        heads[2 * i], heads[2 * i + 1] = halves_of(q[:, i * TILE : (i + 1) * TILE])
    acc[...] = jnp.zeros_like(acc)
    total[...] = jnp.zeros_like(total)
    top[...] = jnp.full(top.shape, NEGATIVE_FILL, jnp.float32)
    low, count = block_range(info)

    def step(j, carry):
        block = low + j
        place = pl.ds(pl.multiple_of(block * CHUNK, CHUNK), CHUNK)
        keys = kv[place, :TILE]
        values_t = kv[place, TILE:].astype(jnp.float32).T.astype(jnp.bfloat16)
        attend_block(info, block, keys, values_t, heads, acc, top, total)
        return carry

    lax.fori_loop(0, count, step, 0)
    lse[...] = top[...] + jnp.log(total[...])
    attend_write(acc, total, out, out_t)


def attn_forward(info, q, kv):
    rows = q.shape[0]
    f32 = jnp.float32
    return big_call(
        attn_forward_kernel,
        (
            shape_of(q.shape, jnp.bfloat16),
            shape_of(q.shape[::-1], f32),
            shape_of((QUERY_HEADS, rows), f32),
        ),
        info,
        q,
        kv,
        smem=1,
        scratch=(
            pltpu.VMEM((QUERY_HEADS, rows, TILE), jnp.bfloat16),
            pltpu.VMEM((QUERY_HEADS, HEAD_SIZE, rows), f32),
            pltpu.VMEM((QUERY_HEADS, rows), f32),
            pltpu.VMEM((QUERY_HEADS, rows), f32),
        ),
        flops=4 * rows * kv.shape[0] * q.shape[1],
    )


def attend_back_start(q, grad, out_t, heads, grads, delta, acc):
    for i in range(PAIRS):
        cols = slice(i * TILE, (i + 1) * TILE)
        heads[2 * i], heads[2 * i + 1] = halves_of(q[:, cols])
        grads[2 * i], grads[2 * i + 1] = halves_of(grad[:, cols])
        both = grad[:, cols].astype(jnp.float32).T * out_t[cols]
        delta[2 * i : 2 * i + 1] = jnp.sum(both[:HEAD_SIZE], axis=0, keepdims=True)
        delta[2 * i + 1 : 2 * i + 2] = jnp.sum(both[HEAD_SIZE:], axis=0, keepdims=True)
    acc[...] = jnp.zeros_like(acc)


def attend_back_block(info, block, keys, values, lse, target, heads, grads, delta, acc):
    keys_t = keys.astype(jnp.float32).T.astype(jnp.bfloat16)
    allowed = attn_mask(info, block)
    d_keys = jnp.zeros((CHUNK, TILE), jnp.float32)
    d_values = jnp.zeros((CHUNK, TILE), jnp.float32)
    for h in range(QUERY_HEADS):
        scores = dot_nt(keys, heads[h])
        probs = jnp.where(allowed, jnp.exp(scores - lse[h : h + 1]), 0.0)
        d_probs = dot_nt(values, grads[h])
        d_scores = (probs * (d_probs - delta[h : h + 1])).astype(jnp.bfloat16)
        d_values = d_values + dot(probs.astype(jnp.bfloat16), grads[h])
        d_keys = d_keys + dot(d_scores, heads[h])
        side = (h % 2) * HEAD_SIZE
        acc[h] = acc[h] + dot(keys_t[side : side + HEAD_SIZE], d_scores)
    target[:, :TILE] = d_keys.astype(jnp.bfloat16)
    target[:, TILE:] = d_values.astype(jnp.bfloat16)


def attend_back_write(acc, dq):
    for i in range(PAIRS):
        pair = jnp.concatenate([acc[2 * i], acc[2 * i + 1]], axis=0)
        dq[:, i * TILE : (i + 1) * TILE] = pair.T * HEAD_SIZE**-0.5


def attn_backward_kernel(info, q, kv, grad, out_t, lse, dq, dkv, heads, grads, delta, acc):
    attend_back_start(q, grad, out_t, heads, grads, delta, acc)
    dkv[...] = jnp.zeros_like(dkv)
    low, count = block_range(info)

    def step(j, carry):
        block = low + j
        place = pl.ds(pl.multiple_of(block * CHUNK, CHUNK), CHUNK)
        attend_back_block(
            info, block, kv[place, :TILE], kv[place, TILE:], lse, dkv.at[place], heads, grads,
            delta, acc,
        )
        return carry

    lax.fori_loop(0, count, step, 0)
    attend_back_write(acc, dq)


def attn_backward(info, q, kv, grad, out_t, lse):
    rows = q.shape[0]
    f32 = jnp.float32
    return big_call(
        attn_backward_kernel,
        (shape_of(q.shape, f32), shape_of(kv.shape, jnp.bfloat16)),
        info,
        q,
        kv,
        grad,
        out_t,
        lse,
        smem=1,
        scratch=(
            pltpu.VMEM((QUERY_HEADS, rows, TILE), jnp.bfloat16),
            pltpu.VMEM((QUERY_HEADS, rows, TILE), jnp.bfloat16),
            pltpu.VMEM((QUERY_HEADS, rows), f32),
            pltpu.VMEM((QUERY_HEADS, HEAD_SIZE, rows), f32),
        ),
        flops=10 * rows * kv.shape[0] * q.shape[1],
    )


def rope_back_kernel(dq, dkv, cosine, sine, out):
    cos, sin = cosine[...], -sine[...]
    for i in range(PAIRS):
        cols = slice(i * TILE, (i + 1) * TILE)
        out[:, cols] = turn(dq[:, cols], cos, sin).astype(jnp.bfloat16)
    base = PAIRS * TILE
    out[:, base : base + TILE] = turn(dkv[:, :TILE], cos, sin).astype(jnp.bfloat16)
    out[:, base + TILE :] = dkv[:, TILE:].astype(jnp.bfloat16)


STATE_ROWS = NS + 16


def lane_pick(value, first):
    rows = value.shape[0]
    lane = lax.broadcasted_iota(jnp.int32, (rows, TILE), 1)
    return jnp.where(lane < MP, value[:, first : first + 1], value[:, first + 1 : first + 2])


def spread_heads(width):
    head = lax.broadcasted_iota(jnp.int32, (TILE, width), 0)
    col = lax.broadcasted_iota(jnp.int32, (TILE, width), 1)
    return jnp.where(head == col // MP, 1.0, 0.0).astype(jnp.bfloat16)


def gather_heads(width):
    head = lax.broadcasted_iota(jnp.int32, (width, TILE), 1)
    col = lax.broadcasted_iota(jnp.int32, (width, TILE), 0)
    return jnp.where(head == col // MP, 1.0, 0.0).astype(jnp.bfloat16)


def head_lanes(rows):
    return lax.broadcasted_iota(jnp.int32, (rows, TILE), 1) < MH


def chunk_places(info, rows):
    at = lax.broadcasted_iota(jnp.int32, (rows, 1), 0) + info[0]
    return seg_start(at, info) - info[0]


def ssm_forward_kernel(info, x, bc, step_in, head_params, y, state, dt_out, cum_out, dt_t, cum_t):
    rows = x.shape[0]
    bias, rate, skip = head_params[0:1], head_params[1:2], head_params[2:3]
    raw = step_in[...] + bias
    dt = jnp.maximum(raw, 0.0) + jnp.log1p(jnp.exp(-jnp.abs(raw)))
    dt = jnp.where(head_lanes(rows), dt, 0.0)
    row = lax.broadcasted_iota(jnp.int32, (rows, rows), 0)
    col = lax.broadcasted_iota(jnp.int32, (rows, rows), 1)
    lower = jnp.where(row >= col, 1.0, 0.0)
    cum = exact(lower, -dt * rate)
    dt_out[...] = dt
    cum_out[...] = cum
    dt_t[...] = dt.T
    cum_t[...] = cum.T
    starts = chunk_places(info, rows)
    last_start = seg_start(info[0] + rows - 1, info) - info[0]
    place = lax.broadcasted_iota(jnp.int32, (rows, 1), 0)
    end = cum[rows - 1 : rows]
    leave = jnp.where(place >= last_start, jnp.exp(jnp.minimum(end - cum, 0.0)) * dt, 0.0)
    narrow_b, narrow_c = bc[:, :NS], bc[:, NS:]
    b_t = narrow_b.astype(jnp.float32).T.astype(jnp.bfloat16)
    products = dot_nt(narrow_c, narrow_b)
    through = jnp.where(last_start < 0, jnp.exp(end), 0.0)
    high = through.astype(jnp.bfloat16).astype(jnp.float32)
    line = lax.broadcasted_iota(jnp.int32, (16, TILE), 0)
    both = jnp.where(line == 0, high, jnp.where(line == 1, through - high, 0.0))
    spread = spread_heads(x.shape[1])
    state[NS:] = dot(both.astype(jnp.bfloat16), spread).astype(jnp.bfloat16)
    skips = jnp.broadcast_to(skip, (8, TILE))
    skip_row = two_part(skips, spread)[:1]
    lane = lax.broadcasted_iota(jnp.int32, (SPAN, TILE), 1)
    for i in range(MH // 2):
        cols = slice(i * TILE, (i + 1) * TILE)
        tile = x[:, cols]
        state[:NS, cols] = dot(
            b_t, (tile.astype(jnp.float32) * lane_pick(leave, 2 * i)).astype(jnp.bfloat16)
        ).astype(jnp.bfloat16)
        for part in range(rows // SPAN):
            here = slice(part * SPAN, (part + 1) * SPAN)
            upto = (part + 1) * SPAN
            allowed = (row[here, :upto] >= col[here, :upto]) & (col[here, :upto] >= starts[here])
            sides = []
            for h in (2 * i, 2 * i + 1):
                spread_log = cum[here, h : h + 1] - cum_t[h : h + 1, :upto]
                decay = jnp.exp(jnp.where(allowed, spread_log, NEGATIVE_FILL))
                mixing = products[here, :upto] * decay * dt_t[h : h + 1, :upto]
                sides.append(dot(mixing.astype(jnp.bfloat16), tile[:upto]))
            own = skip_row[:, cols] * tile[here].astype(jnp.float32)
            y[here, cols] = jnp.where(lane < MP, sides[0], sides[1]) + own


def ssm_forward(info, x, bc, step_in, head_params):
    rows, width = x.shape
    f32 = jnp.float32
    return big_call(
        ssm_forward_kernel,
        (
            shape_of((rows, width), f32),
            shape_of((STATE_ROWS, width), jnp.bfloat16),
            shape_of((rows, TILE), f32),
            shape_of((rows, TILE), f32),
        ),
        info,
        x,
        bc,
        step_in,
        head_params,
        smem=1,
        scratch=(pltpu.VMEM((TILE, rows), f32), pltpu.VMEM((TILE, rows), f32)),
        flops=4 * rows * rows * width,
    )


def entering_of(info, cum):
    rows = cum.shape[0]
    return jnp.where(chunk_places(info, rows) < 0, jnp.exp(jnp.minimum(cum, 0.0)), 0.0)


def ssm_finish_kernel(info, y, bc, cum, state_in, z, gain, ssm_out, normed, scale):
    rows = y.shape[0]
    enter = entering_of(info, cum[...])
    narrow_c = bc[:, NS:]
    squares = jnp.zeros((rows, TILE), jnp.float32)
    tiles = MH // 2
    for i in range(tiles):
        cols = slice(i * TILE, (i + 1) * TILE)
        out = y[:, cols] + lane_pick(enter, 2 * i) * dot(narrow_c, state_in[:, cols])
        ssm_out[:, cols] = out
        gate = z[:, cols]
        gated = out * (gate * jax.nn.sigmoid(gate))
        squares = squares + gated * gated
    mean = jnp.sum(squares, axis=1, keepdims=True) * (1.0 / (tiles * TILE))
    r = lax.rsqrt(mean + NORM_EPS)
    scale[...] = jnp.broadcast_to(r, scale.shape)
    for i in range(tiles):
        cols = slice(i * TILE, (i + 1) * TILE)
        gate = z[:, cols]
        gated = ssm_out[:, cols] * (gate * jax.nn.sigmoid(gate))
        normed[:, cols] = (gated * r * gain[:, cols]).astype(jnp.bfloat16)


def ssm_finish(info, y, bc, cum, state_in, z, gain):
    rows, width = y.shape
    return big_call(
        ssm_finish_kernel,
        (
            shape_of((rows, width), jnp.float32),
            shape_of((rows, width), jnp.bfloat16),
            shape_of((rows, TILE), jnp.float32),
        ),
        info,
        y,
        bc,
        cum,
        state_in,
        z,
        gain,
        smem=1,
        flops=2 * rows * NS * width,
    )


def gate_back_kernel(info, dy, ssm_out, z, scale, gain, cum, bc, d_out, d_z, pull, g_gain):
    rows = dy.shape[0]
    tiles = MH // 2
    r = scale[:, :1]
    enter = entering_of(info, cum[...])
    c_t = bc[:, NS:].astype(jnp.float32).T.astype(jnp.bfloat16)
    inner = jnp.zeros((rows, TILE), jnp.float32)
    for i in range(tiles):
        cols = slice(i * TILE, (i + 1) * TILE)
        gate = z[:, cols]
        gated = ssm_out[:, cols] * (gate * jax.nn.sigmoid(gate))
        product = dy[:, cols] * gated
        g_gain[:, cols] = jnp.sum(product * r, axis=0, keepdims=True)
        inner = inner + product * gain[:, cols]
    coeff = jnp.sum(inner, axis=1, keepdims=True) * (1.0 / (tiles * TILE))
    for i in range(tiles):
        cols = slice(i * TILE, (i + 1) * TILE)
        gate = z[:, cols]
        sig = jax.nn.sigmoid(gate)
        silu = gate * sig
        out = ssm_out[:, cols]
        d_gated = r * (dy[:, cols] * gain[:, cols] - out * silu * (r * r * coeff))
        d_ssm = d_gated * silu
        d_out[:, cols] = d_ssm
        d_z[:, cols] = (d_gated * out * (sig * (1.0 + gate * (1.0 - sig)))).astype(jnp.bfloat16)
        pull[:, cols] = dot(c_t, (d_ssm * lane_pick(enter, 2 * i)).astype(jnp.bfloat16)).astype(
            jnp.bfloat16
        )


def gate_back(info, dy, ssm_out, z, scale, gain, cum, bc):
    rows, width = dy.shape
    return big_call(
        gate_back_kernel,
        (
            shape_of((rows, width), jnp.float32),
            shape_of((rows, width), jnp.bfloat16),
            shape_of((NS, width), jnp.bfloat16),
            shape_of((1, width), jnp.float32),
        ),
        info,
        dy,
        ssm_out,
        z,
        scale,
        gain,
        cum,
        bc,
        smem=1,
        flops=2 * rows * NS * width,
    )


def ssm_back_kernel(info, x, bc, dt, cum, grad, head_params, dx, d_bc, d_cum, d_dt, g_skip, cols_t, d_rows):
    rows, width = x.shape
    skip = head_params[2:3]
    cols_t[...] = cum[...].T
    row = lax.broadcasted_iota(jnp.int32, (rows, rows), 0)
    col = lax.broadcasted_iota(jnp.int32, (rows, rows), 1)
    at = lax.broadcasted_iota(jnp.int32, (1, rows), 1) + info[0]
    starts = seg_start(at, info) - info[0]
    narrow_b, narrow_c = bc[:, :NS], bc[:, NS:]
    products = dot_nt(narrow_b, narrow_c)
    skip_row = two_part(jnp.broadcast_to(skip, (8, TILE)), spread_heads(width))[:1]
    lane = lax.broadcasted_iota(jnp.int32, (SPAN, TILE), 1)
    parts = rows // SPAN
    d_products = [jnp.zeros((SPAN, rows - p * SPAN), jnp.float32) for p in range(parts)]
    d_rows[...] = jnp.zeros_like(d_rows)
    step_sums = [jnp.zeros((SPAN, TILE), jnp.float32) for p in range(parts)]
    skip_sums = []
    for i in range(MH // 2):
        cols = slice(i * TILE, (i + 1) * TILE)
        tile = x[:, cols]
        wide = grad[:, cols]
        narrow = wide.astype(jnp.bfloat16)
        skip_sums.append(jnp.sum(wide * tile.astype(jnp.float32), axis=0, keepdims=True))
        tile_sides = halves_of(tile)
        for part in range(parts):
            here = slice(part * SPAN, (part + 1) * SPAN)
            since = part * SPAN
            allowed = (row[here, since:] <= col[here, since:]) & (
                row[here, since:] >= starts[:, since:]
            )
            sides = []
            for side in range(2):
                h = 2 * i + side
                spread_log = cols_t[h : h + 1, since:] - cum[here, h : h + 1]
                decay = jnp.exp(jnp.where(allowed, spread_log, NEGATIVE_FILL))
                decay_dt = decay * dt[here, h : h + 1]
                mixing = products[here, since:] * decay_dt
                sides.append(dot(mixing.astype(jnp.bfloat16), narrow[since:]))
                d_mixing = dot_nt(tile_sides[side][here], narrow[since:])
                d_products[part] = d_products[part] + d_mixing * decay_dt
                whole = d_mixing * mixing
                d_rows[h : h + 1, since:] += jnp.sum(whole, axis=0, keepdims=True)
                weighed = d_mixing * (products[here, since:] * decay)
                step_sums[part] = jnp.where(
                    lane == h, jnp.sum(weighed, axis=1, keepdims=True), step_sums[part]
                )
            dx[here, cols] = (
                jnp.where(lane < MP, sides[0], sides[1]) + skip_row[:, cols] * wide[here]
            )
    all_steps = jnp.concatenate(step_sums, axis=0)
    d_dt[...] = all_steps
    d_cum[...] = d_rows[...].T - all_steps * dt[...]
    g_skip[...] = jnp.broadcast_to(
        two_part(
            jnp.broadcast_to(jnp.concatenate(skip_sums, axis=1), (8, width)), gather_heads(width)
        ),
        g_skip.shape,
    )
    full = jnp.concatenate(
        [
            d
            if p == 0
            else jnp.concatenate([jnp.zeros((SPAN, p * SPAN), jnp.float32), d], axis=1)
            for p, d in enumerate(d_products)
        ],
        axis=0,
    ).astype(jnp.bfloat16)
    d_bc[:, :NS] = dot(full, narrow_c)
    d_bc[:, NS:] = dot_tn(full, narrow_b)


def ssm_back(info, x, bc, dt, cum, grad, head_params):
    rows, width = x.shape
    f32 = jnp.float32
    return big_call(
        ssm_back_kernel,
        (
            shape_of((rows, width), f32),
            shape_of((rows, 2 * NS), f32),
            shape_of((rows, TILE), f32),
            shape_of((rows, TILE), f32),
            shape_of((8, TILE), f32),
        ),
        info,
        x,
        bc,
        dt,
        cum,
        grad,
        head_params,
        smem=1,
        scratch=(pltpu.VMEM((TILE, rows), f32), pltpu.VMEM((TILE, rows), f32)),
        flops=8 * rows * rows * width,
    )


def state_back_kernel(
    info, x, bc, dt, cum, grad, head_params, step_in, state_in, d_state, dx_in, d_bc_in, d_cum_in,
    d_dt_in, dx, d_bc, d_step, sums,
):
    rows, width = x.shape
    bias, rate = head_params[0:1], head_params[1:2]
    cums, steps = cum[...], dt[...]
    enter = entering_of(info, cums)
    last_start = seg_start(info[0] + rows - 1, info) - info[0]
    place = lax.broadcasted_iota(jnp.int32, (rows, 1), 0)
    end = cums[rows - 1 : rows]
    fade = jnp.where(place >= last_start, jnp.exp(jnp.minimum(end - cums, 0.0)), 0.0)
    leave = fade * steps
    through = jnp.where(last_start < 0, jnp.exp(end), 0.0)
    narrow_b, narrow_c = bc[:, :NS], bc[:, NS:]
    pick = gather_heads(width)
    d_leave = jnp.zeros((rows, TILE), jnp.float32)
    d_enter = jnp.zeros((rows, TILE), jnp.float32)
    d_b = d_bc_in[:, :NS]
    d_c = d_bc_in[:, NS:]
    link = jnp.zeros((8, TILE), jnp.float32)
    for i in range(MH // 2):
        cols = slice(i * TILE, (i + 1) * TILE)
        tile = x[:, cols].astype(jnp.float32)
        wide = grad[:, cols]
        pulled = d_state[:, cols]
        held = state_in[:, cols]
        from_b = dot(narrow_b, pulled)
        leave_tile = lane_pick(leave, 2 * i)
        dx[:, cols] = dx_in[:, cols] + leave_tile * from_b
        d_leave = d_leave + two_part(tile * from_b, pick[cols])
        d_enter = d_enter + two_part(wide * dot(narrow_c, held), pick[cols])
        d_b = d_b + dot_nt((tile * leave_tile).astype(jnp.bfloat16), pulled)
        d_c = d_c + dot_nt((wide * lane_pick(enter, 2 * i)).astype(jnp.bfloat16), held)
        meet = jnp.sum(
            pulled.astype(jnp.float32) * held.astype(jnp.float32), axis=0, keepdims=True
        )
        link = link + two_part(jnp.broadcast_to(meet, (8, TILE)), pick[cols])
    d_bc[:, :NS] = d_b
    d_bc[:, NS:] = d_c
    left = leave * d_leave
    d_cum = d_cum_in[...] + enter * d_enter - left
    at_end = jnp.sum(left, axis=0, keepdims=True) + through * link[:1]
    d_cum = d_cum + jnp.where(place == rows - 1, at_end, 0.0)
    row = lax.broadcasted_iota(jnp.int32, (rows, rows), 0)
    col = lax.broadcasted_iota(jnp.int32, (rows, rows), 1)
    d_log = exact(jnp.where(row <= col, 1.0, 0.0), d_cum)
    d_steps = d_dt_in[...] + fade * d_leave - d_log * rate
    d_pre = d_steps * jax.nn.sigmoid(step_in[...] + bias)
    d_pre = jnp.where(head_lanes(rows), d_pre, 0.0)
    d_step[...] = d_pre.astype(jnp.bfloat16)
    g_rate = jnp.sum(d_log * (-steps * rate), axis=0, keepdims=True)
    g_bias = jnp.sum(d_pre, axis=0, keepdims=True)
    line = lax.broadcasted_iota(jnp.int32, (8, TILE), 0)
    sums[...] = jnp.where(line == 0, g_rate, jnp.where(line == 1, g_bias, 0.0))


def state_back(info, *args):
    rows, width = args[0].shape
    f32 = jnp.float32
    return big_call(
        state_back_kernel,
        (
            shape_of((rows, width), f32),
            shape_of((rows, 2 * NS), f32),
            shape_of((rows, TILE), jnp.bfloat16),
            shape_of((8, TILE), f32),
        ),
        info,
        *args,
        smem=1,
        flops=12 * rows * NS * width,
    )


def join_states(earlier, later):
    decay = later[NS : NS + 1].astype(jnp.float32) + later[NS + 1 : NS + 2].astype(jnp.float32)
    before = earlier[NS : NS + 1].astype(jnp.float32) + earlier[NS + 1 : NS + 2].astype(jnp.float32)
    state = decay * earlier[:NS].astype(jnp.float32) + later[:NS].astype(jnp.float32)
    both = decay * before
    high = both.astype(jnp.bfloat16)
    low = (both - high.astype(jnp.float32)).astype(jnp.bfloat16)
    rest = jnp.zeros((STATE_ROWS - NS - 2, state.shape[1]), jnp.bfloat16)
    return jnp.concatenate([state.astype(jnp.bfloat16), high, low, rest], axis=0)


def scan_states(own, forward):
    place = lax.axis_index("seq")
    count = lax.axis_size("seq")
    nothing = jnp.concatenate(
        [
            jnp.zeros((NS, own.shape[1]), own.dtype),
            jnp.ones((1, own.shape[1]), own.dtype),
            jnp.zeros((STATE_ROWS - NS - 1, own.shape[1]), own.dtype),
        ],
        axis=0,
    )
    everything = lax.all_gather(own, "seq")

    def step(k, before):
        index = k if forward else count - 1 - k
        reached = index < place if forward else index > place
        part = lax.dynamic_index_in_dim(everything, index, 0, False)
        return jnp.where(reached, join_states(before, part), before)

    return lax.fori_loop(0, count, step, nothing)[:NS]


MESH = pl.DeviceIdType.MESH
ANY = pl.BlockSpec(memory_space=pl.ANY)
INTO_VMEM = pl.BlockSpec(memory_space=pltpu.VMEM)


def partners():
    seq, batch = lax.axis_index("seq"), lax.axis_index("batch")
    return {
        "far": (seq + 4 - 8 * (seq // 4), batch),
        "near": (seq + 2 - 4 * (seq // 2 % 2), batch),
        "x": (seq + 1 - 2 * (seq % 2), batch),
        "y": (seq, batch + 2 - 4 * (batch // 2)),
        "core": (seq, batch + 1 - 2 * (batch % 2)),
    }


def greet(others):
    barrier = pltpu.get_barrier_semaphore()
    for other in others:
        pl.semaphore_signal(barrier, inc=1, device_id=other, device_id_type=MESH)
    pl.semaphore_wait(barrier, len(others))


def remote(src, dst, send, recv, other):
    return pltpu.make_async_remote_copy(
        src_ref=src, dst_ref=dst, send_sem=send, recv_sem=recv, device_id=other, device_id_type=MESH
    )


def comm_call(kernel, outs, out_specs, args, in_specs, scratch, number, moved, limit=56):
    return pl.pallas_call(
        kernel,
        out_shape=list(outs),
        in_specs=in_specs,
        out_specs=out_specs,
        scratch_shapes=list(scratch),
        cost_estimate=pl.CostEstimate(flops=0, bytes_accessed=moved, transcendentals=0),
        compiler_params=pltpu.CompilerParams(
            collective_id=number, has_side_effects=True, vmem_limit_bytes=limit * 1024 * 1024
        ),
    )(*args)


def column_chunks(widths):
    pairs = []
    for k in range(0, len(widths), 2):
        pieces = max(1, max(widths[k], widths[k + 1]) // 1024)
        halves = []
        for p in (k, k + 1):
            tiles, first, cuts = widths[p] // TILE, 0, []
            for i in range(pieces):
                cols = (tiles // pieces + (1 if i < tiles % pieces else 0)) * TILE
                cuts.append((p, first, cols))
                first += cols
            halves.append(cuts)
        pairs += list(zip(*halves))
    return pairs


def gather_plan(x_first):
    plan = [("far", [(0, 1, 1)]), ("near", [(0, 2, 2)])]
    if x_first:
        plan += [("x", [(0, 4, 4)]), ("y", [(0, 8, 8)])]
    else:
        plan += [("y", [(0, 4, 8)]), ("x", [(0, 4, 4), (8, 4, 12)])]
    return plan + [("core", [(0, 16, 16)])]


def weight_gather_kernel(count, pairs, *refs):
    ins, outs = refs[:count], refs[count : 2 * count]
    send, recv, local = refs[2 * count :]
    others = partners()
    greet(list(others.values()))
    block = ins[0].shape[0]
    own = []
    for p in range(count):
        copy = pltpu.make_async_copy(ins[p], outs[p].at[pl.ds(0, block)], local.at[p])
        copy.start()
        own.append(copy)
    for copy in own:
        copy.wait()
    plans = [gather_plan(True), gather_plan(False)]
    started = {}
    for wave in range(len(pairs) + 5):
        for n in reversed(range(len(pairs))):
            stage = wave - n
            if stage < 0 or stage > 5:
                continue
            for side in range(2):
                p, column, cols = pairs[n][side]
                if stage > 0:
                    for copy in started[n, side, stage - 1]:
                        copy.wait_recv()
                if stage == 5:
                    continue
                name, moves = plans[side][stage]
                copies = []
                for k, (first, rows, there) in enumerate(moves):
                    copy = remote(
                        outs[p].at[pl.ds(first * block, rows * block), pl.ds(column, cols)],
                        outs[p].at[pl.ds(there * block, rows * block), pl.ds(column, cols)],
                        send.at[2 * n + side, stage, k],
                        recv.at[2 * n + side, stage, k],
                        others[name],
                    )
                    copy.start()
                    copies.append(copy)
                started[n, side, stage] = copies
    for copies in started.values():
        for copy in copies:
            copy.wait_send()


def weight_gather(parts):
    count = len(parts)
    outs = [shape_of((32 * p.shape[0], p.shape[1]), p.dtype) for p in parts]
    pairs = column_chunks([p.shape[1] for p in parts])
    dma = pltpu.SemaphoreType.DMA
    return comm_call(
        lambda *refs: weight_gather_kernel(count, pairs, *refs),
        outs,
        [ANY] * count,
        parts,
        [ANY] * count,
        [dma((2 * len(pairs), 5, 2)), dma((2 * len(pairs), 5, 2)), dma((count,))],
        0,
        64 * sum(p.size for p in parts),
    )


def bit_apart(r):
    me = lax.axis_index("seq")
    far = (r // 4 + me // 4) % 2
    near = (r // 2 % 2 + me // 2 % 2) % 2
    side = (r % 2 + me % 2) % 2
    return 4 * far + 2 * near + side


def join_into(target, earlier, later):
    decay = later[NS : NS + 1].astype(jnp.float32) + later[NS + 1 : NS + 2].astype(jnp.float32)
    before = earlier[NS : NS + 1].astype(jnp.float32) + earlier[NS + 1 : NS + 2].astype(jnp.float32)
    both = decay * before
    high = both.astype(jnp.bfloat16).astype(jnp.float32)
    line = lax.broadcasted_iota(jnp.int32, (STATE_ROWS - NS, both.shape[1]), 0)
    tail = jnp.where(line == 0, high, jnp.where(line == 1, both - high, 0.0))
    for first in range(0, NS, 32):
        rows = slice(first, first + 32)
        target[rows] = (
            decay * earlier[rows].astype(jnp.float32) + later[rows].astype(jnp.float32)
        ).astype(jnp.bfloat16)
    target[NS:] = tail.astype(jnp.bfloat16)


class StateScan:
    def __init__(self, forward, own, result, arrived, sent, before, send, recv, others):
        me = lax.axis_index("seq")
        self.seconds = []
        for bit in (me % 2, me // 2 % 2, me // 4):
            self.seconds.append(bit == 1 if forward else bit == 0)
        self.own, self.result, self.arrived, self.sent, self.before = (
            own, result, arrived, sent, before,
        )
        route = (others["x"], others["near"], others["far"])
        sources = (own, sent.at[0], sent.at[1])
        self.copies = [
            remote(sources[k], arrived.at[k], send.at[k], recv.at[k], route[k]) for k in range(3)
        ]

    def step(self, k):
        if k == 0:
            self.copies[0].start()
            return
        self.copies[k - 1].wait_recv()
        other = self.arrived.at[k - 1]
        mine = self.own if k == 1 else self.sent.at[k - 2]
        second = self.seconds[k - 1]
        before, result = self.before, self.result

        @pl.when(second)
        def _():
            if k < 3:
                join_into(self.sent.at[k - 1], other, mine)
            if k == 1:
                before[0] = other[...]
            elif k == 2:
                join_into(before.at[1], other, before.at[0])
            else:
                decay = before[1, NS : NS + 1].astype(jnp.float32) + before[
                    1, NS + 1 : NS + 2
                ].astype(jnp.float32)
                result[...] = (
                    decay * other[:NS].astype(jnp.float32) + before[1, :NS].astype(jnp.float32)
                ).astype(jnp.bfloat16)

        @pl.when(jnp.logical_not(second))
        def _():
            if k < 3:
                join_into(self.sent.at[k - 1], mine, other)
            if k == 1:
                line = lax.broadcasted_iota(jnp.int32, before.shape[1:], 0)
                before[0] = jnp.where(line == NS, 1.0, 0.0).astype(jnp.bfloat16)
            elif k == 2:
                before[1] = before[0]
            else:
                result[...] = before[1, :NS]

        if k < 3:
            self.copies[k].start()

    def finish(self):
        for copy in self.copies:
            copy.wait_send()


def scan_scratch(width):
    rows = STATE_ROWS
    dma = pltpu.SemaphoreType.DMA
    narrow = jnp.bfloat16
    return [
        pltpu.VMEM((3, rows, width), narrow),
        pltpu.VMEM((2, rows, width), narrow),
        pltpu.VMEM((2, rows, width), narrow),
        dma((3,)),
        dma((3,)),
    ]


def mixer_forward_kernel(
    info, q, pairs, state_own, out, out_t, lse, kv, state_in, heads, acc, top, total,
    arrived, sent, before, scan_send, scan_recv, send, recv,
):
    others = partners()
    greet([others["far"], others["near"], others["x"]])
    me = lax.axis_index("seq")
    rows = pairs.shape[0]

    def at(r):
        return kv.at[pl.ds(r * rows, rows)]

    scan = StateScan(True, state_own, state_in, arrived, sent, before, scan_send, scan_recv, others)
    kv[:rows] = pairs[...]
    routes = {4: ("far", 0), 2: ("near", 0), 6: ("near", 4)}
    routes.update({r: ("x", r - 1) for r in (1, 3, 5, 7)})
    copies = {
        r: remote(at(src), at(r), send.at[r], recv.at[r], others[name])
        for r, (name, src) in routes.items()
    }
    copies[4].start()
    copies[2].start()
    copies[1].start()
    scan.step(0)
    for i in range(PAIRS):
        heads[2 * i], heads[2 * i + 1] = halves_of(q[:, i * TILE : (i + 1) * TILE])
    acc[...] = jnp.zeros_like(acc)
    total[...] = jnp.zeros_like(total)
    top[...] = jnp.full(top.shape, NEGATIVE_FILL, jnp.float32)

    def attend(r):
        block = bit_apart(r)

        @pl.when(block <= me)
        def _():
            place = pl.ds(pl.multiple_of(r * rows, rows), rows)
            keys = kv[place, :TILE]
            values_t = kv[place, TILE:].astype(jnp.float32).T.astype(jnp.bfloat16)
            attend_block(info, block, keys, values_t, heads, acc, top, total)

    attend(0)
    scan.step(1)
    copies[4].wait_recv()
    copies[6].start()
    copies[5].start()
    attend(4)
    copies[2].wait_recv()
    copies[3].start()
    copies[6].wait_recv()
    copies[7].start()
    scan.step(2)

    def several(first, gap, count):
        def body(j, carry):
            attend(first + j * gap)
            return carry

        lax.fori_loop(0, count, body, 0)

    several(2, 4, 2)
    for r in (1, 3, 5, 7):
        copies[r].wait_recv()
    several(1, 2, 4)
    lse[...] = top[...] + jnp.log(total[...])
    attend_write(acc, total, out, out_t)
    scan.step(3)
    scan.finish()
    for copy in copies.values():
        copy.wait_send()


def mixer_forward(info, q, pairs, state_own):
    rows = q.shape[0]
    f32 = jnp.float32
    dma = pltpu.SemaphoreType.DMA
    width = state_own.shape[1]
    outs = (
        shape_of(q.shape, jnp.bfloat16),
        shape_of(q.shape[::-1], f32),
        shape_of((QUERY_HEADS, rows), f32),
        shape_of((8 * rows, pairs.shape[1]), jnp.bfloat16),
        shape_of((NS, width), jnp.bfloat16),
    )
    return comm_call(
        mixer_forward_kernel,
        outs,
        [INTO_VMEM] * 5,
        (info, q, pairs, state_own),
        [pl.BlockSpec(memory_space=pltpu.SMEM)] + [INTO_VMEM] * 3,
        [
            pltpu.VMEM((QUERY_HEADS, rows, TILE), jnp.bfloat16),
            pltpu.VMEM((QUERY_HEADS, HEAD_SIZE, rows), f32),
            pltpu.VMEM((QUERY_HEADS, rows), f32),
            pltpu.VMEM((QUERY_HEADS, rows), f32),
            *scan_scratch(width),
            dma((8,)),
            dma((8,)),
        ],
        1,
        100_000_000,
    )


def mixer_backward_kernel(swaps, info, q, kv, grad, out_t, lse, pull, *refs):
    give, refs = refs[:swaps], refs[swaps:]
    dq, d_own, d_state, refs = refs[0], refs[1], refs[2], refs[3:]
    take, refs = refs[:swaps], refs[swaps:]
    (
        heads, grads, delta, acc, dkv, from_x, from_far, from_near,
        arrived, sent, before, scan_send, scan_recv, send, recv, swap_send, swap_recv,
    ) = refs
    others = partners()
    greet([others["far"], others["near"], others["x"], others["core"]])
    me = lax.axis_index("seq")
    rows = q.shape[0]
    scan = StateScan(False, pull, d_state, arrived, sent, before, scan_send, scan_recv, others)
    scan.step(0)
    swapped = [
        remote(give[k], take[k], swap_send.at[k], swap_recv.at[k], others["core"])
        for k in range(swaps)
    ]
    for copy in swapped:
        copy.start()
    attend_back_start(q, grad, out_t, heads, grads, delta, acc)

    def block_back(r):
        block = bit_apart(r)
        place = pl.ds(pl.multiple_of(r * rows, rows), rows)

        @pl.when(block <= me)
        def _():
            attend_back_block(
                info, block, kv[place, :TILE], kv[place, TILE:], lse, dkv.at[r], heads, grads,
                delta, acc,
            )

        @pl.when(block > me)
        def _():
            dkv[r] = jnp.zeros(dkv.shape[1:], dkv.dtype)

    def several(first, gap, count):
        def body(j, carry):
            block_back(first + j * gap)
            return carry

        lax.fori_loop(0, count, body, 0)

    several(1, 2, 4)
    over_x = [
        remote(dkv.at[2 * k + 1], from_x.at[k], send.at[k], recv.at[k], others["x"])
        for k in range(4)
    ]
    for copy in over_x:
        copy.start()
    scan.step(1)
    several(4, 2, 2)

    def add(target, source):
        target[...] = (target[...].astype(jnp.float32) + source[...].astype(jnp.float32)).astype(
            jnp.bfloat16
        )

    over_far = [
        remote(dkv.at[4 + 2 * k], from_far.at[k], send.at[4 + k], recv.at[4 + k], others["far"])
        for k in range(2)
    ]
    for k in range(2):
        over_x[2 + k].wait_recv()
        add(dkv.at[4 + 2 * k], from_x.at[2 + k])
        over_far[k].start()
    scan.step(2)
    several(0, 2, 2)
    for k in range(2):
        over_x[k].wait_recv()
        add(dkv.at[2 * k], from_x.at[k])
    over_far[1].wait_recv()
    add(dkv.at[2], from_far.at[1])
    over_near = remote(dkv.at[2], from_near, send.at[6], recv.at[6], others["near"])
    over_near.start()
    over_far[0].wait_recv()
    attend_back_write(acc, dq)
    scan.step(3)
    over_near.wait_recv()
    d_own[...] = (
        dkv[0].astype(jnp.float32)
        + from_far[0].astype(jnp.float32)
        + from_near[...].astype(jnp.float32)
    )
    scan.finish()
    for copy in over_x + over_far + [over_near]:
        copy.wait_send()
    for copy in swapped:
        copy.wait()


def mixer_backward(info, q, kv, grad, out_t, lse, pull, give):
    rows = q.shape[0]
    f32 = jnp.float32
    dma = pltpu.SemaphoreType.DMA
    width = pull.shape[1]
    pair = kv.shape[1]
    swaps = len(give)
    narrow = jnp.bfloat16
    outs = [
        shape_of(q.shape, f32),
        shape_of((rows, pair), f32),
        shape_of((NS, width), narrow),
    ] + [shape_of(a.shape, a.dtype) for a in give]
    result = comm_call(
        lambda *refs: mixer_backward_kernel(swaps, *refs),
        outs,
        [INTO_VMEM] * 3 + [ANY] * swaps,
        (info, q, kv, grad, out_t, lse, pull, *give),
        [pl.BlockSpec(memory_space=pltpu.SMEM)] + [INTO_VMEM] * 6 + [ANY] * swaps,
        [
            pltpu.VMEM((QUERY_HEADS, rows, TILE), narrow),
            pltpu.VMEM((QUERY_HEADS, rows, TILE), narrow),
            pltpu.VMEM((QUERY_HEADS, rows), f32),
            pltpu.VMEM((QUERY_HEADS, HEAD_SIZE, rows), f32),
            pltpu.VMEM((8, rows, pair), narrow),
            pltpu.VMEM((4, rows, pair), narrow),
            pltpu.VMEM((2, rows, pair), narrow),
            pltpu.VMEM((rows, pair), narrow),
            *scan_scratch(width),
            dma((7,)),
            dma((7,)),
            dma((swaps,)),
            dma((swaps,)),
        ],
        2,
        100_000_000,
    )
    return result[0], result[1], result[2], result[3:]


def core_swap_kernel(count, *refs):
    give, take = refs[:count], refs[count : 2 * count]
    send, recv = refs[2 * count :]
    other = partners()["core"]
    greet([other])
    copies = [remote(give[k], take[k], send.at[k], recv.at[k], other) for k in range(count)]
    for copy in copies:
        copy.start()
    for copy in copies:
        copy.wait()


def core_swap(give):
    count = len(give)
    dma = pltpu.SemaphoreType.DMA
    return comm_call(
        lambda *refs: core_swap_kernel(count, *refs),
        [shape_of(a.shape, a.dtype) for a in give],
        [ANY] * count,
        give,
        [ANY] * count,
        [dma((count,)), dma((count,))],
        3,
        2 * sum(a.size for a in give),
    )


def weight_scatter_kernel(count, pairs, *refs):
    ins, small, refs = refs[:count], refs[count], refs[count + 1 :]
    outs, small_out, refs = refs[:count], refs[count], refs[count + 1 :]
    arrived, kept, refs = refs[: 4 * count], refs[4 * count : 7 * count], refs[7 * count :]
    small_in, small_mid, send, recv, small_send, small_recv = refs
    others = partners()
    greet(list(others.values()))
    size = ins[0].shape[0]
    routes = (("y", "x", "near", "far"), ("x", "y", "near", "far"))

    def pieces(side, stage):
        rows = size >> stage
        half = rows // 2
        if side == 1 and stage == 0:
            quarter = rows // 4
            return [(quarter, quarter), (3 * quarter, quarter)], [(0, quarter), (2 * quarter, quarter)]
        return [(half, half)], [(0, half)]

    started = {}

    def begin(n, side, stage):
        p, column, width = pairs[n][side]
        cols = pl.ds(column, width)
        source = ins[p] if stage == 0 else kept[3 * p + stage - 1]
        target = arrived[4 * p + stage]
        copies, row = [], 0
        for k, (first, rows) in enumerate(pieces(side, stage)[0]):
            copy = remote(
                source.at[pl.ds(first, rows), cols],
                target.at[pl.ds(row, rows), cols],
                send.at[2 * n + side, stage, k],
                recv.at[2 * n + side, stage, k],
                others[routes[side][stage]],
            )
            copy.start()
            copies.append(copy)
            row += rows
        started[n, side, stage] = copies

    def take(n, side, stage):
        p, column, width = pairs[n][side]
        cols = slice(column, column + width)
        source = ins[p] if stage == 0 else kept[3 * p + stage - 1]
        target = outs[p] if stage == 3 else kept[3 * p + stage]
        got = arrived[4 * p + stage]
        row = 0
        for k, (first, rows) in enumerate(pieces(side, stage)[1]):
            started[n, side, stage][k].wait_recv()

            def add(i, carry):
                at = pl.multiple_of(i * 32, 32)
                here = pl.ds(first + at, 32)
                there = pl.ds(row + at, 32)
                total = source[here, cols].astype(jnp.float32) + got[there, cols].astype(
                    jnp.float32
                )
                target[there, cols] = total.astype(target.dtype)
                return carry

            lax.fori_loop(0, rows // 32, add, 0)
            row += rows

    names = ("core", "y", "x", "near", "far")
    small_copies = []
    for wave in range(max(len(pairs) + 5, 6)):
        if wave <= 5:
            if wave > 0:
                small_copies[wave - 1].wait_recv()
                was = small if wave == 1 else small_mid.at[wave - 2]
                now = small_out if wave == 5 else small_mid.at[wave - 1]
                now[...] = was[...] + small_in[wave - 1]
            if wave < 5:
                source = small if wave == 0 else small_mid.at[wave - 1]
                copy = remote(
                    source,
                    small_in.at[wave],
                    small_send.at[wave],
                    small_recv.at[wave],
                    others[names[wave]],
                )
                copy.start()
                small_copies.append(copy)
        for n in range(len(pairs)):
            stage = wave - n
            if stage < 0 or stage > 4:
                continue
            for side in range(2):
                if stage > 0:
                    take(n, side, stage - 1)
                if stage < 4:
                    begin(n, side, stage)
    for copies in list(started.values()) + [small_copies]:
        for copy in copies:
            copy.wait_send()


def weight_scatter(parts, small):
    count = len(parts)
    size = parts[0].shape[0]
    f32, narrow = jnp.float32, jnp.bfloat16
    dma = pltpu.SemaphoreType.DMA
    pairs = column_chunks([p.shape[1] for p in parts])
    outs = [shape_of((size // 16, p.shape[1]), f32) for p in parts]
    outs.append(shape_of(small.shape, f32))
    scratch = []
    for p in parts:
        scratch += [pltpu.VMEM((size >> (s + 1), p.shape[1]), narrow) for s in range(4)]
    for p in parts:
        scratch += [pltpu.VMEM((size >> (s + 1), p.shape[1]), narrow) for s in range(3)]
    scratch += [
        pltpu.VMEM((5, *small.shape), f32),
        pltpu.VMEM((4, *small.shape), f32),
        dma((2 * len(pairs), 4, 2)),
        dma((2 * len(pairs), 4, 2)),
        dma((5,)),
        dma((5,)),
    ]
    result = comm_call(
        lambda *refs: weight_scatter_kernel(count, pairs, *refs),
        outs,
        [INTO_VMEM] * (count + 1),
        (*parts, small),
        [INTO_VMEM] * (count + 1),
        scratch,
        4,
        8 * sum(p.size for p in parts),
        limit=60,
    )
    return result[:count], result[count]


def pair_heads(value, back=False):
    rows = value.shape[0]
    group = QUERY_HEADS // KEY_VALUE_HEADS
    width = QUERY_HEADS * HEAD_SIZE
    shape = (group, KEY_VALUE_HEADS) if back else (KEY_VALUE_HEADS, group)
    moved = value[:, :width].reshape(rows, *shape, HEAD_SIZE).transpose(0, 2, 1, 3)
    return jnp.concatenate([moved.reshape(rows, width), value[:, width:]], axis=1)


def on_device(
    layer_input,
    seq_lengths,
    w_attn,
    w_ssm_in,
    w_dt,
    w_out,
    w_gate_up,
    w_down,
    norm_gain,
    mlp_gain,
    ssm_gain,
    conv_w,
    conv_b,
    a_log,
    dt_bias,
    d_skip,
    out_grad,
):
    token_rows = layer_input.shape[1]
    query_width = QUERY_HEADS * HEAD_SIZE
    key_value_width = KEY_VALUE_HEADS * HEAD_SIZE
    attn_width = query_width + 2 * key_value_width
    ssm_width = MH * MP
    xbc_width = ssm_width + 2 * NS
    width = layer_input.shape[2]
    fast = is_fast(width)
    seq_lens = seq_lengths[0]
    first_pos = lax.axis_index("seq") * token_rows
    positions = first_pos + jnp.arange(token_rows, dtype=jnp.int32)
    segment, device_places = segments(seq_lens, positions)
    ends = jnp.cumsum(seq_lens)
    info = jnp.stack([first_pos, ends[0], ends[1], ends[2]]).astype(jnp.int32)
    half = HEAD_SIZE // 2
    freqs = ROPE_BASE ** (-jnp.arange(half, dtype=jnp.float32) / half)
    angles = device_places.astype(jnp.float32)[:, None] * jnp.tile(freqs, TILE // half)[None, :]
    cosine, sine = jnp.cos(angles), jnp.sin(angles)
    order = own_order(width, fast)
    wide_order = order.astype(jnp.float32)

    def to_own(value):
        if not fast:
            return value
        return jnp.dot(value, order, preferred_element_type=jnp.float32).astype(value.dtype)

    def to_plain(value):
        if not fast:
            return value
        return jnp.einsum("tc,dc->td", value, order, preferred_element_type=jnp.float32)

    def to_plain_wide(value):
        if not fast:
            return value
        return jnp.einsum("tc,dc->td", value, wide_order, precision=HIGHEST)

    def gain_own(value):
        if not fast:
            return value
        return jnp.dot(value, wide_order, precision=HIGHEST)

    gains = gain_own(jnp.stack([norm_gain, mlp_gain]))
    norm_gain, mlp_gain = gains[0], gains[1]
    x_rows = to_own(layer_input[0]).astype(jnp.float32)
    grad_rows = to_own(out_grad[0])
    head_params = jnp.pad(
        jnp.stack([dt_bias, jnp.exp(a_log), d_skip]), ((0, 5), (0, TILE - MH))
    )
    step_pad = jnp.pad(w_dt, ((0, 0), (0, TILE - MH)))
    out_shard = pair_heads(w_out.T)
    down_shard = w_down.T
    shards = (
        jnp.concatenate([w_ssm_in[:, ssm_width:], step_pad], axis=1),
        jnp.concatenate([pair_heads(w_attn), w_ssm_in[:, :ssm_width]], axis=1),
        out_shard[:, : w_out.shape[0] // 2],
        out_shard[:, w_out.shape[0] // 2 :],
        w_gate_up[:, :FF],
        w_gate_up[:, FF:],
        down_shard[:, : FF // 2],
        down_shard[:, FF // 2 :],
    )
    if fast:
        full = weight_gather(shards)
    else:
        full = [lax.all_gather(p, ("seq", "batch"), axis=0, tiled=True) for p in shards]
    full_conv, full_mix, out_a, out_b, full_gate, full_up, down_a, down_b = full
    scale_one = rms_scale(x_rows)
    normed = (x_rows * scale_one * norm_gain).astype(jnp.bfloat16)
    conv_proj = jnp.dot(normed, full_conv, preferred_element_type=jnp.float32)
    mix_proj = jnp.dot(normed, full_mix, preferred_element_type=jnp.float32)
    queries, own_pairs = big_call(
        rope_kernel,
        (
            shape_of((token_rows, query_width), jnp.bfloat16),
            shape_of((token_rows, 2 * key_value_width), jnp.bfloat16),
        ),
        mix_proj[:, :attn_width],
        cosine,
        sine,
    )
    gate_z = mix_proj[:, attn_width:]
    raw_xbc = conv_proj[:, :xbc_width]
    step_proj = conv_proj[:, xbc_width:]
    rim_rows = shifted(raw_xbc[token_rows - (CONV - 1) :], "seq", 1)
    extended = jnp.concatenate([rim_rows, raw_xbc], axis=0)
    ext_pos = first_pos - (CONV - 1) + jnp.arange(token_rows + CONV - 1, dtype=jnp.int32)
    ext_segment = segments(seq_lens, ext_pos)[0]

    def conv_local(ext_rows, conv_weight, conv_bias):
        return conv_mix(ext_rows, ext_segment, conv_weight, conv_bias)

    conv_out, conv_pullback = jax.vjp(conv_local, extended, conv_w, conv_b)
    conv_narrow = conv_out.astype(jnp.bfloat16)
    inputs_x, inputs_bc = conv_narrow[:, :ssm_width], conv_narrow[:, ssm_width:]
    ssm_local, state_own, steps_dt, running_decay = ssm_forward(
        info, inputs_x, inputs_bc, step_proj, head_params
    )
    if fast:
        attended, attended_t, log_total, all_pairs, state_in = mixer_forward(
            info, queries, own_pairs, state_own
        )
    else:
        all_pairs = lax.all_gather(own_pairs, "seq", axis=0, tiled=True)
        state_in = scan_states(state_own, True)
        attended, attended_t, log_total = attn_forward(info, queries, all_pairs)
    ssm_flat, ssm_normed, scale_gated = ssm_finish(
        info, ssm_local, inputs_bc, running_decay, state_in, gate_z, ssm_gain[None]
    )
    joined = jnp.concatenate([attended, ssm_normed], axis=1)
    half_in = joined.shape[1] // 2

    def narrow_out(left, parts):
        cut = left.shape[1] // 2
        return jnp.einsum(
            "tc,dc->td", left[:, :cut], parts[0], preferred_element_type=jnp.float32
        ) + jnp.einsum("tc,dc->td", left[:, cut:], parts[1], preferred_element_type=jnp.float32)

    middle = x_rows + narrow_out(joined, (out_a, out_b))
    scale_two = rms_scale(middle)
    normed_two = (middle * scale_two * mlp_gain).astype(jnp.bfloat16)
    gate_part = jnp.dot(normed_two, full_gate, preferred_element_type=jnp.float32)
    up_part = jnp.dot(normed_two, full_up, preferred_element_type=jnp.float32)
    hidden = (jax.nn.silu(gate_part) * up_part).astype(jnp.bfloat16)
    layer_out = middle + narrow_out(hidden, (down_a, down_b))
    d_hidden = jnp.concatenate(
        [
            jnp.dot(grad_rows, down_a, preferred_element_type=jnp.float32),
            jnp.dot(grad_rows, down_b, preferred_element_type=jnp.float32),
        ],
        axis=1,
    )
    sig_gate = jax.nn.sigmoid(gate_part)
    d_gate = (d_hidden * up_part * (sig_gate * (1.0 + gate_part * (1.0 - sig_gate)))).astype(
        jnp.bfloat16
    )
    d_up = (d_hidden * gate_part * sig_gate).astype(jnp.bfloat16)
    d_normed_two = narrow_out(jnp.concatenate([d_gate, d_up], axis=1), (full_gate, full_up))
    d_middle_norm, g_mlp_gain = norm_back(middle, scale_two, mlp_gain, d_normed_two)
    d_middle = grad_rows.astype(jnp.float32) + d_middle_norm
    d_mixer = d_middle.astype(jnp.bfloat16)
    d_joined = jnp.concatenate(
        [
            jnp.dot(d_mixer, out_a, preferred_element_type=jnp.float32),
            jnp.dot(d_mixer, out_b, preferred_element_type=jnp.float32),
        ],
        axis=1,
    )
    attended_gradient = d_joined[:, :query_width].astype(jnp.bfloat16)
    d_ssm_out, d_gate_z, pull, g_ssm_gain = gate_back(
        info,
        d_joined[:, query_width:],
        ssm_flat,
        gate_z,
        scale_gated,
        ssm_gain[None],
        running_decay,
        inputs_bc,
    )
    pull = jnp.concatenate([pull, state_own[NS:]], axis=0)
    lefts = [normed, normed_two, d_mixer, grad_rows]
    rights = [hidden, joined, d_gate, d_up]
    if fast:
        cut = width // 2
        d_queries, own_d_pairs, d_state, theirs = mixer_backward(
            info,
            queries,
            all_pairs,
            attended_gradient,
            attended_t,
            log_total,
            pull,
            [a[:, cut:] for a in lefts] + rights,
        )
        lefts = [jnp.concatenate([a[:, :cut], b], axis=0) for a, b in zip(lefts, theirs)]
        rights = [jnp.concatenate([a, b], axis=0) for a, b in zip(rights, theirs[4:])]
    else:
        d_state = scan_states(pull, False)
        d_queries, d_pairs = attn_backward(
            info, queries, all_pairs, attended_gradient, attended_t, log_total
        )
        own_d_pairs = lax.psum_scatter(
            d_pairs.astype(jnp.float32), "seq", scatter_dimension=0, tiled=True
        )
    dx_part, d_bc_part, d_cum_part, d_dt_part, g_skip_rows = ssm_back(
        info, inputs_x, inputs_bc, steps_dt, running_decay, d_ssm_out, head_params
    )
    g_inputs_x, g_inputs_bc, d_step_pad, head_sums = state_back(
        info,
        inputs_x,
        inputs_bc,
        steps_dt,
        running_decay,
        d_ssm_out,
        head_params,
        step_proj,
        state_in,
        d_state,
        dx_part,
        d_bc_part,
        d_cum_part,
        d_dt_part,
    )
    g_a_log, g_dt_bias, g_d_skip = head_sums[0, :MH], head_sums[1, :MH], g_skip_rows[0, :MH]
    d_conv_out = jnp.concatenate([g_inputs_x, g_inputs_bc], axis=1)
    g_extended, g_conv_w, g_conv_b = conv_pullback(d_conv_out)
    back_rim = shifted(g_extended[: CONV - 1], "seq", -1)
    d_raw = g_extended[CONV - 1 :] + jnp.concatenate(
        [jnp.zeros((token_rows - (CONV - 1), xbc_width), jnp.float32), back_rim], axis=0
    )
    d_conv_proj = jnp.concatenate([d_raw.astype(jnp.bfloat16), d_step_pad], axis=1)
    (d_attn_proj,) = big_call(
        rope_back_kernel,
        (shape_of((token_rows, attn_width), jnp.bfloat16),),
        d_queries,
        own_d_pairs,
        cosine,
        sine,
    )
    d_mix_proj = jnp.concatenate([d_attn_proj, d_gate_z], axis=1)
    d_normed = jnp.einsum(
        "tc,dc->td", d_conv_proj, full_conv, preferred_element_type=jnp.float32
    ) + jnp.einsum("tc,dc->td", d_mix_proj, full_mix, preferred_element_type=jnp.float32)
    d_input_norm, g_norm_gain = norm_back(x_rows, scale_one, norm_gain, d_normed)
    input_grad = d_middle + d_input_norm
    last = [d_conv_proj, d_mix_proj]
    if fast:
        last = [jnp.concatenate([a, b], axis=0) for a, b in zip(last, core_swap(last))]

    def partial(left, right):
        grad = jnp.einsum("td,tc->dc", left, right, preferred_element_type=jnp.float32)
        return grad.astype(jnp.bfloat16) if fast else grad

    all_normed, all_normed_two, all_d_mixer, all_grad = lefts
    all_hidden, all_joined, all_d_gate, all_d_up = rights
    half_ff = FF // 2
    partials = [
        partial(all_grad, all_hidden[:, :half_ff]),
        partial(all_grad, all_hidden[:, half_ff:]),
        partial(all_normed_two, all_d_gate),
        partial(all_normed_two, all_d_up),
        partial(all_d_mixer, all_joined[:, :half_in]),
        partial(all_d_mixer, all_joined[:, half_in:]),
        partial(all_normed, last[0]),
        partial(all_normed, last[1]),
    ]
    gain_grads = to_plain_wide(jnp.stack([g_norm_gain, g_mlp_gain]))
    small = (
        gain_grads[0],
        gain_grads[1],
        g_ssm_gain[0],
        g_conv_w,
        g_conv_b,
        g_a_log,
        g_dt_bias,
        g_d_skip,
    )
    if fast:
        sums, small_total = weight_scatter(partials, pack_small(small))
    else:
        axes = ("seq", "batch")
        sums = [lax.psum_scatter(g, axes, scatter_dimension=0, tiled=True) for g in partials]
        small_total = lax.psum(pack_small(small), axes)
    small_sums = unpack_small(small_total, small)
    g_conv_in, g_mix_in = sums[6], sums[7]
    grad_attn = pair_heads(g_mix_in[:, :attn_width], True)
    grad_ssm_in = jnp.concatenate([g_mix_in[:, attn_width:], g_conv_in[:, :xbc_width]], axis=1)
    grad_dt = g_conv_in[:, xbc_width : xbc_width + MH]
    grad_out = pair_heads(jnp.concatenate(sums[4:6], axis=1), True).T
    grad_gate_up = jnp.concatenate(sums[2:4], axis=1)
    grad_down = jnp.concatenate(sums[:2], axis=1).T
    return (
        to_plain(layer_out.astype(jnp.bfloat16)).astype(jnp.bfloat16)[None],
        to_plain_wide(input_grad)[None],
        grad_attn,
        grad_ssm_in,
        grad_dt,
        grad_out,
        grad_gate_up,
        grad_down,
        *small_sums,
    )


def solution(mesh):
    return jax.shard_map(
        on_device,
        mesh=mesh,
        in_specs=(
            P("batch", "seq", None),
            P("batch", None),
            P(("seq", "batch"), None),
            P(("seq", "batch"), None),
            P(("seq", "batch"), None),
            P(None, ("seq", "batch")),
            P(("seq", "batch"), None),
            P(None, ("seq", "batch")),
            P(),
            P(),
            P(),
            P(),
            P(),
            P(),
            P(),
            P(),
            P("batch", "seq", None),
        ),
        out_specs=(
            P("batch", "seq", None),
            P("batch", "seq", None),
            P(("seq", "batch"), None),
            P(("seq", "batch"), None),
            P(("seq", "batch"), None),
            P(None, ("seq", "batch")),
            P(("seq", "batch"), None),
            P(None, ("seq", "batch")),
            P(),
            P(),
            P(),
            P(),
            P(),
            P(),
            P(),
            P(),
        ),
        check_vma=False,
    )
```

```python
import jax
import jax.numpy as jnp
from jax import lax
from jax.experimental import pallas as pl
from jax.experimental.pallas import tpu as pltpu
from jax.sharding import PartitionSpec as P

QUERY_HEADS = 8
KEY_VALUE_HEADS = 2
HEAD_SIZE = 64
MH = 24
MP = 64
NS = 128
FF = 2048
CONV = 4
SPAN = 128


HIGHEST = lax.Precision.HIGHEST
NEGATIVE_FILL = -1e30
ROPE_BASE = 10000.0
NORM_EPS = 1e-06


def shifted(block, axis, distance):
    devices = range(lax.axis_size(axis))
    route = [(i - distance, i) for i in devices if i - distance in devices]
    return lax.ppermute(block, axis, route)


def is_fast(width):
    return lax.axis_size("seq") == 8 and lax.axis_size("batch") == 4 and width % (32 * 32) == 0


def pack_small(arrays):
    flat = jnp.concatenate([a.reshape(-1) for a in arrays])
    return jnp.pad(flat, (0, -flat.shape[0] % 1024)).reshape(-1, 128)


def unpack_small(flat, arrays):
    flat = flat.reshape(-1)
    out, start = [], 0
    for a in arrays:
        out.append(flat[start : start + a.size].reshape(a.shape))
        start += a.size
    return out


def rms_scale(value_rows):
    return lax.rsqrt(jnp.mean(value_rows * value_rows, axis=-1, keepdims=True) + NORM_EPS)


def norm_back(value_rows, scales, gains, grads):
    gain_grad = jnp.sum(grads * value_rows * scales, axis=0)
    inner = grads * gains
    coeff = jnp.mean(inner * value_rows, axis=-1, keepdims=True)
    return (scales * (inner - value_rows * scales * scales * coeff), gain_grad)


def segments(lengths, positions):
    ends = jnp.cumsum(lengths)
    passed = ends[None, :] <= positions[:, None]
    segment = jnp.sum(passed.astype(jnp.int32), axis=1)
    device_places = positions - jnp.sum(jnp.where(passed, lengths[None, :], 0), axis=1)
    return (segment, device_places)


def conv_mix(extended, ext_segment, conv_weight, conv_bias):
    row_count = extended.shape[0] - (CONV - 1)
    summed = conv_bias[None, :]
    for lagged in range(CONV):
        same_seq = (ext_segment[lagged : lagged + row_count] == ext_segment[CONV - 1 :]).astype(
            extended.dtype
        )
        summed = (
            summed
            + conv_weight[lagged][None, :]
            * extended[lagged : lagged + row_count]
            * same_seq[:, None]
        )
    return jax.nn.silu(summed)


TILE = 128
PAIRS = QUERY_HEADS // 2
CHUNK = 256


def dot(left, right):
    return jnp.dot(left, right, preferred_element_type=jnp.float32)


def dot_nt(left, right):
    return lax.dot_general(
        left, right, (((1,), (1,)), ((), ())), preferred_element_type=jnp.float32
    )


def dot_tn(left, right):
    return lax.dot_general(
        left, right, (((0,), (0,)), ((), ())), preferred_element_type=jnp.float32
    )


def exact(left, right):
    return jnp.dot(left, right, precision=HIGHEST, preferred_element_type=jnp.float32)


def two_part(left, right):
    high = left.astype(jnp.bfloat16)
    low = (left - high.astype(jnp.float32)).astype(jnp.bfloat16)
    return dot(high, right) + dot(low, right)


def seg_start(where_at, info):
    start = jnp.zeros_like(where_at)
    for k in range(1, 4):
        start = jnp.where(where_at >= info[k], jnp.maximum(start, info[k]), start)
    return start


def big_call(kernel, outs, *args, scratch=(), flops=0, smem=0, limit=48):
    specs = [pl.BlockSpec(memory_space=pltpu.SMEM)] * smem
    specs += [pl.BlockSpec(memory_space=pltpu.VMEM)] * (len(args) - smem)
    moved = sum(a.size * a.dtype.itemsize for a in args)
    moved += sum(o.size * o.dtype.itemsize for o in outs)
    return pl.pallas_call(
        kernel,
        out_shape=list(outs),
        in_specs=specs,
        out_specs=[pl.BlockSpec(memory_space=pltpu.VMEM)] * len(outs),
        scratch_shapes=list(scratch),
        cost_estimate=pl.CostEstimate(flops=flops, bytes_accessed=moved, transcendentals=0),
        compiler_params=pltpu.CompilerParams(vmem_limit_bytes=limit * 1024 * 1024),
    )(*args)


def shape_of(shape, dtype):
    return jax.ShapeDtypeStruct(shape, dtype)


def turn(value, cosine, sine):
    lane = lax.broadcasted_iota(jnp.int32, value.shape, 1) % HEAD_SIZE
    mixed = jnp.where(
        lane < HEAD_SIZE // 2,
        -pltpu.roll(value, TILE - HEAD_SIZE // 2, 1),
        pltpu.roll(value, HEAD_SIZE // 2, 1),
    )
    return value * cosine + mixed * sine


def rope_kernel(proj, cosine, sine, q_out, kv_out):
    cos, sin = cosine[...], sine[...]
    for i in range(PAIRS):
        cols = pl.ds(i * TILE, TILE)
        turned = turn(proj[:, cols], cos, sin).astype(jnp.bfloat16)
        q_out[:, cols] = (turned.astype(jnp.float32) * HEAD_SIZE**-0.5).astype(jnp.bfloat16)
    base = PAIRS * TILE
    kv_out[:, :TILE] = turn(proj[:, base : base + TILE], cos, sin).astype(jnp.bfloat16)
    kv_out[:, TILE:] = proj[:, base + TILE : base + 2 * TILE].astype(jnp.bfloat16)


def halves_of(value):
    lane = lax.broadcasted_iota(jnp.int32, value.shape, 1)
    wide = value.astype(jnp.float32)
    first = jnp.where(lane < HEAD_SIZE, wide, 0.0).astype(value.dtype)
    return first, jnp.where(lane < HEAD_SIZE, 0.0, wide).astype(value.dtype)


def block_range(info):
    first = info[0]
    low = seg_start(first, info) // CHUNK
    return low, first // CHUNK - low + 1


def attn_mask(info, block):
    rows = lax.broadcasted_iota(jnp.int32, (CHUNK, CHUNK), 0) + block * CHUNK
    at = lax.broadcasted_iota(jnp.int32, (1, CHUNK), 1) + info[0]
    return (rows <= at) & (rows >= seg_start(at, info))


def attend_start(q, heads, acc, top, total):
    for i in range(PAIRS):
        heads[2 * i], heads[2 * i + 1] = halves_of(q[:, i * TILE : (i + 1) * TILE])
    acc[...] = jnp.zeros_like(acc)
    total[...] = jnp.zeros_like(total)
    top[...] = jnp.full(top.shape, NEGATIVE_FILL, jnp.float32)


def attend_block(info, block, keys, values_t, heads, acc, top, total):
    allowed = attn_mask(info, block)
    for h in range(QUERY_HEADS):
        scores = jnp.where(allowed, dot_nt(keys, heads[h]), NEGATIVE_FILL)
        old = top[h : h + 1]
        new = jnp.maximum(old, jnp.max(scores, axis=0, keepdims=True))
        probs = jnp.where(allowed, jnp.exp(scores - new), 0.0)
        shrink = jnp.exp(old - new)
        top[h : h + 1] = new
        total[h : h + 1] = total[h : h + 1] * shrink + jnp.sum(probs, axis=0, keepdims=True)
        side = (h % 2) * HEAD_SIZE
        acc[h] = acc[h] * shrink + dot(
            values_t[side : side + HEAD_SIZE], probs.astype(jnp.bfloat16)
        )


def attend_write(acc, total, out, out_t):
    for i in range(PAIRS):
        pair = jnp.concatenate(
            [acc[2 * i] / total[2 * i : 2 * i + 1], acc[2 * i + 1] / total[2 * i + 1 : 2 * i + 2]],
            axis=0,
        )
        out_t[i * TILE : (i + 1) * TILE] = pair
        out[:, i * TILE : (i + 1) * TILE] = pair.T.astype(jnp.bfloat16)


def attn_forward_kernel(info, q, kv, out, out_t, lse, heads, acc, top, total):
    attend_start(q, heads, acc, top, total)
    low, count = block_range(info)

    def step(j, carry):
        block = low + j
        place = pl.ds(pl.multiple_of(block * CHUNK, CHUNK), CHUNK)
        keys = kv[place, :TILE]
        values_t = kv[place, TILE:].astype(jnp.float32).T.astype(jnp.bfloat16)
        attend_block(info, block, keys, values_t, heads, acc, top, total)
        return carry

    lax.fori_loop(0, count, step, 0)
    lse[...] = top[...] + jnp.log(total[...])
    attend_write(acc, total, out, out_t)


def attn_forward(info, q, kv):
    rows = q.shape[0]
    f32 = jnp.float32
    return big_call(
        attn_forward_kernel,
        (
            shape_of(q.shape, jnp.bfloat16),
            shape_of(q.shape[::-1], f32),
            shape_of((QUERY_HEADS, rows), f32),
        ),
        info,
        q,
        kv,
        smem=1,
        scratch=(
            pltpu.VMEM((QUERY_HEADS, rows, TILE), jnp.bfloat16),
            pltpu.VMEM((QUERY_HEADS, HEAD_SIZE, rows), f32),
            pltpu.VMEM((QUERY_HEADS, rows), f32),
            pltpu.VMEM((QUERY_HEADS, rows), f32),
        ),
        flops=4 * rows * kv.shape[0] * q.shape[1],
    )


def attend_back_start(q, grad, out_t, heads, grads, delta, acc):
    for i in range(PAIRS):
        cols = slice(i * TILE, (i + 1) * TILE)
        heads[2 * i], heads[2 * i + 1] = halves_of(q[:, cols])
        grads[2 * i], grads[2 * i + 1] = halves_of(grad[:, cols])
        both = grad[:, cols].astype(jnp.float32).T * out_t[cols]
        delta[2 * i : 2 * i + 1] = jnp.sum(both[:HEAD_SIZE], axis=0, keepdims=True)
        delta[2 * i + 1 : 2 * i + 2] = jnp.sum(both[HEAD_SIZE:], axis=0, keepdims=True)
    acc[...] = jnp.zeros_like(acc)


def attend_back_block(info, block, keys, values, lse, target, heads, grads, delta, acc):
    keys_t = keys.astype(jnp.float32).T.astype(jnp.bfloat16)
    allowed = attn_mask(info, block)
    d_keys = jnp.zeros((CHUNK, TILE), jnp.float32)
    d_values = jnp.zeros((CHUNK, TILE), jnp.float32)
    for h in range(QUERY_HEADS):
        scores = dot_nt(keys, heads[h])
        probs = jnp.where(allowed, jnp.exp(scores - lse[h : h + 1]), 0.0)
        d_probs = dot_nt(values, grads[h])
        d_scores = (probs * (d_probs - delta[h : h + 1])).astype(jnp.bfloat16)
        d_values = d_values + dot(probs.astype(jnp.bfloat16), grads[h])
        d_keys = d_keys + dot(d_scores, heads[h])
        side = (h % 2) * HEAD_SIZE
        acc[h] = acc[h] + dot(keys_t[side : side + HEAD_SIZE], d_scores)
    target[:, :TILE] = d_keys.astype(jnp.bfloat16)
    target[:, TILE:] = d_values.astype(jnp.bfloat16)


def attend_back_write(acc, dq):
    for i in range(PAIRS):
        pair = jnp.concatenate([acc[2 * i], acc[2 * i + 1]], axis=0)
        dq[:, i * TILE : (i + 1) * TILE] = pair.T * HEAD_SIZE**-0.5


def attn_backward_kernel(info, q, kv, grad, out_t, lse, dq, dkv, heads, grads, delta, acc):
    attend_back_start(q, grad, out_t, heads, grads, delta, acc)
    dkv[...] = jnp.zeros_like(dkv)
    low, count = block_range(info)

    def step(j, carry):
        block = low + j
        place = pl.ds(pl.multiple_of(block * CHUNK, CHUNK), CHUNK)
        attend_back_block(
            info, block, kv[place, :TILE], kv[place, TILE:], lse, dkv.at[place], heads, grads,
            delta, acc,
        )
        return carry

    lax.fori_loop(0, count, step, 0)
    attend_back_write(acc, dq)


def attn_backward(info, q, kv, grad, out_t, lse):
    rows = q.shape[0]
    f32 = jnp.float32
    return big_call(
        attn_backward_kernel,
        (shape_of(q.shape, f32), shape_of(kv.shape, jnp.bfloat16)),
        info,
        q,
        kv,
        grad,
        out_t,
        lse,
        smem=1,
        scratch=(
            pltpu.VMEM((QUERY_HEADS, rows, TILE), jnp.bfloat16),
            pltpu.VMEM((QUERY_HEADS, rows, TILE), jnp.bfloat16),
            pltpu.VMEM((QUERY_HEADS, rows), f32),
            pltpu.VMEM((QUERY_HEADS, HEAD_SIZE, rows), f32),
        ),
        flops=10 * rows * kv.shape[0] * q.shape[1],
    )


def rope_back_kernel(dq, dkv, cosine, sine, out):
    cos, sin = cosine[...], -sine[...]
    for i in range(PAIRS):
        cols = slice(i * TILE, (i + 1) * TILE)
        out[:, cols] = turn(dq[:, cols], cos, sin).astype(jnp.bfloat16)
    base = PAIRS * TILE
    out[:, base : base + TILE] = turn(dkv[:, :TILE], cos, sin).astype(jnp.bfloat16)
    out[:, base + TILE :] = dkv[:, TILE:].astype(jnp.bfloat16)


STATE_ROWS = NS + 16


def lane_pick(value, first):
    rows = value.shape[0]
    lane = lax.broadcasted_iota(jnp.int32, (rows, TILE), 1)
    return jnp.where(lane < MP, value[:, first : first + 1], value[:, first + 1 : first + 2])


def spread_heads(width):
    head = lax.broadcasted_iota(jnp.int32, (TILE, width), 0)
    col = lax.broadcasted_iota(jnp.int32, (TILE, width), 1)
    return jnp.where(head == col // MP, 1.0, 0.0).astype(jnp.bfloat16)


def gather_heads(width):
    head = lax.broadcasted_iota(jnp.int32, (width, TILE), 1)
    col = lax.broadcasted_iota(jnp.int32, (width, TILE), 0)
    return jnp.where(head == col // MP, 1.0, 0.0).astype(jnp.bfloat16)


def head_lanes(rows):
    return lax.broadcasted_iota(jnp.int32, (rows, TILE), 1) < MH


def chunk_places(info, rows):
    at = lax.broadcasted_iota(jnp.int32, (rows, 1), 0) + info[0]
    return seg_start(at, info) - info[0]


def ssm_states(info, x, bc, step_in, head_params, state, dt_out, cum_out, dt_t, cum_t):
    rows = x.shape[0]
    bias, rate = head_params[0:1], head_params[1:2]
    raw = step_in[...] + bias
    dt = jnp.maximum(raw, 0.0) + jnp.log1p(jnp.exp(-jnp.abs(raw)))
    dt = jnp.where(head_lanes(rows), dt, 0.0)
    row = lax.broadcasted_iota(jnp.int32, (rows, rows), 0)
    col = lax.broadcasted_iota(jnp.int32, (rows, rows), 1)
    lower = jnp.where(row >= col, 1.0, 0.0)
    cum = exact(lower, -dt * rate)
    dt_out[...] = dt
    cum_out[...] = cum
    dt_t[...] = dt.T
    cum_t[...] = cum.T
    last_start = seg_start(info[0] + rows - 1, info) - info[0]
    place = lax.broadcasted_iota(jnp.int32, (rows, 1), 0)
    end = cum[rows - 1 : rows]
    leave = jnp.where(place >= last_start, jnp.exp(jnp.minimum(end - cum, 0.0)) * dt, 0.0)
    b_t = bc[:, :NS].astype(jnp.float32).T.astype(jnp.bfloat16)
    through = jnp.where(last_start < 0, jnp.exp(end), 0.0)
    high = through.astype(jnp.bfloat16).astype(jnp.float32)
    line = lax.broadcasted_iota(jnp.int32, (16, TILE), 0)
    both = jnp.where(line == 0, high, jnp.where(line == 1, through - high, 0.0))
    spread = spread_heads(x.shape[1])
    state[NS:] = dot(both.astype(jnp.bfloat16), spread).astype(jnp.bfloat16)
    for i in range(MH // 2):
        cols = slice(i * TILE, (i + 1) * TILE)
        weighed = x[:, cols].astype(jnp.float32) * lane_pick(leave, 2 * i)
        state[:NS, cols] = dot(b_t, weighed.astype(jnp.bfloat16)).astype(jnp.bfloat16)


def ssm_local(info, x, bc, head_params, y, cum, dt_t, cum_t):
    rows = x.shape[0]
    row = lax.broadcasted_iota(jnp.int32, (rows, rows), 0)
    col = lax.broadcasted_iota(jnp.int32, (rows, rows), 1)
    starts = chunk_places(info, rows)
    products = dot_nt(bc[:, NS:], bc[:, :NS])
    skips = jnp.broadcast_to(head_params[2:3], (8, TILE))
    skip_row = two_part(skips, spread_heads(x.shape[1]))[:1]
    lane = lax.broadcasted_iota(jnp.int32, (SPAN, TILE), 1)
    for i in range(MH // 2):
        cols = slice(i * TILE, (i + 1) * TILE)
        tile = x[:, cols]
        for part in range(rows // SPAN):
            here = slice(part * SPAN, (part + 1) * SPAN)
            upto = (part + 1) * SPAN
            allowed = (row[here, :upto] >= col[here, :upto]) & (col[here, :upto] >= starts[here])
            sides = []
            for h in (2 * i, 2 * i + 1):
                spread_log = cum[here, h : h + 1] - cum_t[h : h + 1, :upto]
                decay = jnp.exp(jnp.where(allowed, spread_log, NEGATIVE_FILL))
                mixing = products[here, :upto] * decay * dt_t[h : h + 1, :upto]
                sides.append(dot(mixing.astype(jnp.bfloat16), tile[:upto]))
            own = skip_row[:, cols] * tile[here].astype(jnp.float32)
            y[here, cols] = jnp.where(lane < MP, sides[0], sides[1]) + own


def ssm_forward_kernel(info, x, bc, step_in, head_params, y, state, dt_out, cum_out, dt_t, cum_t):
    ssm_states(info, x, bc, step_in, head_params, state, dt_out, cum_out, dt_t, cum_t)
    ssm_local(info, x, bc, head_params, y, cum_out, dt_t, cum_t)


def ssm_forward(info, x, bc, step_in, head_params):
    rows, width = x.shape
    f32 = jnp.float32
    return big_call(
        ssm_forward_kernel,
        (
            shape_of((rows, width), f32),
            shape_of((STATE_ROWS, width), jnp.bfloat16),
            shape_of((rows, TILE), f32),
            shape_of((rows, TILE), f32),
        ),
        info,
        x,
        bc,
        step_in,
        head_params,
        smem=1,
        scratch=(pltpu.VMEM((TILE, rows), f32), pltpu.VMEM((TILE, rows), f32)),
        flops=4 * rows * rows * width,
    )


def entering_of(info, cum):
    rows = cum.shape[0]
    return jnp.where(chunk_places(info, rows) < 0, jnp.exp(jnp.minimum(cum, 0.0)), 0.0)


def ssm_finish_kernel(info, y, bc, cum, state_in, z, gain, ssm_out, normed, scale):
    rows = y.shape[0]
    enter = entering_of(info, cum[...])
    narrow_c = bc[:, NS:]
    squares = jnp.zeros((rows, TILE), jnp.float32)
    tiles = MH // 2
    for i in range(tiles):
        cols = slice(i * TILE, (i + 1) * TILE)
        out = y[:, cols] + lane_pick(enter, 2 * i) * dot(narrow_c, state_in[:, cols])
        ssm_out[:, cols] = out
        gate = z[:, cols]
        gated = out * (gate * jax.nn.sigmoid(gate))
        squares = squares + gated * gated
    mean = jnp.sum(squares, axis=1, keepdims=True) * (1.0 / (tiles * TILE))
    r = lax.rsqrt(mean + NORM_EPS)
    scale[...] = jnp.broadcast_to(r, scale.shape)
    for i in range(tiles):
        cols = slice(i * TILE, (i + 1) * TILE)
        gate = z[:, cols]
        gated = ssm_out[:, cols] * (gate * jax.nn.sigmoid(gate))
        normed[:, cols] = (gated * r * gain[:, cols]).astype(jnp.bfloat16)


def ssm_finish(info, y, bc, cum, state_in, z, gain):
    rows, width = y.shape
    return big_call(
        ssm_finish_kernel,
        (
            shape_of((rows, width), jnp.float32),
            shape_of((rows, width), jnp.bfloat16),
            shape_of((rows, TILE), jnp.float32),
        ),
        info,
        y,
        bc,
        cum,
        state_in,
        z,
        gain,
        smem=1,
        flops=2 * rows * NS * width,
    )


def gate_back_kernel(info, dy, ssm_out, z, scale, gain, cum, bc, d_out, d_z, pull, g_gain):
    rows = dy.shape[0]
    tiles = MH // 2
    r = scale[:, :1]
    enter = entering_of(info, cum[...])
    c_t = bc[:, NS:].astype(jnp.float32).T.astype(jnp.bfloat16)
    inner = jnp.zeros((rows, TILE), jnp.float32)
    for i in range(tiles):
        cols = slice(i * TILE, (i + 1) * TILE)
        gate = z[:, cols]
        gated = ssm_out[:, cols] * (gate * jax.nn.sigmoid(gate))
        product = dy[:, cols] * gated
        g_gain[:, cols] = jnp.sum(product * r, axis=0, keepdims=True)
        inner = inner + product * gain[:, cols]
    coeff = jnp.sum(inner, axis=1, keepdims=True) * (1.0 / (tiles * TILE))
    for i in range(tiles):
        cols = slice(i * TILE, (i + 1) * TILE)
        gate = z[:, cols]
        sig = jax.nn.sigmoid(gate)
        silu = gate * sig
        out = ssm_out[:, cols]
        d_gated = r * (dy[:, cols] * gain[:, cols] - out * silu * (r * r * coeff))
        d_ssm = d_gated * silu
        d_out[:, cols] = d_ssm
        d_z[:, cols] = (d_gated * out * (sig * (1.0 + gate * (1.0 - sig)))).astype(jnp.bfloat16)
        pull[:, cols] = dot(c_t, (d_ssm * lane_pick(enter, 2 * i)).astype(jnp.bfloat16)).astype(
            jnp.bfloat16
        )


def gate_back(info, dy, ssm_out, z, scale, gain, cum, bc):
    rows, width = dy.shape
    return big_call(
        gate_back_kernel,
        (
            shape_of((rows, width), jnp.float32),
            shape_of((rows, width), jnp.bfloat16),
            shape_of((NS, width), jnp.bfloat16),
            shape_of((1, width), jnp.float32),
        ),
        info,
        dy,
        ssm_out,
        z,
        scale,
        gain,
        cum,
        bc,
        smem=1,
        flops=2 * rows * NS * width,
    )


def ssm_back_kernel(info, x, bc, dt, cum, grad, head_params, dx, d_bc, d_cum, d_dt, g_skip, cols_t, d_rows):
    rows, width = x.shape
    skip = head_params[2:3]
    cols_t[...] = cum[...].T
    row = lax.broadcasted_iota(jnp.int32, (rows, rows), 0)
    col = lax.broadcasted_iota(jnp.int32, (rows, rows), 1)
    at = lax.broadcasted_iota(jnp.int32, (1, rows), 1) + info[0]
    starts = seg_start(at, info) - info[0]
    narrow_b, narrow_c = bc[:, :NS], bc[:, NS:]
    products = dot_nt(narrow_b, narrow_c)
    skip_row = two_part(jnp.broadcast_to(skip, (8, TILE)), spread_heads(width))[:1]
    lane = lax.broadcasted_iota(jnp.int32, (SPAN, TILE), 1)
    parts = rows // SPAN
    d_products = [jnp.zeros((SPAN, rows - p * SPAN), jnp.float32) for p in range(parts)]
    d_rows[...] = jnp.zeros_like(d_rows)
    step_sums = [jnp.zeros((SPAN, TILE), jnp.float32) for p in range(parts)]
    skip_sums = []
    for i in range(MH // 2):
        cols = slice(i * TILE, (i + 1) * TILE)
        tile = x[:, cols]
        wide = grad[:, cols]
        narrow = wide.astype(jnp.bfloat16)
        skip_sums.append(jnp.sum(wide * tile.astype(jnp.float32), axis=0, keepdims=True))
        tile_sides = halves_of(tile)
        for part in range(parts):
            here = slice(part * SPAN, (part + 1) * SPAN)
            since = part * SPAN
            allowed = (row[here, since:] <= col[here, since:]) & (
                row[here, since:] >= starts[:, since:]
            )
            sides = []
            for side in range(2):
                h = 2 * i + side
                spread_log = cols_t[h : h + 1, since:] - cum[here, h : h + 1]
                decay = jnp.exp(jnp.where(allowed, spread_log, NEGATIVE_FILL))
                decay_dt = decay * dt[here, h : h + 1]
                mixing = products[here, since:] * decay_dt
                sides.append(dot(mixing.astype(jnp.bfloat16), narrow[since:]))
                d_mixing = dot_nt(tile_sides[side][here], narrow[since:])
                d_products[part] = d_products[part] + d_mixing * decay_dt
                whole = d_mixing * mixing
                d_rows[h : h + 1, since:] += jnp.sum(whole, axis=0, keepdims=True)
                weighed = d_mixing * (products[here, since:] * decay)
                step_sums[part] = jnp.where(
                    lane == h, jnp.sum(weighed, axis=1, keepdims=True), step_sums[part]
                )
            dx[here, cols] = (
                jnp.where(lane < MP, sides[0], sides[1]) + skip_row[:, cols] * wide[here]
            )
    all_steps = jnp.concatenate(step_sums, axis=0)
    d_dt[...] = all_steps
    d_cum[...] = d_rows[...].T - all_steps * dt[...]
    g_skip[...] = jnp.broadcast_to(
        two_part(
            jnp.broadcast_to(jnp.concatenate(skip_sums, axis=1), (8, width)), gather_heads(width)
        ),
        g_skip.shape,
    )
    full = jnp.concatenate(
        [
            d
            if p == 0
            else jnp.concatenate([jnp.zeros((SPAN, p * SPAN), jnp.float32), d], axis=1)
            for p, d in enumerate(d_products)
        ],
        axis=0,
    ).astype(jnp.bfloat16)
    d_bc[:, :NS] = dot(full, narrow_c)
    d_bc[:, NS:] = dot_tn(full, narrow_b)


def ssm_back(info, x, bc, dt, cum, grad, head_params):
    rows, width = x.shape
    f32 = jnp.float32
    return big_call(
        ssm_back_kernel,
        (
            shape_of((rows, width), f32),
            shape_of((rows, 2 * NS), f32),
            shape_of((rows, TILE), f32),
            shape_of((rows, TILE), f32),
            shape_of((8, TILE), f32),
        ),
        info,
        x,
        bc,
        dt,
        cum,
        grad,
        head_params,
        smem=1,
        scratch=(pltpu.VMEM((TILE, rows), f32), pltpu.VMEM((TILE, rows), f32)),
        flops=8 * rows * rows * width,
    )


def state_back_kernel(
    info, x, bc, dt, cum, grad, head_params, step_in, state_in, d_state, dx_in, d_bc_in, d_cum_in,
    d_dt_in, dx, d_bc, d_step, sums,
):
    rows, width = x.shape
    bias, rate = head_params[0:1], head_params[1:2]
    cums, steps = cum[...], dt[...]
    enter = entering_of(info, cums)
    last_start = seg_start(info[0] + rows - 1, info) - info[0]
    place = lax.broadcasted_iota(jnp.int32, (rows, 1), 0)
    end = cums[rows - 1 : rows]
    fade = jnp.where(place >= last_start, jnp.exp(jnp.minimum(end - cums, 0.0)), 0.0)
    leave = fade * steps
    through = jnp.where(last_start < 0, jnp.exp(end), 0.0)
    narrow_b, narrow_c = bc[:, :NS], bc[:, NS:]
    pick = gather_heads(width)
    d_leave = jnp.zeros((rows, TILE), jnp.float32)
    d_enter = jnp.zeros((rows, TILE), jnp.float32)
    d_b = d_bc_in[:, :NS]
    d_c = d_bc_in[:, NS:]
    link = jnp.zeros((8, TILE), jnp.float32)
    for i in range(MH // 2):
        cols = slice(i * TILE, (i + 1) * TILE)
        tile = x[:, cols].astype(jnp.float32)
        wide = grad[:, cols]
        pulled = d_state[:, cols]
        held = state_in[:, cols]
        from_b = dot(narrow_b, pulled)
        leave_tile = lane_pick(leave, 2 * i)
        dx[:, cols] = dx_in[:, cols] + leave_tile * from_b
        d_leave = d_leave + two_part(tile * from_b, pick[cols])
        d_enter = d_enter + two_part(wide * dot(narrow_c, held), pick[cols])
        d_b = d_b + dot_nt((tile * leave_tile).astype(jnp.bfloat16), pulled)
        d_c = d_c + dot_nt((wide * lane_pick(enter, 2 * i)).astype(jnp.bfloat16), held)
        meet = jnp.sum(
            pulled.astype(jnp.float32) * held.astype(jnp.float32), axis=0, keepdims=True
        )
        link = link + two_part(jnp.broadcast_to(meet, (8, TILE)), pick[cols])
    d_bc[:, :NS] = d_b
    d_bc[:, NS:] = d_c
    left = leave * d_leave
    d_cum = d_cum_in[...] + enter * d_enter - left
    at_end = jnp.sum(left, axis=0, keepdims=True) + through * link[:1]
    d_cum = d_cum + jnp.where(place == rows - 1, at_end, 0.0)
    row = lax.broadcasted_iota(jnp.int32, (rows, rows), 0)
    col = lax.broadcasted_iota(jnp.int32, (rows, rows), 1)
    d_log = exact(jnp.where(row <= col, 1.0, 0.0), d_cum)
    d_steps = d_dt_in[...] + fade * d_leave - d_log * rate
    d_pre = d_steps * jax.nn.sigmoid(step_in[...] + bias)
    d_pre = jnp.where(head_lanes(rows), d_pre, 0.0)
    d_step[...] = d_pre.astype(jnp.bfloat16)
    g_rate = jnp.sum(d_log * (-steps * rate), axis=0, keepdims=True)
    g_bias = jnp.sum(d_pre, axis=0, keepdims=True)
    line = lax.broadcasted_iota(jnp.int32, (8, TILE), 0)
    sums[...] = jnp.where(line == 0, g_rate, jnp.where(line == 1, g_bias, 0.0))


def state_back(info, *args):
    rows, width = args[0].shape
    f32 = jnp.float32
    return big_call(
        state_back_kernel,
        (
            shape_of((rows, width), f32),
            shape_of((rows, 2 * NS), f32),
            shape_of((rows, TILE), jnp.bfloat16),
            shape_of((8, TILE), f32),
        ),
        info,
        *args,
        smem=1,
        flops=12 * rows * NS * width,
    )


def join_states(earlier, later):
    decay = later[NS : NS + 1].astype(jnp.float32) + later[NS + 1 : NS + 2].astype(jnp.float32)
    before = earlier[NS : NS + 1].astype(jnp.float32) + earlier[NS + 1 : NS + 2].astype(jnp.float32)
    state = decay * earlier[:NS].astype(jnp.float32) + later[:NS].astype(jnp.float32)
    both = decay * before
    high = both.astype(jnp.bfloat16)
    low = (both - high.astype(jnp.float32)).astype(jnp.bfloat16)
    rest = jnp.zeros((STATE_ROWS - NS - 2, state.shape[1]), jnp.bfloat16)
    return jnp.concatenate([state.astype(jnp.bfloat16), high, low, rest], axis=0)


def scan_states(own, forward):
    place = lax.axis_index("seq")
    count = lax.axis_size("seq")
    nothing = jnp.concatenate(
        [
            jnp.zeros((NS, own.shape[1]), own.dtype),
            jnp.ones((1, own.shape[1]), own.dtype),
            jnp.zeros((STATE_ROWS - NS - 1, own.shape[1]), own.dtype),
        ],
        axis=0,
    )
    everything = lax.all_gather(own, "seq")

    def step(k, before):
        index = k if forward else count - 1 - k
        reached = index < place if forward else index > place
        part = lax.dynamic_index_in_dim(everything, index, 0, False)
        return jnp.where(reached, join_states(before, part), before)

    return lax.fori_loop(0, count, step, nothing)[:NS]


MESH = pl.DeviceIdType.MESH
ANY = pl.BlockSpec(memory_space=pl.ANY)
INTO_VMEM = pl.BlockSpec(memory_space=pltpu.VMEM)


def partners():
    seq, batch = lax.axis_index("seq"), lax.axis_index("batch")
    return {
        "far": (seq + 4 - 8 * (seq // 4), batch),
        "near": (seq + 2 - 4 * (seq // 2 % 2), batch),
        "x": (seq + 1 - 2 * (seq % 2), batch),
        "y": (seq, batch + 2 - 4 * (batch // 2)),
        "core": (seq, batch + 1 - 2 * (batch % 2)),
    }


def greet(others):
    barrier = pltpu.get_barrier_semaphore()
    for other in others:
        pl.semaphore_signal(barrier, inc=1, device_id=other, device_id_type=MESH)
    pl.semaphore_wait(barrier, len(others))


def remote(src, dst, send, recv, other):
    return pltpu.make_async_remote_copy(
        src_ref=src, dst_ref=dst, send_sem=send, recv_sem=recv, device_id=other, device_id_type=MESH
    )


def comm_call(kernel, outs, out_specs, args, in_specs, scratch, number, moved, limit=56):
    return pl.pallas_call(
        kernel,
        out_shape=list(outs),
        in_specs=in_specs,
        out_specs=out_specs,
        scratch_shapes=list(scratch),
        cost_estimate=pl.CostEstimate(flops=0, bytes_accessed=moved, transcendentals=0),
        compiler_params=pltpu.CompilerParams(
            collective_id=number, has_side_effects=True, vmem_limit_bytes=limit * 1024 * 1024
        ),
    )(*args)


def column_chunks(widths):
    pairs = []
    for p, width in enumerate(widths):
        tiles, first, cuts = width // TILE, 0, []
        pieces = 2 * max(1, width // 2048)
        for i in range(pieces):
            cols = (tiles // pieces + (1 if i < tiles % pieces else 0)) * TILE
            cuts.append((p, first, cols))
            first += cols
        pairs += [tuple(cuts[i : i + 2]) for i in range(0, pieces, 2)]
    return pairs


def gather_plan(x_first):
    plan = [("far", [(0, 1, 1)]), ("near", [(0, 2, 2)])]
    if x_first:
        plan += [("x", [(0, 4, 4)]), ("y", [(0, 8, 8)])]
    else:
        plan += [("y", [(0, 4, 8)]), ("x", [(0, 4, 4), (8, 4, 12)])]
    return plan + [("core", [(0, 16, 16)])]


def bit_apart(r):
    me = lax.axis_index("seq")
    far = (r // 4 + me // 4) % 2
    near = (r // 2 % 2 + me // 2 % 2) % 2
    side = (r % 2 + me % 2) % 2
    return 4 * far + 2 * near + side


def join_into(target, earlier, later):
    decay = later[NS : NS + 1].astype(jnp.float32) + later[NS + 1 : NS + 2].astype(jnp.float32)
    before = earlier[NS : NS + 1].astype(jnp.float32) + earlier[NS + 1 : NS + 2].astype(jnp.float32)
    both = decay * before
    high = both.astype(jnp.bfloat16).astype(jnp.float32)
    line = lax.broadcasted_iota(jnp.int32, (STATE_ROWS - NS, both.shape[1]), 0)
    tail = jnp.where(line == 0, high, jnp.where(line == 1, both - high, 0.0))
    for first in range(0, NS, 32):
        rows = slice(first, first + 32)
        target[rows] = (
            decay * earlier[rows].astype(jnp.float32) + later[rows].astype(jnp.float32)
        ).astype(jnp.bfloat16)
    target[NS:] = tail.astype(jnp.bfloat16)


class StateScan:
    def __init__(self, forward, own, result, arrived, sent, before, send, recv, others):
        me = lax.axis_index("seq")
        self.seconds = []
        for bit in (me % 2, me // 2 % 2, me // 4):
            self.seconds.append(bit == 1 if forward else bit == 0)
        self.own, self.result, self.arrived, self.sent, self.before = (
            own, result, arrived, sent, before,
        )
        route = (others["x"], others["near"], others["far"])
        sources = (own, sent.at[0], sent.at[1])
        self.copies = [
            remote(sources[k], arrived.at[k], send.at[k], recv.at[k], route[k]) for k in range(3)
        ]

    def step(self, k):
        if k == 0:
            self.copies[0].start()
            return
        self.copies[k - 1].wait_recv()
        other = self.arrived.at[k - 1]
        mine = self.own if k == 1 else self.sent.at[k - 2]
        second = self.seconds[k - 1]
        before, result = self.before, self.result

        @pl.when(second)
        def _():
            if k < 3:
                join_into(self.sent.at[k - 1], other, mine)
            if k == 1:
                before[0] = other[...]
            elif k == 2:
                join_into(before.at[1], other, before.at[0])
            else:
                decay = before[1, NS : NS + 1].astype(jnp.float32) + before[
                    1, NS + 1 : NS + 2
                ].astype(jnp.float32)
                result[...] = (
                    decay * other[:NS].astype(jnp.float32) + before[1, :NS].astype(jnp.float32)
                ).astype(jnp.bfloat16)

        @pl.when(jnp.logical_not(second))
        def _():
            if k < 3:
                join_into(self.sent.at[k - 1], mine, other)
            if k == 1:
                line = lax.broadcasted_iota(jnp.int32, before.shape[1:], 0)
                before[0] = jnp.where(line == NS, 1.0, 0.0).astype(jnp.bfloat16)
            elif k == 2:
                before[1] = before[0]
            else:
                result[...] = before[1, :NS]

        if k < 3:
            self.copies[k].start()

    def finish(self):
        for copy in self.copies:
            copy.wait_send()


def scan_scratch(width):
    rows = STATE_ROWS
    dma = pltpu.SemaphoreType.DMA
    narrow = jnp.bfloat16
    return [
        pltpu.VMEM((3, rows, width), narrow),
        pltpu.VMEM((2, rows, width), narrow),
        pltpu.VMEM((2, rows, width), narrow),
        dma((3,)),
        dma((3,)),
    ]


RIM = 8
COLS = 384


def own_order_into(target):
    width = target.shape[0]
    per = width // 32
    me = lax.axis_index("seq") * 4 + lax.axis_index("batch")
    step = 128

    def fill(i, carry):
        first = pl.multiple_of(i * step, step)
        row = lax.broadcasted_iota(jnp.int32, (step, width), 0) + first
        col = lax.broadcasted_iota(jnp.int32, (step, width), 1)
        j = col // per
        flipped = (j & 1) * 16 + (j & 2) * 4 + (j & 4) + (j & 8) // 4 + (j & 16) // 16
        source = (flipped ^ me) * per + col % per
        target[pl.ds(first, step)] = jnp.where(row == source, 1.0, 0.0).astype(target.dtype)
        return carry

    lax.fori_loop(0, width // step, fill, 0)


def three_part(left, right):
    high = left.astype(jnp.bfloat16)
    rest = left - high.astype(jnp.float32)
    mid = rest.astype(jnp.bfloat16)
    low = (rest - mid.astype(jnp.float32)).astype(jnp.bfloat16)
    return dot(high, right) + dot(mid, right) + dot(low, right)


class Gather:
    def __init__(self, ins, outs, pairs, send, recv, local, others):
        self.ins, self.outs, self.pairs = ins, outs, pairs
        self.send, self.recv, self.local, self.others = send, recv, local, others
        self.plans = [gather_plan(True), gather_plan(False)]
        self.started = {}
        self.block = ins[0].shape[0]

    def own(self):
        copies = []
        for p in range(len(self.ins)):
            copy = pltpu.make_async_copy(
                self.ins[p], self.outs[p].at[pl.ds(0, self.block)], self.local.at[p]
            )
            copy.start()
            copies.append(copy)
        for copy in copies:
            copy.wait()

    def step(self, n, stage):
        for side in range(2):
            p, column, cols = self.pairs[n][side]
            if stage > 0:
                for copy in self.started[n, side, stage - 1]:
                    copy.wait_recv()
            if stage == 5:
                continue
            name, moves = self.plans[side][stage]
            copies = []
            for k, (first, rows, there) in enumerate(moves):
                block = self.block
                copy = remote(
                    self.outs[p].at[pl.ds(first * block, rows * block), pl.ds(column, cols)],
                    self.outs[p].at[pl.ds(there * block, rows * block), pl.ds(column, cols)],
                    self.send.at[2 * n + side, stage, k],
                    self.recv.at[2 * n + side, stage, k],
                    self.others[name],
                )
                copy.start()
                copies.append(copy)
            self.started[n, side, stage] = copies

    def finish(self):
        for copies in self.started.values():
            for copy in copies:
                copy.wait_send()


def around():
    seq, batch = lax.axis_index("seq"), lax.axis_index("batch")
    return ((seq + 7) % 8, batch), ((seq + 1) % 8, batch)


def conv_masks(info, rows):
    at = lax.broadcasted_iota(jnp.int32, (rows, 1), 0) + info[0]
    start = seg_start(at, info)
    return [jnp.where(at - (CONV - 1) + i >= start, 1.0, 0.0) for i in range(CONV)]


def conv_forward(info, raw, conv_w, conv_b, pre, x, bc):
    rows = x.shape[0]
    masks = conv_masks(info, rows)
    tiles = pre.shape[1] // TILE
    split = x.shape[1] // TILE
    for i in range(tiles):
        cols = slice(i * TILE, (i + 1) * TILE)
        total = jnp.broadcast_to(conv_b[:, cols], (rows, TILE))
        for k in range(CONV):
            first = RIM - (CONV - 1) + k
            shifted_rows = jnp.where(masks[k] > 0.0, raw[first : first + rows, cols], 0.0)
            total = total + conv_w[k : k + 1, cols] * shifted_rows
        pre[:, cols] = total
        out = (total * jax.nn.sigmoid(total)).astype(jnp.bfloat16)
        if i < split:
            x[:, cols] = out
        else:
            bc[:, (i - split) * TILE : (i - split + 1) * TILE] = out


def front_kernel(count, pairs, info, layer_x, layer_g, gains, cosine, sine, head_params, conv_w, conv_b, *refs):
    ins, refs = refs[:count], refs[count:]
    fulls, refs = refs[:count], refs[count:]
    (
        x_own, g_own, gains_own, normed, q, kv, gate_z, raw, pre, x, bc, y, state, dt, cum,
        out, out_t, lse, state_in, order,
    ) = refs[:20]
    (
        attn_proj, dt_t, cum_t, heads, acc, top, total, arrived, sent, before,
        scan_send, scan_recv, send, recv, w_send, w_recv, w_local, rim_send, rim_recv,
    ) = refs[20:]
    others = partners()
    previous, following = around()
    greet(list(others.values()) + [previous, following])
    me = lax.axis_index("seq")
    rows, width = layer_x.shape
    gather = Gather(ins, fulls, pairs, w_send, w_recv, w_local, others)
    gather.own()

    def pump(*steps):
        for n, stage in steps:
            gather.step(n, stage)

    pump((0, 0), (1, 0))
    own_order_into(order)
    pump((0, 1), (1, 1))
    x_own[...] = dot(layer_x[...], order[...]).astype(jnp.bfloat16)
    pump((0, 2), (2, 0))
    gains_own[...] = three_part(gains[...], order[...])
    wide = x_own[...].astype(jnp.float32)
    scale = lax.rsqrt(jnp.mean(wide * wide, axis=-1, keepdims=True) + NORM_EPS)
    normed[...] = (wide * scale * gains_own[0:1]).astype(jnp.bfloat16)
    pump((1, 2), (0, 3), (2, 1), (3, 0))
    g_own[...] = dot(layer_g[...], order[...]).astype(jnp.bfloat16)
    pump((0, 4), (1, 3), (3, 1), (4, 0))
    pump((0, 5))

    full_conv, full_mix = fulls[0], fulls[1]
    xbc = pre.shape[1]
    conv_cols = full_conv.shape[1] // COLS
    attn_cols = attn_proj.shape[1] // COLS
    gate_cols = gate_z.shape[1] // COLS

    def project(weights, first, target, row, count_cols):
        def one(j, carry):
            cols = pl.ds(pl.multiple_of(j * COLS, TILE), COLS)
            there = pl.ds(pl.multiple_of(first + j * COLS, TILE), COLS)
            target[row : row + rows, cols] = dot(normed[...], weights[:, there])
            return carry

        lax.fori_loop(0, count_cols, one, 0)

    def at(r):
        return kv.at[pl.ds(r * rows, rows)]

    routes = {4: ("far", 0), 2: ("near", 0), 6: ("near", 4)}
    routes.update({r: ("x", r - 1) for r in (1, 3, 5, 7)})
    copies = {
        r: remote(at(src), at(r), send.at[r], recv.at[r], others[name])
        for r, (name, src) in routes.items()
    }
    project(full_conv, 0, raw, RIM, conv_cols)
    rim = remote(
        raw.at[pl.ds(rows, RIM)], raw.at[pl.ds(0, RIM)], rim_send.at[0], rim_recv.at[0], following
    )
    rim.start()
    pump((1, 4), (2, 2), (4, 1), (5, 0))
    rim.wait_recv()
    conv_forward(info, raw, conv_w, conv_b, pre, x, bc)
    step_in = raw.at[pl.ds(RIM, rows), pl.ds(xbc, TILE)]
    ssm_states(info, x, bc, step_in, head_params, state, dt, cum, dt_t, cum_t)
    scan = StateScan(True, state, state_in, arrived, sent, before, scan_send, scan_recv, others)
    scan.step(0)
    pump((1, 5))
    project(full_mix, 0, attn_proj, 0, attn_cols)
    rope_kernel(attn_proj, cosine, sine, q, kv.at[pl.ds(0, rows)])
    copies[4].start()
    copies[2].start()
    copies[1].start()
    pump((5, 1), (2, 3), (3, 2))
    project(full_mix, attn_proj.shape[1], gate_z, 0, gate_cols)
    attend_start(q, heads, acc, top, total)

    def attend(r):
        block = bit_apart(r)

        @pl.when(block <= me)
        def _():
            place = pl.ds(pl.multiple_of(r * rows, rows), rows)
            keys = kv[place, :TILE]
            values_t = kv[place, TILE:].astype(jnp.float32).T.astype(jnp.bfloat16)
            attend_block(info, block, keys, values_t, heads, acc, top, total)

    def several(first, gap, count_blocks):
        def body(j, carry):
            attend(first + j * gap)
            return carry

        lax.fori_loop(0, count_blocks, body, 0)

    scan.step(1)
    copies[4].wait_recv()
    copies[6].start()
    copies[5].start()
    copies[2].wait_recv()
    copies[3].start()
    copies[6].wait_recv()
    copies[7].start()
    several(0, 4, 2)
    pump((3, 3), (4, 2), (2, 4))
    ssm_local(info, x, bc, head_params, y, cum, dt_t, cum_t)
    scan.step(2)
    several(2, 4, 2)
    pump((4, 3), (5, 2), (3, 4))
    for r in (1, 3, 5, 7):
        copies[r].wait_recv()
    several(1, 2, 4)
    lse[...] = top[...] + jnp.log(total[...])
    attend_write(acc, total, out, out_t)
    scan.step(3)
    pump((5, 3), (4, 4), (2, 5))
    pump((5, 4), (3, 5), (4, 5), (5, 5))
    gather.finish()
    scan.finish()
    rim.wait_send()
    for copy in copies.values():
        copy.wait_send()


def front(info, layer_x, layer_g, gains, cosine, sine, head_params, conv_w, conv_b, shards):
    count = len(shards)
    rows, width = layer_x.shape
    f32, narrow = jnp.float32, jnp.bfloat16
    pairs = column_chunks([p.shape[1] for p in shards])
    query_width = QUERY_HEADS * HEAD_SIZE
    pair_width = 2 * KEY_VALUE_HEADS * HEAD_SIZE
    ssm_width = MH * MP
    xbc = conv_w.shape[1]
    fulls = [shape_of((32 * p.shape[0], p.shape[1]), p.dtype) for p in shards]
    outs = fulls + [
        shape_of((rows, width), narrow),
        shape_of((rows, width), narrow),
        shape_of(gains.shape, f32),
        shape_of((rows, width), narrow),
        shape_of((rows, query_width), narrow),
        shape_of((8 * rows, pair_width), narrow),
        shape_of((rows, ssm_width), f32),
        shape_of((rows + RIM, shards[0].shape[1]), f32),
        shape_of((rows, xbc), f32),
        shape_of((rows, ssm_width), narrow),
        shape_of((rows, 2 * NS), narrow),
        shape_of((rows, ssm_width), f32),
        shape_of((STATE_ROWS, ssm_width), narrow),
        shape_of((rows, TILE), f32),
        shape_of((rows, TILE), f32),
        shape_of((rows, query_width), narrow),
        shape_of((query_width, rows), f32),
        shape_of((QUERY_HEADS, rows), f32),
        shape_of((NS, ssm_width), narrow),
        shape_of((width, width), narrow),
    ]
    dma = pltpu.SemaphoreType.DMA
    scratch = [
        pltpu.VMEM((rows, query_width + pair_width), f32),
        pltpu.VMEM((TILE, rows), f32),
        pltpu.VMEM((TILE, rows), f32),
        pltpu.VMEM((QUERY_HEADS, rows, TILE), narrow),
        pltpu.VMEM((QUERY_HEADS, HEAD_SIZE, rows), f32),
        pltpu.VMEM((QUERY_HEADS, rows), f32),
        pltpu.VMEM((QUERY_HEADS, rows), f32),
        *scan_scratch(ssm_width),
        dma((8,)),
        dma((8,)),
        dma((2 * len(pairs), 5, 2)),
        dma((2 * len(pairs), 5, 2)),
        dma((count,)),
        dma((1,)),
        dma((1,)),
    ]
    result = comm_call(
        lambda *refs: front_kernel(count, pairs, *refs),
        outs,
        [INTO_VMEM] * 2 + [ANY] * (count - 2) + [INTO_VMEM] * 20,
        (info, layer_x, layer_g, gains, cosine, sine, head_params, conv_w, conv_b, *shards),
        [pl.BlockSpec(memory_space=pltpu.SMEM)] + [INTO_VMEM] * 8 + [ANY] * count,
        scratch,
        0,
        200_000_000,
    )
    return result[:count], result[count:]


def turn_over(value):
    return value.astype(jnp.float32).T.astype(jnp.bfloat16)


class Scatter:
    def __init__(self, ins, outs, arrived, pairs, send, recv, others):
        self.ins, self.outs, self.arrived, self.pairs = ins, outs, arrived, pairs
        self.send, self.recv, self.others = send, recv, others
        self.routes = (("y", "x", "near", "far"), ("x", "y", "near", "far"))
        self.size = ins[0].shape[0]
        self.started = {}

    def source(self, p, stage):
        return self.ins[p] if stage == 0 else self.arrived[4 * p + stage - 1]

    def pieces(self, side, stage):
        rows = self.size >> stage
        if side == 1 and stage == 0:
            quarter = rows // 4
            return [quarter, 3 * quarter], [0, 2 * quarter], quarter
        return [rows // 2], [0], rows // 2

    def step(self, n, stage):
        for side in range(2):
            if stage > 0:
                self.take(n, side, stage - 1)
            if stage < 4:
                self.begin(n, side, stage)

    def begin(self, n, side, stage):
        p, column, width = self.pairs[n][side]
        cols = pl.ds(column, width)
        sent, unused_kept, rows = self.pieces(side, stage)
        copies = []
        for k, first in enumerate(sent):
            copy = remote(
                self.source(p, stage).at[pl.ds(first, rows), cols],
                self.arrived[4 * p + stage].at[pl.ds(k * rows, rows), cols],
                self.send.at[2 * n + side, stage, k],
                self.recv.at[2 * n + side, stage, k],
                self.others[self.routes[side][stage]],
            )
            copy.start()
            copies.append(copy)
        self.started[n, side, stage] = copies

    def take(self, n, side, stage):
        p, column, width = self.pairs[n][side]
        cols = slice(column, column + width)
        source, got = self.source(p, stage), self.arrived[4 * p + stage]
        target = self.outs[p] if stage == 3 else got
        unused_sent, kept, rows = self.pieces(side, stage)
        for k, first in enumerate(kept):
            self.started[n, side, stage][k].wait_recv()

            def add(i, carry):
                at = pl.multiple_of(i * 32, 32)
                there = pl.ds(k * rows + at, 32)
                total = source[pl.ds(first + at, 32), cols].astype(jnp.float32) + got[
                    there, cols
                ].astype(jnp.float32)
                target[there, cols] = total.astype(target.dtype)
                return carry

            lax.fori_loop(0, rows // 32, add, 0)

    def finish(self):
        for copies in self.started.values():
            for copy in copies:
                copy.wait_send()


def scatter_scratch(widths, size):
    scratch = []
    for width in widths:
        scratch += [pltpu.VMEM((size >> (s + 1), width), jnp.bfloat16) for s in range(4)]
    return scratch


def weight_products(left_t, right, theirs, target):
    rows = right.shape[0]
    step = 256 if right.shape[1] % 256 == 0 else TILE

    def one(j, carry):
        cols = pl.ds(pl.multiple_of(j * step, step), step)
        product = dot(left_t[:, :rows], right[:, cols]) + dot(left_t[:, rows:], theirs[:, cols])
        target[:, cols] = product.astype(target.dtype)
        return carry

    lax.fori_loop(0, right.shape[1] // step, one, 0)


def conv_back_start(info, dx, d_bc, pre, raw, d_pre, g_conv):
    rows, split = dx.shape[0], dx.shape[1] // TILE
    masks = conv_masks(info, rows)
    g_conv[...] = jnp.zeros_like(g_conv)
    for i in range(pre.shape[1] // TILE):
        cols = slice(i * TILE, (i + 1) * TILE)
        if i < split:
            grad = dx[:, cols]
        else:
            grad = d_bc[:, (i - split) * TILE : (i - split + 1) * TILE]
        value = pre[:, cols]
        sig = jax.nn.sigmoid(value)
        grad = grad * (sig * (1.0 + value * (1.0 - sig)))
        d_pre[:rows, cols] = grad
        for k in range(CONV):
            first = RIM - (CONV - 1) + k
            term = jnp.where(masks[k] > 0.0, raw[first : first + rows, cols], 0.0)
            g_conv[k : k + 1, cols] = jnp.sum(grad * term, axis=0, keepdims=True)
        g_conv[CONV : CONV + 1, cols] = jnp.sum(grad, axis=0, keepdims=True)


def conv_back_end(info, d_pre, conv_w, d_raw):
    rows = d_raw.shape[0]
    at = lax.broadcasted_iota(jnp.int32, (rows, 1), 0) + info[0]
    masks = [
        jnp.where(seg_start(at + (CONV - 1) - k, info) <= at, 1.0, 0.0) for k in range(CONV)
    ]
    for i in range(d_pre.shape[1] // TILE):
        cols = slice(i * TILE, (i + 1) * TILE)
        total = jnp.zeros((rows, TILE), jnp.float32)
        for k in range(CONV):
            first = CONV - 1 - k
            part = jnp.where(masks[k] > 0.0, d_pre[first : first + rows, cols], 0.0)
            total = total + conv_w[k : k + 1, cols] * part
        d_raw[:, cols] = total.astype(jnp.bfloat16)


def back_kernel(pairs, *refs):
    (
        info, head_params, conv_w, cosine, sine, q, kv, grad, out_t, lse, pull, x, bc, dt, cum,
        d_ssm, raw, state_in, pre, normed, normed_two, d_mixer, grad_rows, hidden, joined, d_gu,
        d_z,
    ) = refs[:27]
    (
        d_conv, d_attn, g_conv, head_sums, g_skip, their_normed, out_down, out_gu, out_out, out_z,
    ) = refs[27:37]
    refs = refs[37:]
    partials, refs = refs[:4], refs[4:]
    arrived_w, refs = refs[:16], refs[16:]
    (
        half_grad, half_two, half_mixer, their_hidden, their_joined, their_gu, their_z, left_t,
        heads, grads, delta, acc, dkv, from_x, from_far, from_near, dq, d_pair, d_state,
        dx, d_bc, d_cum, d_dt, cols_t, d_rows, d_pre,
        arrived, sent, before, scan_send, scan_recv, send, recv, swap_send, swap_recv,
        w_send, w_recv, rim_send, rim_recv,
    ) = refs
    others = partners()
    previous, following = around()
    greet(list(others.values()) + [previous, following])
    me = lax.axis_index("seq")
    rows = q.shape[0]
    half = normed.shape[1] // 2
    xbc = pre.shape[1]
    scan = StateScan(False, pull, d_state, arrived, sent, before, scan_send, scan_recv, others)
    scan.step(0)
    behind = pl.ds(half, half)
    given = [
        (grad_rows.at[:, behind], half_grad),
        (hidden, their_hidden),
        (normed_two.at[:, behind], half_two),
        (d_gu, their_gu),
        (d_mixer.at[:, behind], half_mixer),
        (joined, their_joined),
        (normed.at[:, behind], their_normed),
        (d_z, their_z),
    ]
    swaps = [
        remote(give, take, swap_send.at[k], swap_recv.at[k], others["core"])
        for k, (give, take) in enumerate(given)
    ]
    for copy in swaps:
        copy.start()
    scatter = Scatter(
        partials, (out_down, out_gu, out_out, out_z), arrived_w, pairs, w_send, w_recv, others
    )

    def weights(k, left, left_half, right, theirs):
        swaps[2 * k].wait_recv()
        swaps[2 * k + 1].wait_recv()
        left_t[:, :rows] = turn_over(left[:, :half])
        left_t[:, rows:] = turn_over(left_half[...])
        weight_products(left_t, right, theirs, partials[k])

    def pump(*steps):
        for n, stage in steps:
            scatter.step(n, stage)

    attend_back_start(q, grad, out_t, heads, grads, delta, acc)

    def block_back(r):
        block = bit_apart(r)
        place = pl.ds(pl.multiple_of(r * rows, rows), rows)

        @pl.when(block <= me)
        def _():
            attend_back_block(
                info, block, kv[place, :TILE], kv[place, TILE:], lse, dkv.at[r], heads, grads,
                delta, acc,
            )

        @pl.when(block > me)
        def _():
            dkv[r] = jnp.zeros(dkv.shape[1:], dkv.dtype)

    def several(first, gap, count):
        def body(j, carry):
            block_back(first + j * gap)
            return carry

        lax.fori_loop(0, count, body, 0)

    def add(target, source):
        target[...] = (target[...].astype(jnp.float32) + source[...].astype(jnp.float32)).astype(
            jnp.bfloat16
        )

    several(1, 2, 4)
    over_x = [
        remote(dkv.at[2 * k + 1], from_x.at[k], send.at[k], recv.at[k], others["x"])
        for k in range(4)
    ]
    for copy in over_x:
        copy.start()
    scan.step(1)
    weights(0, grad_rows, half_grad, hidden, their_hidden)
    pump((0, 0))
    several(4, 2, 2)
    over_far = [
        remote(dkv.at[4 + 2 * k], from_far.at[k], send.at[4 + k], recv.at[4 + k], others["far"])
        for k in range(2)
    ]
    for k in range(2):
        over_x[2 + k].wait_recv()
        add(dkv.at[4 + 2 * k], from_x.at[2 + k])
        over_far[k].start()
    scan.step(2)
    weights(1, normed_two, half_two, d_gu, their_gu)
    pump((1, 0), (0, 1))
    several(0, 2, 2)
    for k in range(2):
        over_x[k].wait_recv()
        add(dkv.at[2 * k], from_x.at[k])
    over_far[1].wait_recv()
    add(dkv.at[2], from_far.at[1])
    over_near = remote(dkv.at[2], from_near, send.at[6], recv.at[6], others["near"])
    over_near.start()
    pump((2, 0), (1, 1), (0, 2))
    ssm_back_kernel(
        info, x, bc, dt, cum, d_ssm, head_params, dx, d_bc, d_cum, d_dt, g_skip, cols_t, d_rows
    )
    scan.step(3)
    weights(2, d_mixer, half_mixer, joined, their_joined)
    pump((3, 0), (2, 1), (1, 2), (0, 3))
    d_step = d_conv.at[:, pl.ds(xbc, TILE)]
    step_in = raw.at[pl.ds(RIM, rows), pl.ds(xbc, TILE)]
    state_back_kernel(
        info, x, bc, dt, cum, d_ssm, head_params, step_in, state_in, d_state, dx, d_bc, d_cum,
        d_dt, dx, d_bc, d_step, head_sums,
    )
    conv_back_start(info, dx, d_bc, pre, raw, d_pre, g_conv)
    rim = remote(
        d_pre.at[pl.ds(0, RIM)], d_pre.at[pl.ds(rows, RIM)], rim_send.at[0], rim_recv.at[0],
        previous,
    )
    rim.start()
    weights(3, normed, their_normed, d_z, their_z)
    pump((4, 0), (3, 1), (2, 2), (1, 3), (0, 4))
    over_far[0].wait_recv()
    over_near.wait_recv()
    attend_back_write(acc, dq)
    d_pair[...] = (
        dkv[0].astype(jnp.float32)
        + from_far[0].astype(jnp.float32)
        + from_near[...].astype(jnp.float32)
    )
    rope_back_kernel(dq, d_pair, cosine, sine, d_attn)
    rim.wait_recv()
    conv_back_end(info, d_pre, conv_w, d_conv.at[:, pl.ds(0, xbc)])
    pump((4, 1), (3, 2), (2, 3), (1, 4))
    pump((4, 2), (3, 3), (2, 4))
    pump((4, 3), (3, 4))
    pump((4, 4))
    scatter.finish()
    scan.finish()
    rim.wait_send()
    for copy in over_x + over_far + [over_near] + swaps:
        copy.wait_send()


def back(info, *args):
    (
        head_params, conv_w, cosine, sine, q, kv, grad, out_t, lse, pull, x, bc, dt, cum,
        d_ssm, raw, state_in, pre, normed, normed_two, d_mixer, grad_rows, hidden, joined, d_gu,
        d_z,
    ) = args
    rows, query_width = q.shape
    width = normed.shape[1]
    half = width // 2
    pair = kv.shape[1]
    ssm_width, xbc = x.shape[1], pre.shape[1]
    f32, narrow = jnp.float32, jnp.bfloat16
    dma = pltpu.SemaphoreType.DMA
    widths = [hidden.shape[1], d_gu.shape[1], joined.shape[1], d_z.shape[1]]
    pairs = column_chunks(widths)
    own = half // 16
    outs = [
        shape_of((rows, xbc + TILE), narrow),
        shape_of((rows, query_width + pair), narrow),
        shape_of((8, xbc), f32),
        shape_of((8, TILE), f32),
        shape_of((8, TILE), f32),
        shape_of((rows, half), narrow),
    ] + [shape_of((own, w), f32) for w in widths]
    scratch = [pltpu.VMEM((half, w), narrow) for w in widths]
    scratch += scatter_scratch(widths, half)
    scratch += [pltpu.VMEM((rows, half), narrow)] * 3
    scratch += [pltpu.VMEM(a.shape, narrow) for a in (hidden, joined, d_gu, d_z)]
    scratch += [
        pltpu.VMEM((half, 2 * rows), narrow),
        pltpu.VMEM((QUERY_HEADS, rows, TILE), narrow),
        pltpu.VMEM((QUERY_HEADS, rows, TILE), narrow),
        pltpu.VMEM((QUERY_HEADS, rows), f32),
        pltpu.VMEM((QUERY_HEADS, HEAD_SIZE, rows), f32),
        pltpu.VMEM((8, rows, pair), narrow),
        pltpu.VMEM((4, rows, pair), narrow),
        pltpu.VMEM((2, rows, pair), narrow),
        pltpu.VMEM((rows, pair), narrow),
        pltpu.VMEM((rows, query_width), f32),
        pltpu.VMEM((rows, pair), f32),
        pltpu.VMEM((NS, ssm_width), narrow),
        pltpu.VMEM((rows, ssm_width), f32),
        pltpu.VMEM((rows, 2 * NS), f32),
        pltpu.VMEM((rows, TILE), f32),
        pltpu.VMEM((rows, TILE), f32),
        pltpu.VMEM((TILE, rows), f32),
        pltpu.VMEM((TILE, rows), f32),
        pltpu.VMEM((rows + RIM, xbc), f32),
        *scan_scratch(ssm_width),
        dma((7,)),
        dma((7,)),
        dma((8,)),
        dma((8,)),
        dma((2 * len(pairs), 4, 2)),
        dma((2 * len(pairs), 4, 2)),
        dma((1,)),
        dma((1,)),
    ]
    return comm_call(
        lambda *refs: back_kernel(pairs, *refs),
        outs,
        [INTO_VMEM] * len(outs),
        (info, *args),
        [pl.BlockSpec(memory_space=pltpu.SMEM)] + [INTO_VMEM] * len(args),
        scratch,
        2,
        200_000_000,
        limit=62,
    )


def dot_nt_two(left, right):
    high = left.astype(jnp.bfloat16)
    low = (left - high.astype(jnp.float32)).astype(jnp.bfloat16)
    return dot_nt(high, right) + dot_nt(low, right)


def last_kernel(pairs, *refs):
    (
        d_conv, d_attn, d_z, full_conv, full_mix, normed, their_normed, x_own, d_middle, gains,
        order, g_mlp, small,
    ) = refs[:13]
    input_grad, out_conv, out_attn, small_out = refs[13:17]
    refs = refs[17:]
    partials, arrived_w = refs[:2], refs[2:10]
    (
        their_conv, their_attn, left_t, d_normed, small_own, small_in, small_mid, swap_send,
        swap_recv, w_send, w_recv, small_send, small_recv,
    ) = refs[10:]
    others = partners()
    greet(list(others.values()))
    rows, width = normed.shape
    half = width // 2
    swaps = [
        remote(give, take, swap_send.at[k], swap_recv.at[k], others["core"])
        for k, (give, take) in enumerate(((d_conv, their_conv), (d_attn, their_attn)))
    ]
    for copy in swaps:
        copy.start()
    scatter = Scatter(partials, (out_conv, out_attn), arrived_w, pairs, w_send, w_recv, others)
    left_t[:, :rows] = turn_over(normed[:, :half])
    left_t[:, rows:] = turn_over(their_normed[...])
    swaps[0].wait_recv()
    weight_products(left_t, d_conv, their_conv, partials[0])
    scatter.step(0, 0)
    swaps[1].wait_recv()
    weight_products(left_t, d_attn, their_attn, partials[1])
    scatter.step(1, 0)
    step = 256
    attn = d_attn.shape[1]

    def back_out(j, carry):
        here = pl.ds(pl.multiple_of(j * step, step), step)
        d_normed[:, here] = (
            dot_nt(d_conv[...], full_conv[here])
            + dot_nt(d_attn[...], full_mix[here, :attn])
            + dot_nt(d_z[...], full_mix[here, attn:])
        )
        return carry

    lax.fori_loop(0, width // step, back_out, 0)
    scatter.step(0, 1)
    wide = x_own[...].astype(jnp.float32)
    r = lax.rsqrt(jnp.mean(wide * wide, axis=-1, keepdims=True) + NORM_EPS)
    grads = d_normed[...]
    g_norm = jnp.sum(grads * wide * r, axis=0, keepdims=True)
    line = lax.broadcasted_iota(jnp.int32, (8, width), 0)
    both = jnp.where(line == 0, g_norm, jnp.where(line == 1, g_mlp[...], 0.0))
    both = dot_nt_two(both, order[...])
    small_own[16:] = small[...]
    for k in range(width // TILE):
        for which in range(2):
            small_own[8 * which + k : 8 * which + k + 1] = both[
                which : which + 1, k * TILE : (k + 1) * TILE
            ]
    names = ("core", "y", "x", "near", "far")
    small_copies = []

    def small_step(k):
        if k > 0:
            small_copies[k - 1].wait_recv()
            was = small_own if k == 1 else small_mid.at[k - 2]
            now = small_out if k == 5 else small_mid.at[k - 1]
            now[...] = was[...] + small_in[k - 1]
        if k < 5:
            source = small_own if k == 0 else small_mid.at[k - 1]
            copy = remote(
                source, small_in.at[k], small_send.at[k], small_recv.at[k], others[names[k]]
            )
            copy.start()
            small_copies.append(copy)

    small_step(0)
    scatter.step(1, 1)
    inner = grads * gains[0:1]
    coeff = jnp.mean(inner * wide, axis=-1, keepdims=True)
    d_normed[...] = d_middle[...] + r * (inner - wide * (r * r * coeff))
    small_step(1)
    scatter.step(0, 2)

    def plain(j, carry):
        here = pl.ds(pl.multiple_of(j * step, step), step)
        input_grad[:, here] = dot_nt_two(d_normed[...], order[here])
        return carry

    lax.fori_loop(0, width // step, plain, 0)
    small_step(2)
    scatter.step(1, 2)
    scatter.step(0, 3)
    small_step(3)
    scatter.step(1, 3)
    scatter.step(0, 4)
    small_step(4)
    scatter.step(1, 4)
    small_step(5)
    scatter.finish()
    for copy in swaps + small_copies:
        copy.wait_send()


def last(d_conv, d_attn, d_z, full_conv, full_mix, normed, their_normed, x_own, d_middle, gains, order, g_mlp, small):
    args = (
        d_conv, d_attn, d_z, full_conv, full_mix, normed, their_normed, x_own, d_middle, gains,
        order, g_mlp, small,
    )
    rows, width = normed.shape
    half = width // 2
    f32, narrow = jnp.float32, jnp.bfloat16
    dma = pltpu.SemaphoreType.DMA
    widths = [d_conv.shape[1], d_attn.shape[1]]
    pairs = column_chunks(widths)
    total = (small.shape[0] + 16, TILE)
    outs = [shape_of((rows, width), f32)]
    outs += [shape_of((half // 16, w), f32) for w in widths]
    outs.append(shape_of(total, f32))
    scratch = [pltpu.VMEM((half, w), narrow) for w in widths]
    scratch += scatter_scratch(widths, half)
    scratch += [
        pltpu.VMEM(d_conv.shape, narrow),
        pltpu.VMEM(d_attn.shape, narrow),
        pltpu.VMEM((half, 2 * rows), narrow),
        pltpu.VMEM((rows, width), f32),
        pltpu.VMEM(total, f32),
        pltpu.VMEM((5, *total), f32),
        pltpu.VMEM((4, *total), f32),
        dma((2,)),
        dma((2,)),
        dma((2 * len(pairs), 4, 2)),
        dma((2 * len(pairs), 4, 2)),
        dma((5,)),
        dma((5,)),
    ]
    return comm_call(
        lambda *refs: last_kernel(pairs, *refs),
        outs,
        [INTO_VMEM] * len(outs),
        args,
        [INTO_VMEM] * len(args),
        scratch,
        4,
        100_000_000,
    )


def pair_heads(value, back=False):
    rows = value.shape[0]
    group = QUERY_HEADS // KEY_VALUE_HEADS
    width = QUERY_HEADS * HEAD_SIZE
    shape = (group, KEY_VALUE_HEADS) if back else (KEY_VALUE_HEADS, group)
    moved = value[:, :width].reshape(rows, *shape, HEAD_SIZE).transpose(0, 2, 1, 3)
    return jnp.concatenate([moved.reshape(rows, width), value[:, width:]], axis=1)


def on_device(
    layer_input,
    seq_lengths,
    w_attn,
    w_ssm_in,
    w_dt,
    w_out,
    w_gate_up,
    w_down,
    norm_gain,
    mlp_gain,
    ssm_gain,
    conv_w,
    conv_b,
    a_log,
    dt_bias,
    d_skip,
    out_grad,
):
    token_rows = layer_input.shape[1]
    query_width = QUERY_HEADS * HEAD_SIZE
    key_value_width = KEY_VALUE_HEADS * HEAD_SIZE
    attn_width = query_width + 2 * key_value_width
    ssm_width = MH * MP
    xbc_width = ssm_width + 2 * NS
    width = layer_input.shape[2]
    fast = is_fast(width)
    seq_lens = seq_lengths[0]
    first_pos = lax.axis_index("seq") * token_rows
    positions = first_pos + jnp.arange(token_rows, dtype=jnp.int32)
    segment, device_places = segments(seq_lens, positions)
    ends = jnp.cumsum(seq_lens)
    info = jnp.stack([first_pos, ends[0], ends[1], ends[2]]).astype(jnp.int32)
    half = HEAD_SIZE // 2
    freqs = ROPE_BASE ** (-jnp.arange(half, dtype=jnp.float32) / half)
    angles = device_places.astype(jnp.float32)[:, None] * jnp.tile(freqs, TILE // half)[None, :]
    cosine, sine = jnp.cos(angles), jnp.sin(angles)
    head_params = jnp.pad(
        jnp.stack([dt_bias, jnp.exp(a_log), d_skip]), ((0, 5), (0, TILE - MH))
    )
    step_pad = jnp.pad(w_dt, ((0, 0), (0, TILE - MH)))
    shards = (
        jnp.concatenate([w_ssm_in[:, ssm_width:], step_pad], axis=1),
        jnp.concatenate([pair_heads(w_attn), w_ssm_in[:, :ssm_width]], axis=1),
        pair_heads(w_out.T),
        w_gate_up,
        w_down.T,
    )
    gains = jnp.pad(jnp.stack([norm_gain, mlp_gain]), ((0, 6), (0, 0)))
    if fast:
        full, made = front(
            info,
            layer_input[0],
            out_grad[0],
            gains,
            cosine,
            sine,
            head_params,
            jnp.pad(conv_w, ((0, 4), (0, 0))),
            conv_b[None],
            shards,
        )
        (
            x_narrow, grad_rows, gains, normed, queries, all_pairs, gate_z, raw_rows, pre_conv,
            inputs_x, inputs_bc, ssm_own, state_own, steps_dt, running_decay,
            attended, attended_t, log_total, state_in, order,
        ) = made
        full_conv, full_mix, full_out, full_gu, full_down = full
        norm_gain, mlp_gain = gains[0], gains[1]
        x_rows = x_narrow.astype(jnp.float32)
        scale_one = rms_scale(x_rows)
    else:
        order = None
        ext_pos = first_pos - (CONV - 1) + jnp.arange(token_rows + CONV - 1, dtype=jnp.int32)
        ext_segment = segments(seq_lens, ext_pos)[0]

        def conv_local(ext_rows, conv_weight, conv_bias):
            return conv_mix(ext_rows, ext_segment, conv_weight, conv_bias)

        full = [lax.all_gather(p, ("seq", "batch"), axis=0, tiled=True) for p in shards]
        full_conv, full_mix, full_out, full_gu, full_down = full
        x_rows = layer_input[0].astype(jnp.float32)
        grad_rows = out_grad[0]
        scale_one = rms_scale(x_rows)
        normed = (x_rows * scale_one * norm_gain).astype(jnp.bfloat16)
        conv_proj = jnp.dot(normed, full_conv, preferred_element_type=jnp.float32)
        mix_proj = jnp.dot(normed, full_mix, preferred_element_type=jnp.float32)
        queries, own_pairs = big_call(
            rope_kernel,
            (
                shape_of((token_rows, query_width), jnp.bfloat16),
                shape_of((token_rows, 2 * key_value_width), jnp.bfloat16),
            ),
            mix_proj[:, :attn_width],
            cosine,
            sine,
        )
        gate_z = mix_proj[:, attn_width:]
        raw_xbc = conv_proj[:, :xbc_width]
        step_proj = conv_proj[:, xbc_width:]
        rim_rows = shifted(raw_xbc[token_rows - (CONV - 1) :], "seq", 1)
        extended = jnp.concatenate([rim_rows, raw_xbc], axis=0)
        conv_out, conv_pullback = jax.vjp(conv_local, extended, conv_w, conv_b)
        conv_narrow = conv_out.astype(jnp.bfloat16)
        inputs_x, inputs_bc = conv_narrow[:, :ssm_width], conv_narrow[:, ssm_width:]
        ssm_own, state_own, steps_dt, running_decay = ssm_forward(
            info, inputs_x, inputs_bc, step_proj, head_params
        )
        all_pairs = lax.all_gather(own_pairs, "seq", axis=0, tiled=True)
        state_in = scan_states(state_own, True)
        attended, attended_t, log_total = attn_forward(info, queries, all_pairs)

    def to_plain(value):
        if not fast:
            return value
        return jnp.einsum("tc,dc->td", value, order, preferred_element_type=jnp.float32)

    ssm_flat, ssm_normed, scale_gated = ssm_finish(
        info, ssm_own, inputs_bc, running_decay, state_in, gate_z, ssm_gain[None]
    )
    joined = jnp.concatenate([attended, ssm_normed], axis=1)

    def into_width(left, weight):
        return jnp.einsum("tc,dc->td", left, weight, preferred_element_type=jnp.float32)

    def out_of_width(left, weight):
        return jnp.dot(left, weight, preferred_element_type=jnp.float32)

    middle = x_rows + into_width(joined, full_out)
    scale_two = rms_scale(middle)
    normed_two = (middle * scale_two * mlp_gain).astype(jnp.bfloat16)
    gate_up = out_of_width(normed_two, full_gu)
    gate_part, up_part = gate_up[:, :FF], gate_up[:, FF:]
    sig_gate = jax.nn.sigmoid(gate_part)
    hidden = (gate_part * sig_gate * up_part).astype(jnp.bfloat16)
    layer_out = middle + into_width(hidden, full_down)
    d_hidden = out_of_width(grad_rows, full_down)
    d_gate = d_hidden * up_part * (sig_gate * (1.0 + gate_part * (1.0 - sig_gate)))
    d_up = d_hidden * gate_part * sig_gate
    d_gate_up = jnp.concatenate([d_gate, d_up], axis=1).astype(jnp.bfloat16)
    d_normed_two = into_width(d_gate_up, full_gu)
    d_middle_norm, g_mlp_gain = norm_back(middle, scale_two, mlp_gain, d_normed_two)
    d_middle = grad_rows.astype(jnp.float32) + d_middle_norm
    d_mixer = d_middle.astype(jnp.bfloat16)
    d_joined = out_of_width(d_mixer, full_out)
    attended_gradient = d_joined[:, :query_width].astype(jnp.bfloat16)
    d_ssm_out, d_gate_z, pull, g_ssm_gain = gate_back(
        info,
        d_joined[:, query_width:],
        ssm_flat,
        gate_z,
        scale_gated,
        ssm_gain[None],
        running_decay,
        inputs_bc,
    )
    pull = jnp.concatenate([pull, state_own[NS:]], axis=0)
    if fast:
        (
            d_conv_proj, d_attn_proj, g_conv, head_sums, g_skip_rows, their_normed,
            sum_down, sum_gu, sum_out, sum_z,
        ) = back(
            info,
            head_params,
            jnp.pad(conv_w, ((0, 4), (0, 0))),
            cosine,
            sine,
            queries,
            all_pairs,
            attended_gradient,
            attended_t,
            log_total,
            pull,
            inputs_x,
            inputs_bc,
            steps_dt,
            running_decay,
            d_ssm_out,
            raw_rows,
            state_in,
            pre_conv,
            normed,
            normed_two,
            d_mixer,
            grad_rows,
            hidden,
            joined,
            d_gate_up,
            d_gate_z,
        )
        small = (
            g_ssm_gain[0],
            g_conv[:CONV],
            g_conv[CONV],
            head_sums[0, :MH],
            head_sums[1, :MH],
            g_skip_rows[0, :MH],
        )
        input_grad, sum_conv, sum_attn, totals = last(
            d_conv_proj,
            d_attn_proj,
            d_gate_z,
            full_conv,
            full_mix,
            normed,
            their_normed,
            x_narrow,
            d_middle,
            gains,
            order,
            g_mlp_gain[None],
            pack_small(small),
        )
        small_sums = [totals[:8].reshape(-1), totals[8:16].reshape(-1)]
        small_sums += unpack_small(totals[16:], small)
    else:
        d_state = scan_states(pull, False)
        d_queries, d_pairs = attn_backward(
            info, queries, all_pairs, attended_gradient, attended_t, log_total
        )
        own_d_pairs = lax.psum_scatter(
            d_pairs.astype(jnp.float32), "seq", scatter_dimension=0, tiled=True
        )
        dx_part, d_bc_part, d_cum_part, d_dt_part, g_skip_rows = ssm_back(
            info, inputs_x, inputs_bc, steps_dt, running_decay, d_ssm_out, head_params
        )
        g_inputs_x, g_inputs_bc, d_step_pad, head_sums = state_back(
            info,
            inputs_x,
            inputs_bc,
            steps_dt,
            running_decay,
            d_ssm_out,
            head_params,
            step_proj,
            state_in,
            d_state,
            dx_part,
            d_bc_part,
            d_cum_part,
            d_dt_part,
        )
        g_extended, g_conv_w, g_conv_b = conv_pullback(
            jnp.concatenate([g_inputs_x, g_inputs_bc], axis=1)
        )
        back_rim = shifted(g_extended[: CONV - 1], "seq", -1)
        d_raw = g_extended[CONV - 1 :] + jnp.concatenate(
            [jnp.zeros((token_rows - (CONV - 1), xbc_width), jnp.float32), back_rim], axis=0
        )
        d_conv_proj = jnp.concatenate([d_raw.astype(jnp.bfloat16), d_step_pad], axis=1)
        (d_attn_proj,) = big_call(
            rope_back_kernel,
            (shape_of((token_rows, attn_width), jnp.bfloat16),),
            d_queries,
            own_d_pairs,
            cosine,
            sine,
        )
        d_mix_proj = jnp.concatenate([d_attn_proj, d_gate_z], axis=1)
        d_normed = into_width(d_conv_proj, full_conv) + into_width(d_mix_proj, full_mix)
        d_input_norm, g_norm_gain = norm_back(x_rows, scale_one, norm_gain, d_normed)
        input_grad = d_middle + d_input_norm
        axes = ("seq", "batch")

        def summed(left, right):
            grad = jnp.einsum("td,tc->dc", left, right, preferred_element_type=jnp.float32)
            return lax.psum_scatter(grad, axes, scatter_dimension=0, tiled=True)

        sum_down, sum_gu = summed(grad_rows, hidden), summed(normed_two, d_gate_up)
        sum_out, sum_conv = summed(d_mixer, joined), summed(normed, d_conv_proj)
        sum_mix = summed(normed, d_mix_proj)
        sum_attn, sum_z = sum_mix[:, :attn_width], sum_mix[:, attn_width:]
        small = (
            g_norm_gain,
            g_mlp_gain,
            g_ssm_gain[0],
            g_conv_w,
            g_conv_b,
            head_sums[0, :MH],
            head_sums[1, :MH],
            g_skip_rows[0, :MH],
        )
        small_sums = unpack_small(lax.psum(pack_small(small), axes), small)
    grad_attn = pair_heads(sum_attn, True)
    grad_ssm_in = jnp.concatenate([sum_z, sum_conv[:, :xbc_width]], axis=1)
    grad_dt = sum_conv[:, xbc_width : xbc_width + MH]
    grad_out = pair_heads(sum_out, True).T
    grad_gate_up = sum_gu
    grad_down = sum_down.T
    return (
        to_plain(layer_out.astype(jnp.bfloat16)).astype(jnp.bfloat16)[None],
        input_grad[None],
        grad_attn,
        grad_ssm_in,
        grad_dt,
        grad_out,
        grad_gate_up,
        grad_down,
        *small_sums,
    )


def solution(mesh):
    return jax.shard_map(
        on_device,
        mesh=mesh,
        in_specs=(
            P("batch", "seq", None),
            P("batch", None),
            P(("seq", "batch"), None),
            P(("seq", "batch"), None),
            P(("seq", "batch"), None),
            P(None, ("seq", "batch")),
            P(("seq", "batch"), None),
            P(None, ("seq", "batch")),
            P(),
            P(),
            P(),
            P(),
            P(),
            P(),
            P(),
            P(),
            P("batch", "seq", None),
        ),
        out_specs=(
            P("batch", "seq", None),
            P("batch", "seq", None),
            P(("seq", "batch"), None),
            P(("seq", "batch"), None),
            P(("seq", "batch"), None),
            P(None, ("seq", "batch")),
            P(("seq", "batch"), None),
            P(None, ("seq", "batch")),
            P(),
            P(),
            P(),
            P(),
            P(),
            P(),
            P(),
            P(),
        ),
        check_vma=False,
    )
```

```python
import jax
import jax.numpy as jnp
import numpy as np
from jax import lax
from jax.experimental import pallas as pl
from jax.experimental.pallas import tpu as pltpu
from jax.sharding import PartitionSpec as P

QUERY_HEADS = 8
KEY_VALUE_HEADS = 2
HEAD_SIZE = 64
MH = 24
MP = 64
NS = 128
FF = 2048
CONV = 4
SPAN = 128


HIGHEST = lax.Precision.HIGHEST
NEGATIVE_FILL = -1e30
ROPE_BASE = 10000.0
NORM_EPS = 1e-06


def shifted(block, axis, distance):
    devices = range(lax.axis_size(axis))
    route = [(i - distance, i) for i in devices if i - distance in devices]
    return lax.ppermute(block, axis, route)


def is_fast(width):
    return lax.axis_size("seq") == 8 and lax.axis_size("batch") == 4 and width % (32 * 32) == 0


def pack_small(arrays):
    flat = jnp.concatenate([a.reshape(-1) for a in arrays])
    return jnp.pad(flat, (0, -flat.shape[0] % 1024)).reshape(-1, 128)


def unpack_small(flat, arrays):
    flat = flat.reshape(-1)
    out, start = [], 0
    for a in arrays:
        out.append(flat[start : start + a.size].reshape(a.shape))
        start += a.size
    return out


def rms_scale(value_rows):
    return lax.rsqrt(jnp.mean(value_rows * value_rows, axis=-1, keepdims=True) + NORM_EPS)


def norm_back(value_rows, scales, gains, grads):
    gain_grad = jnp.sum(grads * value_rows * scales, axis=0)
    inner = grads * gains
    coeff = jnp.mean(inner * value_rows, axis=-1, keepdims=True)
    return (scales * (inner - value_rows * scales * scales * coeff), gain_grad)


def segments(lengths, positions):
    ends = jnp.cumsum(lengths)
    passed = ends[None, :] <= positions[:, None]
    segment = jnp.sum(passed.astype(jnp.int32), axis=1)
    device_places = positions - jnp.sum(jnp.where(passed, lengths[None, :], 0), axis=1)
    return (segment, device_places)


def conv_mix(extended, ext_segment, conv_weight, conv_bias):
    row_count = extended.shape[0] - (CONV - 1)
    summed = conv_bias[None, :]
    for lagged in range(CONV):
        same_seq = (ext_segment[lagged : lagged + row_count] == ext_segment[CONV - 1 :]).astype(
            extended.dtype
        )
        summed = (
            summed
            + conv_weight[lagged][None, :]
            * extended[lagged : lagged + row_count]
            * same_seq[:, None]
        )
    return jax.nn.silu(summed)


TILE = 128
PAIRS = QUERY_HEADS // 2
CHUNK = 256


def dot(left, right):
    return jnp.dot(left, right, preferred_element_type=jnp.float32)


def dot_nt(left, right):
    return lax.dot_general(
        left, right, (((1,), (1,)), ((), ())), preferred_element_type=jnp.float32
    )


def dot_tn(left, right):
    return lax.dot_general(
        left, right, (((0,), (0,)), ((), ())), preferred_element_type=jnp.float32
    )


def exact(left, right):
    return jnp.dot(left, right, precision=HIGHEST, preferred_element_type=jnp.float32)


def two_part(left, right):
    high = left.astype(jnp.bfloat16)
    low = (left - high.astype(jnp.float32)).astype(jnp.bfloat16)
    return dot(high, right) + dot(low, right)


def seg_start(where_at, info):
    start = jnp.zeros_like(where_at)
    for k in range(1, 4):
        start = jnp.where(where_at >= info[k], jnp.maximum(start, info[k]), start)
    return start


def big_call(kernel, outs, *args, scratch=(), flops=0, smem=0, limit=48):
    specs = [pl.BlockSpec(memory_space=pltpu.SMEM)] * smem
    specs += [pl.BlockSpec(memory_space=pltpu.VMEM)] * (len(args) - smem)
    moved = sum(a.size * a.dtype.itemsize for a in args)
    moved += sum(o.size * o.dtype.itemsize for o in outs)
    return pl.pallas_call(
        kernel,
        out_shape=list(outs),
        in_specs=specs,
        out_specs=[pl.BlockSpec(memory_space=pltpu.VMEM)] * len(outs),
        scratch_shapes=list(scratch),
        cost_estimate=pl.CostEstimate(flops=flops, bytes_accessed=moved, transcendentals=0),
        compiler_params=pltpu.CompilerParams(vmem_limit_bytes=limit * 1024 * 1024),
    )(*args)


def shape_of(shape, dtype):
    return jax.ShapeDtypeStruct(shape, dtype)


def turn(value, cosine, sine):
    lane = lax.broadcasted_iota(jnp.int32, value.shape, 1) % HEAD_SIZE
    mixed = jnp.where(
        lane < HEAD_SIZE // 2,
        -pltpu.roll(value, TILE - HEAD_SIZE // 2, 1),
        pltpu.roll(value, HEAD_SIZE // 2, 1),
    )
    return value * cosine + mixed * sine


def rope_kernel(proj, cosine, sine, q_out, kv_out):
    cos, sin = cosine[...], sine[...]
    for i in range(PAIRS):
        cols = pl.ds(i * TILE, TILE)
        turned = turn(proj[:, cols], cos, sin).astype(jnp.bfloat16)
        q_out[:, cols] = (turned.astype(jnp.float32) * HEAD_SIZE**-0.5).astype(jnp.bfloat16)
    base = PAIRS * TILE
    kv_out[:, :TILE] = turn(proj[:, base : base + TILE], cos, sin).astype(jnp.bfloat16)
    kv_out[:, TILE:] = proj[:, base + TILE : base + 2 * TILE].astype(jnp.bfloat16)


def halves_of(value):
    lane = lax.broadcasted_iota(jnp.int32, value.shape, 1)
    wide = value.astype(jnp.float32)
    first = jnp.where(lane < HEAD_SIZE, wide, 0.0).astype(value.dtype)
    return first, jnp.where(lane < HEAD_SIZE, 0.0, wide).astype(value.dtype)


def block_range(info):
    first = info[0]
    low = seg_start(first, info) // CHUNK
    return low, first // CHUNK - low + 1


def attn_mask(info, block):
    rows = lax.broadcasted_iota(jnp.int32, (CHUNK, CHUNK), 0) + block * CHUNK
    at = lax.broadcasted_iota(jnp.int32, (1, CHUNK), 1) + info[0]
    return (rows <= at) & (rows >= seg_start(at, info))


def attend_start(q, heads, acc, top, total):
    for i in range(PAIRS):
        heads[2 * i], heads[2 * i + 1] = halves_of(q[:, i * TILE : (i + 1) * TILE])
    acc[...] = jnp.zeros_like(acc)
    total[...] = jnp.zeros_like(total)
    top[...] = jnp.full(top.shape, NEGATIVE_FILL, jnp.float32)


def attend_block(info, block, keys, values_t, heads, acc, top, total):
    allowed = attn_mask(info, block)
    for h in range(QUERY_HEADS):
        scores = jnp.where(allowed, dot_nt(keys, heads[h]), NEGATIVE_FILL)
        old = top[h : h + 1]
        new = jnp.maximum(old, jnp.max(scores, axis=0, keepdims=True))
        probs = jnp.where(allowed, jnp.exp(scores - new), 0.0)
        shrink = jnp.exp(old - new)
        top[h : h + 1] = new
        total[h : h + 1] = total[h : h + 1] * shrink + jnp.sum(probs, axis=0, keepdims=True)
        side = (h % 2) * HEAD_SIZE
        acc[h] = acc[h] * shrink + dot(
            values_t[side : side + HEAD_SIZE], probs.astype(jnp.bfloat16)
        )


def attend_write(acc, total, out, out_t):
    for i in range(PAIRS):
        pair = jnp.concatenate(
            [acc[2 * i] / total[2 * i : 2 * i + 1], acc[2 * i + 1] / total[2 * i + 1 : 2 * i + 2]],
            axis=0,
        )
        out_t[i * TILE : (i + 1) * TILE] = pair
        out[:, i * TILE : (i + 1) * TILE] = pair.T.astype(jnp.bfloat16)


def attn_forward_kernel(info, q, kv, out, out_t, lse, heads, acc, top, total):
    attend_start(q, heads, acc, top, total)
    low, count = block_range(info)

    def step(j, carry):
        block = low + j
        place = pl.ds(pl.multiple_of(block * CHUNK, CHUNK), CHUNK)
        keys = kv[place, :TILE]
        values_t = kv[place, TILE:].astype(jnp.float32).T.astype(jnp.bfloat16)
        attend_block(info, block, keys, values_t, heads, acc, top, total)
        return carry

    lax.fori_loop(0, count, step, 0)
    lse[...] = top[...] + jnp.log(total[...])
    attend_write(acc, total, out, out_t)


def attn_forward(info, q, kv):
    rows = q.shape[0]
    f32 = jnp.float32
    return big_call(
        attn_forward_kernel,
        (
            shape_of(q.shape, jnp.bfloat16),
            shape_of(q.shape[::-1], f32),
            shape_of((QUERY_HEADS, rows), f32),
        ),
        info,
        q,
        kv,
        smem=1,
        scratch=(
            pltpu.VMEM((QUERY_HEADS, rows, TILE), jnp.bfloat16),
            pltpu.VMEM((QUERY_HEADS, HEAD_SIZE, rows), f32),
            pltpu.VMEM((QUERY_HEADS, rows), f32),
            pltpu.VMEM((QUERY_HEADS, rows), f32),
        ),
        flops=4 * rows * kv.shape[0] * q.shape[1],
    )


def attend_back_start(q, grad, out_t, heads, grads, delta, acc):
    for i in range(PAIRS):
        cols = slice(i * TILE, (i + 1) * TILE)
        heads[2 * i], heads[2 * i + 1] = halves_of(q[:, cols])
        grads[2 * i], grads[2 * i + 1] = halves_of(grad[:, cols])
        both = grad[:, cols].astype(jnp.float32).T * out_t[cols]
        delta[2 * i : 2 * i + 1] = jnp.sum(both[:HEAD_SIZE], axis=0, keepdims=True)
        delta[2 * i + 1 : 2 * i + 2] = jnp.sum(both[HEAD_SIZE:], axis=0, keepdims=True)
    acc[...] = jnp.zeros_like(acc)


def attend_back_block(info, block, keys, values, lse, target, heads, grads, delta, acc):
    keys_t = keys.astype(jnp.float32).T.astype(jnp.bfloat16)
    allowed = attn_mask(info, block)
    d_keys = jnp.zeros((CHUNK, TILE), jnp.float32)
    d_values = jnp.zeros((CHUNK, TILE), jnp.float32)
    for h in range(QUERY_HEADS):
        scores = dot_nt(keys, heads[h])
        probs = jnp.where(allowed, jnp.exp(scores - lse[h : h + 1]), 0.0)
        d_probs = dot_nt(values, grads[h])
        d_scores = (probs * (d_probs - delta[h : h + 1])).astype(jnp.bfloat16)
        d_values = d_values + dot(probs.astype(jnp.bfloat16), grads[h])
        d_keys = d_keys + dot(d_scores, heads[h])
        side = (h % 2) * HEAD_SIZE
        acc[h] = acc[h] + dot(keys_t[side : side + HEAD_SIZE], d_scores)
    target[:, :TILE] = d_keys.astype(jnp.bfloat16)
    target[:, TILE:] = d_values.astype(jnp.bfloat16)


def attend_back_write(acc, dq):
    for i in range(PAIRS):
        pair = jnp.concatenate([acc[2 * i], acc[2 * i + 1]], axis=0)
        dq[:, i * TILE : (i + 1) * TILE] = pair.T * HEAD_SIZE**-0.5


def attn_backward_kernel(info, q, kv, grad, out_t, lse, dq, dkv, heads, grads, delta, acc):
    attend_back_start(q, grad, out_t, heads, grads, delta, acc)
    dkv[...] = jnp.zeros_like(dkv)
    low, count = block_range(info)

    def step(j, carry):
        block = low + j
        place = pl.ds(pl.multiple_of(block * CHUNK, CHUNK), CHUNK)
        attend_back_block(
            info, block, kv[place, :TILE], kv[place, TILE:], lse, dkv.at[place], heads, grads,
            delta, acc,
        )
        return carry

    lax.fori_loop(0, count, step, 0)
    attend_back_write(acc, dq)


def attn_backward(info, q, kv, grad, out_t, lse):
    rows = q.shape[0]
    f32 = jnp.float32
    return big_call(
        attn_backward_kernel,
        (shape_of(q.shape, f32), shape_of(kv.shape, jnp.bfloat16)),
        info,
        q,
        kv,
        grad,
        out_t,
        lse,
        smem=1,
        scratch=(
            pltpu.VMEM((QUERY_HEADS, rows, TILE), jnp.bfloat16),
            pltpu.VMEM((QUERY_HEADS, rows, TILE), jnp.bfloat16),
            pltpu.VMEM((QUERY_HEADS, rows), f32),
            pltpu.VMEM((QUERY_HEADS, HEAD_SIZE, rows), f32),
        ),
        flops=10 * rows * kv.shape[0] * q.shape[1],
    )


def rope_back_kernel(dq, dkv, cosine, sine, out):
    cos, sin = cosine[...], -sine[...]
    for i in range(PAIRS):
        cols = slice(i * TILE, (i + 1) * TILE)
        out[:, cols] = turn(dq[:, cols], cos, sin).astype(jnp.bfloat16)
    base = PAIRS * TILE
    out[:, base : base + TILE] = turn(dkv[:, :TILE], cos, sin).astype(jnp.bfloat16)
    out[:, base + TILE :] = dkv[:, TILE:].astype(jnp.bfloat16)


STATE_ROWS = NS + 16


def lane_pick(value, first):
    rows = value.shape[0]
    lane = lax.broadcasted_iota(jnp.int32, (rows, TILE), 1)
    return jnp.where(lane < MP, value[:, first : first + 1], value[:, first + 1 : first + 2])


def spread_heads(width):
    head = lax.broadcasted_iota(jnp.int32, (TILE, width), 0)
    col = lax.broadcasted_iota(jnp.int32, (TILE, width), 1)
    return jnp.where(head == col // MP, 1.0, 0.0).astype(jnp.bfloat16)


def gather_heads(width):
    head = lax.broadcasted_iota(jnp.int32, (width, TILE), 1)
    col = lax.broadcasted_iota(jnp.int32, (width, TILE), 0)
    return jnp.where(head == col // MP, 1.0, 0.0).astype(jnp.bfloat16)


def head_lanes(rows):
    return lax.broadcasted_iota(jnp.int32, (rows, TILE), 1) < MH


def chunk_places(info, rows):
    at = lax.broadcasted_iota(jnp.int32, (rows, 1), 0) + info[0]
    return seg_start(at, info) - info[0]


def ssm_states(info, x, bc, step_in, head_params, state, dt_out, cum_out, dt_t, cum_t):
    rows = x.shape[0]
    bias, rate = head_params[0:1], head_params[1:2]
    raw = step_in[...] + bias
    dt = jnp.maximum(raw, 0.0) + jnp.log1p(jnp.exp(-jnp.abs(raw)))
    dt = jnp.where(head_lanes(rows), dt, 0.0)
    row = lax.broadcasted_iota(jnp.int32, (rows, rows), 0)
    col = lax.broadcasted_iota(jnp.int32, (rows, rows), 1)
    lower = jnp.where(row >= col, 1.0, 0.0)
    cum = exact(lower, -dt * rate)
    dt_out[...] = dt
    cum_out[...] = cum
    dt_t[...] = dt.T
    cum_t[...] = cum.T
    last_start = seg_start(info[0] + rows - 1, info) - info[0]
    place = lax.broadcasted_iota(jnp.int32, (rows, 1), 0)
    end = cum[rows - 1 : rows]
    leave = jnp.where(place >= last_start, jnp.exp(jnp.minimum(end - cum, 0.0)) * dt, 0.0)
    b_t = bc[:, :NS].astype(jnp.float32).T.astype(jnp.bfloat16)
    through = jnp.where(last_start < 0, jnp.exp(end), 0.0)
    high = through.astype(jnp.bfloat16).astype(jnp.float32)
    line = lax.broadcasted_iota(jnp.int32, (16, TILE), 0)
    both = jnp.where(line == 0, high, jnp.where(line == 1, through - high, 0.0))
    spread = spread_heads(x.shape[1])
    state[NS:] = dot(both.astype(jnp.bfloat16), spread).astype(jnp.bfloat16)
    for i in range(MH // 2):
        cols = slice(i * TILE, (i + 1) * TILE)
        weighed = x[:, cols].astype(jnp.float32) * lane_pick(leave, 2 * i)
        state[:NS, cols] = dot(b_t, weighed.astype(jnp.bfloat16)).astype(jnp.bfloat16)


def ssm_local(info, x, bc, head_params, y, cum, dt_t, cum_t):
    rows = x.shape[0]
    row = lax.broadcasted_iota(jnp.int32, (rows, rows), 0)
    col = lax.broadcasted_iota(jnp.int32, (rows, rows), 1)
    starts = chunk_places(info, rows)
    products = dot_nt(bc[:, NS:], bc[:, :NS])
    skips = jnp.broadcast_to(head_params[2:3], (8, TILE))
    skip_row = two_part(skips, spread_heads(x.shape[1]))[:1]
    lane = lax.broadcasted_iota(jnp.int32, (SPAN, TILE), 1)
    for i in range(MH // 2):
        cols = slice(i * TILE, (i + 1) * TILE)
        tile = x[:, cols]
        for part in range(rows // SPAN):
            here = slice(part * SPAN, (part + 1) * SPAN)
            upto = (part + 1) * SPAN
            allowed = (row[here, :upto] >= col[here, :upto]) & (col[here, :upto] >= starts[here])
            sides = []
            for h in (2 * i, 2 * i + 1):
                spread_log = cum[here, h : h + 1] - cum_t[h : h + 1, :upto]
                decay = jnp.exp(jnp.where(allowed, spread_log, NEGATIVE_FILL))
                mixing = products[here, :upto] * decay * dt_t[h : h + 1, :upto]
                sides.append(dot(mixing.astype(jnp.bfloat16), tile[:upto]))
            own = skip_row[:, cols] * tile[here].astype(jnp.float32)
            y[here, cols] = jnp.where(lane < MP, sides[0], sides[1]) + own


def ssm_forward_kernel(info, x, bc, step_in, head_params, y, state, dt_out, cum_out, dt_t, cum_t):
    ssm_states(info, x, bc, step_in, head_params, state, dt_out, cum_out, dt_t, cum_t)
    ssm_local(info, x, bc, head_params, y, cum_out, dt_t, cum_t)


def ssm_forward(info, x, bc, step_in, head_params):
    rows, width = x.shape
    f32 = jnp.float32
    return big_call(
        ssm_forward_kernel,
        (
            shape_of((rows, width), f32),
            shape_of((STATE_ROWS, width), jnp.bfloat16),
            shape_of((rows, TILE), f32),
            shape_of((rows, TILE), f32),
        ),
        info,
        x,
        bc,
        step_in,
        head_params,
        smem=1,
        scratch=(pltpu.VMEM((TILE, rows), f32), pltpu.VMEM((TILE, rows), f32)),
        flops=4 * rows * rows * width,
    )


def entering_of(info, cum):
    rows = cum.shape[0]
    return jnp.where(chunk_places(info, rows) < 0, jnp.exp(jnp.minimum(cum, 0.0)), 0.0)


def ssm_finish_kernel(info, y, bc, cum, state_in, z, gain, ssm_out, normed, scale):
    rows = y.shape[0]
    enter = entering_of(info, cum[...])
    narrow_c = bc[:, NS:]
    squares = jnp.zeros((rows, TILE), jnp.float32)
    tiles = MH // 2
    for i in range(tiles):
        cols = slice(i * TILE, (i + 1) * TILE)
        out = y[:, cols] + lane_pick(enter, 2 * i) * dot(narrow_c, state_in[:, cols])
        ssm_out[:, cols] = out
        gate = z[:, cols]
        gated = out * (gate * jax.nn.sigmoid(gate))
        squares = squares + gated * gated
    mean = jnp.sum(squares, axis=1, keepdims=True) * (1.0 / (tiles * TILE))
    r = lax.rsqrt(mean + NORM_EPS)
    scale[...] = jnp.broadcast_to(r, scale.shape)
    for i in range(tiles):
        cols = slice(i * TILE, (i + 1) * TILE)
        gate = z[:, cols]
        gated = ssm_out[:, cols] * (gate * jax.nn.sigmoid(gate))
        normed[:, cols] = (gated * r * gain[i : i + 1]).astype(jnp.bfloat16)


def ssm_finish(info, y, bc, cum, state_in, z, gain):
    rows, width = y.shape
    return big_call(
        ssm_finish_kernel,
        (
            shape_of((rows, width), jnp.float32),
            shape_of((rows, width), jnp.bfloat16),
            shape_of((rows, TILE), jnp.float32),
        ),
        info,
        y,
        bc,
        cum,
        state_in,
        z,
        gain,
        smem=1,
        flops=2 * rows * NS * width,
    )


def gate_back_kernel(info, dy, ssm_out, z, scale, gain, cum, bc, d_out, d_z, pull, g_gain):
    rows = dy.shape[0]
    tiles = MH // 2
    r = scale[:, :1]
    enter = entering_of(info, cum[...])
    c_t = bc[:, NS:].astype(jnp.float32).T.astype(jnp.bfloat16)
    inner = jnp.zeros((rows, TILE), jnp.float32)
    for i in range(tiles):
        cols = slice(i * TILE, (i + 1) * TILE)
        gate = z[:, cols]
        gated = ssm_out[:, cols] * (gate * jax.nn.sigmoid(gate))
        product = dy[:, cols] * gated
        g_gain[i : i + 1] = jnp.sum(product * r, axis=0, keepdims=True)
        inner = inner + product * gain[i : i + 1]
    coeff = jnp.sum(inner, axis=1, keepdims=True) * (1.0 / (tiles * TILE))
    for i in range(tiles):
        cols = slice(i * TILE, (i + 1) * TILE)
        gate = z[:, cols]
        sig = jax.nn.sigmoid(gate)
        silu = gate * sig
        out = ssm_out[:, cols]
        d_gated = r * (dy[:, cols] * gain[i : i + 1] - out * silu * (r * r * coeff))
        d_ssm = d_gated * silu
        d_out[:, cols] = d_ssm
        d_z[:, cols] = (d_gated * out * (sig * (1.0 + gate * (1.0 - sig)))).astype(jnp.bfloat16)
        pull[:, cols] = dot(c_t, (d_ssm * lane_pick(enter, 2 * i)).astype(jnp.bfloat16)).astype(
            jnp.bfloat16
        )


def gate_back(info, dy, ssm_out, z, scale, gain, cum, bc):
    rows, width = dy.shape
    return big_call(
        gate_back_kernel,
        (
            shape_of((rows, width), jnp.float32),
            shape_of((rows, width), jnp.bfloat16),
            shape_of((NS, width), jnp.bfloat16),
            shape_of(gain.shape, jnp.float32),
        ),
        info,
        dy,
        ssm_out,
        z,
        scale,
        gain,
        cum,
        bc,
        smem=1,
        flops=2 * rows * NS * width,
    )


def ssm_back_kernel(info, x, bc, dt, cum, grad, head_params, dx, d_bc, d_cum, d_dt, g_skip, cols_t, d_rows, between=None):
    rows, width = x.shape
    skip = head_params[2:3]
    cols_t[...] = cum[...].T
    row = lax.broadcasted_iota(jnp.int32, (rows, rows), 0)
    col = lax.broadcasted_iota(jnp.int32, (rows, rows), 1)
    at = lax.broadcasted_iota(jnp.int32, (1, rows), 1) + info[0]
    starts = seg_start(at, info) - info[0]
    narrow_b, narrow_c = bc[:, :NS], bc[:, NS:]
    products = dot_nt(narrow_b, narrow_c)
    skip_row = two_part(jnp.broadcast_to(skip, (8, TILE)), spread_heads(width))[:1]
    lane = lax.broadcasted_iota(jnp.int32, (SPAN, TILE), 1)
    parts = rows // SPAN
    d_products = [jnp.zeros((SPAN, rows - p * SPAN), jnp.float32) for p in range(parts)]
    d_rows[...] = jnp.zeros_like(d_rows)
    step_sums = [jnp.zeros((SPAN, TILE), jnp.float32) for p in range(parts)]
    skip_sums = []
    for i in range(MH // 2):
        cols = slice(i * TILE, (i + 1) * TILE)
        tile = x[:, cols]
        wide = grad[:, cols]
        narrow = wide.astype(jnp.bfloat16)
        skip_sums.append(jnp.sum(wide * tile.astype(jnp.float32), axis=0, keepdims=True))
        tile_sides = halves_of(tile)
        for part in range(parts):
            here = slice(part * SPAN, (part + 1) * SPAN)
            since = part * SPAN
            allowed = (row[here, since:] <= col[here, since:]) & (
                row[here, since:] >= starts[:, since:]
            )
            sides = []
            for side in range(2):
                h = 2 * i + side
                spread_log = cols_t[h : h + 1, since:] - cum[here, h : h + 1]
                decay = jnp.exp(jnp.where(allowed, spread_log, NEGATIVE_FILL))
                decay_dt = decay * dt[here, h : h + 1]
                mixing = products[here, since:] * decay_dt
                sides.append(dot(mixing.astype(jnp.bfloat16), narrow[since:]))
                d_mixing = dot_nt(tile_sides[side][here], narrow[since:])
                d_products[part] = d_products[part] + d_mixing * decay_dt
                whole = d_mixing * mixing
                d_rows[h : h + 1, since:] += jnp.sum(whole, axis=0, keepdims=True)
                weighed = d_mixing * (products[here, since:] * decay)
                step_sums[part] = jnp.where(
                    lane == h, jnp.sum(weighed, axis=1, keepdims=True), step_sums[part]
                )
            dx[here, cols] = (
                jnp.where(lane < MP, sides[0], sides[1]) + skip_row[:, cols] * wide[here]
            )
        if between is not None:
            between(i)
    all_steps = jnp.concatenate(step_sums, axis=0)
    d_dt[...] = all_steps
    d_cum[...] = d_rows[...].T - all_steps * dt[...]
    g_skip[...] = jnp.broadcast_to(
        two_part(
            jnp.broadcast_to(jnp.concatenate(skip_sums, axis=1), (8, width)), gather_heads(width)
        ),
        g_skip.shape,
    )
    full = jnp.concatenate(
        [
            d
            if p == 0
            else jnp.concatenate([jnp.zeros((SPAN, p * SPAN), jnp.float32), d], axis=1)
            for p, d in enumerate(d_products)
        ],
        axis=0,
    ).astype(jnp.bfloat16)
    d_bc[:, :NS] = dot(full, narrow_c)
    d_bc[:, NS:] = dot_tn(full, narrow_b)


def ssm_back(info, x, bc, dt, cum, grad, head_params):
    rows, width = x.shape
    f32 = jnp.float32
    return big_call(
        ssm_back_kernel,
        (
            shape_of((rows, width), f32),
            shape_of((rows, 2 * NS), f32),
            shape_of((rows, TILE), f32),
            shape_of((rows, TILE), f32),
            shape_of((8, TILE), f32),
        ),
        info,
        x,
        bc,
        dt,
        cum,
        grad,
        head_params,
        smem=1,
        scratch=(pltpu.VMEM((TILE, rows), f32), pltpu.VMEM((TILE, rows), f32)),
        flops=8 * rows * rows * width,
    )


def state_back_kernel(
    info, x, bc, dt, cum, grad, head_params, step_in, state_in, d_state, dx_in, d_bc_in, d_cum_in,
    d_dt_in, dx, d_bc, d_step, sums,
):
    rows, width = x.shape
    bias, rate = head_params[0:1], head_params[1:2]
    cums, steps = cum[...], dt[...]
    enter = entering_of(info, cums)
    last_start = seg_start(info[0] + rows - 1, info) - info[0]
    place = lax.broadcasted_iota(jnp.int32, (rows, 1), 0)
    end = cums[rows - 1 : rows]
    fade = jnp.where(place >= last_start, jnp.exp(jnp.minimum(end - cums, 0.0)), 0.0)
    leave = fade * steps
    through = jnp.where(last_start < 0, jnp.exp(end), 0.0)
    narrow_b, narrow_c = bc[:, :NS], bc[:, NS:]
    pick = gather_heads(width)
    d_leave = jnp.zeros((rows, TILE), jnp.float32)
    d_enter = jnp.zeros((rows, TILE), jnp.float32)
    d_b = d_bc_in[:, :NS]
    d_c = d_bc_in[:, NS:]
    link = jnp.zeros((8, TILE), jnp.float32)
    for i in range(MH // 2):
        cols = slice(i * TILE, (i + 1) * TILE)
        tile = x[:, cols].astype(jnp.float32)
        wide = grad[:, cols]
        pulled = d_state[:, cols]
        held = state_in[:, cols]
        from_b = dot(narrow_b, pulled)
        leave_tile = lane_pick(leave, 2 * i)
        dx[:, cols] = dx_in[:, cols] + leave_tile * from_b
        d_leave = d_leave + two_part(tile * from_b, pick[cols])
        d_enter = d_enter + two_part(wide * dot(narrow_c, held), pick[cols])
        d_b = d_b + dot_nt((tile * leave_tile).astype(jnp.bfloat16), pulled)
        d_c = d_c + dot_nt((wide * lane_pick(enter, 2 * i)).astype(jnp.bfloat16), held)
        meet = jnp.sum(
            pulled.astype(jnp.float32) * held.astype(jnp.float32), axis=0, keepdims=True
        )
        link = link + two_part(jnp.broadcast_to(meet, (8, TILE)), pick[cols])
    d_bc[:, :NS] = d_b
    d_bc[:, NS:] = d_c
    left = leave * d_leave
    d_cum = d_cum_in[...] + enter * d_enter - left
    at_end = jnp.sum(left, axis=0, keepdims=True) + through * link[:1]
    d_cum = d_cum + jnp.where(place == rows - 1, at_end, 0.0)
    row = lax.broadcasted_iota(jnp.int32, (rows, rows), 0)
    col = lax.broadcasted_iota(jnp.int32, (rows, rows), 1)
    d_log = exact(jnp.where(row <= col, 1.0, 0.0), d_cum)
    d_steps = d_dt_in[...] + fade * d_leave - d_log * rate
    d_pre = d_steps * jax.nn.sigmoid(step_in[...] + bias)
    d_pre = jnp.where(head_lanes(rows), d_pre, 0.0)
    d_step[...] = d_pre.astype(jnp.bfloat16)
    g_rate = jnp.sum(d_log * (-steps * rate), axis=0, keepdims=True)
    g_bias = jnp.sum(d_pre, axis=0, keepdims=True)
    line = lax.broadcasted_iota(jnp.int32, (8, TILE), 0)
    sums[...] = jnp.where(line == 0, g_rate, jnp.where(line == 1, g_bias, 0.0))


def state_back(info, *args):
    rows, width = args[0].shape
    f32 = jnp.float32
    return big_call(
        state_back_kernel,
        (
            shape_of((rows, width), f32),
            shape_of((rows, 2 * NS), f32),
            shape_of((rows, TILE), jnp.bfloat16),
            shape_of((8, TILE), f32),
        ),
        info,
        *args,
        smem=1,
        flops=12 * rows * NS * width,
    )


def join_states(earlier, later):
    decay = later[NS : NS + 1].astype(jnp.float32) + later[NS + 1 : NS + 2].astype(jnp.float32)
    before = earlier[NS : NS + 1].astype(jnp.float32) + earlier[NS + 1 : NS + 2].astype(jnp.float32)
    state = decay * earlier[:NS].astype(jnp.float32) + later[:NS].astype(jnp.float32)
    both = decay * before
    high = both.astype(jnp.bfloat16)
    low = (both - high.astype(jnp.float32)).astype(jnp.bfloat16)
    rest = jnp.zeros((STATE_ROWS - NS - 2, state.shape[1]), jnp.bfloat16)
    return jnp.concatenate([state.astype(jnp.bfloat16), high, low, rest], axis=0)


def scan_states(own, forward):
    place = lax.axis_index("seq")
    count = lax.axis_size("seq")
    nothing = jnp.concatenate(
        [
            jnp.zeros((NS, own.shape[1]), own.dtype),
            jnp.ones((1, own.shape[1]), own.dtype),
            jnp.zeros((STATE_ROWS - NS - 1, own.shape[1]), own.dtype),
        ],
        axis=0,
    )
    everything = lax.all_gather(own, "seq")

    def step(k, before):
        index = k if forward else count - 1 - k
        reached = index < place if forward else index > place
        part = lax.dynamic_index_in_dim(everything, index, 0, False)
        return jnp.where(reached, join_states(before, part), before)

    return lax.fori_loop(0, count, step, nothing)[:NS]


MESH = pl.DeviceIdType.MESH
ANY = pl.BlockSpec(memory_space=pl.ANY)
INTO_VMEM = pl.BlockSpec(memory_space=pltpu.VMEM)


def partners():
    seq, batch = lax.axis_index("seq"), lax.axis_index("batch")
    return {
        "far": (seq + 4 - 8 * (seq // 4), batch),
        "near": (seq + 2 - 4 * (seq // 2 % 2), batch),
        "x": (seq + 1 - 2 * (seq % 2), batch),
        "y": (seq, batch + 2 - 4 * (batch // 2)),
        "core": (seq, batch + 1 - 2 * (batch % 2)),
    }


def greet(others):
    barrier = pltpu.get_barrier_semaphore()
    for other in others:
        pl.semaphore_signal(barrier, inc=1, device_id=other, device_id_type=MESH)
    pl.semaphore_wait(barrier, len(others))


def remote(src, dst, send, recv, other):
    return pltpu.make_async_remote_copy(
        src_ref=src, dst_ref=dst, send_sem=send, recv_sem=recv, device_id=other, device_id_type=MESH
    )


def comm_call(kernel, outs, out_specs, args, in_specs, scratch, number, moved, limit=56):
    return pl.pallas_call(
        kernel,
        out_shape=list(outs),
        in_specs=in_specs,
        out_specs=out_specs,
        scratch_shapes=list(scratch),
        cost_estimate=pl.CostEstimate(flops=0, bytes_accessed=moved, transcendentals=0),
        compiler_params=pltpu.CompilerParams(
            collective_id=number, has_side_effects=True, vmem_limit_bytes=limit * 1024 * 1024
        ),
    )(*args)


def column_chunks(widths, aim=512):
    pairs = []
    for p, width in enumerate(widths):
        tiles, first, cuts = width // TILE, 0, []
        pieces = 2 * max(1, (width + aim // 2) // (2 * aim))
        for i in range(pieces):
            cols = (tiles // pieces + (1 if i < tiles % pieces else 0)) * TILE
            cuts.append((p, first, cols, ("xy", "yx")[i % 2]))
            first += cols
        pairs += [tuple(cuts[i : i + 2]) for i in range(0, pieces, 2)]
    return pairs


def pairs_of(pairs, array):
    return [n for n, (one, other) in enumerate(pairs) if one[0] == array]


BITS = {"far": 1, "near": 2, "x": 4, "y": 8, "core": 16}
ORDERS = {
    "xy": ("far", "near", "x", "y"),
    "yx": ("far", "near", "y", "x"),
}


def runs(places):
    out = []
    for place in places:
        if out and out[-1][0] + out[-1][1] == place:
            out[-1] = (out[-1][0], out[-1][1] + 1)
        else:
            out.append((place, 1))
    return out


def gather_plan(order):
    held, plan = [0], []
    for name in ORDERS[order] + ("core",):
        plan.append((name, [(f, k, f + BITS[name]) for f, k in runs(held)]))
        held = sorted(held + [block + BITS[name] for block in held])
    return plan


def scatter_plan(order):
    held, plan = list(range(16)), []
    for name in reversed(ORDERS[order]):
        bit = BITS[name]
        sent = [i for i, block in enumerate(held) if block & bit]
        kept = [i for i, block in enumerate(held) if not block & bit]
        plan.append((name, runs(sent), runs(kept)))
        held = [held[i] for i in kept]
    return plan


def bit_apart(r):
    me = lax.axis_index("seq")
    far = (r // 4 + me // 4) % 2
    near = (r // 2 % 2 + me // 2 % 2) % 2
    side = (r % 2 + me % 2) % 2
    return 4 * far + 2 * near + side


def join_into(target, earlier, later):
    decay = later[NS : NS + 1].astype(jnp.float32) + later[NS + 1 : NS + 2].astype(jnp.float32)
    before = earlier[NS : NS + 1].astype(jnp.float32) + earlier[NS + 1 : NS + 2].astype(jnp.float32)
    both = decay * before
    high = both.astype(jnp.bfloat16).astype(jnp.float32)
    line = lax.broadcasted_iota(jnp.int32, (STATE_ROWS - NS, both.shape[1]), 0)
    tail = jnp.where(line == 0, high, jnp.where(line == 1, both - high, 0.0))
    for first in range(0, NS, 32):
        rows = slice(first, first + 32)
        target[rows] = (
            decay * earlier[rows].astype(jnp.float32) + later[rows].astype(jnp.float32)
        ).astype(jnp.bfloat16)
    target[NS:] = tail.astype(jnp.bfloat16)


SCAN_PARTS = 2


class StateScan:
    def __init__(self, forward, own, result, arrived, sent, before, send, recv, others):
        me = lax.axis_index("seq")
        self.seconds = []
        for bit in (me % 2, me // 2 % 2, me // 4):
            self.seconds.append(bit == 1 if forward else bit == 0)
        route = (others["x"], others["near"], others["far"])
        width = own.shape[1] // SCAN_PARTS
        self.parts = []
        for part in range(SCAN_PARTS):
            cols = pl.ds(part * width, width)
            here = (slice(None), cols)
            sources = (own.at[here], sent.at[0].at[here], sent.at[1].at[here])
            targets = [arrived.at[k].at[here] for k in range(3)]
            copies = [
                remote(sources[k], targets[k], send.at[k, part], recv.at[k, part], route[k])
                for k in range(3)
            ]
            befores = [before.at[k].at[here] for k in range(2)]
            self.parts.append((sources, targets, copies, befores, result.at[here]))

    def step(self, k):
        for part in self.parts:
            self.part_step(k, *part)

    def part_step(self, k, sources, targets, copies, before, result):
        if k == 0:
            copies[0].start()
            return
        copies[k - 1].wait_recv()
        other, mine = targets[k - 1], sources[k - 1]
        second = self.seconds[k - 1]

        @pl.when(second)
        def _():
            if k < 3:
                join_into(sources[k], other, mine)
            if k == 1:
                before[0][...] = other[...]
            elif k == 2:
                join_into(before[1], other, before[0])
            else:
                last = before[1]
                decay = last[NS : NS + 1].astype(jnp.float32) + last[NS + 1 : NS + 2].astype(
                    jnp.float32
                )
                result[...] = (
                    decay * other[:NS].astype(jnp.float32) + last[:NS].astype(jnp.float32)
                ).astype(jnp.bfloat16)

        @pl.when(jnp.logical_not(second))
        def _():
            if k < 3:
                join_into(sources[k], mine, other)
            if k == 1:
                line = lax.broadcasted_iota(jnp.int32, before[0].shape, 0)
                before[0][...] = jnp.where(line == NS, 1.0, 0.0).astype(jnp.bfloat16)
            elif k == 2:
                before[1][...] = before[0][...]
            else:
                result[...] = before[1][:NS]

        if k < 3:
            copies[k].start()

    def finish(self):
        for part in self.parts:
            for copy in part[2]:
                copy.wait_send()


def scan_scratch(width):
    rows = STATE_ROWS
    dma = pltpu.SemaphoreType.DMA
    narrow = jnp.bfloat16
    return [
        pltpu.VMEM((3, rows, width), narrow),
        pltpu.VMEM((2, rows, width), narrow),
        pltpu.VMEM((2, rows, width), narrow),
        dma((3, SCAN_PARTS)),
        dma((3, SCAN_PARTS)),
    ]


RIM = 8
COLS = 384


def own_order_into(target):
    width = target.shape[0]
    per = width // 32
    me = lax.axis_index("seq") * 4 + lax.axis_index("batch")
    step = 128

    def fill(i, carry):
        first = pl.multiple_of(i * step, step)
        row = lax.broadcasted_iota(jnp.int32, (step, width), 0) + first
        col = lax.broadcasted_iota(jnp.int32, (step, width), 1)
        j = col // per
        flipped = (j & 1) * 16 + (j & 2) * 4 + (j & 4) + (j & 8) // 4 + (j & 16) // 16
        source = (flipped ^ me) * per + col % per
        target[pl.ds(first, step)] = jnp.where(row == source, 1.0, 0.0).astype(target.dtype)
        return carry

    lax.fori_loop(0, width // step, fill, 0)


def three_part(left, right):
    high = left.astype(jnp.bfloat16)
    rest = left - high.astype(jnp.float32)
    mid = rest.astype(jnp.bfloat16)
    low = (rest - mid.astype(jnp.float32)).astype(jnp.bfloat16)
    return dot(high, right) + dot(mid, right) + dot(low, right)


def places_of(lens, rows):
    one, two, three = lens[0, 0], lens[0, 1], lens[0, 2]
    return [lax.axis_index("seq") * rows, one, one + two, one + two + three]


def head_rows(bias, rate_log, skip, target):
    lane = lax.broadcasted_iota(jnp.int32, (1, TILE), 1)
    for k, source in enumerate((bias, rate_log, skip)):
        row = jnp.zeros((1, TILE), jnp.float32)
        for h in range(MH):
            row = jnp.where(lane == h, source[h], row)
        if k == 1:
            row = jnp.where(lane < MH, jnp.exp(row), 0.0)
        target[k : k + 1] = row


def pair_columns(value, back):
    tiles = [value[:, i * TILE : (i + 1) * TILE] for i in range(PAIRS)]
    turned = [pltpu.roll(tile, HEAD_SIZE, 1) for tile in tiles]
    lane = lax.broadcasted_iota(jnp.int32, tiles[0].shape, 1)

    def head(i, side):
        return tiles[i // 2] if i % 2 == side else turned[i // 2]

    out = []
    for i in range(PAIRS):
        if back:
            first, second = 2 * i, 2 * i + 1
            group = QUERY_HEADS // KEY_VALUE_HEADS
            first, second = [2 * (h % group) + h // group for h in (first, second)]
        else:
            first, second = i, i + PAIRS
        out.append(jnp.where(lane < HEAD_SIZE, head(first, 0), head(second, 1)))
    return jnp.concatenate(out, axis=1)


def shards_into(w_attn, w_ssm_in, w_dt, w_out, w_down, conv, mix, out, down):
    f32, narrow = jnp.float32, jnp.bfloat16
    ssm_width = MH * MP
    xbc = w_ssm_in.shape[1] - ssm_width
    query = QUERY_HEADS * HEAD_SIZE
    attn = w_attn.shape[1]
    conv[:, :xbc] = w_ssm_in[:, ssm_width:]
    conv[:, xbc:] = jnp.zeros((conv.shape[0], TILE), narrow)
    conv[:, xbc : xbc + MH] = w_dt[...]
    mix[:, :query] = pair_columns(w_attn[:, :query].astype(f32), False).astype(narrow)
    mix[:, query:attn] = w_attn[:, query:]
    mix[:, attn:] = w_ssm_in[:, :ssm_width]
    turned = []
    for i in range(w_out.shape[0] // TILE):
        here = slice(i * TILE, (i + 1) * TILE)
        tile = w_out[here].astype(f32).T
        if i < PAIRS:
            turned.append(tile)
        else:
            out[:, here] = tile.astype(narrow)
        down[:, here] = w_down[here].astype(f32).T.astype(narrow)
    out[:, :query] = pair_columns(jnp.concatenate(turned, axis=1), False).astype(narrow)


class Gather:
    def __init__(self, ins, outs, pairs, send, recv, local, others):
        self.ins, self.outs, self.pairs = ins, outs, pairs
        self.send, self.recv, self.local, self.others = send, recv, local, others
        self.started = {}
        self.block = ins[0].shape[0]

    def own(self):
        copies = []
        for p in range(len(self.ins)):
            copy = pltpu.make_async_copy(
                self.ins[p], self.outs[p].at[pl.ds(0, self.block)], self.local.at[p]
            )
            copy.start()
            copies.append(copy)
        for copy in copies:
            copy.wait()

    def step(self, n, stage):
        for side in range(2):
            p, column, cols, order = self.pairs[n][side]
            if stage > 0:
                for copy in self.started[n, side, stage - 1]:
                    copy.wait_recv()
            if stage == 5:
                continue
            name, moves = gather_plan(order)[stage]
            copies = []
            for k, (first, rows, there) in enumerate(moves):
                block = self.block
                copy = remote(
                    self.outs[p].at[pl.ds(first * block, rows * block), pl.ds(column, cols)],
                    self.outs[p].at[pl.ds(there * block, rows * block), pl.ds(column, cols)],
                    self.send.at[2 * n + side, stage, k],
                    self.recv.at[2 * n + side, stage, k],
                    self.others[name],
                )
                copy.start()
                copies.append(copy)
            self.started[n, side, stage] = copies

    def finish(self):
        for copies in self.started.values():
            for copy in copies:
                copy.wait_send()


def around():
    seq, batch = lax.axis_index("seq"), lax.axis_index("batch")
    return ((seq + 7) % 8, batch), ((seq + 1) % 8, batch)


def conv_masks(info, rows):
    at = lax.broadcasted_iota(jnp.int32, (rows, 1), 0) + info[0]
    start = seg_start(at, info)
    return [jnp.where(at - (CONV - 1) + i >= start, 1.0, 0.0) for i in range(CONV)]


def conv_forward(info, raw, conv_w, conv_b, pre, x, bc):
    rows = x.shape[0]
    masks = conv_masks(info, rows)
    tiles = pre.shape[1] // TILE
    split = x.shape[1] // TILE
    for i in range(tiles):
        cols = slice(i * TILE, (i + 1) * TILE)
        total = jnp.broadcast_to(conv_b[i : i + 1], (rows, TILE))
        for k in range(CONV):
            first = RIM - (CONV - 1) + k
            shifted_rows = jnp.where(masks[k] > 0.0, raw[first : first + rows, cols], 0.0)
            total = total + conv_w[k : k + 1, cols] * shifted_rows
        pre[:, cols] = total
        out = (total * jax.nn.sigmoid(total)).astype(jnp.bfloat16)
        if i < split:
            x[:, cols] = out
        else:
            bc[:, (i - split) * TILE : (i - split + 1) * TILE] = out


def front_kernel(
    count, pairs, lens, bias, rate_log, skip, layer_x, layer_g, norm_gain, mlp_gain, freqs, conv_w,
    conv_b, w_attn, w_ssm_in, w_dt, w_out, w_gate_up, w_down, *refs
):
    fulls, refs = refs[:count], refs[count:]
    (
        x_own, g_own, gains_own, normed, q, kv, gate_z, raw, pre, x, bc, y, state, dt, cum,
        out, out_t, lse, state_in, order, cosine, sine, head_params,
    ) = refs[:23]
    (
        s_conv, s_mix, s_out, s_down, gains,
        attn_proj, dt_t, cum_t, heads, acc, top, total, arrived, sent, before,
        scan_send, scan_recv, send, recv, w_send, w_recv, w_local, rim_send, rim_recv,
    ) = refs[23:]
    ins = (s_conv, s_mix, s_out, w_gate_up, s_down)
    others = partners()
    previous, following = around()
    greet(list(others.values()) + [previous, following])
    me = lax.axis_index("seq")
    rows, width = layer_x.shape
    info = places_of(lens, rows)
    shards_into(w_attn, w_ssm_in, w_dt, w_out, w_down, s_conv, s_mix, s_out, s_down)
    gather = Gather(ins, fulls, pairs, w_send, w_recv, w_local, others)
    gather.own()

    first = len(pairs_of(pairs, 0)) + len(pairs_of(pairs, 1))
    waves = {}
    for n in reversed(range(len(pairs))):
        for stage in range(6):
            late = 1 if n >= first and stage >= 2 else 0
            waves.setdefault(n + stage + late, []).append((n, stage))

    def pump(*which):
        for wave in which:
            for n, stage in waves.pop(wave, []):
                gather.step(n, stage)

    conv_wave = pairs_of(pairs, 0)[-1] + 5
    mix_wave = pairs_of(pairs, 1)[-1] + 5
    pump(0)
    own_order_into(order)
    head_rows(bias, rate_log, skip, head_params)
    gains[...] = jnp.zeros_like(gains)
    for k, source in enumerate((norm_gain, mlp_gain)):
        for i in range(width // TILE):
            gains[k : k + 1, i * TILE : (i + 1) * TILE] = source[i : i + 1]
    pump(1)
    at = lax.broadcasted_iota(jnp.int32, (rows, 1), 0) + info[0]
    angles = (at - seg_start(at, info)).astype(jnp.float32) * freqs[...]
    cosine[...] = jnp.cos(angles)
    sine[...] = jnp.sin(angles)
    x_own[...] = dot(layer_x[...], order[...]).astype(jnp.bfloat16)
    pump(2)
    gains_own[...] = three_part(gains[...], order[...])
    wide = x_own[...].astype(jnp.float32)
    scale = lax.rsqrt(jnp.mean(wide * wide, axis=-1, keepdims=True) + NORM_EPS)
    normed[...] = (wide * scale * gains_own[0:1]).astype(jnp.bfloat16)
    pump(3)
    g_own[...] = dot(layer_g[...], order[...]).astype(jnp.bfloat16)
    pump(*range(4, conv_wave + 1))

    full_conv, full_mix = fulls[0], fulls[1]
    xbc = pre.shape[1]
    conv_cols = full_conv.shape[1] // COLS
    attn_cols = attn_proj.shape[1] // COLS
    gate_cols = gate_z.shape[1] // COLS

    def project(weights, first, target, row, count_cols):
        def one(j, carry):
            cols = pl.ds(pl.multiple_of(j * COLS, TILE), COLS)
            there = pl.ds(pl.multiple_of(first + j * COLS, TILE), COLS)
            target[row : row + rows, cols] = dot(normed[...], weights[:, there])
            return carry

        lax.fori_loop(0, count_cols, one, 0)

    def at(r):
        return kv.at[pl.ds(r * rows, rows)]

    routes = {4: ("far", 0), 2: ("near", 0), 6: ("near", 4)}
    routes.update({r: ("x", r - 1) for r in (1, 3, 5, 7)})
    copies = {
        r: remote(at(src), at(r), send.at[r], recv.at[r], others[name])
        for r, (name, src) in routes.items()
    }
    project(full_conv, 0, raw, RIM, conv_cols)
    rim = remote(
        raw.at[pl.ds(rows, RIM)], raw.at[pl.ds(0, RIM)], rim_send.at[0], rim_recv.at[0], following
    )
    rim.start()
    pump(*range(conv_wave + 1, mix_wave))
    rim.wait_recv()
    conv_forward(info, raw, conv_w, conv_b, pre, x, bc)
    step_in = raw.at[pl.ds(RIM, rows), pl.ds(xbc, TILE)]
    ssm_states(info, x, bc, step_in, head_params, state, dt, cum, dt_t, cum_t)
    scan = StateScan(True, state, state_in, arrived, sent, before, scan_send, scan_recv, others)
    scan.step(0)
    pump(mix_wave)
    project(full_mix, 0, attn_proj, 0, attn_cols)
    rope_kernel(attn_proj, cosine, sine, q, kv.at[pl.ds(0, rows)])
    copies[4].start()
    copies[2].start()
    copies[1].start()
    pump(mix_wave + 1)
    project(full_mix, attn_proj.shape[1], gate_z, 0, gate_cols)
    attend_start(q, heads, acc, top, total)

    def attend(r):
        block = bit_apart(r)

        @pl.when(block <= me)
        def _():
            place = pl.ds(pl.multiple_of(r * rows, rows), rows)
            keys = kv[place, :TILE]
            values_t = kv[place, TILE:].astype(jnp.float32).T.astype(jnp.bfloat16)
            attend_block(info, block, keys, values_t, heads, acc, top, total)

    def several(first, gap, count_blocks):
        def body(j, carry):
            attend(first + j * gap)
            return carry

        lax.fori_loop(0, count_blocks, body, 0)

    scan.step(1)
    copies[4].wait_recv()
    copies[6].start()
    copies[5].start()
    copies[2].wait_recv()
    copies[3].start()
    copies[6].wait_recv()
    copies[7].start()
    pump(mix_wave + 2)
    several(0, 4, 2)
    pump(mix_wave + 3)
    ssm_local(info, x, bc, head_params, y, cum, dt_t, cum_t)
    scan.step(2)
    pump(mix_wave + 4)
    several(2, 4, 2)
    pump(mix_wave + 5)
    for r in (1, 3, 5, 7):
        copies[r].wait_recv()
    several(1, 2, 2)
    pump(mix_wave + 6)
    several(5, 2, 2)
    pump(mix_wave + 7)
    lse[...] = top[...] + jnp.log(total[...])
    attend_write(acc, total, out, out_t)
    scan.step(3)
    pump(*sorted(waves))
    gather.finish()
    scan.finish()
    rim.wait_send()
    for copy in copies.values():
        copy.wait_send()


def front(lens, bias, rate_log, skip, layer_x, layer_g, norm_gain, mlp_gain, freqs, conv_w, conv_b, weights):
    w_attn, w_ssm_in, w_dt, w_out, w_gate_up, w_down = weights
    rows, width = layer_x.shape
    f32, narrow = jnp.float32, jnp.bfloat16
    block = w_attn.shape[0]
    query_width = QUERY_HEADS * HEAD_SIZE
    pair_width = 2 * KEY_VALUE_HEADS * HEAD_SIZE
    ssm_width = MH * MP
    xbc = conv_w.shape[1]
    widths = [
        xbc + TILE, w_attn.shape[1] + ssm_width, w_out.shape[0], w_gate_up.shape[1],
        w_down.shape[0],
    ]
    count = len(widths)
    pairs = column_chunks(widths)
    fulls = [shape_of((width, w), narrow) for w in widths]
    outs = fulls + [
        shape_of((rows, width), narrow),
        shape_of((rows, width), narrow),
        shape_of((8, width), f32),
        shape_of((rows, width), narrow),
        shape_of((rows, query_width), narrow),
        shape_of((8 * rows, pair_width), narrow),
        shape_of((rows, ssm_width), f32),
        shape_of((rows + RIM, widths[0]), f32),
        shape_of((rows, xbc), f32),
        shape_of((rows, ssm_width), narrow),
        shape_of((rows, 2 * NS), narrow),
        shape_of((rows, ssm_width), f32),
        shape_of((STATE_ROWS, ssm_width), narrow),
        shape_of((rows, TILE), f32),
        shape_of((rows, TILE), f32),
        shape_of((rows, query_width), narrow),
        shape_of((query_width, rows), f32),
        shape_of((QUERY_HEADS, rows), f32),
        shape_of((NS, ssm_width), narrow),
        shape_of((width, width), narrow),
        shape_of((rows, TILE), f32),
        shape_of((rows, TILE), f32),
        shape_of((8, TILE), f32),
    ]
    dma = pltpu.SemaphoreType.DMA
    scratch = [
        *(pltpu.VMEM((block, widths[k]), narrow) for k in (0, 1, 2, 4)),
        pltpu.VMEM((8, width), f32),
        pltpu.VMEM((rows, query_width + pair_width), f32),
        pltpu.VMEM((TILE, rows), f32),
        pltpu.VMEM((TILE, rows), f32),
        pltpu.VMEM((QUERY_HEADS, rows, TILE), narrow),
        pltpu.VMEM((QUERY_HEADS, HEAD_SIZE, rows), f32),
        pltpu.VMEM((QUERY_HEADS, rows), f32),
        pltpu.VMEM((QUERY_HEADS, rows), f32),
        *scan_scratch(ssm_width),
        dma((8,)),
        dma((8,)),
        dma((2 * len(pairs), 5, 4)),
        dma((2 * len(pairs), 5, 4)),
        dma((count,)),
        dma((1,)),
        dma((1,)),
    ]
    result = comm_call(
        lambda *refs: front_kernel(count, pairs, *refs),
        outs,
        [INTO_VMEM] * 2 + [ANY] * (count - 2) + [INTO_VMEM] * 23,
        (
            lens, bias, rate_log, skip, layer_x, layer_g, norm_gain, mlp_gain, freqs, conv_w,
            conv_b, *weights,
        ),
        [pl.BlockSpec(memory_space=pltpu.SMEM)] * 4 + [INTO_VMEM] * 13,
        scratch,
        0,
        200_000_000,
    )
    return result[:count], result[count:]


def middle_kernel(
    lens, y, bc, cum, state_in, state_own, z, ssm_gain, attended, x_own, g_own, gains, order,
    hbm_out, hbm_gu, hbm_down,
    layer_out, joined, hidden, d_gu, normed_two, d_mixer, d_middle, d_ssm, d_z, pull, att_grad,
    g_ssm, g_mlp,
    w_out, w_gu, w_down, ssm_out, scale, middle, gate_up, d_normed, dy, narrow, sems,
):
    rows, width = x_own.shape
    info = places_of(lens, rows)
    copies = [
        pltpu.make_async_copy(src, dst, sems.at[k])
        for k, (src, dst) in enumerate(((hbm_out, w_out), (hbm_gu, w_gu), (hbm_down, w_down)))
    ]
    for copy in copies:
        copy.start()
    attn = attended.shape[1]
    ff = hidden.shape[1]
    step = 256

    def tiles(count, body):
        def one(j, carry):
            body(pl.ds(pl.multiple_of(j * step, step), step), j * step)
            return carry

        lax.fori_loop(0, count // step, one, 0)

    joined[:, :attn] = attended[...]
    ssm_finish_kernel(
        info, y, bc, cum, state_in, z, ssm_gain, ssm_out,
        joined.at[:, pl.ds(attn, joined.shape[1] - attn)], scale,
    )
    copies[0].wait()

    def add_mixers(here, first):
        middle[:, here] = x_own[:, here].astype(jnp.float32) + dot_nt(joined[...], w_out[here])

    tiles(width, add_mixers)
    wide = middle[...]
    r = lax.rsqrt(jnp.mean(wide * wide, axis=-1, keepdims=True) + NORM_EPS)
    normed_two[...] = (wide * r * gains[1:2]).astype(jnp.bfloat16)
    copies[1].wait()

    def up_project(here, first):
        there = pl.ds(pl.multiple_of(ff + first, step), step)
        gate = dot(normed_two[...], w_gu[:, here])
        up = dot(normed_two[...], w_gu[:, there])
        gate_up[:, here] = gate
        gate_up[:, there] = up
        hidden[:, here] = (gate * jax.nn.sigmoid(gate) * up).astype(jnp.bfloat16)

    tiles(ff, up_project)
    copies[2].wait()

    def down_project(here, first):
        narrow[:, here] = (middle[:, here] + dot_nt(hidden[...], w_down[here])).astype(jnp.bfloat16)

    tiles(width, down_project)

    def plain(here, first):
        layer_out[:, here] = dot_nt(narrow[...], order[here]).astype(jnp.bfloat16)

    tiles(width, plain)

    def down_back(here, first):
        there = pl.ds(pl.multiple_of(ff + first, step), step)
        d_hidden = dot(g_own[...], w_down[:, here])
        gate, up = gate_up[:, here], gate_up[:, there]
        sig = jax.nn.sigmoid(gate)
        d_gate = d_hidden * up * (sig * (1.0 + gate * (1.0 - sig)))
        d_gu[:, here] = d_gate.astype(jnp.bfloat16)
        d_gu[:, there] = (d_hidden * gate * sig).astype(jnp.bfloat16)

    tiles(ff, down_back)

    def up_back(here, first):
        d_normed[:, here] = dot_nt(d_gu[...], w_gu[here])

    tiles(width, up_back)
    grads = d_normed[...]
    wide = middle[...]
    g_mlp[...] = jnp.sum(grads * wide * r, axis=0, keepdims=True)
    inner = grads * gains[1:2]
    coeff = jnp.mean(inner * wide, axis=-1, keepdims=True)
    total = g_own[...].astype(jnp.float32) + r * (inner - wide * (r * r * coeff))
    d_middle[...] = total
    d_mixer[...] = total.astype(jnp.bfloat16)

    def att_back(here, first):
        att_grad[:, here] = dot(d_mixer[...], w_out[:, here]).astype(jnp.bfloat16)

    tiles(attn, att_back)

    def ssm_part(here, first):
        there = pl.ds(pl.multiple_of(attn + first, step), step)
        dy[:, here] = dot(d_mixer[...], w_out[:, there])

    tiles(dy.shape[1], ssm_part)
    gate_back_kernel(
        info, dy, ssm_out, z, scale, ssm_gain, cum, bc, d_ssm, d_z, pull.at[pl.ds(0, NS)], g_ssm
    )
    pull[NS:] = state_own[NS:]


def middle_part(lens, y, bc, cum, state_in, state_own, z, ssm_gain, attended, x_own, g_own, gains, order, w_out, w_gu, w_down):
    rows, width = x_own.shape
    ssm_width, attn = y.shape[1], attended.shape[1]
    ff = w_down.shape[1]
    f32, narrow = jnp.float32, jnp.bfloat16
    outs = [
        shape_of((rows, width), narrow),
        shape_of((rows, attn + ssm_width), narrow),
        shape_of((rows, ff), narrow),
        shape_of((rows, 2 * ff), narrow),
        shape_of((rows, width), narrow),
        shape_of((rows, width), narrow),
        shape_of((rows, width), f32),
        shape_of((rows, ssm_width), f32),
        shape_of((rows, ssm_width), narrow),
        shape_of((STATE_ROWS, ssm_width), narrow),
        shape_of((rows, attn), narrow),
        shape_of(ssm_gain.shape, f32),
        shape_of((1, width), f32),
    ]
    args = (
        lens, y, bc, cum, state_in, state_own, z, ssm_gain, attended, x_own, g_own, gains, order,
        w_out, w_gu, w_down,
    )
    return pl.pallas_call(
        middle_kernel,
        out_shape=outs,
        in_specs=[pl.BlockSpec(memory_space=pltpu.SMEM)] + [INTO_VMEM] * 12 + [ANY] * 3,
        out_specs=[INTO_VMEM] * len(outs),
        scratch_shapes=[
            pltpu.VMEM(w_out.shape, narrow),
            pltpu.VMEM(w_gu.shape, narrow),
            pltpu.VMEM(w_down.shape, narrow),
            pltpu.VMEM((rows, ssm_width), f32),
            pltpu.VMEM((rows, TILE), f32),
            pltpu.VMEM((rows, width), f32),
            pltpu.VMEM((rows, 2 * ff), f32),
            pltpu.VMEM((rows, width), f32),
            pltpu.VMEM((rows, ssm_width), f32),
            pltpu.VMEM((rows, width), narrow),
            pltpu.SemaphoreType.DMA((3,)),
        ],
        compiler_params=pltpu.CompilerParams(vmem_limit_bytes=60 * 1024 * 1024),
    )(*args)


def turn_over(value):
    return value.astype(jnp.float32).T.astype(jnp.bfloat16)


class Scatter:
    def __init__(self, ins, outs, arrived, pairs, send, recv, others):
        self.ins, self.outs, self.arrived, self.pairs = ins, outs, arrived, pairs
        self.send, self.recv, self.others = send, recv, others
        self.block = ins[0].shape[0] // 16
        self.started = {}

    def source(self, p, stage):
        return self.ins[p] if stage == 0 else self.arrived[4 * p + stage - 1]

    def step(self, n, stage):
        for side in range(2):
            if stage > 0:
                self.take(n, side, stage - 1)
            if stage < 4:
                self.begin(n, side, stage)

    def begin(self, n, side, stage):
        p, column, width, order = self.pairs[n][side]
        cols = pl.ds(column, width)
        name, sent, unused_kept = scatter_plan(order)[stage]
        copies, row, block = [], 0, self.block
        for k, (first, count) in enumerate(sent):
            copy = remote(
                self.source(p, stage).at[pl.ds(first * block, count * block), cols],
                self.arrived[4 * p + stage].at[pl.ds(row * block, count * block), cols],
                self.send.at[2 * n + side, stage, k],
                self.recv.at[2 * n + side, stage, k],
                self.others[name],
            )
            copy.start()
            copies.append(copy)
            row += count
        self.started[n, side, stage] = copies

    def take(self, n, side, stage):
        p, column, width, order = self.pairs[n][side]
        cols = slice(column, column + width)
        source, got = self.source(p, stage), self.arrived[4 * p + stage]
        target = self.outs[p] if stage == 3 else got
        unused_name, unused_sent, kept = scatter_plan(order)[stage]
        row, block = 0, self.block
        for k, (first, count) in enumerate(kept):
            self.started[n, side, stage][k].wait_recv()

            def add(i, carry):
                at = pl.multiple_of(i * block, block)
                there = pl.ds(row * block + at, block)
                total = source[pl.ds(first * block + at, block), cols].astype(jnp.float32) + got[
                    there, cols
                ].astype(jnp.float32)
                target[there, cols] = total.astype(target.dtype)
                return carry

            lax.fori_loop(0, count, add, 0)
            row += count

    def finish(self):
        for copies in self.started.values():
            for copy in copies:
                copy.wait_send()


def scatter_scratch(widths, size):
    scratch = []
    for width in widths:
        scratch += [pltpu.VMEM((size >> (s + 1), width), jnp.bfloat16) for s in range(4)]
    return scratch


def weight_products(left_t, right, theirs, target):
    rows = right.shape[0]
    step = 256 if right.shape[1] % 256 == 0 else TILE

    def one(j, carry):
        cols = pl.ds(pl.multiple_of(j * step, step), step)
        product = dot(left_t[:, :rows], right[:, cols]) + dot(left_t[:, rows:], theirs[:, cols])
        target[:, cols] = product.astype(target.dtype)
        return carry

    lax.fori_loop(0, right.shape[1] // step, one, 0)


def conv_back_start(info, dx, d_bc, pre, raw, d_pre, g_conv):
    rows, split = dx.shape[0], dx.shape[1] // TILE
    masks = conv_masks(info, rows)
    g_conv[...] = jnp.zeros_like(g_conv)
    for i in range(pre.shape[1] // TILE):
        cols = slice(i * TILE, (i + 1) * TILE)
        if i < split:
            grad = dx[:, cols]
        else:
            grad = d_bc[:, (i - split) * TILE : (i - split + 1) * TILE]
        value = pre[:, cols]
        sig = jax.nn.sigmoid(value)
        grad = grad * (sig * (1.0 + value * (1.0 - sig)))
        d_pre[:rows, cols] = grad
        for k in range(CONV):
            first = RIM - (CONV - 1) + k
            term = jnp.where(masks[k] > 0.0, raw[first : first + rows, cols], 0.0)
            g_conv[k : k + 1, cols] = jnp.sum(grad * term, axis=0, keepdims=True)
        g_conv[CONV : CONV + 1, cols] = jnp.sum(grad, axis=0, keepdims=True)


def conv_back_end(info, d_pre, conv_w, d_raw):
    rows = d_raw.shape[0]
    at = lax.broadcasted_iota(jnp.int32, (rows, 1), 0) + info[0]
    masks = [
        jnp.where(seg_start(at + (CONV - 1) - k, info) <= at, 1.0, 0.0) for k in range(CONV)
    ]
    for i in range(d_pre.shape[1] // TILE):
        cols = slice(i * TILE, (i + 1) * TILE)
        total = jnp.zeros((rows, TILE), jnp.float32)
        for k in range(CONV):
            first = CONV - 1 - k
            part = jnp.where(masks[k] > 0.0, d_pre[first : first + rows, cols], 0.0)
            total = total + conv_w[k : k + 1, cols] * part
        d_raw[:, cols] = total.astype(jnp.bfloat16)


def back_kernel(pairs, *refs):
    (
        lens, head_params, conv_w, cosine, sine, q, kv, grad, out_t, lse, pull, x, bc, dt, cum,
        d_ssm, raw, state_in, pre, normed, normed_two, d_mixer, grad_rows, hidden, joined, d_gu,
        d_z,
    ) = refs[:27]
    (
        d_conv, d_attn, g_conv, head_sums, g_skip, their_normed, out_down, out_gu, out_out, out_z,
    ) = refs[27:37]
    refs = refs[37:]
    partials, refs = refs[:4], refs[4:]
    arrived_w, refs = refs[:16], refs[16:]
    (
        half_grad, half_two, half_mixer, their_hidden, their_joined, their_gu, their_z, left_t,
        heads, grads, delta, acc, dkv, from_x, from_far, from_near, dq, d_pair, d_state,
        dx, d_bc, d_cum, d_dt, cols_t, d_rows, d_pre,
        arrived, sent, before, scan_send, scan_recv, send, recv, swap_send, swap_recv,
        w_send, w_recv, rim_send, rim_recv,
    ) = refs
    others = partners()
    previous, following = around()
    greet(list(others.values()) + [previous, following])
    me = lax.axis_index("seq")
    rows = q.shape[0]
    info = places_of(lens, rows)
    half = normed.shape[1] // 2
    xbc = pre.shape[1]
    scan = StateScan(False, pull, d_state, arrived, sent, before, scan_send, scan_recv, others)
    scan.step(0)
    behind = pl.ds(half, half)
    given = [
        (grad_rows.at[:, behind], half_grad),
        (hidden, their_hidden),
        (normed_two.at[:, behind], half_two),
        (d_gu, their_gu),
        (d_mixer.at[:, behind], half_mixer),
        (joined, their_joined),
        (normed.at[:, behind], their_normed),
        (d_z, their_z),
    ]
    swaps = [
        remote(give, take, swap_send.at[k], swap_recv.at[k], others["core"])
        for k, (give, take) in enumerate(given)
    ]
    for copy in swaps:
        copy.start()
    scatter = Scatter(
        partials, (out_down, out_gu, out_out, out_z), arrived_w, pairs, w_send, w_recv, others
    )

    def weights(k, left, left_half, right, theirs):
        swaps[2 * k].wait_recv()
        swaps[2 * k + 1].wait_recv()
        left_t[:, :rows] = turn_over(left[:, :half])
        left_t[:, rows:] = turn_over(left_half[...])
        weight_products(left_t, right, theirs, partials[k])

    def pump(*steps):
        for n, stage in steps:
            scatter.step(n, stage)

    attend_back_start(q, grad, out_t, heads, grads, delta, acc)

    def block_back(r):
        block = bit_apart(r)
        place = pl.ds(pl.multiple_of(r * rows, rows), rows)

        @pl.when(block <= me)
        def _():
            attend_back_block(
                info, block, kv[place, :TILE], kv[place, TILE:], lse, dkv.at[r], heads, grads,
                delta, acc,
            )

        @pl.when(block > me)
        def _():
            dkv[r] = jnp.zeros(dkv.shape[1:], dkv.dtype)

    def several(first, gap, count):
        def body(j, carry):
            block_back(first + j * gap)
            return carry

        lax.fori_loop(0, count, body, 0)

    def add(target, source):
        target[...] = (target[...].astype(jnp.float32) + source[...].astype(jnp.float32)).astype(
            jnp.bfloat16
        )

    weights(0, grad_rows, half_grad, hidden, their_hidden)
    pump((0, 0))
    several(1, 2, 4)
    over_x = [
        remote(dkv.at[2 * k + 1], from_x.at[k], send.at[k], recv.at[k], others["x"])
        for k in range(4)
    ]
    for copy in over_x:
        copy.start()
    scan.step(1)
    weights(1, normed_two, half_two, d_gu, their_gu)
    pump((1, 0), (0, 1))
    several(4, 2, 2)
    over_far = [
        remote(dkv.at[4 + 2 * k], from_far.at[k], send.at[4 + k], recv.at[4 + k], others["far"])
        for k in range(2)
    ]
    for k in range(2):
        over_x[2 + k].wait_recv()
        add(dkv.at[4 + 2 * k], from_x.at[2 + k])
        over_far[k].start()
    scan.step(2)
    pump((2, 0), (1, 1), (0, 2))
    several(0, 2, 2)
    for k in range(2):
        over_x[k].wait_recv()
        add(dkv.at[2 * k], from_x.at[k])
    over_far[1].wait_recv()
    add(dkv.at[2], from_far.at[1])
    over_near = remote(dkv.at[2], from_near, send.at[6], recv.at[6], others["near"])
    over_near.start()
    weights(2, d_mixer, half_mixer, joined, their_joined)
    weights(3, normed, their_normed, d_z, their_z)
    pump((3, 0), (2, 1), (1, 2), (0, 3))
    ssm_back_kernel(
        info, x, bc, dt, cum, d_ssm, head_params, dx, d_bc, d_cum, d_dt, g_skip, cols_t, d_rows
    )
    pump((4, 0), (3, 1), (2, 2), (1, 3), (0, 4))
    scan.step(3)
    d_step = d_conv.at[:, pl.ds(xbc, TILE)]
    step_in = raw.at[pl.ds(RIM, rows), pl.ds(xbc, TILE)]
    state_back_kernel(
        info, x, bc, dt, cum, d_ssm, head_params, step_in, state_in, d_state, dx, d_bc, d_cum,
        d_dt, dx, d_bc, d_step, head_sums,
    )
    conv_back_start(info, dx, d_bc, pre, raw, d_pre, g_conv)
    rim = remote(
        d_pre.at[pl.ds(0, RIM)], d_pre.at[pl.ds(rows, RIM)], rim_send.at[0], rim_recv.at[0],
        previous,
    )
    rim.start()
    pump((4, 1), (3, 2), (2, 3), (1, 4))
    over_far[0].wait_recv()
    over_near.wait_recv()
    attend_back_write(acc, dq)
    d_pair[...] = (
        dkv[0].astype(jnp.float32)
        + from_far[0].astype(jnp.float32)
        + from_near[...].astype(jnp.float32)
    )
    rope_back_kernel(dq, d_pair, cosine, sine, d_attn)
    rim.wait_recv()
    conv_back_end(info, d_pre, conv_w, d_conv.at[:, pl.ds(0, xbc)])
    pump((4, 2), (3, 3), (2, 4))
    pump((4, 3), (3, 4))
    pump((4, 4))
    scatter.finish()
    scan.finish()
    rim.wait_send()
    for copy in over_x + over_far + [over_near] + swaps:
        copy.wait_send()


def back(lens, *args):
    (
        head_params, conv_w, cosine, sine, q, kv, grad, out_t, lse, pull, x, bc, dt, cum,
        d_ssm, raw, state_in, pre, normed, normed_two, d_mixer, grad_rows, hidden, joined, d_gu,
        d_z,
    ) = args
    rows, query_width = q.shape
    width = normed.shape[1]
    half = width // 2
    pair = kv.shape[1]
    ssm_width, xbc = x.shape[1], pre.shape[1]
    f32, narrow = jnp.float32, jnp.bfloat16
    dma = pltpu.SemaphoreType.DMA
    widths = [hidden.shape[1], d_gu.shape[1], joined.shape[1], d_z.shape[1]]
    pairs = column_chunks(widths, 1024)
    own = half // 16
    outs = [
        shape_of((rows, xbc + TILE), narrow),
        shape_of((rows, query_width + pair), narrow),
        shape_of((8, xbc), f32),
        shape_of((8, TILE), f32),
        shape_of((8, TILE), f32),
        shape_of((rows, half), narrow),
    ] + [shape_of((own, w), f32) for w in widths]
    scratch = [pltpu.VMEM((half, w), narrow) for w in widths]
    scratch += scatter_scratch(widths, half)
    scratch += [pltpu.VMEM((rows, half), narrow)] * 3
    scratch += [pltpu.VMEM(a.shape, narrow) for a in (hidden, joined, d_gu, d_z)]
    scratch += [
        pltpu.VMEM((half, 2 * rows), narrow),
        pltpu.VMEM((QUERY_HEADS, rows, TILE), narrow),
        pltpu.VMEM((QUERY_HEADS, rows, TILE), narrow),
        pltpu.VMEM((QUERY_HEADS, rows), f32),
        pltpu.VMEM((QUERY_HEADS, HEAD_SIZE, rows), f32),
        pltpu.VMEM((8, rows, pair), narrow),
        pltpu.VMEM((4, rows, pair), narrow),
        pltpu.VMEM((2, rows, pair), narrow),
        pltpu.VMEM((rows, pair), narrow),
        pltpu.VMEM((rows, query_width), f32),
        pltpu.VMEM((rows, pair), f32),
        pltpu.VMEM((NS, ssm_width), narrow),
        pltpu.VMEM((rows, ssm_width), f32),
        pltpu.VMEM((rows, 2 * NS), f32),
        pltpu.VMEM((rows, TILE), f32),
        pltpu.VMEM((rows, TILE), f32),
        pltpu.VMEM((TILE, rows), f32),
        pltpu.VMEM((TILE, rows), f32),
        pltpu.VMEM((rows + RIM, xbc), f32),
        *scan_scratch(ssm_width),
        dma((7,)),
        dma((7,)),
        dma((8,)),
        dma((8,)),
        dma((2 * len(pairs), 4, 4)),
        dma((2 * len(pairs), 4, 4)),
        dma((1,)),
        dma((1,)),
    ]
    return comm_call(
        lambda *refs: back_kernel(pairs, *refs),
        outs,
        [INTO_VMEM] * len(outs),
        (lens, *args),
        [pl.BlockSpec(memory_space=pltpu.SMEM)] + [INTO_VMEM] * len(args),
        scratch,
        2,
        200_000_000,
        limit=62,
    )


def dot_nt_two(left, right):
    high = left.astype(jnp.bfloat16)
    low = (left - high.astype(jnp.float32)).astype(jnp.bfloat16)
    return dot_nt(high, right) + dot_nt(low, right)


def last_kernel(pairs, *refs):
    (
        d_conv, d_attn, d_z, full_conv, full_mix, normed, their_normed, x_own, d_middle, gains,
        order, g_mlp, g_ssm, g_conv, head_sums, g_skip, sum_down, sum_out, sum_z,
    ) = refs[:19]
    (
        input_grad, g_attn_out, g_in_out, g_dt_out, g_out_out, g_down_out,
        norm_total, mlp_total, ssm_total, conv_total, conv_b_total, head_total,
    ) = refs[19:31]
    refs = refs[31:]
    partials, arrived_w = refs[:2], refs[2:10]
    (
        out_conv, out_attn, their_conv, their_attn, left_t, d_normed, small_own, small_in, small_mid,
        small_out, swap_send, swap_recv, w_send, w_recv, small_send, small_recv,
    ) = refs[10:]
    others = partners()
    greet(list(others.values()))
    rows, width = normed.shape
    half = width // 2
    swaps = [
        remote(give, take, swap_send.at[k], swap_recv.at[k], others["core"])
        for k, (give, take) in enumerate(((d_conv, their_conv), (d_attn, their_attn)))
    ]
    for copy in swaps:
        copy.start()
    scatter = Scatter(partials, (out_conv, out_attn), arrived_w, pairs, w_send, w_recv, others)
    left_t[:, :rows] = turn_over(normed[:, :half])
    left_t[:, rows:] = turn_over(their_normed[...])
    swaps[0].wait_recv()
    weight_products(left_t, d_conv, their_conv, partials[0])
    scatter.step(0, 0)
    scatter.step(1, 0)
    swaps[1].wait_recv()
    weight_products(left_t, d_attn, their_attn, partials[1])
    scatter.step(2, 0)
    step = 256
    attn = d_attn.shape[1]

    def back_out(j, carry):
        here = pl.ds(pl.multiple_of(j * step, step), step)
        d_normed[:, here] = (
            dot_nt(d_conv[...], full_conv[here])
            + dot_nt(d_attn[...], full_mix[here, :attn])
            + dot_nt(d_z[...], full_mix[here, attn:])
        )
        return carry

    lax.fori_loop(0, width // step, back_out, 0)
    scatter.step(0, 1)
    scatter.step(1, 1)
    wide = x_own[...].astype(jnp.float32)
    r = lax.rsqrt(jnp.mean(wide * wide, axis=-1, keepdims=True) + NORM_EPS)
    grads = d_normed[...]
    g_norm = jnp.sum(grads * wide * r, axis=0, keepdims=True)
    line = lax.broadcasted_iota(jnp.int32, (8, width), 0)
    both = jnp.where(line == 0, g_norm, jnp.where(line == 1, g_mlp[...], 0.0))
    both = dot_nt_two(both, order[...])
    small_own[16:] = jnp.zeros((small_own.shape[0] - 16, TILE), jnp.float32)
    small_own[16:28] = g_ssm[...]
    small_own[28:30] = head_sums[0:2]
    small_own[30:31] = g_skip[0:1]
    conv_tiles = g_conv.shape[1] // TILE
    for k in range(CONV + 1):
        for i in range(conv_tiles):
            place = 32 + 16 * k + i
            small_own[place : place + 1] = g_conv[k : k + 1, i * TILE : (i + 1) * TILE]
    for k in range(width // TILE):
        for which in range(2):
            small_own[8 * which + k : 8 * which + k + 1] = both[
                which : which + 1, k * TILE : (k + 1) * TILE
            ]
    names = ("core", "y", "x", "near", "far")
    small_copies = []

    def small_step(k):
        if k > 0:
            small_copies[k - 1].wait_recv()
            was = small_own if k == 1 else small_mid.at[k - 2]
            now = small_out if k == 5 else small_mid.at[k - 1]
            now[...] = was[...] + small_in[k - 1]
        if k < 5:
            source = small_own if k == 0 else small_mid.at[k - 1]
            copy = remote(
                source, small_in.at[k], small_send.at[k], small_recv.at[k], others[names[k]]
            )
            copy.start()
            small_copies.append(copy)

    scatter.step(2, 1)
    scatter.step(0, 2)
    small_step(0)
    inner = grads * gains[0:1]
    coeff = jnp.mean(inner * wide, axis=-1, keepdims=True)
    d_normed[...] = d_middle[...] + r * (inner - wide * (r * r * coeff))
    scatter.step(1, 2)
    small_step(1)
    scatter.step(0, 3)
    scatter.step(2, 2)

    def plain(j, carry):
        here = pl.ds(pl.multiple_of(j * step, step), step)
        input_grad[:, here] = dot_nt_two(d_normed[...], order[here])
        return carry

    lax.fori_loop(0, width // step, plain, 0)
    small_step(2)
    query = QUERY_HEADS * HEAD_SIZE
    g_in_out[:, : sum_z.shape[1]] = sum_z[...]
    moved = pair_columns(sum_out[:, :query], True)
    for i in range(sum_out.shape[1] // TILE):
        here = slice(i * TILE, (i + 1) * TILE)
        tile = moved[:, here] if i < PAIRS else sum_out[:, here]
        g_out_out[here] = tile.T
        g_down_out[here] = sum_down[:, here].T
    scatter.step(1, 3)
    scatter.step(2, 3)
    small_step(3)
    scatter.step(0, 4)
    small_step(4)
    scatter.step(1, 4)
    scatter.step(2, 4)
    small_step(5)
    norm_total[...] = small_out[:8]
    mlp_total[...] = small_out[8:16]
    ssm_total[...] = small_out[16:28]
    head_total[...] = small_out[24:32]
    for k in range(CONV):
        for i in range(conv_tiles):
            place = 32 + 16 * k + i
            conv_total[k : k + 1, i * TILE : (i + 1) * TILE] = small_out[place : place + 1]
    conv_b_total[...] = small_out[32 + 16 * CONV : 32 + 16 * CONV + conv_tiles]
    g_in_out[:, g_in_out.shape[1] - g_conv.shape[1] :] = out_conv[:, : g_conv.shape[1]]
    g_dt_out[...] = out_conv[:, g_conv.shape[1] : g_conv.shape[1] + MH]
    query = QUERY_HEADS * HEAD_SIZE
    g_attn_out[:, :query] = pair_columns(out_attn[:, :query], True)
    g_attn_out[:, query:] = out_attn[:, query:]
    scatter.finish()
    for copy in swaps + small_copies:
        copy.wait_send()


def last(*args):
    d_conv, d_attn, d_z, normed = args[0], args[1], args[2], args[5]
    g_conv = args[13]
    rows, width = normed.shape
    half = width // 2
    f32, narrow = jnp.float32, jnp.bfloat16
    dma = pltpu.SemaphoreType.DMA
    widths = [d_conv.shape[1], d_attn.shape[1]]
    pairs = column_chunks(widths)
    total = (32 + 16 * (CONV + 1), TILE)
    block = half // 16
    xbc = g_conv.shape[1]
    joined, ff = args[17].shape[1], args[16].shape[1]
    outs = [
        shape_of((rows, width), f32),
        shape_of((block, widths[1]), f32),
        shape_of((block, d_z.shape[1] + xbc), f32),
        shape_of((block, MH), f32),
        shape_of((joined, block), f32),
        shape_of((ff, block), f32),
        shape_of((8, TILE), f32),
        shape_of((8, TILE), f32),
        shape_of((12, TILE), f32),
        shape_of((CONV, xbc), f32),
        shape_of((xbc // TILE, TILE), f32),
        shape_of((8, TILE), f32),
    ]
    scratch = [pltpu.VMEM((half, w), narrow) for w in widths]
    scratch += scatter_scratch(widths, half)
    scratch += [pltpu.VMEM((block, w), f32) for w in widths]
    scratch += [
        pltpu.VMEM(d_conv.shape, narrow),
        pltpu.VMEM(d_attn.shape, narrow),
        pltpu.VMEM((half, 2 * rows), narrow),
        pltpu.VMEM((rows, width), f32),
        pltpu.VMEM(total, f32),
        pltpu.VMEM((5, *total), f32),
        pltpu.VMEM((4, *total), f32),
        pltpu.VMEM(total, f32),
        dma((2,)),
        dma((2,)),
        dma((2 * len(pairs), 4, 4)),
        dma((2 * len(pairs), 4, 4)),
        dma((5,)),
        dma((5,)),
    ]
    return comm_call(
        lambda *refs: last_kernel(pairs, *refs),
        outs,
        [INTO_VMEM] * len(outs),
        args,
        [INTO_VMEM] * len(args),
        scratch,
        4,
        100_000_000,
    )


def pair_heads(value, back=False):
    rows = value.shape[0]
    group = QUERY_HEADS // KEY_VALUE_HEADS
    width = QUERY_HEADS * HEAD_SIZE
    shape = (group, KEY_VALUE_HEADS) if back else (KEY_VALUE_HEADS, group)
    moved = value[:, :width].reshape(rows, *shape, HEAD_SIZE).transpose(0, 2, 1, 3)
    return jnp.concatenate([moved.reshape(rows, width), value[:, width:]], axis=1)


def plain_layer(
    layer_input,
    seq_lengths,
    w_attn,
    w_ssm_in,
    w_dt,
    w_out,
    w_gate_up,
    w_down,
    norm_gain,
    mlp_gain,
    ssm_gain,
    conv_w,
    conv_b,
    a_log,
    dt_bias,
    d_skip,
    out_grad,
):
    token_rows = layer_input.shape[1]
    query_width = QUERY_HEADS * HEAD_SIZE
    key_value_width = KEY_VALUE_HEADS * HEAD_SIZE
    attn_width = query_width + 2 * key_value_width
    ssm_width = MH * MP
    xbc_width = ssm_width + 2 * NS
    seq_lens = seq_lengths[0]
    first_pos = lax.axis_index("seq") * token_rows
    positions = first_pos + jnp.arange(token_rows, dtype=jnp.int32)
    segment, device_places = segments(seq_lens, positions)
    ends = jnp.cumsum(seq_lens)
    info = jnp.stack([first_pos, ends[0], ends[1], ends[2]]).astype(jnp.int32)
    half = HEAD_SIZE // 2
    freqs = ROPE_BASE ** (-jnp.arange(half, dtype=jnp.float32) / half)
    angles = device_places.astype(jnp.float32)[:, None] * jnp.tile(freqs, TILE // half)[None, :]
    cosine, sine = jnp.cos(angles), jnp.sin(angles)
    head_params = jnp.pad(
        jnp.stack([dt_bias, jnp.exp(a_log), d_skip]), ((0, 5), (0, TILE - MH))
    )
    step_pad = jnp.pad(w_dt, ((0, 0), (0, TILE - MH)))
    shards = (
        jnp.concatenate([w_ssm_in[:, ssm_width:], step_pad], axis=1),
        jnp.concatenate([pair_heads(w_attn), w_ssm_in[:, :ssm_width]], axis=1),
        pair_heads(w_out.T),
        w_gate_up,
        w_down.T,
    )
    ext_pos = first_pos - (CONV - 1) + jnp.arange(token_rows + CONV - 1, dtype=jnp.int32)
    ext_segment = segments(seq_lens, ext_pos)[0]

    def conv_local(ext_rows, conv_weight, conv_bias):
        return conv_mix(ext_rows, ext_segment, conv_weight, conv_bias)

    full = [lax.all_gather(p, ("seq", "batch"), axis=0, tiled=True) for p in shards]
    full_conv, full_mix, full_out, full_gu, full_down = full
    x_rows = layer_input[0].astype(jnp.float32)
    grad_rows = out_grad[0]
    scale_one = rms_scale(x_rows)
    normed = (x_rows * scale_one * norm_gain).astype(jnp.bfloat16)
    conv_proj = jnp.dot(normed, full_conv, preferred_element_type=jnp.float32)
    mix_proj = jnp.dot(normed, full_mix, preferred_element_type=jnp.float32)
    queries, own_pairs = big_call(
        rope_kernel,
        (
            shape_of((token_rows, query_width), jnp.bfloat16),
            shape_of((token_rows, 2 * key_value_width), jnp.bfloat16),
        ),
        mix_proj[:, :attn_width],
        cosine,
        sine,
    )
    gate_z = mix_proj[:, attn_width:]
    raw_xbc = conv_proj[:, :xbc_width]
    step_proj = conv_proj[:, xbc_width:]
    rim_rows = shifted(raw_xbc[token_rows - (CONV - 1) :], "seq", 1)
    extended = jnp.concatenate([rim_rows, raw_xbc], axis=0)
    conv_out, conv_pullback = jax.vjp(conv_local, extended, conv_w, conv_b)
    conv_narrow = conv_out.astype(jnp.bfloat16)
    inputs_x, inputs_bc = conv_narrow[:, :ssm_width], conv_narrow[:, ssm_width:]
    ssm_own, state_own, steps_dt, running_decay = ssm_forward(
        info, inputs_x, inputs_bc, step_proj, head_params
    )
    all_pairs = lax.all_gather(own_pairs, "seq", axis=0, tiled=True)
    state_in = scan_states(state_own, True)
    attended, attended_t, log_total = attn_forward(info, queries, all_pairs)

    ssm_flat, ssm_normed, scale_gated = ssm_finish(
        info, ssm_own, inputs_bc, running_decay, state_in, gate_z, ssm_gain.reshape(-1, TILE)
    )
    joined = jnp.concatenate([attended, ssm_normed], axis=1)

    def into_width(left, weight):
        return jnp.einsum("tc,dc->td", left, weight, preferred_element_type=jnp.float32)

    def out_of_width(left, weight):
        return jnp.dot(left, weight, preferred_element_type=jnp.float32)

    middle = x_rows + into_width(joined, full_out)
    scale_two = rms_scale(middle)
    normed_two = (middle * scale_two * mlp_gain).astype(jnp.bfloat16)
    gate_up = out_of_width(normed_two, full_gu)
    gate_part, up_part = gate_up[:, :FF], gate_up[:, FF:]
    sig_gate = jax.nn.sigmoid(gate_part)
    hidden = (gate_part * sig_gate * up_part).astype(jnp.bfloat16)
    layer_out = middle + into_width(hidden, full_down)
    d_hidden = out_of_width(grad_rows, full_down)
    d_gate = d_hidden * up_part * (sig_gate * (1.0 + gate_part * (1.0 - sig_gate)))
    d_up = d_hidden * gate_part * sig_gate
    d_gate_up = jnp.concatenate([d_gate, d_up], axis=1).astype(jnp.bfloat16)
    d_normed_two = into_width(d_gate_up, full_gu)
    d_middle_norm, g_mlp_gain = norm_back(middle, scale_two, mlp_gain, d_normed_two)
    d_middle = grad_rows.astype(jnp.float32) + d_middle_norm
    d_mixer = d_middle.astype(jnp.bfloat16)
    d_joined = out_of_width(d_mixer, full_out)
    attended_gradient = d_joined[:, :query_width].astype(jnp.bfloat16)
    d_ssm_out, d_gate_z, pull, g_ssm_gain = gate_back(
        info,
        d_joined[:, query_width:],
        ssm_flat,
        gate_z,
        scale_gated,
        ssm_gain.reshape(-1, TILE),
        running_decay,
        inputs_bc,
    )
    pull = jnp.concatenate([pull, state_own[NS:]], axis=0)
    d_state = scan_states(pull, False)
    d_queries, d_pairs = attn_backward(
        info, queries, all_pairs, attended_gradient, attended_t, log_total
    )
    own_d_pairs = lax.psum_scatter(
        d_pairs.astype(jnp.float32), "seq", scatter_dimension=0, tiled=True
    )
    dx_part, d_bc_part, d_cum_part, d_dt_part, g_skip_rows = ssm_back(
        info, inputs_x, inputs_bc, steps_dt, running_decay, d_ssm_out, head_params
    )
    g_inputs_x, g_inputs_bc, d_step_pad, head_sums = state_back(
        info,
        inputs_x,
        inputs_bc,
        steps_dt,
        running_decay,
        d_ssm_out,
        head_params,
        step_proj,
        state_in,
        d_state,
        dx_part,
        d_bc_part,
        d_cum_part,
        d_dt_part,
    )
    g_extended, g_conv_w, g_conv_b = conv_pullback(
        jnp.concatenate([g_inputs_x, g_inputs_bc], axis=1)
    )
    back_rim = shifted(g_extended[: CONV - 1], "seq", -1)
    d_raw = g_extended[CONV - 1 :] + jnp.concatenate(
        [jnp.zeros((token_rows - (CONV - 1), xbc_width), jnp.float32), back_rim], axis=0
    )
    d_conv_proj = jnp.concatenate([d_raw.astype(jnp.bfloat16), d_step_pad], axis=1)
    (d_attn_proj,) = big_call(
        rope_back_kernel,
        (shape_of((token_rows, attn_width), jnp.bfloat16),),
        d_queries,
        own_d_pairs,
        cosine,
        sine,
    )
    d_mix_proj = jnp.concatenate([d_attn_proj, d_gate_z], axis=1)
    d_normed = into_width(d_conv_proj, full_conv) + into_width(d_mix_proj, full_mix)
    d_input_norm, g_norm_gain = norm_back(x_rows, scale_one, norm_gain, d_normed)
    input_grad = d_middle + d_input_norm
    axes = ("seq", "batch")

    def summed(left, right):
        grad = jnp.einsum("td,tc->dc", left, right, preferred_element_type=jnp.float32)
        return lax.psum_scatter(grad, axes, scatter_dimension=0, tiled=True)

    sum_down, sum_gu = summed(grad_rows, hidden), summed(normed_two, d_gate_up)
    sum_out, sum_conv = summed(d_mixer, joined), summed(normed, d_conv_proj)
    sum_mix = summed(normed, d_mix_proj)
    sum_attn, sum_z = sum_mix[:, :attn_width], sum_mix[:, attn_width:]
    small = (
        g_norm_gain,
        g_mlp_gain,
        g_ssm_gain.reshape(-1),
        g_conv_w,
        g_conv_b,
        head_sums[0, :MH],
        head_sums[1, :MH],
        g_skip_rows[0, :MH],
    )
    small_sums = unpack_small(lax.psum(pack_small(small), axes), small)
    grad_attn = pair_heads(sum_attn, True)
    grad_ssm_in = jnp.concatenate([sum_z, sum_conv[:, :xbc_width]], axis=1)
    grad_dt = sum_conv[:, xbc_width : xbc_width + MH]
    grad_out = pair_heads(sum_out, True).T
    grad_gate_up = sum_gu
    grad_down = sum_down.T
    return (
        layer_out.astype(jnp.bfloat16)[None],
        input_grad[None],
        grad_attn,
        grad_ssm_in,
        grad_dt,
        grad_out,
        grad_gate_up,
        grad_down,
        *small_sums,
    )


def on_device(
    layer_input,
    seq_lengths,
    w_attn,
    w_ssm_in,
    w_dt,
    w_out,
    w_gate_up,
    w_down,
    norm_gain,
    mlp_gain,
    ssm_gain,
    conv_w,
    conv_b,
    a_log,
    dt_bias,
    d_skip,
    out_grad,
):
    if not is_fast(layer_input.shape[2]):
        return plain_layer(
            layer_input, seq_lengths, w_attn, w_ssm_in, w_dt, w_out, w_gate_up, w_down, norm_gain,
            mlp_gain, ssm_gain, conv_w, conv_b, a_log, dt_bias, d_skip, out_grad,
        )
    half = HEAD_SIZE // 2
    freqs = np.float32(ROPE_BASE) ** (-np.arange(half, dtype=np.float32) / np.float32(half))
    freqs = jnp.asarray(np.tile(freqs.astype(np.float32), TILE // half)[None])
    full, made = front(
        seq_lengths,
        dt_bias,
        a_log,
        d_skip,
        layer_input[0],
        out_grad[0],
        norm_gain.reshape(-1, TILE),
        mlp_gain.reshape(-1, TILE),
        freqs,
        conv_w,
        conv_b.reshape(-1, TILE),
        (w_attn, w_ssm_in, w_dt, w_out, w_gate_up, w_down),
    )
    full_conv, full_mix, full_out, full_gu, full_down = full
    (
        x_own, g_own, gains, normed, queries, all_pairs, gate_z, raw_rows, pre_conv, inputs_x,
        inputs_bc, ssm_own, state_own, steps_dt, running_decay, attended, attended_t, log_total,
        state_in, order, cosine, sine, head_params,
    ) = made
    (
        layer_out, joined, hidden, d_gate_up, normed_two, d_mixer, d_middle, d_ssm_out, d_gate_z,
        pull, attended_gradient, g_ssm_gain, g_mlp_gain,
    ) = middle_part(
        seq_lengths, ssm_own, inputs_bc, running_decay, state_in, state_own, gate_z,
        ssm_gain.reshape(-1, TILE), attended, x_own, g_own, gains, order, full_out, full_gu,
        full_down,
    )
    (
        d_conv_proj, d_attn_proj, g_conv, head_sums, g_skip_rows, their_normed, sum_down, sum_gu,
        sum_out, sum_z,
    ) = back(
        seq_lengths, head_params, conv_w, cosine, sine, queries, all_pairs, attended_gradient,
        attended_t, log_total, pull, inputs_x, inputs_bc, steps_dt, running_decay, d_ssm_out,
        raw_rows, state_in, pre_conv, normed, normed_two, d_mixer, g_own, hidden, joined,
        d_gate_up, d_gate_z,
    )
    (
        input_grad, grad_attn, grad_ssm_in, grad_dt, grad_out, grad_down, g_norm, g_mlp, g_ssm,
        g_conv_w, g_conv_b, heads,
    ) = last(
        d_conv_proj, d_attn_proj, d_gate_z, full_conv, full_mix, normed, their_normed, x_own,
        d_middle, gains, order, g_mlp_gain, g_ssm_gain, g_conv, head_sums, g_skip_rows, sum_down,
        sum_out, sum_z,
    )
    return (
        layer_out[None],
        input_grad[None],
        grad_attn,
        grad_ssm_in,
        grad_dt,
        grad_out,
        sum_gu,
        grad_down,
        g_norm.reshape(-1),
        g_mlp.reshape(-1),
        g_ssm.reshape(-1),
        g_conv_w,
        g_conv_b.reshape(-1),
        heads[4, :MH],
        heads[5, :MH],
        heads[6, :MH],
    )


def solution(mesh):
    return jax.shard_map(
        on_device,
        mesh=mesh,
        in_specs=(
            P("batch", "seq", None),
            P("batch", None),
            P(("seq", "batch"), None),
            P(("seq", "batch"), None),
            P(("seq", "batch"), None),
            P(None, ("seq", "batch")),
            P(("seq", "batch"), None),
            P(None, ("seq", "batch")),
            P(),
            P(),
            P(),
            P(),
            P(),
            P(),
            P(),
            P(),
            P("batch", "seq", None),
        ),
        out_specs=(
            P("batch", "seq", None),
            P("batch", "seq", None),
            P(("seq", "batch"), None),
            P(("seq", "batch"), None),
            P(("seq", "batch"), None),
            P(None, ("seq", "batch")),
            P(("seq", "batch"), None),
            P(None, ("seq", "batch")),
            P(),
            P(),
            P(),
            P(),
            P(),
            P(),
            P(),
            P(),
        ),
        check_vma=False,
    )
```

```python
import jax
import jax.numpy as jnp
import numpy as np
from jax import lax
from jax.experimental import pallas as pl
from jax.experimental.pallas import tpu as pltpu
from jax.sharding import PartitionSpec as P

QUERY_HEADS = 8
KEY_VALUE_HEADS = 2
HEAD_SIZE = 64
MH = 24
MP = 64
NS = 128
FF = 2048
CONV = 4
SPAN = 128


HIGHEST = lax.Precision.HIGHEST
NEGATIVE_FILL = -1e30
ROPE_BASE = 10000.0
NORM_EPS = 1e-06


def shifted(block, axis, distance):
    devices = range(lax.axis_size(axis))
    route = [(i - distance, i) for i in devices if i - distance in devices]
    return lax.ppermute(block, axis, route)


def is_fast(width):
    return lax.axis_size("seq") == 8 and lax.axis_size("batch") == 4 and width % (32 * 32) == 0


def pack_small(arrays):
    flat = jnp.concatenate([a.reshape(-1) for a in arrays])
    return jnp.pad(flat, (0, -flat.shape[0] % 1024)).reshape(-1, 128)


def unpack_small(flat, arrays):
    flat = flat.reshape(-1)
    out, start = [], 0
    for a in arrays:
        out.append(flat[start : start + a.size].reshape(a.shape))
        start += a.size
    return out


def rms_scale(value_rows):
    return lax.rsqrt(jnp.mean(value_rows * value_rows, axis=-1, keepdims=True) + NORM_EPS)


def norm_back(value_rows, scales, gains, grads):
    gain_grad = jnp.sum(grads * value_rows * scales, axis=0)
    inner = grads * gains
    coeff = jnp.mean(inner * value_rows, axis=-1, keepdims=True)
    return (scales * (inner - value_rows * scales * scales * coeff), gain_grad)


def segments(lengths, positions):
    ends = jnp.cumsum(lengths)
    passed = ends[None, :] <= positions[:, None]
    segment = jnp.sum(passed.astype(jnp.int32), axis=1)
    device_places = positions - jnp.sum(jnp.where(passed, lengths[None, :], 0), axis=1)
    return (segment, device_places)


def conv_mix(extended, ext_segment, conv_weight, conv_bias):
    row_count = extended.shape[0] - (CONV - 1)
    summed = conv_bias[None, :]
    for lagged in range(CONV):
        same_seq = (ext_segment[lagged : lagged + row_count] == ext_segment[CONV - 1 :]).astype(
            extended.dtype
        )
        summed = (
            summed
            + conv_weight[lagged][None, :]
            * extended[lagged : lagged + row_count]
            * same_seq[:, None]
        )
    return jax.nn.silu(summed)


TILE = 128
PAIRS = QUERY_HEADS // 2
CHUNK = 256


def dot(left, right):
    return jnp.dot(left, right, preferred_element_type=jnp.float32)


def dot_nt(left, right):
    return lax.dot_general(
        left, right, (((1,), (1,)), ((), ())), preferred_element_type=jnp.float32
    )


def dot_tn(left, right):
    return lax.dot_general(
        left, right, (((0,), (0,)), ((), ())), preferred_element_type=jnp.float32
    )


def exact(left, right):
    return jnp.dot(left, right, precision=HIGHEST, preferred_element_type=jnp.float32)


def two_part(left, right):
    high = left.astype(jnp.bfloat16)
    low = (left - high.astype(jnp.float32)).astype(jnp.bfloat16)
    return dot(high, right) + dot(low, right)


def seg_start(where_at, info):
    start = jnp.zeros_like(where_at)
    for k in range(1, 4):
        start = jnp.where(where_at >= info[k], jnp.maximum(start, info[k]), start)
    return start


def big_call(kernel, outs, *args, scratch=(), flops=0, smem=0, limit=48):
    specs = [pl.BlockSpec(memory_space=pltpu.SMEM)] * smem
    specs += [pl.BlockSpec(memory_space=pltpu.VMEM)] * (len(args) - smem)
    moved = sum(a.size * a.dtype.itemsize for a in args)
    moved += sum(o.size * o.dtype.itemsize for o in outs)
    return pl.pallas_call(
        kernel,
        out_shape=list(outs),
        in_specs=specs,
        out_specs=[pl.BlockSpec(memory_space=pltpu.VMEM)] * len(outs),
        scratch_shapes=list(scratch),
        cost_estimate=pl.CostEstimate(flops=flops, bytes_accessed=moved, transcendentals=0),
        compiler_params=pltpu.CompilerParams(vmem_limit_bytes=limit * 1024 * 1024),
    )(*args)


def shape_of(shape, dtype):
    return jax.ShapeDtypeStruct(shape, dtype)


def turn(value, cosine, sine):
    lane = lax.broadcasted_iota(jnp.int32, value.shape, 1) % HEAD_SIZE
    mixed = jnp.where(
        lane < HEAD_SIZE // 2,
        -pltpu.roll(value, TILE - HEAD_SIZE // 2, 1),
        pltpu.roll(value, HEAD_SIZE // 2, 1),
    )
    return value * cosine + mixed * sine


def rope_kernel(proj, cosine, sine, q_out, kv_out):
    cos, sin = cosine[...], sine[...]
    for i in range(PAIRS):
        cols = pl.ds(i * TILE, TILE)
        turned = turn(proj[:, cols], cos, sin).astype(jnp.bfloat16)
        q_out[:, cols] = (turned.astype(jnp.float32) * HEAD_SIZE**-0.5).astype(jnp.bfloat16)
    base = PAIRS * TILE
    kv_out[:, :TILE] = turn(proj[:, base : base + TILE], cos, sin).astype(jnp.bfloat16)
    kv_out[:, TILE:] = proj[:, base + TILE : base + 2 * TILE].astype(jnp.bfloat16)


def halves_of(value):
    lane = lax.broadcasted_iota(jnp.int32, value.shape, 1)
    wide = value.astype(jnp.float32)
    first = jnp.where(lane < HEAD_SIZE, wide, 0.0).astype(value.dtype)
    return first, jnp.where(lane < HEAD_SIZE, 0.0, wide).astype(value.dtype)


def block_range(info):
    first = info[0]
    low = seg_start(first, info) // CHUNK
    return low, first // CHUNK - low + 1


def attn_mask(info, block):
    rows = lax.broadcasted_iota(jnp.int32, (CHUNK, CHUNK), 0) + block * CHUNK
    at = lax.broadcasted_iota(jnp.int32, (1, CHUNK), 1) + info[0]
    return (rows <= at) & (rows >= seg_start(at, info))


def attend_start(q, heads, acc, top, total):
    for i in range(PAIRS):
        heads[2 * i], heads[2 * i + 1] = halves_of(q[:, i * TILE : (i + 1) * TILE])
    acc[...] = jnp.zeros_like(acc)
    total[...] = jnp.zeros_like(total)
    top[...] = jnp.full(top.shape, NEGATIVE_FILL, jnp.float32)


def attend_block(info, block, keys, values_t, heads, acc, top, total):
    allowed = attn_mask(info, block)
    for h in range(QUERY_HEADS):
        scores = jnp.where(allowed, dot_nt(keys, heads[h]), NEGATIVE_FILL)
        old = top[h : h + 1]
        new = jnp.maximum(old, jnp.max(scores, axis=0, keepdims=True))
        probs = jnp.where(allowed, jnp.exp(scores - new), 0.0)
        shrink = jnp.exp(old - new)
        top[h : h + 1] = new
        total[h : h + 1] = total[h : h + 1] * shrink + jnp.sum(probs, axis=0, keepdims=True)
        side = (h % 2) * HEAD_SIZE
        acc[h] = acc[h] * shrink + dot(
            values_t[side : side + HEAD_SIZE], probs.astype(jnp.bfloat16)
        )


def attend_write(acc, total, out, out_t):
    for i in range(PAIRS):
        pair = jnp.concatenate(
            [acc[2 * i] / total[2 * i : 2 * i + 1], acc[2 * i + 1] / total[2 * i + 1 : 2 * i + 2]],
            axis=0,
        )
        out_t[i * TILE : (i + 1) * TILE] = pair
        out[:, i * TILE : (i + 1) * TILE] = pair.T.astype(jnp.bfloat16)


def attn_forward_kernel(info, q, kv, out, out_t, lse, heads, acc, top, total):
    attend_start(q, heads, acc, top, total)
    low, count = block_range(info)

    def step(j, carry):
        block = low + j
        place = pl.ds(pl.multiple_of(block * CHUNK, CHUNK), CHUNK)
        keys = kv[place, :TILE]
        values_t = kv[place, TILE:].astype(jnp.float32).T.astype(jnp.bfloat16)
        attend_block(info, block, keys, values_t, heads, acc, top, total)
        return carry

    lax.fori_loop(0, count, step, 0)
    lse[...] = top[...] + jnp.log(total[...])
    attend_write(acc, total, out, out_t)


def attn_forward(info, q, kv):
    rows = q.shape[0]
    f32 = jnp.float32
    return big_call(
        attn_forward_kernel,
        (
            shape_of(q.shape, jnp.bfloat16),
            shape_of(q.shape[::-1], f32),
            shape_of((QUERY_HEADS, rows), f32),
        ),
        info,
        q,
        kv,
        smem=1,
        scratch=(
            pltpu.VMEM((QUERY_HEADS, rows, TILE), jnp.bfloat16),
            pltpu.VMEM((QUERY_HEADS, HEAD_SIZE, rows), f32),
            pltpu.VMEM((QUERY_HEADS, rows), f32),
            pltpu.VMEM((QUERY_HEADS, rows), f32),
        ),
        flops=4 * rows * kv.shape[0] * q.shape[1],
    )


def attend_back_start(q, grad, out_t, heads, grads, delta, acc):
    for i in range(PAIRS):
        cols = slice(i * TILE, (i + 1) * TILE)
        heads[2 * i], heads[2 * i + 1] = halves_of(q[:, cols])
        grads[2 * i], grads[2 * i + 1] = halves_of(grad[:, cols])
        both = grad[:, cols].astype(jnp.float32).T * out_t[cols]
        delta[2 * i : 2 * i + 1] = jnp.sum(both[:HEAD_SIZE], axis=0, keepdims=True)
        delta[2 * i + 1 : 2 * i + 2] = jnp.sum(both[HEAD_SIZE:], axis=0, keepdims=True)
    acc[...] = jnp.zeros_like(acc)


def attend_back_block(info, block, keys, values, lse, target, heads, grads, delta, acc):
    keys_t = keys.astype(jnp.float32).T.astype(jnp.bfloat16)
    allowed = attn_mask(info, block)
    d_keys = jnp.zeros((CHUNK, TILE), jnp.float32)
    d_values = jnp.zeros((CHUNK, TILE), jnp.float32)
    for h in range(QUERY_HEADS):
        scores = dot_nt(keys, heads[h])
        probs = jnp.where(allowed, jnp.exp(scores - lse[h : h + 1]), 0.0)
        d_probs = dot_nt(values, grads[h])
        d_scores = (probs * (d_probs - delta[h : h + 1])).astype(jnp.bfloat16)
        d_values = d_values + dot(probs.astype(jnp.bfloat16), grads[h])
        d_keys = d_keys + dot(d_scores, heads[h])
        side = (h % 2) * HEAD_SIZE
        acc[h] = acc[h] + dot(keys_t[side : side + HEAD_SIZE], d_scores)
    target[:, :TILE] = d_keys.astype(jnp.bfloat16)
    target[:, TILE:] = d_values.astype(jnp.bfloat16)


def attend_back_write(acc, dq):
    for i in range(PAIRS):
        pair = jnp.concatenate([acc[2 * i], acc[2 * i + 1]], axis=0)
        dq[:, i * TILE : (i + 1) * TILE] = pair.T * HEAD_SIZE**-0.5


def attn_backward_kernel(info, q, kv, grad, out_t, lse, dq, dkv, heads, grads, delta, acc):
    attend_back_start(q, grad, out_t, heads, grads, delta, acc)
    dkv[...] = jnp.zeros_like(dkv)
    low, count = block_range(info)

    def step(j, carry):
        block = low + j
        place = pl.ds(pl.multiple_of(block * CHUNK, CHUNK), CHUNK)
        attend_back_block(
            info, block, kv[place, :TILE], kv[place, TILE:], lse, dkv.at[place], heads, grads,
            delta, acc,
        )
        return carry

    lax.fori_loop(0, count, step, 0)
    attend_back_write(acc, dq)


def attn_backward(info, q, kv, grad, out_t, lse):
    rows = q.shape[0]
    f32 = jnp.float32
    return big_call(
        attn_backward_kernel,
        (shape_of(q.shape, f32), shape_of(kv.shape, jnp.bfloat16)),
        info,
        q,
        kv,
        grad,
        out_t,
        lse,
        smem=1,
        scratch=(
            pltpu.VMEM((QUERY_HEADS, rows, TILE), jnp.bfloat16),
            pltpu.VMEM((QUERY_HEADS, rows, TILE), jnp.bfloat16),
            pltpu.VMEM((QUERY_HEADS, rows), f32),
            pltpu.VMEM((QUERY_HEADS, HEAD_SIZE, rows), f32),
        ),
        flops=10 * rows * kv.shape[0] * q.shape[1],
    )


def rope_back_kernel(dq, dkv, cosine, sine, out):
    cos, sin = cosine[...], -sine[...]
    for i in range(PAIRS):
        cols = slice(i * TILE, (i + 1) * TILE)
        out[:, cols] = turn(dq[:, cols], cos, sin).astype(jnp.bfloat16)
    base = PAIRS * TILE
    out[:, base : base + TILE] = turn(dkv[:, :TILE], cos, sin).astype(jnp.bfloat16)
    out[:, base + TILE :] = dkv[:, TILE:].astype(jnp.bfloat16)


STATE_ROWS = NS + 16


def lane_pick(value, first):
    rows = value.shape[0]
    lane = lax.broadcasted_iota(jnp.int32, (rows, TILE), 1)
    return jnp.where(lane < MP, value[:, first : first + 1], value[:, first + 1 : first + 2])


def spread_heads(width):
    head = lax.broadcasted_iota(jnp.int32, (TILE, width), 0)
    col = lax.broadcasted_iota(jnp.int32, (TILE, width), 1)
    return jnp.where(head == col // MP, 1.0, 0.0).astype(jnp.bfloat16)


def gather_heads(width):
    head = lax.broadcasted_iota(jnp.int32, (width, TILE), 1)
    col = lax.broadcasted_iota(jnp.int32, (width, TILE), 0)
    return jnp.where(head == col // MP, 1.0, 0.0).astype(jnp.bfloat16)


def head_lanes(rows):
    return lax.broadcasted_iota(jnp.int32, (rows, TILE), 1) < MH


def chunk_places(info, rows):
    at = lax.broadcasted_iota(jnp.int32, (rows, 1), 0) + info[0]
    return seg_start(at, info) - info[0]


def ssm_states(info, x, bc, step_in, head_params, state, dt_out, cum_out, dt_t, cum_t):
    rows = x.shape[0]
    bias, rate = head_params[0:1], head_params[1:2]
    raw = step_in[...] + bias
    dt = jnp.maximum(raw, 0.0) + jnp.log1p(jnp.exp(-jnp.abs(raw)))
    dt = jnp.where(head_lanes(rows), dt, 0.0)
    row = lax.broadcasted_iota(jnp.int32, (rows, rows), 0)
    col = lax.broadcasted_iota(jnp.int32, (rows, rows), 1)
    lower = jnp.where(row >= col, 1.0, 0.0)
    cum = exact(lower, -dt * rate)
    dt_out[...] = dt
    cum_out[...] = cum
    dt_t[...] = dt.T
    cum_t[...] = cum.T
    last_start = seg_start(info[0] + rows - 1, info) - info[0]
    place = lax.broadcasted_iota(jnp.int32, (rows, 1), 0)
    end = cum[rows - 1 : rows]
    leave = jnp.where(place >= last_start, jnp.exp(jnp.minimum(end - cum, 0.0)) * dt, 0.0)
    b_t = bc[:, :NS].astype(jnp.float32).T.astype(jnp.bfloat16)
    through = jnp.where(last_start < 0, jnp.exp(end), 0.0)
    high = through.astype(jnp.bfloat16).astype(jnp.float32)
    line = lax.broadcasted_iota(jnp.int32, (16, TILE), 0)
    both = jnp.where(line == 0, high, jnp.where(line == 1, through - high, 0.0))
    spread = spread_heads(x.shape[1])
    state[NS:] = dot(both.astype(jnp.bfloat16), spread).astype(jnp.bfloat16)
    for i in range(MH // 2):
        cols = slice(i * TILE, (i + 1) * TILE)
        weighed = x[:, cols].astype(jnp.float32) * lane_pick(leave, 2 * i)
        state[:NS, cols] = dot(b_t, weighed.astype(jnp.bfloat16)).astype(jnp.bfloat16)


def ssm_local(info, x, bc, head_params, y, cum, dt_t, cum_t):
    rows = x.shape[0]
    row = lax.broadcasted_iota(jnp.int32, (rows, rows), 0)
    col = lax.broadcasted_iota(jnp.int32, (rows, rows), 1)
    starts = chunk_places(info, rows)
    products = dot_nt(bc[:, NS:], bc[:, :NS])
    skips = jnp.broadcast_to(head_params[2:3], (8, TILE))
    skip_row = two_part(skips, spread_heads(x.shape[1]))[:1]
    lane = lax.broadcasted_iota(jnp.int32, (SPAN, TILE), 1)
    for i in range(MH // 2):
        cols = slice(i * TILE, (i + 1) * TILE)
        tile = x[:, cols]
        for part in range(rows // SPAN):
            here = slice(part * SPAN, (part + 1) * SPAN)
            upto = (part + 1) * SPAN
            allowed = (row[here, :upto] >= col[here, :upto]) & (col[here, :upto] >= starts[here])
            sides = []
            for h in (2 * i, 2 * i + 1):
                spread_log = cum[here, h : h + 1] - cum_t[h : h + 1, :upto]
                decay = jnp.exp(jnp.where(allowed, spread_log, NEGATIVE_FILL))
                mixing = products[here, :upto] * decay * dt_t[h : h + 1, :upto]
                sides.append(dot(mixing.astype(jnp.bfloat16), tile[:upto]))
            own = skip_row[:, cols] * tile[here].astype(jnp.float32)
            y[here, cols] = jnp.where(lane < MP, sides[0], sides[1]) + own


def ssm_forward_kernel(info, x, bc, step_in, head_params, y, state, dt_out, cum_out, dt_t, cum_t):
    ssm_states(info, x, bc, step_in, head_params, state, dt_out, cum_out, dt_t, cum_t)
    ssm_local(info, x, bc, head_params, y, cum_out, dt_t, cum_t)


def ssm_forward(info, x, bc, step_in, head_params):
    rows, width = x.shape
    f32 = jnp.float32
    return big_call(
        ssm_forward_kernel,
        (
            shape_of((rows, width), f32),
            shape_of((STATE_ROWS, width), jnp.bfloat16),
            shape_of((rows, TILE), f32),
            shape_of((rows, TILE), f32),
        ),
        info,
        x,
        bc,
        step_in,
        head_params,
        smem=1,
        scratch=(pltpu.VMEM((TILE, rows), f32), pltpu.VMEM((TILE, rows), f32)),
        flops=4 * rows * rows * width,
    )


def entering_of(info, cum):
    rows = cum.shape[0]
    return jnp.where(chunk_places(info, rows) < 0, jnp.exp(jnp.minimum(cum, 0.0)), 0.0)


def ssm_finish_kernel(info, y, bc, cum, state_in, z, gain, ssm_out, normed, scale):
    rows = y.shape[0]
    enter = entering_of(info, cum[...])
    narrow_c = bc[:, NS:]
    squares = jnp.zeros((rows, TILE), jnp.float32)
    tiles = MH // 2
    for i in range(tiles):
        cols = slice(i * TILE, (i + 1) * TILE)
        out = y[:, cols] + lane_pick(enter, 2 * i) * dot(narrow_c, state_in[:, cols])
        ssm_out[:, cols] = out
        gate = z[:, cols]
        gated = out * (gate * jax.nn.sigmoid(gate))
        squares = squares + gated * gated
    mean = jnp.sum(squares, axis=1, keepdims=True) * (1.0 / (tiles * TILE))
    r = lax.rsqrt(mean + NORM_EPS)
    scale[...] = jnp.broadcast_to(r, scale.shape)
    for i in range(tiles):
        cols = slice(i * TILE, (i + 1) * TILE)
        gate = z[:, cols]
        gated = ssm_out[:, cols] * (gate * jax.nn.sigmoid(gate))
        normed[:, cols] = (gated * r * gain[i : i + 1]).astype(jnp.bfloat16)


def ssm_finish(info, y, bc, cum, state_in, z, gain):
    rows, width = y.shape
    return big_call(
        ssm_finish_kernel,
        (
            shape_of((rows, width), jnp.float32),
            shape_of((rows, width), jnp.bfloat16),
            shape_of((rows, TILE), jnp.float32),
        ),
        info,
        y,
        bc,
        cum,
        state_in,
        z,
        gain,
        smem=1,
        flops=2 * rows * NS * width,
    )


def gate_back_kernel(info, dy, ssm_out, z, scale, gain, cum, bc, d_out, d_z, pull, g_gain):
    rows = dy.shape[0]
    tiles = MH // 2
    r = scale[:, :1]
    enter = entering_of(info, cum[...])
    c_t = bc[:, NS:].astype(jnp.float32).T.astype(jnp.bfloat16)
    inner = jnp.zeros((rows, TILE), jnp.float32)
    for i in range(tiles):
        cols = slice(i * TILE, (i + 1) * TILE)
        gate = z[:, cols]
        gated = ssm_out[:, cols] * (gate * jax.nn.sigmoid(gate))
        product = dy[:, cols] * gated
        g_gain[i : i + 1] = jnp.sum(product * r, axis=0, keepdims=True)
        inner = inner + product * gain[i : i + 1]
    coeff = jnp.sum(inner, axis=1, keepdims=True) * (1.0 / (tiles * TILE))
    for i in range(tiles):
        cols = slice(i * TILE, (i + 1) * TILE)
        gate = z[:, cols]
        sig = jax.nn.sigmoid(gate)
        silu = gate * sig
        out = ssm_out[:, cols]
        d_gated = r * (dy[:, cols] * gain[i : i + 1] - out * silu * (r * r * coeff))
        d_ssm = d_gated * silu
        d_out[:, cols] = d_ssm
        d_z[:, cols] = (d_gated * out * (sig * (1.0 + gate * (1.0 - sig)))).astype(jnp.bfloat16)
        pull[:, cols] = dot(c_t, (d_ssm * lane_pick(enter, 2 * i)).astype(jnp.bfloat16)).astype(
            jnp.bfloat16
        )


def gate_back(info, dy, ssm_out, z, scale, gain, cum, bc):
    rows, width = dy.shape
    return big_call(
        gate_back_kernel,
        (
            shape_of((rows, width), jnp.float32),
            shape_of((rows, width), jnp.bfloat16),
            shape_of((NS, width), jnp.bfloat16),
            shape_of(gain.shape, jnp.float32),
        ),
        info,
        dy,
        ssm_out,
        z,
        scale,
        gain,
        cum,
        bc,
        smem=1,
        flops=2 * rows * NS * width,
    )


def ssm_back_kernel(info, x, bc, dt, cum, grad, head_params, dx, d_bc, d_cum, d_dt, g_skip, cols_t, d_rows, between=None):
    rows, width = x.shape
    skip = head_params[2:3]
    cols_t[...] = cum[...].T
    row = lax.broadcasted_iota(jnp.int32, (rows, rows), 0)
    col = lax.broadcasted_iota(jnp.int32, (rows, rows), 1)
    at = lax.broadcasted_iota(jnp.int32, (1, rows), 1) + info[0]
    starts = seg_start(at, info) - info[0]
    narrow_b, narrow_c = bc[:, :NS], bc[:, NS:]
    products = dot_nt(narrow_b, narrow_c)
    skip_row = two_part(jnp.broadcast_to(skip, (8, TILE)), spread_heads(width))[:1]
    lane = lax.broadcasted_iota(jnp.int32, (SPAN, TILE), 1)
    parts = rows // SPAN
    d_products = [jnp.zeros((SPAN, rows - p * SPAN), jnp.float32) for p in range(parts)]
    d_rows[...] = jnp.zeros_like(d_rows)
    step_sums = [jnp.zeros((SPAN, TILE), jnp.float32) for p in range(parts)]
    skip_sums = []
    for i in range(MH // 2):
        cols = slice(i * TILE, (i + 1) * TILE)
        tile = x[:, cols]
        wide = grad[:, cols]
        narrow = wide.astype(jnp.bfloat16)
        skip_sums.append(jnp.sum(wide * tile.astype(jnp.float32), axis=0, keepdims=True))
        tile_sides = halves_of(tile)
        for part in range(parts):
            here = slice(part * SPAN, (part + 1) * SPAN)
            since = part * SPAN
            allowed = (row[here, since:] <= col[here, since:]) & (
                row[here, since:] >= starts[:, since:]
            )
            sides = []
            for side in range(2):
                h = 2 * i + side
                spread_log = cols_t[h : h + 1, since:] - cum[here, h : h + 1]
                decay = jnp.exp(jnp.where(allowed, spread_log, NEGATIVE_FILL))
                decay_dt = decay * dt[here, h : h + 1]
                mixing = products[here, since:] * decay_dt
                sides.append(dot(mixing.astype(jnp.bfloat16), narrow[since:]))
                d_mixing = dot_nt(tile_sides[side][here], narrow[since:])
                d_products[part] = d_products[part] + d_mixing * decay_dt
                whole = d_mixing * mixing
                d_rows[h : h + 1, since:] += jnp.sum(whole, axis=0, keepdims=True)
                weighed = d_mixing * (products[here, since:] * decay)
                step_sums[part] = jnp.where(
                    lane == h, jnp.sum(weighed, axis=1, keepdims=True), step_sums[part]
                )
            dx[here, cols] = (
                jnp.where(lane < MP, sides[0], sides[1]) + skip_row[:, cols] * wide[here]
            )
        if between is not None:
            between(i)
    all_steps = jnp.concatenate(step_sums, axis=0)
    d_dt[...] = all_steps
    d_cum[...] = d_rows[...].T - all_steps * dt[...]
    g_skip[...] = jnp.broadcast_to(
        two_part(
            jnp.broadcast_to(jnp.concatenate(skip_sums, axis=1), (8, width)), gather_heads(width)
        ),
        g_skip.shape,
    )
    full = jnp.concatenate(
        [
            d
            if p == 0
            else jnp.concatenate([jnp.zeros((SPAN, p * SPAN), jnp.float32), d], axis=1)
            for p, d in enumerate(d_products)
        ],
        axis=0,
    ).astype(jnp.bfloat16)
    d_bc[:, :NS] = dot(full, narrow_c)
    d_bc[:, NS:] = dot_tn(full, narrow_b)


def ssm_back(info, x, bc, dt, cum, grad, head_params):
    rows, width = x.shape
    f32 = jnp.float32
    return big_call(
        ssm_back_kernel,
        (
            shape_of((rows, width), f32),
            shape_of((rows, 2 * NS), f32),
            shape_of((rows, TILE), f32),
            shape_of((rows, TILE), f32),
            shape_of((8, TILE), f32),
        ),
        info,
        x,
        bc,
        dt,
        cum,
        grad,
        head_params,
        smem=1,
        scratch=(pltpu.VMEM((TILE, rows), f32), pltpu.VMEM((TILE, rows), f32)),
        flops=8 * rows * rows * width,
    )


def state_back_kernel(
    info, x, bc, dt, cum, grad, head_params, step_in, state_in, d_state, dx_in, d_bc_in, d_cum_in,
    d_dt_in, dx, d_bc, d_step, sums,
):
    rows, width = x.shape
    bias, rate = head_params[0:1], head_params[1:2]
    cums, steps = cum[...], dt[...]
    enter = entering_of(info, cums)
    last_start = seg_start(info[0] + rows - 1, info) - info[0]
    place = lax.broadcasted_iota(jnp.int32, (rows, 1), 0)
    end = cums[rows - 1 : rows]
    fade = jnp.where(place >= last_start, jnp.exp(jnp.minimum(end - cums, 0.0)), 0.0)
    leave = fade * steps
    through = jnp.where(last_start < 0, jnp.exp(end), 0.0)
    narrow_b, narrow_c = bc[:, :NS], bc[:, NS:]
    pick = gather_heads(width)
    d_leave = jnp.zeros((rows, TILE), jnp.float32)
    d_enter = jnp.zeros((rows, TILE), jnp.float32)
    d_b = d_bc_in[:, :NS]
    d_c = d_bc_in[:, NS:]
    link = jnp.zeros((8, TILE), jnp.float32)
    for i in range(MH // 2):
        cols = slice(i * TILE, (i + 1) * TILE)
        tile = x[:, cols].astype(jnp.float32)
        wide = grad[:, cols]
        pulled = d_state[:, cols]
        held = state_in[:, cols]
        from_b = dot(narrow_b, pulled)
        leave_tile = lane_pick(leave, 2 * i)
        dx[:, cols] = dx_in[:, cols] + leave_tile * from_b
        d_leave = d_leave + two_part(tile * from_b, pick[cols])
        d_enter = d_enter + two_part(wide * dot(narrow_c, held), pick[cols])
        d_b = d_b + dot_nt((tile * leave_tile).astype(jnp.bfloat16), pulled)
        d_c = d_c + dot_nt((wide * lane_pick(enter, 2 * i)).astype(jnp.bfloat16), held)
        meet = jnp.sum(
            pulled.astype(jnp.float32) * held.astype(jnp.float32), axis=0, keepdims=True
        )
        link = link + two_part(jnp.broadcast_to(meet, (8, TILE)), pick[cols])
    d_bc[:, :NS] = d_b
    d_bc[:, NS:] = d_c
    left = leave * d_leave
    d_cum = d_cum_in[...] + enter * d_enter - left
    at_end = jnp.sum(left, axis=0, keepdims=True) + through * link[:1]
    d_cum = d_cum + jnp.where(place == rows - 1, at_end, 0.0)
    row = lax.broadcasted_iota(jnp.int32, (rows, rows), 0)
    col = lax.broadcasted_iota(jnp.int32, (rows, rows), 1)
    d_log = exact(jnp.where(row <= col, 1.0, 0.0), d_cum)
    d_steps = d_dt_in[...] + fade * d_leave - d_log * rate
    d_pre = d_steps * jax.nn.sigmoid(step_in[...] + bias)
    d_pre = jnp.where(head_lanes(rows), d_pre, 0.0)
    d_step[...] = d_pre.astype(jnp.bfloat16)
    g_rate = jnp.sum(d_log * (-steps * rate), axis=0, keepdims=True)
    g_bias = jnp.sum(d_pre, axis=0, keepdims=True)
    line = lax.broadcasted_iota(jnp.int32, (8, TILE), 0)
    sums[...] = jnp.where(line == 0, g_rate, jnp.where(line == 1, g_bias, 0.0))


def state_back(info, *args):
    rows, width = args[0].shape
    f32 = jnp.float32
    return big_call(
        state_back_kernel,
        (
            shape_of((rows, width), f32),
            shape_of((rows, 2 * NS), f32),
            shape_of((rows, TILE), jnp.bfloat16),
            shape_of((8, TILE), f32),
        ),
        info,
        *args,
        smem=1,
        flops=12 * rows * NS * width,
    )


def join_states(earlier, later):
    decay = later[NS : NS + 1].astype(jnp.float32) + later[NS + 1 : NS + 2].astype(jnp.float32)
    before = earlier[NS : NS + 1].astype(jnp.float32) + earlier[NS + 1 : NS + 2].astype(jnp.float32)
    state = decay * earlier[:NS].astype(jnp.float32) + later[:NS].astype(jnp.float32)
    both = decay * before
    high = both.astype(jnp.bfloat16)
    low = (both - high.astype(jnp.float32)).astype(jnp.bfloat16)
    rest = jnp.zeros((STATE_ROWS - NS - 2, state.shape[1]), jnp.bfloat16)
    return jnp.concatenate([state.astype(jnp.bfloat16), high, low, rest], axis=0)


def scan_states(own, forward):
    place = lax.axis_index("seq")
    count = lax.axis_size("seq")
    nothing = jnp.concatenate(
        [
            jnp.zeros((NS, own.shape[1]), own.dtype),
            jnp.ones((1, own.shape[1]), own.dtype),
            jnp.zeros((STATE_ROWS - NS - 1, own.shape[1]), own.dtype),
        ],
        axis=0,
    )
    everything = lax.all_gather(own, "seq")

    def step(k, before):
        index = k if forward else count - 1 - k
        reached = index < place if forward else index > place
        part = lax.dynamic_index_in_dim(everything, index, 0, False)
        return jnp.where(reached, join_states(before, part), before)

    return lax.fori_loop(0, count, step, nothing)[:NS]


MESH = pl.DeviceIdType.MESH
ANY = pl.BlockSpec(memory_space=pl.ANY)
INTO_VMEM = pl.BlockSpec(memory_space=pltpu.VMEM)


def partners():
    seq, batch = lax.axis_index("seq"), lax.axis_index("batch")
    return {
        "far": (seq + 4 - 8 * (seq // 4), batch),
        "near": (seq + 2 - 4 * (seq // 2 % 2), batch),
        "x": (seq + 1 - 2 * (seq % 2), batch),
        "y": (seq, batch + 2 - 4 * (batch // 2)),
        "core": (seq, batch + 1 - 2 * (batch % 2)),
    }


def greet(others):
    barrier = pltpu.get_barrier_semaphore()
    for other in others:
        pl.semaphore_signal(barrier, inc=1, device_id=other, device_id_type=MESH)
    pl.semaphore_wait(barrier, len(others))


def remote(src, dst, send, recv, other):
    return pltpu.make_async_remote_copy(
        src_ref=src, dst_ref=dst, send_sem=send, recv_sem=recv, device_id=other, device_id_type=MESH
    )


def comm_call(kernel, outs, out_specs, args, in_specs, scratch, number, moved, limit=56):
    return pl.pallas_call(
        kernel,
        out_shape=list(outs),
        in_specs=in_specs,
        out_specs=out_specs,
        scratch_shapes=list(scratch),
        cost_estimate=pl.CostEstimate(flops=0, bytes_accessed=moved, transcendentals=0),
        compiler_params=pltpu.CompilerParams(
            collective_id=number, has_side_effects=True, vmem_limit_bytes=limit * 1024 * 1024
        ),
    )(*args)


def column_chunks(widths, aim=512, lean=0, z_last=None):
    pairs, late = [], []
    for p, width in enumerate(widths):
        tiles, first = width // TILE, 0
        orders, to = (("xyz", "yxz"), late) if p == z_last else (("xy", "yx"), pairs)
        count = max(1, (width + aim // 2) // (2 * aim)) if p != z_last else max(1, width // 512)
        for i in range(count):
            both = tiles // count + (1 if i < tiles % count else 0)
            one = (both + (0 if p == z_last else lean) + 1) // 2
            pair = []
            for cols, order in ((one * TILE, orders[0]), ((both - one) * TILE, orders[1])):
                pair.append((p, first, cols, order))
                first += cols
            to.append(tuple(pair))
    return pairs + late


def pairs_of(pairs, array):
    return [n for n, (one, other) in enumerate(pairs) if one[0] == array]


BITS = {"far": 1, "near": 2, "x": 4, "y": 8, "core": 16}
ORDERS = {
    "xy": ("far", "near", "x", "y"),
    "yx": ("far", "near", "y", "x"),
    "xyz": ("x", "y", "far", "near"),
    "yxz": ("y", "x", "far", "near"),
}


def runs(places):
    out = []
    for place in places:
        if out and out[-1][0] + out[-1][1] == place:
            out[-1] = (out[-1][0], out[-1][1] + 1)
        else:
            out.append((place, 1))
    return out


def gather_plan(order):
    held, plan = [0], []
    for name in ORDERS[order] + ("core",):
        plan.append((name, [(f, k, f + BITS[name]) for f, k in runs(held)]))
        held = sorted(held + [block + BITS[name] for block in held])
    return plan


def scatter_plan(order):
    held, plan = list(range(16)), []
    for name in reversed(ORDERS[order]):
        bit = BITS[name]
        sent = [i for i, block in enumerate(held) if block & bit]
        kept = [i for i, block in enumerate(held) if not block & bit]
        plan.append((name, runs(sent), runs(kept)))
        held = [held[i] for i in kept]
    return plan


def bit_apart(r):
    me = lax.axis_index("seq")
    far = (r // 4 + me // 4) % 2
    near = (r // 2 % 2 + me // 2 % 2) % 2
    side = (r % 2 + me % 2) % 2
    return 4 * far + 2 * near + side


def join_into(target, earlier, later):
    decay = later[NS : NS + 1].astype(jnp.float32) + later[NS + 1 : NS + 2].astype(jnp.float32)
    before = earlier[NS : NS + 1].astype(jnp.float32) + earlier[NS + 1 : NS + 2].astype(jnp.float32)
    both = decay * before
    high = both.astype(jnp.bfloat16).astype(jnp.float32)
    line = lax.broadcasted_iota(jnp.int32, (STATE_ROWS - NS, both.shape[1]), 0)
    tail = jnp.where(line == 0, high, jnp.where(line == 1, both - high, 0.0))
    for first in range(0, NS, 32):
        rows = slice(first, first + 32)
        target[rows] = (
            decay * earlier[rows].astype(jnp.float32) + later[rows].astype(jnp.float32)
        ).astype(jnp.bfloat16)
    target[NS:] = tail.astype(jnp.bfloat16)


SCAN_PARTS = 2


class StateScan:
    def __init__(self, forward, own, result, arrived, sent, before, send, recv, others):
        me = lax.axis_index("seq")
        self.seconds = []
        for bit in (me % 2, me // 2 % 2, me // 4):
            self.seconds.append(bit == 1 if forward else bit == 0)
        route = (others["x"], others["near"], others["far"])
        width = own.shape[1] // SCAN_PARTS
        self.parts = []
        for part in range(SCAN_PARTS):
            cols = pl.ds(part * width, width)
            here = (slice(None), cols)
            sources = (own.at[here], sent.at[0].at[here], sent.at[1].at[here])
            targets = [arrived.at[k].at[here] for k in range(3)]
            copies = [
                remote(sources[k], targets[k], send.at[k, part], recv.at[k, part], route[k])
                for k in range(3)
            ]
            befores = [before.at[k].at[here] for k in range(2)]
            self.parts.append((sources, targets, copies, befores, result.at[here]))

    def step(self, k):
        for part in self.parts:
            self.part_step(k, *part)

    def part_step(self, k, sources, targets, copies, before, result):
        if k == 0:
            copies[0].start()
            return
        copies[k - 1].wait_recv()
        other, mine = targets[k - 1], sources[k - 1]
        second = self.seconds[k - 1]

        @pl.when(second)
        def _():
            if k < 3:
                join_into(sources[k], other, mine)
            if k == 1:
                before[0][...] = other[...]
            elif k == 2:
                join_into(before[1], other, before[0])
            else:
                last = before[1]
                decay = last[NS : NS + 1].astype(jnp.float32) + last[NS + 1 : NS + 2].astype(
                    jnp.float32
                )
                result[...] = (
                    decay * other[:NS].astype(jnp.float32) + last[:NS].astype(jnp.float32)
                ).astype(jnp.bfloat16)

        @pl.when(jnp.logical_not(second))
        def _():
            if k < 3:
                join_into(sources[k], mine, other)
            if k == 1:
                line = lax.broadcasted_iota(jnp.int32, before[0].shape, 0)
                before[0][...] = jnp.where(line == NS, 1.0, 0.0).astype(jnp.bfloat16)
            elif k == 2:
                before[1][...] = before[0][...]
            else:
                result[...] = before[1][:NS]

        if k < 3:
            copies[k].start()

    def finish(self):
        for part in self.parts:
            for copy in part[2]:
                copy.wait_send()


def scan_scratch(width):
    rows = STATE_ROWS
    dma = pltpu.SemaphoreType.DMA
    narrow = jnp.bfloat16
    return [
        pltpu.VMEM((3, rows, width), narrow),
        pltpu.VMEM((2, rows, width), narrow),
        pltpu.VMEM((2, rows, width), narrow),
        dma((3, SCAN_PARTS)),
        dma((3, SCAN_PARTS)),
    ]


RIM = 8
COLS = 384


def own_order_into(target):
    width = target.shape[0]
    per = width // 32
    me = lax.axis_index("seq") * 4 + lax.axis_index("batch")
    step = 128

    def fill(i, carry):
        first = pl.multiple_of(i * step, step)
        row = lax.broadcasted_iota(jnp.int32, (step, width), 0) + first
        col = lax.broadcasted_iota(jnp.int32, (step, width), 1)
        j = col // per
        flipped = (j & 1) * 16 + (j & 2) * 4 + (j & 4) + (j & 8) // 4 + (j & 16) // 16
        source = (flipped ^ me) * per + col % per
        target[pl.ds(first, step)] = jnp.where(row == source, 1.0, 0.0).astype(target.dtype)
        return carry

    lax.fori_loop(0, width // step, fill, 0)


def three_part(left, right):
    high = left.astype(jnp.bfloat16)
    rest = left - high.astype(jnp.float32)
    mid = rest.astype(jnp.bfloat16)
    low = (rest - mid.astype(jnp.float32)).astype(jnp.bfloat16)
    return dot(high, right) + dot(mid, right) + dot(low, right)


def places_of(lens, rows):
    one, two, three = lens[0, 0], lens[0, 1], lens[0, 2]
    return [lax.axis_index("seq") * rows, one, one + two, one + two + three]


def head_rows(bias, rate_log, skip, target):
    lane = lax.broadcasted_iota(jnp.int32, (1, TILE), 1)
    for k, source in enumerate((bias, rate_log, skip)):
        row = jnp.zeros((1, TILE), jnp.float32)
        for h in range(MH):
            row = jnp.where(lane == h, source[h], row)
        if k == 1:
            row = jnp.where(lane < MH, jnp.exp(row), 0.0)
        target[k : k + 1] = row


def pair_columns(value, back):
    tiles = [value[:, i * TILE : (i + 1) * TILE] for i in range(PAIRS)]
    turned = [pltpu.roll(tile, HEAD_SIZE, 1) for tile in tiles]
    lane = lax.broadcasted_iota(jnp.int32, tiles[0].shape, 1)

    def head(i, side):
        return tiles[i // 2] if i % 2 == side else turned[i // 2]

    out = []
    for i in range(PAIRS):
        if back:
            first, second = 2 * i, 2 * i + 1
            group = QUERY_HEADS // KEY_VALUE_HEADS
            first, second = [2 * (h % group) + h // group for h in (first, second)]
        else:
            first, second = i, i + PAIRS
        out.append(jnp.where(lane < HEAD_SIZE, head(first, 0), head(second, 1)))
    return jnp.concatenate(out, axis=1)


def shards_into(w_attn, w_ssm_in, w_dt, w_out, conv, mix, out):
    f32, narrow = jnp.float32, jnp.bfloat16
    ssm_width = MH * MP
    xbc = w_ssm_in.shape[1] - ssm_width
    query = QUERY_HEADS * HEAD_SIZE
    attn = w_attn.shape[1]
    conv[:, :xbc] = w_ssm_in[:, ssm_width:]
    conv[:, xbc:] = jnp.zeros((conv.shape[0], TILE), narrow)
    block = conv.shape[0]
    row = lax.broadcasted_iota(jnp.int32, (block, block), 0)
    same = row == lax.broadcasted_iota(jnp.int32, (block, block), 1)
    conv[:, xbc : xbc + MH] = dot_nt(jnp.where(same, 1.0, 0.0).astype(narrow), w_dt[...]).astype(
        narrow
    )
    mix[:, :query] = pair_columns(w_attn[:, :query].astype(f32), False).astype(narrow)
    mix[:, query:attn] = w_attn[:, query:]
    mix[:, attn:] = w_ssm_in[:, :ssm_width]
    out[:, :query] = pair_columns(w_out[:, :query].astype(f32), False).astype(narrow)
    out[:, query:] = w_out[:, query:]


class Gather:
    def __init__(self, ins, outs, pairs, send, recv, local, others):
        self.ins, self.outs, self.pairs = ins, outs, pairs
        self.send, self.recv, self.local, self.others = send, recv, local, others
        self.started = {}
        self.block = ins[0].shape[0]

    def own(self):
        copies = []
        for p in range(len(self.ins)):
            copy = pltpu.make_async_copy(
                self.ins[p], self.outs[p].at[pl.ds(0, self.block)], self.local.at[p]
            )
            copy.start()
            copies.append(copy)
        for copy in copies:
            copy.wait()

    def step(self, n, stage):
        for side in range(2):
            p, column, cols, order = self.pairs[n][side]
            if stage > 0:
                for copy in self.started[n, side, stage - 1]:
                    copy.wait_recv()
            if stage == 5:
                continue
            name, moves = gather_plan(order)[stage]
            copies = []
            for k, (first, rows, there) in enumerate(moves):
                block = self.block
                copy = remote(
                    self.outs[p].at[pl.ds(first * block, rows * block), pl.ds(column, cols)],
                    self.outs[p].at[pl.ds(there * block, rows * block), pl.ds(column, cols)],
                    self.send.at[2 * n + side, stage, k],
                    self.recv.at[2 * n + side, stage, k],
                    self.others[name],
                )
                copy.start()
                copies.append(copy)
            self.started[n, side, stage] = copies

    def finish(self):
        for copies in self.started.values():
            for copy in copies:
                copy.wait_send()


def around():
    seq, batch = lax.axis_index("seq"), lax.axis_index("batch")
    return ((seq + 7) % 8, batch), ((seq + 1) % 8, batch)


def conv_masks(info, rows):
    at = lax.broadcasted_iota(jnp.int32, (rows, 1), 0) + info[0]
    start = seg_start(at, info)
    return [jnp.where(at - (CONV - 1) + i >= start, 1.0, 0.0) for i in range(CONV)]


def conv_forward(info, raw, conv_w, conv_b, pre, x, bc):
    rows = x.shape[0]
    masks = conv_masks(info, rows)
    tiles = pre.shape[1] // TILE
    split = x.shape[1] // TILE
    for i in range(tiles):
        cols = slice(i * TILE, (i + 1) * TILE)
        total = jnp.broadcast_to(conv_b[i : i + 1], (rows, TILE))
        for k in range(CONV):
            first = RIM - (CONV - 1) + k
            shifted_rows = jnp.where(masks[k] > 0.0, raw[first : first + rows, cols], 0.0)
            total = total + conv_w[k : k + 1, cols] * shifted_rows
        pre[:, cols] = total
        out = (total * jax.nn.sigmoid(total)).astype(jnp.bfloat16)
        if i < split:
            x[:, cols] = out
        else:
            bc[:, (i - split) * TILE : (i - split + 1) * TILE] = out


def front_kernel(
    count, pairs, lens, bias, rate_log, skip, layer_x, layer_g, norm_gain, mlp_gain, freqs, conv_w,
    conv_b, w_attn, w_ssm_in, w_dt, w_out, w_gate_up, w_down, *refs
):
    fulls, refs = refs[:count], refs[count:]
    (
        x_own, g_own, gains_own, normed, q, kv, gate_z, raw, pre, x, bc, y, state, dt, cum,
        out, out_t, lse, state_in, order, cosine, sine, head_params,
    ) = refs[:23]
    (
        s_conv, s_mix, s_out, gains,
        attn_proj, dt_t, cum_t, heads, acc, top, total, arrived, sent, before,
        scan_send, scan_recv, send, recv, w_send, w_recv, w_local, rim_send, rim_recv,
    ) = refs[23:]
    ins = (s_conv, s_mix, s_out, w_gate_up, w_down)
    others = partners()
    previous, following = around()
    greet(list(others.values()) + [previous, following])
    me = lax.axis_index("seq")
    rows, width = layer_x.shape
    info = places_of(lens, rows)
    shards_into(w_attn, w_ssm_in, w_dt, w_out, s_conv, s_mix, s_out)
    gather = Gather(ins, fulls, pairs, w_send, w_recv, w_local, others)
    gather.own()

    first = len(pairs_of(pairs, 0)) + len(pairs_of(pairs, 1))
    small = pairs_of(pairs, 2)
    waves = {}
    for n in reversed(range(len(pairs))):
        for stage in range(6):
            late = 1 if n >= first and stage >= 2 else 0
            wave = n - small[0] + 2 * stage if n in small else n + stage + late
            waves.setdefault(wave, []).append((n, stage))

    def pump(*which):
        for wave in which:
            for n, stage in waves.pop(wave, []):
                gather.step(n, stage)

    conv_wave = pairs_of(pairs, 0)[-1] + 5
    mix_wave = pairs_of(pairs, 1)[-1] + 5
    pump(0)
    own_order_into(order)
    head_rows(bias, rate_log, skip, head_params)
    gains[...] = jnp.zeros_like(gains)
    for k, source in enumerate((norm_gain, mlp_gain)):
        for i in range(width // TILE):
            gains[k : k + 1, i * TILE : (i + 1) * TILE] = source[i : i + 1]
    pump(1)
    at = lax.broadcasted_iota(jnp.int32, (rows, 1), 0) + info[0]
    angles = (at - seg_start(at, info)).astype(jnp.float32) * freqs[...]
    cosine[...] = jnp.cos(angles)
    sine[...] = jnp.sin(angles)
    x_own[...] = dot(layer_x[...], order[...]).astype(jnp.bfloat16)
    pump(2)
    gains_own[...] = three_part(gains[...], order[...])
    wide = x_own[...].astype(jnp.float32)
    scale = lax.rsqrt(jnp.mean(wide * wide, axis=-1, keepdims=True) + NORM_EPS)
    normed[...] = (wide * scale * gains_own[0:1]).astype(jnp.bfloat16)
    pump(3)
    g_own[...] = dot(layer_g[...], order[...]).astype(jnp.bfloat16)
    pump(*range(4, conv_wave + 1))

    full_conv, full_mix = fulls[0], fulls[1]
    xbc = pre.shape[1]
    conv_cols = full_conv.shape[1] // COLS
    attn_cols = attn_proj.shape[1] // COLS
    gate_cols = gate_z.shape[1] // COLS

    def project(weights, first, target, row, count_cols):
        def one(j, carry):
            cols = pl.ds(pl.multiple_of(j * COLS, TILE), COLS)
            there = pl.ds(pl.multiple_of(first + j * COLS, TILE), COLS)
            target[row : row + rows, cols] = dot(normed[...], weights[:, there])
            return carry

        lax.fori_loop(0, count_cols, one, 0)

    def at(r):
        return kv.at[pl.ds(r * rows, rows)]

    routes = {4: ("far", 0), 2: ("near", 0), 6: ("near", 4)}
    routes.update({r: ("x", r - 1) for r in (1, 3, 5, 7)})
    copies = {
        r: remote(at(src), at(r), send.at[r], recv.at[r], others[name])
        for r, (name, src) in routes.items()
    }
    project(full_conv, 0, raw, RIM, conv_cols)
    rim = remote(
        raw.at[pl.ds(rows, RIM)], raw.at[pl.ds(0, RIM)], rim_send.at[0], rim_recv.at[0], following
    )
    rim.start()
    pump(*range(conv_wave + 1, mix_wave))
    rim.wait_recv()
    conv_forward(info, raw, conv_w, conv_b, pre, x, bc)
    step_in = raw.at[pl.ds(RIM, rows), pl.ds(xbc, TILE)]
    ssm_states(info, x, bc, step_in, head_params, state, dt, cum, dt_t, cum_t)
    scan = StateScan(True, state, state_in, arrived, sent, before, scan_send, scan_recv, others)
    scan.step(0)
    pump(mix_wave)
    project(full_mix, 0, attn_proj, 0, attn_cols)
    rope_kernel(attn_proj, cosine, sine, q, kv.at[pl.ds(0, rows)])
    copies[4].start()
    copies[2].start()
    copies[1].start()
    pump(mix_wave + 1)
    project(full_mix, attn_proj.shape[1], gate_z, 0, gate_cols)
    attend_start(q, heads, acc, top, total)

    def attend(r):
        block = bit_apart(r)

        @pl.when(block <= me)
        def _():
            place = pl.ds(pl.multiple_of(r * rows, rows), rows)
            keys = kv[place, :TILE]
            values_t = kv[place, TILE:].astype(jnp.float32).T.astype(jnp.bfloat16)
            attend_block(info, block, keys, values_t, heads, acc, top, total)

    def several(first, gap, count_blocks):
        def body(j, carry):
            attend(first + j * gap)
            return carry

        lax.fori_loop(0, count_blocks, body, 0)

    scan.step(1)
    copies[4].wait_recv()
    copies[6].start()
    copies[5].start()
    copies[2].wait_recv()
    copies[3].start()
    copies[6].wait_recv()
    copies[7].start()
    pump(mix_wave + 2)
    several(0, 4, 2)
    pump(mix_wave + 3)
    ssm_local(info, x, bc, head_params, y, cum, dt_t, cum_t)
    scan.step(2)
    pump(mix_wave + 4)
    several(2, 4, 2)
    pump(mix_wave + 5)
    for r in (1, 3, 5, 7):
        copies[r].wait_recv()
    several(1, 2, 2)
    pump(mix_wave + 6)
    several(5, 2, 2)
    pump(mix_wave + 7)
    lse[...] = top[...] + jnp.log(total[...])
    attend_write(acc, total, out, out_t)
    scan.step(3)
    pump(*sorted(waves))
    gather.finish()
    scan.finish()
    rim.wait_send()
    for copy in copies.values():
        copy.wait_send()


def front(lens, bias, rate_log, skip, layer_x, layer_g, norm_gain, mlp_gain, freqs, conv_w, conv_b, weights):
    w_attn, w_ssm_in, w_dt, w_out, w_gate_up, w_down = weights
    rows, width = layer_x.shape
    f32, narrow = jnp.float32, jnp.bfloat16
    block = w_attn.shape[0]
    query_width = QUERY_HEADS * HEAD_SIZE
    pair_width = 2 * KEY_VALUE_HEADS * HEAD_SIZE
    ssm_width = MH * MP
    xbc = conv_w.shape[1]
    widths = [
        xbc + TILE, w_attn.shape[1] + ssm_width, w_out.shape[1], w_gate_up.shape[1],
        w_down.shape[1],
    ]
    count = len(widths)
    pairs = column_chunks(widths, z_last=2)
    fulls = [shape_of((width, w), narrow) for w in widths]
    outs = fulls + [
        shape_of((rows, width), narrow),
        shape_of((rows, width), narrow),
        shape_of((8, width), f32),
        shape_of((rows, width), narrow),
        shape_of((rows, query_width), narrow),
        shape_of((8 * rows, pair_width), narrow),
        shape_of((rows, ssm_width), f32),
        shape_of((rows + RIM, widths[0]), f32),
        shape_of((rows, xbc), f32),
        shape_of((rows, ssm_width), narrow),
        shape_of((rows, 2 * NS), narrow),
        shape_of((rows, ssm_width), f32),
        shape_of((STATE_ROWS, ssm_width), narrow),
        shape_of((rows, TILE), f32),
        shape_of((rows, TILE), f32),
        shape_of((rows, query_width), narrow),
        shape_of((query_width, rows), f32),
        shape_of((QUERY_HEADS, rows), f32),
        shape_of((NS, ssm_width), narrow),
        shape_of((width, width), narrow),
        shape_of((rows, TILE), f32),
        shape_of((rows, TILE), f32),
        shape_of((8, TILE), f32),
    ]
    dma = pltpu.SemaphoreType.DMA
    scratch = [
        *(pltpu.VMEM((block, widths[k]), narrow) for k in (0, 1, 2)),
        pltpu.VMEM((8, width), f32),
        pltpu.VMEM((rows, query_width + pair_width), f32),
        pltpu.VMEM((TILE, rows), f32),
        pltpu.VMEM((TILE, rows), f32),
        pltpu.VMEM((QUERY_HEADS, rows, TILE), narrow),
        pltpu.VMEM((QUERY_HEADS, HEAD_SIZE, rows), f32),
        pltpu.VMEM((QUERY_HEADS, rows), f32),
        pltpu.VMEM((QUERY_HEADS, rows), f32),
        *scan_scratch(ssm_width),
        dma((8,)),
        dma((8,)),
        dma((2 * len(pairs), 5, 4)),
        dma((2 * len(pairs), 5, 4)),
        dma((count,)),
        dma((1,)),
        dma((1,)),
    ]
    result = comm_call(
        lambda *refs: front_kernel(count, pairs, *refs),
        outs,
        [INTO_VMEM] * 2 + [ANY] * (count - 2) + [INTO_VMEM] * 23,
        (
            lens, bias, rate_log, skip, layer_x, layer_g, norm_gain, mlp_gain, freqs, conv_w,
            conv_b, *weights,
        ),
        [pl.BlockSpec(memory_space=pltpu.SMEM)] * 4 + [INTO_VMEM] * 13,
        scratch,
        0,
        200_000_000,
    )
    return result[:count], result[count:]


def middle_kernel(
    lens, y, bc, cum, state_in, state_own, z, ssm_gain, attended, x_own, g_own, gains, order,
    hbm_out, hbm_gu, hbm_down,
    layer_out, joined, hidden, d_gu, normed_two, d_mixer, d_middle, d_ssm, d_z, pull, att_grad,
    g_ssm, g_mlp,
    w_out, w_gu, w_down, ssm_out, scale, middle, gate_up, d_normed, dy, narrow, sems,
):
    rows, width = x_own.shape
    info = places_of(lens, rows)
    copies = [
        pltpu.make_async_copy(src, dst, sems.at[k])
        for k, (src, dst) in enumerate(((hbm_out, w_out), (hbm_gu, w_gu), (hbm_down, w_down)))
    ]
    for copy in copies:
        copy.start()
    attn = attended.shape[1]
    ff = hidden.shape[1]
    step = 512

    def tiles(count, body):
        def one(j, carry):
            body(pl.ds(pl.multiple_of(j * step, step), step), j * step)
            return carry

        lax.fori_loop(0, count // step, one, 0)

    joined[:, :attn] = attended[...]
    ssm_finish_kernel(
        info, y, bc, cum, state_in, z, ssm_gain, ssm_out,
        joined.at[:, pl.ds(attn, joined.shape[1] - attn)], scale,
    )
    copies[0].wait()

    def add_mixers(here, first):
        middle[:, here] = x_own[:, here].astype(jnp.float32) + dot_nt(joined[...], w_out[here])

    tiles(width, add_mixers)
    wide = middle[...]
    r = lax.rsqrt(jnp.mean(wide * wide, axis=-1, keepdims=True) + NORM_EPS)
    normed_two[...] = (wide * r * gains[1:2]).astype(jnp.bfloat16)
    copies[1].wait()

    def up_project(here, first):
        there = pl.ds(pl.multiple_of(ff + first, step), step)
        gate = dot(normed_two[...], w_gu[:, here])
        up = dot(normed_two[...], w_gu[:, there])
        gate_up[:, here] = gate
        gate_up[:, there] = up
        hidden[:, here] = (gate * jax.nn.sigmoid(gate) * up).astype(jnp.bfloat16)

    tiles(ff, up_project)
    copies[2].wait()

    def down_project(here, first):
        narrow[:, here] = (middle[:, here] + dot_nt(hidden[...], w_down[here])).astype(jnp.bfloat16)

    tiles(width, down_project)

    def plain(here, first):
        layer_out[:, here] = dot_nt(narrow[...], order[here]).astype(jnp.bfloat16)

    tiles(width, plain)

    def down_back(here, first):
        there = pl.ds(pl.multiple_of(ff + first, step), step)
        d_hidden = dot(g_own[...], w_down[:, here])
        gate, up = gate_up[:, here], gate_up[:, there]
        sig = jax.nn.sigmoid(gate)
        d_gate = d_hidden * up * (sig * (1.0 + gate * (1.0 - sig)))
        d_gu[:, here] = d_gate.astype(jnp.bfloat16)
        d_gu[:, there] = (d_hidden * gate * sig).astype(jnp.bfloat16)

    tiles(ff, down_back)

    def up_back(here, first):
        d_normed[:, here] = dot_nt(d_gu[...], w_gu[here])

    tiles(width, up_back)
    grads = d_normed[...]
    wide = middle[...]
    g_mlp[...] = jnp.sum(grads * wide * r, axis=0, keepdims=True)
    inner = grads * gains[1:2]
    coeff = jnp.mean(inner * wide, axis=-1, keepdims=True)
    total = g_own[...].astype(jnp.float32) + r * (inner - wide * (r * r * coeff))
    d_middle[...] = total
    d_mixer[...] = total.astype(jnp.bfloat16)

    def att_back(here, first):
        att_grad[:, here] = dot(d_mixer[...], w_out[:, here]).astype(jnp.bfloat16)

    tiles(attn, att_back)

    def ssm_part(here, first):
        there = pl.ds(pl.multiple_of(attn + first, step), step)
        dy[:, here] = dot(d_mixer[...], w_out[:, there])

    tiles(dy.shape[1], ssm_part)
    gate_back_kernel(
        info, dy, ssm_out, z, scale, ssm_gain, cum, bc, d_ssm, d_z, pull.at[pl.ds(0, NS)], g_ssm
    )
    pull[NS:] = state_own[NS:]


def middle_part(lens, y, bc, cum, state_in, state_own, z, ssm_gain, attended, x_own, g_own, gains, order, w_out, w_gu, w_down):
    rows, width = x_own.shape
    ssm_width, attn = y.shape[1], attended.shape[1]
    ff = w_down.shape[1]
    f32, narrow = jnp.float32, jnp.bfloat16
    outs = [
        shape_of((rows, width), narrow),
        shape_of((rows, attn + ssm_width), narrow),
        shape_of((rows, ff), narrow),
        shape_of((rows, 2 * ff), narrow),
        shape_of((rows, width), narrow),
        shape_of((rows, width), narrow),
        shape_of((rows, width), f32),
        shape_of((rows, ssm_width), f32),
        shape_of((rows, ssm_width), narrow),
        shape_of((STATE_ROWS, ssm_width), narrow),
        shape_of((rows, attn), narrow),
        shape_of(ssm_gain.shape, f32),
        shape_of((1, width), f32),
    ]
    args = (
        lens, y, bc, cum, state_in, state_own, z, ssm_gain, attended, x_own, g_own, gains, order,
        w_out, w_gu, w_down,
    )
    return pl.pallas_call(
        middle_kernel,
        out_shape=outs,
        in_specs=[pl.BlockSpec(memory_space=pltpu.SMEM)] + [INTO_VMEM] * 12 + [ANY] * 3,
        out_specs=[INTO_VMEM] * len(outs),
        scratch_shapes=[
            pltpu.VMEM(w_out.shape, narrow),
            pltpu.VMEM(w_gu.shape, narrow),
            pltpu.VMEM(w_down.shape, narrow),
            pltpu.VMEM((rows, ssm_width), f32),
            pltpu.VMEM((rows, TILE), f32),
            pltpu.VMEM((rows, width), f32),
            pltpu.VMEM((rows, 2 * ff), f32),
            pltpu.VMEM((rows, width), f32),
            pltpu.VMEM((rows, ssm_width), f32),
            pltpu.VMEM((rows, width), narrow),
            pltpu.SemaphoreType.DMA((3,)),
        ],
        compiler_params=pltpu.CompilerParams(vmem_limit_bytes=60 * 1024 * 1024),
    )(*args)


def turn_over(value):
    return value.astype(jnp.float32).T.astype(jnp.bfloat16)


class Scatter:
    def __init__(self, ins, outs, arrived, pairs, send, recv, others):
        self.ins, self.outs, self.arrived, self.pairs = ins, outs, arrived, pairs
        self.send, self.recv, self.others = send, recv, others
        self.block = ins[0].shape[0] // 16
        self.started = {}

    def source(self, p, stage):
        return self.ins[p] if stage == 0 else self.arrived[4 * p + stage - 1]

    def step(self, n, stage):
        for side in range(2):
            if stage > 0:
                self.take(n, side, stage - 1)
            if stage < 4:
                self.begin(n, side, stage)

    def begin(self, n, side, stage):
        p, column, width, order = self.pairs[n][side]
        cols = pl.ds(column, width)
        name, sent, unused_kept = scatter_plan(order)[stage]
        copies, row, block = [], 0, self.block
        for k, (first, count) in enumerate(sent):
            copy = remote(
                self.source(p, stage).at[pl.ds(first * block, count * block), cols],
                self.arrived[4 * p + stage].at[pl.ds(row * block, count * block), cols],
                self.send.at[2 * n + side, stage, k],
                self.recv.at[2 * n + side, stage, k],
                self.others[name],
            )
            copy.start()
            copies.append(copy)
            row += count
        self.started[n, side, stage] = copies

    def take(self, n, side, stage):
        p, column, width, order = self.pairs[n][side]
        cols = slice(column, column + width)
        source, got = self.source(p, stage), self.arrived[4 * p + stage]
        target = self.outs[p] if stage == 3 else got
        unused_name, unused_sent, kept = scatter_plan(order)[stage]
        row, block = 0, self.block
        for k, (first, count) in enumerate(kept):
            self.started[n, side, stage][k].wait_recv()

            def add(i, carry):
                at = pl.multiple_of(i * block, block)
                there = pl.ds(row * block + at, block)
                total = source[pl.ds(first * block + at, block), cols].astype(jnp.float32) + got[
                    there, cols
                ].astype(jnp.float32)
                target[there, cols] = total.astype(target.dtype)
                return carry

            lax.fori_loop(0, count, add, 0)
            row += count

    def finish(self):
        for copies in self.started.values():
            for copy in copies:
                copy.wait_send()


def scatter_scratch(widths, size):
    scratch = []
    for width in widths:
        scratch += [pltpu.VMEM((size >> (s + 1), width), jnp.bfloat16) for s in range(4)]
    return scratch


def weight_products(left_t, right, theirs, target):
    rows = right.shape[0]
    step = 256 if right.shape[1] % 256 == 0 else TILE

    def one(j, carry):
        cols = pl.ds(pl.multiple_of(j * step, step), step)
        product = dot(left_t[:, :rows], right[:, cols]) + dot(left_t[:, rows:], theirs[:, cols])
        target[:, cols] = product.astype(target.dtype)
        return carry

    lax.fori_loop(0, right.shape[1] // step, one, 0)


def conv_back_start(info, dx, d_bc, pre, raw, d_pre, g_conv):
    rows, split = dx.shape[0], dx.shape[1] // TILE
    masks = conv_masks(info, rows)
    g_conv[...] = jnp.zeros_like(g_conv)
    for i in range(pre.shape[1] // TILE):
        cols = slice(i * TILE, (i + 1) * TILE)
        if i < split:
            grad = dx[:, cols]
        else:
            grad = d_bc[:, (i - split) * TILE : (i - split + 1) * TILE]
        value = pre[:, cols]
        sig = jax.nn.sigmoid(value)
        grad = grad * (sig * (1.0 + value * (1.0 - sig)))
        d_pre[:rows, cols] = grad
        for k in range(CONV):
            first = RIM - (CONV - 1) + k
            term = jnp.where(masks[k] > 0.0, raw[first : first + rows, cols], 0.0)
            g_conv[k : k + 1, cols] = jnp.sum(grad * term, axis=0, keepdims=True)
        g_conv[CONV : CONV + 1, cols] = jnp.sum(grad, axis=0, keepdims=True)


def conv_back_end(info, d_pre, conv_w, d_raw):
    rows = d_raw.shape[0]
    at = lax.broadcasted_iota(jnp.int32, (rows, 1), 0) + info[0]
    masks = [
        jnp.where(seg_start(at + (CONV - 1) - k, info) <= at, 1.0, 0.0) for k in range(CONV)
    ]
    for i in range(d_pre.shape[1] // TILE):
        cols = slice(i * TILE, (i + 1) * TILE)
        total = jnp.zeros((rows, TILE), jnp.float32)
        for k in range(CONV):
            first = CONV - 1 - k
            part = jnp.where(masks[k] > 0.0, d_pre[first : first + rows, cols], 0.0)
            total = total + conv_w[k : k + 1, cols] * part
        d_raw[:, cols] = total.astype(jnp.bfloat16)


def back_kernel(pairs, *refs):
    (
        lens, head_params, conv_w, cosine, sine, q, kv, grad, out_t, lse, pull, x, bc, dt, cum,
        d_ssm, raw, state_in, pre, normed, normed_two, d_mixer, grad_rows, hidden, joined, d_gu,
        d_z,
    ) = refs[:27]
    (
        d_conv, d_attn, g_conv, head_sums, g_skip, their_normed, out_down, out_gu, out_out, out_z,
    ) = refs[27:37]
    refs = refs[37:]
    partials, refs = refs[:4], refs[4:]
    arrived_w, refs = refs[:16], refs[16:]
    (
        half_grad, half_two, half_mixer, their_hidden, their_joined, their_gu, their_z, left_t,
        heads, grads, delta, acc, dkv, from_x, from_far, from_near, dq, d_pair, d_state,
        dx, d_bc, d_cum, d_dt, cols_t, d_rows, d_pre,
        arrived, sent, before, scan_send, scan_recv, send, recv, swap_send, swap_recv,
        w_send, w_recv, rim_send, rim_recv,
    ) = refs
    others = partners()
    previous, following = around()
    greet(list(others.values()) + [previous, following])
    me = lax.axis_index("seq")
    rows = q.shape[0]
    info = places_of(lens, rows)
    half = normed.shape[1] // 2
    xbc = pre.shape[1]
    scan = StateScan(False, pull, d_state, arrived, sent, before, scan_send, scan_recv, others)
    scan.step(0)
    behind = pl.ds(half, half)
    given = [
        (grad_rows.at[:, behind], half_grad),
        (hidden, their_hidden),
        (d_mixer.at[:, behind], half_mixer),
        (joined, their_joined),
        (normed_two.at[:, behind], half_two),
        (d_gu, their_gu),
        (normed.at[:, behind], their_normed),
        (d_z, their_z),
    ]
    swaps = [
        remote(give, take, swap_send.at[k], swap_recv.at[k], others["core"])
        for k, (give, take) in enumerate(given)
    ]
    for copy in swaps:
        copy.start()
    scatter = Scatter(
        partials, (out_down, out_gu, out_out, out_z), arrived_w, pairs, w_send, w_recv, others
    )

    def weights(k, left, left_half, right, theirs):
        first = 2 * (0, 2, 1, 3)[k]
        swaps[first].wait_recv()
        swaps[first + 1].wait_recv()
        left_t[:, :rows] = turn_over(left[:, :half])
        left_t[:, rows:] = turn_over(left_half[...])
        weight_products(left_t, right, theirs, partials[k])

    small = pairs_of(pairs, 2)
    waves = {}
    for n in range(len(pairs)):
        for stage in range(5):
            begin = n - small[0] if n in small else n
            waves.setdefault(begin + stage, []).append((n, stage))

    def pump(wave):
        for n, stage in waves.pop(wave):
            scatter.step(n, stage)

    attend_back_start(q, grad, out_t, heads, grads, delta, acc)

    def block_back(r):
        block = bit_apart(r)
        place = pl.ds(pl.multiple_of(r * rows, rows), rows)

        @pl.when(block <= me)
        def _():
            attend_back_block(
                info, block, kv[place, :TILE], kv[place, TILE:], lse, dkv.at[r], heads, grads,
                delta, acc,
            )

        @pl.when(block > me)
        def _():
            dkv[r] = jnp.zeros(dkv.shape[1:], dkv.dtype)

    def several(first, gap, count):
        def body(j, carry):
            block_back(first + j * gap)
            return carry

        lax.fori_loop(0, count, body, 0)

    def add(target, source):
        target[...] = (target[...].astype(jnp.float32) + source[...].astype(jnp.float32)).astype(
            jnp.bfloat16
        )

    weights(0, grad_rows, half_grad, hidden, their_hidden)
    weights(2, d_mixer, half_mixer, joined, their_joined)
    pump(0)
    several(1, 2, 4)
    over_x = [
        remote(dkv.at[2 * k + 1], from_x.at[k], send.at[k], recv.at[k], others["x"])
        for k in range(4)
    ]
    for copy in over_x:
        copy.start()
    scan.step(1)
    weights(1, normed_two, half_two, d_gu, their_gu)
    pump(1)
    several(4, 2, 2)
    over_far = [
        remote(dkv.at[4 + 2 * k], from_far.at[k], send.at[4 + k], recv.at[4 + k], others["far"])
        for k in range(2)
    ]
    for k in range(2):
        over_x[2 + k].wait_recv()
        add(dkv.at[4 + 2 * k], from_x.at[2 + k])
        over_far[k].start()
    scan.step(2)
    pump(2)
    several(0, 2, 2)
    for k in range(2):
        over_x[k].wait_recv()
        add(dkv.at[2 * k], from_x.at[k])
    over_far[1].wait_recv()
    add(dkv.at[2], from_far.at[1])
    over_near = remote(dkv.at[2], from_near, send.at[6], recv.at[6], others["near"])
    over_near.start()
    weights(3, normed, their_normed, d_z, their_z)
    pump(3)
    ssm_back_kernel(
        info, x, bc, dt, cum, d_ssm, head_params, dx, d_bc, d_cum, d_dt, g_skip, cols_t, d_rows
    )
    pump(4)
    scan.step(3)
    d_step = d_conv.at[:, pl.ds(xbc, TILE)]
    step_in = raw.at[pl.ds(RIM, rows), pl.ds(xbc, TILE)]
    state_back_kernel(
        info, x, bc, dt, cum, d_ssm, head_params, step_in, state_in, d_state, dx, d_bc, d_cum,
        d_dt, dx, d_bc, d_step, head_sums,
    )
    conv_back_start(info, dx, d_bc, pre, raw, d_pre, g_conv)
    rim = remote(
        d_pre.at[pl.ds(0, RIM)], d_pre.at[pl.ds(rows, RIM)], rim_send.at[0], rim_recv.at[0],
        previous,
    )
    rim.start()
    pump(5)
    over_far[0].wait_recv()
    over_near.wait_recv()
    attend_back_write(acc, dq)
    d_pair[...] = (
        dkv[0].astype(jnp.float32)
        + from_far[0].astype(jnp.float32)
        + from_near[...].astype(jnp.float32)
    )
    rope_back_kernel(dq, d_pair, cosine, sine, d_attn)
    rim.wait_recv()
    conv_back_end(info, d_pre, conv_w, d_conv.at[:, pl.ds(0, xbc)])
    for wave in sorted(waves):
        pump(wave)
    scatter.finish()
    scan.finish()
    rim.wait_send()
    for copy in over_x + over_far + [over_near] + swaps:
        copy.wait_send()


def back(lens, *args):
    (
        head_params, conv_w, cosine, sine, q, kv, grad, out_t, lse, pull, x, bc, dt, cum,
        d_ssm, raw, state_in, pre, normed, normed_two, d_mixer, grad_rows, hidden, joined, d_gu,
        d_z,
    ) = args
    rows, query_width = q.shape
    width = normed.shape[1]
    half = width // 2
    pair = kv.shape[1]
    ssm_width, xbc = x.shape[1], pre.shape[1]
    f32, narrow = jnp.float32, jnp.bfloat16
    dma = pltpu.SemaphoreType.DMA
    widths = [hidden.shape[1], d_gu.shape[1], joined.shape[1], d_z.shape[1]]
    pairs = column_chunks(widths, 1024, 4, 2)
    own = half // 16
    outs = [
        shape_of((rows, xbc + TILE), narrow),
        shape_of((rows, query_width + pair), narrow),
        shape_of((8, xbc), f32),
        shape_of((8, TILE), f32),
        shape_of((8, TILE), f32),
        shape_of((rows, half), narrow),
    ] + [shape_of((own, w), f32) for w in widths]
    scratch = [pltpu.VMEM((half, w), narrow) for w in widths]
    scratch += scatter_scratch(widths, half)
    scratch += [pltpu.VMEM((rows, half), narrow)] * 3
    scratch += [pltpu.VMEM(a.shape, narrow) for a in (hidden, joined, d_gu, d_z)]
    scratch += [
        pltpu.VMEM((half, 2 * rows), narrow),
        pltpu.VMEM((QUERY_HEADS, rows, TILE), narrow),
        pltpu.VMEM((QUERY_HEADS, rows, TILE), narrow),
        pltpu.VMEM((QUERY_HEADS, rows), f32),
        pltpu.VMEM((QUERY_HEADS, HEAD_SIZE, rows), f32),
        pltpu.VMEM((8, rows, pair), narrow),
        pltpu.VMEM((4, rows, pair), narrow),
        pltpu.VMEM((2, rows, pair), narrow),
        pltpu.VMEM((rows, pair), narrow),
        pltpu.VMEM((rows, query_width), f32),
        pltpu.VMEM((rows, pair), f32),
        pltpu.VMEM((NS, ssm_width), narrow),
        pltpu.VMEM((rows, ssm_width), f32),
        pltpu.VMEM((rows, 2 * NS), f32),
        pltpu.VMEM((rows, TILE), f32),
        pltpu.VMEM((rows, TILE), f32),
        pltpu.VMEM((TILE, rows), f32),
        pltpu.VMEM((TILE, rows), f32),
        pltpu.VMEM((rows + RIM, xbc), f32),
        *scan_scratch(ssm_width),
        dma((7,)),
        dma((7,)),
        dma((8,)),
        dma((8,)),
        dma((2 * len(pairs), 4, 4)),
        dma((2 * len(pairs), 4, 4)),
        dma((1,)),
        dma((1,)),
    ]
    return comm_call(
        lambda *refs: back_kernel(pairs, *refs),
        outs,
        [INTO_VMEM] * len(outs),
        (lens, *args),
        [pl.BlockSpec(memory_space=pltpu.SMEM)] + [INTO_VMEM] * len(args),
        scratch,
        2,
        200_000_000,
        limit=62,
    )


def dot_nt_two(left, right):
    high = left.astype(jnp.bfloat16)
    low = (left - high.astype(jnp.float32)).astype(jnp.bfloat16)
    return dot_nt(high, right) + dot_nt(low, right)


def last_kernel(pairs, *refs):
    (
        d_conv, d_attn, d_z, full_conv, full_mix, normed, their_normed, x_own, d_middle, gains,
        order, g_mlp, g_ssm, g_conv, head_sums, g_skip, sum_out, sum_z,
    ) = refs[:18]
    (
        input_grad, g_attn_out, g_in_out, g_dt_out, g_out_out,
        norm_total, mlp_total, ssm_total, conv_total, conv_b_total, head_total,
    ) = refs[18:29]
    refs = refs[29:]
    partials, arrived_w = refs[:2], refs[2:10]
    (
        out_conv, out_attn, their_conv, their_attn, left_t, d_normed, small_own, small_in, small_mid,
        small_out, swap_send, swap_recv, w_send, w_recv, small_send, small_recv,
    ) = refs[10:]
    others = partners()
    greet(list(others.values()))
    rows, width = normed.shape
    half = width // 2
    swaps = [
        remote(give, take, swap_send.at[k], swap_recv.at[k], others["core"])
        for k, (give, take) in enumerate(((d_conv, their_conv), (d_attn, their_attn)))
    ]
    for copy in swaps:
        copy.start()
    scatter = Scatter(partials, (out_conv, out_attn), arrived_w, pairs, w_send, w_recv, others)
    left_t[:, :rows] = turn_over(normed[:, :half])
    left_t[:, rows:] = turn_over(their_normed[...])
    swaps[0].wait_recv()
    weight_products(left_t, d_conv, their_conv, partials[0])
    scatter.step(0, 0)
    scatter.step(1, 0)
    swaps[1].wait_recv()
    weight_products(left_t, d_attn, their_attn, partials[1])
    scatter.step(2, 0)
    step = 256
    attn = d_attn.shape[1]

    def back_out(j, carry):
        here = pl.ds(pl.multiple_of(j * step, step), step)
        d_normed[:, here] = (
            dot_nt(d_conv[...], full_conv[here])
            + dot_nt(d_attn[...], full_mix[here, :attn])
            + dot_nt(d_z[...], full_mix[here, attn:])
        )
        return carry

    lax.fori_loop(0, width // step, back_out, 0)
    scatter.step(0, 1)
    scatter.step(1, 1)
    wide = x_own[...].astype(jnp.float32)
    r = lax.rsqrt(jnp.mean(wide * wide, axis=-1, keepdims=True) + NORM_EPS)
    grads = d_normed[...]
    g_norm = jnp.sum(grads * wide * r, axis=0, keepdims=True)
    line = lax.broadcasted_iota(jnp.int32, (8, width), 0)
    both = jnp.where(line == 0, g_norm, jnp.where(line == 1, g_mlp[...], 0.0))
    both = dot_nt_two(both, order[...])
    small_own[16:] = jnp.zeros((small_own.shape[0] - 16, TILE), jnp.float32)
    small_own[16:28] = g_ssm[...]
    small_own[28:30] = head_sums[0:2]
    small_own[30:31] = g_skip[0:1]
    conv_tiles = g_conv.shape[1] // TILE
    for k in range(CONV + 1):
        for i in range(conv_tiles):
            place = 32 + 16 * k + i
            small_own[place : place + 1] = g_conv[k : k + 1, i * TILE : (i + 1) * TILE]
    for k in range(width // TILE):
        for which in range(2):
            small_own[8 * which + k : 8 * which + k + 1] = both[
                which : which + 1, k * TILE : (k + 1) * TILE
            ]
    names = ("core", "y", "x", "near", "far")
    small_copies = []

    def small_step(k):
        if k > 0:
            small_copies[k - 1].wait_recv()
            was = small_own if k == 1 else small_mid.at[k - 2]
            now = small_out if k == 5 else small_mid.at[k - 1]
            now[...] = was[...] + small_in[k - 1]
        if k < 5:
            source = small_own if k == 0 else small_mid.at[k - 1]
            copy = remote(
                source, small_in.at[k], small_send.at[k], small_recv.at[k], others[names[k]]
            )
            copy.start()
            small_copies.append(copy)

    scatter.step(2, 1)
    scatter.step(0, 2)
    small_step(0)
    inner = grads * gains[0:1]
    coeff = jnp.mean(inner * wide, axis=-1, keepdims=True)
    d_normed[...] = d_middle[...] + r * (inner - wide * (r * r * coeff))
    scatter.step(1, 2)
    small_step(1)
    scatter.step(0, 3)
    scatter.step(2, 2)

    def plain(j, carry):
        here = pl.ds(pl.multiple_of(j * step, step), step)
        input_grad[:, here] = dot_nt_two(d_normed[...], order[here])
        return carry

    lax.fori_loop(0, width // step, plain, 0)
    small_step(2)
    query = QUERY_HEADS * HEAD_SIZE
    g_in_out[:, : sum_z.shape[1]] = sum_z[...]
    g_out_out[:, :query] = pair_columns(sum_out[:, :query], True)
    g_out_out[:, query:] = sum_out[:, query:]
    scatter.step(1, 3)
    scatter.step(2, 3)
    small_step(3)
    scatter.step(0, 4)
    small_step(4)
    scatter.step(1, 4)
    scatter.step(2, 4)
    small_step(5)
    norm_total[...] = small_out[:8]
    mlp_total[...] = small_out[8:16]
    ssm_total[...] = small_out[16:28]
    head_total[...] = small_out[24:32]
    for k in range(CONV):
        for i in range(conv_tiles):
            place = 32 + 16 * k + i
            conv_total[k : k + 1, i * TILE : (i + 1) * TILE] = small_out[place : place + 1]
    conv_b_total[...] = small_out[32 + 16 * CONV : 32 + 16 * CONV + conv_tiles]
    g_in_out[:, g_in_out.shape[1] - g_conv.shape[1] :] = out_conv[:, : g_conv.shape[1]]
    g_dt_out[...] = out_conv[:, g_conv.shape[1] : g_conv.shape[1] + MH]
    query = QUERY_HEADS * HEAD_SIZE
    g_attn_out[:, :query] = pair_columns(out_attn[:, :query], True)
    g_attn_out[:, query:] = out_attn[:, query:]
    scatter.finish()
    for copy in swaps + small_copies:
        copy.wait_send()


def last(*args):
    d_conv, d_attn, d_z, normed = args[0], args[1], args[2], args[5]
    g_conv = args[13]
    rows, width = normed.shape
    half = width // 2
    f32, narrow = jnp.float32, jnp.bfloat16
    dma = pltpu.SemaphoreType.DMA
    widths = [d_conv.shape[1], d_attn.shape[1]]
    pairs = column_chunks(widths)
    total = (32 + 16 * (CONV + 1), TILE)
    block = half // 16
    xbc = g_conv.shape[1]
    joined = args[16].shape[1]
    outs = [
        shape_of((rows, width), f32),
        shape_of((block, widths[1]), f32),
        shape_of((block, d_z.shape[1] + xbc), f32),
        shape_of((block, MH), f32),
        shape_of((block, joined), f32),
        shape_of((8, TILE), f32),
        shape_of((8, TILE), f32),
        shape_of((12, TILE), f32),
        shape_of((CONV, xbc), f32),
        shape_of((xbc // TILE, TILE), f32),
        shape_of((8, TILE), f32),
    ]
    scratch = [pltpu.VMEM((half, w), narrow) for w in widths]
    scratch += scatter_scratch(widths, half)
    scratch += [pltpu.VMEM((block, w), f32) for w in widths]
    scratch += [
        pltpu.VMEM(d_conv.shape, narrow),
        pltpu.VMEM(d_attn.shape, narrow),
        pltpu.VMEM((half, 2 * rows), narrow),
        pltpu.VMEM((rows, width), f32),
        pltpu.VMEM(total, f32),
        pltpu.VMEM((5, *total), f32),
        pltpu.VMEM((4, *total), f32),
        pltpu.VMEM(total, f32),
        dma((2,)),
        dma((2,)),
        dma((2 * len(pairs), 4, 4)),
        dma((2 * len(pairs), 4, 4)),
        dma((5,)),
        dma((5,)),
    ]
    return comm_call(
        lambda *refs: last_kernel(pairs, *refs),
        outs,
        [INTO_VMEM] * len(outs),
        args,
        [INTO_VMEM] * len(args),
        scratch,
        4,
        100_000_000,
    )


def settle_kernel(*refs):
    count = len(refs) // 2
    sems = refs[2 * count]
    copies = [
        pltpu.make_async_copy(refs[k], refs[count + k], sems.at[k]) for k in range(count)
    ]
    for copy in copies:
        copy.start()
    for copy in copies:
        copy.wait()


def settle(*arrays):
    count = len(arrays)
    return pl.pallas_call(
        settle_kernel,
        out_shape=[shape_of(a.shape, a.dtype) for a in arrays],
        in_specs=[ANY] * count,
        out_specs=[INTO_VMEM] * count,
        scratch_shapes=[pltpu.SemaphoreType.DMA((count,))],
        compiler_params=pltpu.CompilerParams(vmem_limit_bytes=60 * 1024 * 1024),
    )(*arrays)


def pair_heads(value, back=False):
    rows = value.shape[0]
    group = QUERY_HEADS // KEY_VALUE_HEADS
    width = QUERY_HEADS * HEAD_SIZE
    shape = (group, KEY_VALUE_HEADS) if back else (KEY_VALUE_HEADS, group)
    moved = value[:, :width].reshape(rows, *shape, HEAD_SIZE).transpose(0, 2, 1, 3)
    return jnp.concatenate([moved.reshape(rows, width), value[:, width:]], axis=1)


def plain_layer(
    layer_input,
    seq_lengths,
    w_attn,
    w_ssm_in,
    w_dt,
    w_out,
    w_gate_up,
    w_down,
    norm_gain,
    mlp_gain,
    ssm_gain,
    conv_w,
    conv_b,
    a_log,
    dt_bias,
    d_skip,
    out_grad,
):
    token_rows = layer_input.shape[1]
    query_width = QUERY_HEADS * HEAD_SIZE
    key_value_width = KEY_VALUE_HEADS * HEAD_SIZE
    attn_width = query_width + 2 * key_value_width
    ssm_width = MH * MP
    xbc_width = ssm_width + 2 * NS
    seq_lens = seq_lengths[0]
    first_pos = lax.axis_index("seq") * token_rows
    positions = first_pos + jnp.arange(token_rows, dtype=jnp.int32)
    segment, device_places = segments(seq_lens, positions)
    ends = jnp.cumsum(seq_lens)
    info = jnp.stack([first_pos, ends[0], ends[1], ends[2]]).astype(jnp.int32)
    half = HEAD_SIZE // 2
    freqs = ROPE_BASE ** (-jnp.arange(half, dtype=jnp.float32) / half)
    angles = device_places.astype(jnp.float32)[:, None] * jnp.tile(freqs, TILE // half)[None, :]
    cosine, sine = jnp.cos(angles), jnp.sin(angles)
    head_params = jnp.pad(
        jnp.stack([dt_bias, jnp.exp(a_log), d_skip]), ((0, 5), (0, TILE - MH))
    )
    step_pad = jnp.pad(w_dt, ((0, 0), (0, TILE - MH)))
    shards = (
        jnp.concatenate([w_ssm_in[:, ssm_width:], step_pad], axis=1),
        jnp.concatenate([pair_heads(w_attn), w_ssm_in[:, :ssm_width]], axis=1),
        pair_heads(w_out.T),
        w_gate_up,
        w_down.T,
    )
    ext_pos = first_pos - (CONV - 1) + jnp.arange(token_rows + CONV - 1, dtype=jnp.int32)
    ext_segment = segments(seq_lens, ext_pos)[0]

    def conv_local(ext_rows, conv_weight, conv_bias):
        return conv_mix(ext_rows, ext_segment, conv_weight, conv_bias)

    full = [lax.all_gather(p, ("seq", "batch"), axis=0, tiled=True) for p in shards]
    full_conv, full_mix, full_out, full_gu, full_down = full
    x_rows = layer_input[0].astype(jnp.float32)
    grad_rows = out_grad[0]
    scale_one = rms_scale(x_rows)
    normed = (x_rows * scale_one * norm_gain).astype(jnp.bfloat16)
    conv_proj = jnp.dot(normed, full_conv, preferred_element_type=jnp.float32)
    mix_proj = jnp.dot(normed, full_mix, preferred_element_type=jnp.float32)
    queries, own_pairs = big_call(
        rope_kernel,
        (
            shape_of((token_rows, query_width), jnp.bfloat16),
            shape_of((token_rows, 2 * key_value_width), jnp.bfloat16),
        ),
        mix_proj[:, :attn_width],
        cosine,
        sine,
    )
    gate_z = mix_proj[:, attn_width:]
    raw_xbc = conv_proj[:, :xbc_width]
    step_proj = conv_proj[:, xbc_width:]
    rim_rows = shifted(raw_xbc[token_rows - (CONV - 1) :], "seq", 1)
    extended = jnp.concatenate([rim_rows, raw_xbc], axis=0)
    conv_out, conv_pullback = jax.vjp(conv_local, extended, conv_w, conv_b)
    conv_narrow = conv_out.astype(jnp.bfloat16)
    inputs_x, inputs_bc = conv_narrow[:, :ssm_width], conv_narrow[:, ssm_width:]
    ssm_own, state_own, steps_dt, running_decay = ssm_forward(
        info, inputs_x, inputs_bc, step_proj, head_params
    )
    all_pairs = lax.all_gather(own_pairs, "seq", axis=0, tiled=True)
    state_in = scan_states(state_own, True)
    attended, attended_t, log_total = attn_forward(info, queries, all_pairs)

    ssm_flat, ssm_normed, scale_gated = ssm_finish(
        info, ssm_own, inputs_bc, running_decay, state_in, gate_z, ssm_gain.reshape(-1, TILE)
    )
    joined = jnp.concatenate([attended, ssm_normed], axis=1)

    def into_width(left, weight):
        return jnp.einsum("tc,dc->td", left, weight, preferred_element_type=jnp.float32)

    def out_of_width(left, weight):
        return jnp.dot(left, weight, preferred_element_type=jnp.float32)

    middle = x_rows + into_width(joined, full_out)
    scale_two = rms_scale(middle)
    normed_two = (middle * scale_two * mlp_gain).astype(jnp.bfloat16)
    gate_up = out_of_width(normed_two, full_gu)
    gate_part, up_part = gate_up[:, :FF], gate_up[:, FF:]
    sig_gate = jax.nn.sigmoid(gate_part)
    hidden = (gate_part * sig_gate * up_part).astype(jnp.bfloat16)
    layer_out = middle + into_width(hidden, full_down)
    d_hidden = out_of_width(grad_rows, full_down)
    d_gate = d_hidden * up_part * (sig_gate * (1.0 + gate_part * (1.0 - sig_gate)))
    d_up = d_hidden * gate_part * sig_gate
    d_gate_up = jnp.concatenate([d_gate, d_up], axis=1).astype(jnp.bfloat16)
    d_normed_two = into_width(d_gate_up, full_gu)
    d_middle_norm, g_mlp_gain = norm_back(middle, scale_two, mlp_gain, d_normed_two)
    d_middle = grad_rows.astype(jnp.float32) + d_middle_norm
    d_mixer = d_middle.astype(jnp.bfloat16)
    d_joined = out_of_width(d_mixer, full_out)
    attended_gradient = d_joined[:, :query_width].astype(jnp.bfloat16)
    d_ssm_out, d_gate_z, pull, g_ssm_gain = gate_back(
        info,
        d_joined[:, query_width:],
        ssm_flat,
        gate_z,
        scale_gated,
        ssm_gain.reshape(-1, TILE),
        running_decay,
        inputs_bc,
    )
    pull = jnp.concatenate([pull, state_own[NS:]], axis=0)
    d_state = scan_states(pull, False)
    d_queries, d_pairs = attn_backward(
        info, queries, all_pairs, attended_gradient, attended_t, log_total
    )
    own_d_pairs = lax.psum_scatter(
        d_pairs.astype(jnp.float32), "seq", scatter_dimension=0, tiled=True
    )
    dx_part, d_bc_part, d_cum_part, d_dt_part, g_skip_rows = ssm_back(
        info, inputs_x, inputs_bc, steps_dt, running_decay, d_ssm_out, head_params
    )
    g_inputs_x, g_inputs_bc, d_step_pad, head_sums = state_back(
        info,
        inputs_x,
        inputs_bc,
        steps_dt,
        running_decay,
        d_ssm_out,
        head_params,
        step_proj,
        state_in,
        d_state,
        dx_part,
        d_bc_part,
        d_cum_part,
        d_dt_part,
    )
    g_extended, g_conv_w, g_conv_b = conv_pullback(
        jnp.concatenate([g_inputs_x, g_inputs_bc], axis=1)
    )
    back_rim = shifted(g_extended[: CONV - 1], "seq", -1)
    d_raw = g_extended[CONV - 1 :] + jnp.concatenate(
        [jnp.zeros((token_rows - (CONV - 1), xbc_width), jnp.float32), back_rim], axis=0
    )
    d_conv_proj = jnp.concatenate([d_raw.astype(jnp.bfloat16), d_step_pad], axis=1)
    (d_attn_proj,) = big_call(
        rope_back_kernel,
        (shape_of((token_rows, attn_width), jnp.bfloat16),),
        d_queries,
        own_d_pairs,
        cosine,
        sine,
    )
    d_mix_proj = jnp.concatenate([d_attn_proj, d_gate_z], axis=1)
    d_normed = into_width(d_conv_proj, full_conv) + into_width(d_mix_proj, full_mix)
    d_input_norm, g_norm_gain = norm_back(x_rows, scale_one, norm_gain, d_normed)
    input_grad = d_middle + d_input_norm
    axes = ("seq", "batch")

    def summed(left, right):
        grad = jnp.einsum("td,tc->dc", left, right, preferred_element_type=jnp.float32)
        return lax.psum_scatter(grad, axes, scatter_dimension=0, tiled=True)

    sum_down, sum_gu = summed(grad_rows, hidden), summed(normed_two, d_gate_up)
    sum_out, sum_conv = summed(d_mixer, joined), summed(normed, d_conv_proj)
    sum_mix = summed(normed, d_mix_proj)
    sum_attn, sum_z = sum_mix[:, :attn_width], sum_mix[:, attn_width:]
    small = (
        g_norm_gain,
        g_mlp_gain,
        g_ssm_gain.reshape(-1),
        g_conv_w,
        g_conv_b,
        head_sums[0, :MH],
        head_sums[1, :MH],
        g_skip_rows[0, :MH],
    )
    small_sums = unpack_small(lax.psum(pack_small(small), axes), small)
    grad_attn = pair_heads(sum_attn, True)
    grad_ssm_in = jnp.concatenate([sum_z, sum_conv[:, :xbc_width]], axis=1)
    grad_dt = sum_conv[:, xbc_width : xbc_width + MH]
    grad_out = pair_heads(sum_out, True).T
    grad_gate_up = sum_gu
    grad_down = sum_down.T
    return (
        layer_out.astype(jnp.bfloat16)[None],
        input_grad[None],
        grad_attn,
        grad_ssm_in,
        grad_dt,
        grad_out,
        grad_gate_up,
        grad_down,
        *small_sums,
    )


def on_device(
    layer_input,
    seq_lengths,
    w_attn,
    w_ssm_in,
    w_dt,
    w_out,
    w_gate_up,
    w_down,
    norm_gain,
    mlp_gain,
    ssm_gain,
    conv_w,
    conv_b,
    a_log,
    dt_bias,
    d_skip,
    out_grad,
):
    if not is_fast(layer_input.shape[2]):
        return plain_layer(
            layer_input, seq_lengths, w_attn, w_ssm_in, w_dt, w_out, w_gate_up, w_down, norm_gain,
            mlp_gain, ssm_gain, conv_w, conv_b, a_log, dt_bias, d_skip, out_grad,
        )
    half = HEAD_SIZE // 2
    freqs = np.float32(ROPE_BASE) ** (-np.arange(half, dtype=np.float32) / np.float32(half))
    freqs = jnp.asarray(np.tile(freqs.astype(np.float32), TILE // half)[None])
    full, made = front(
        seq_lengths,
        dt_bias,
        a_log,
        d_skip,
        layer_input[0],
        out_grad[0],
        norm_gain.reshape(-1, TILE),
        mlp_gain.reshape(-1, TILE),
        freqs,
        conv_w,
        conv_b.reshape(-1, TILE),
        (w_attn, w_ssm_in, w_dt.T, w_out.T, w_gate_up, w_down.T),
    )
    full_conv, full_mix, full_out, full_gu, full_down = full
    (
        x_own, g_own, gains, normed, queries, all_pairs, gate_z, raw_rows, pre_conv, inputs_x,
        inputs_bc, ssm_own, state_own, steps_dt, running_decay, attended, attended_t, log_total,
        state_in, order, cosine, sine, head_params,
    ) = made
    (
        layer_out, joined, hidden, d_gate_up, normed_two, d_mixer, d_middle, d_ssm_out, d_gate_z,
        pull, attended_gradient, g_ssm_gain, g_mlp_gain,
    ) = middle_part(
        seq_lengths, ssm_own, inputs_bc, running_decay, state_in, state_own, gate_z,
        ssm_gain.reshape(-1, TILE), attended, x_own, g_own, gains, order, full_out, full_gu,
        full_down,
    )
    (
        d_conv_proj, d_attn_proj, g_conv, head_sums, g_skip_rows, their_normed, sum_down, sum_gu,
        sum_out, sum_z,
    ) = back(
        seq_lengths, head_params, conv_w, cosine, sine, queries, all_pairs, attended_gradient,
        attended_t, log_total, pull, inputs_x, inputs_bc, steps_dt, running_decay, d_ssm_out,
        raw_rows, state_in, pre_conv, normed, normed_two, d_mixer, g_own, hidden, joined,
        d_gate_up, d_gate_z,
    )
    (
        input_grad, grad_attn, grad_ssm_in, grad_dt, grad_out, g_norm, g_mlp, g_ssm, g_conv_w,
        g_conv_b, heads,
    ) = last(
        d_conv_proj, d_attn_proj, d_gate_z, full_conv, full_mix, normed, their_normed, x_own,
        d_middle, gains, order, g_mlp_gain, g_ssm_gain, g_conv, head_sums, g_skip_rows, sum_out,
        sum_z,
    )
    (
        input_grad, grad_attn, grad_ssm_in, grad_dt, grad_out, sum_gu, sum_down, g_norm, g_mlp,
        g_ssm, g_conv_w, g_conv_b, heads,
    ) = settle(
        input_grad, grad_attn, grad_ssm_in, grad_dt, grad_out, sum_gu, sum_down, g_norm, g_mlp,
        g_ssm, g_conv_w, g_conv_b, heads,
    )
    return (
        layer_out[None],
        input_grad[None],
        grad_attn,
        grad_ssm_in,
        grad_dt,
        grad_out.T,
        sum_gu,
        sum_down.T,
        g_norm.reshape(-1),
        g_mlp.reshape(-1),
        g_ssm.reshape(-1),
        g_conv_w,
        g_conv_b.reshape(-1),
        heads[4, :MH],
        heads[5, :MH],
        heads[6, :MH],
    )


def solution(mesh):
    return jax.shard_map(
        on_device,
        mesh=mesh,
        in_specs=(
            P("batch", "seq", None),
            P("batch", None),
            P(("seq", "batch"), None),
            P(("seq", "batch"), None),
            P(("seq", "batch"), None),
            P(None, ("seq", "batch")),
            P(("seq", "batch"), None),
            P(None, ("seq", "batch")),
            P(),
            P(),
            P(),
            P(),
            P(),
            P(),
            P(),
            P(),
            P("batch", "seq", None),
        ),
        out_specs=(
            P("batch", "seq", None),
            P("batch", "seq", None),
            P(("seq", "batch"), None),
            P(("seq", "batch"), None),
            P(("seq", "batch"), None),
            P(None, ("seq", "batch")),
            P(("seq", "batch"), None),
            P(None, ("seq", "batch")),
            P(),
            P(),
            P(),
            P(),
            P(),
            P(),
            P(),
            P(),
        ),
        check_vma=False,
    )
```

```python
import jax
import jax.numpy as jnp
import numpy as np
from jax import lax
from jax.experimental import pallas as pl
from jax.experimental.pallas import tpu as pltpu
from jax.sharding import PartitionSpec as P

QUERY_HEADS = 8
KEY_VALUE_HEADS = 2
HEAD_SIZE = 64
MH = 24
MP = 64
NS = 128
FF = 2048
CONV = 4
SPAN = 128


HIGHEST = lax.Precision.HIGHEST
NEGATIVE_FILL = -1e30
ROPE_BASE = 10000.0
NORM_EPS = 1e-06


def shifted(block, axis, distance):
    devices = range(lax.axis_size(axis))
    route = [(i - distance, i) for i in devices if i - distance in devices]
    return lax.ppermute(block, axis, route)


def is_fast(width):
    return lax.axis_size("seq") == 8 and lax.axis_size("batch") == 4 and width % (32 * 32) == 0


def pack_small(arrays):
    flat = jnp.concatenate([a.reshape(-1) for a in arrays])
    return jnp.pad(flat, (0, -flat.shape[0] % 1024)).reshape(-1, 128)


def unpack_small(flat, arrays):
    flat = flat.reshape(-1)
    out, start = [], 0
    for a in arrays:
        out.append(flat[start : start + a.size].reshape(a.shape))
        start += a.size
    return out


def rms_scale(value_rows):
    return lax.rsqrt(jnp.mean(value_rows * value_rows, axis=-1, keepdims=True) + NORM_EPS)


def norm_back(value_rows, scales, gains, grads):
    gain_grad = jnp.sum(grads * value_rows * scales, axis=0)
    inner = grads * gains
    coeff = jnp.mean(inner * value_rows, axis=-1, keepdims=True)
    return (scales * (inner - value_rows * scales * scales * coeff), gain_grad)


def segments(lengths, positions):
    ends = jnp.cumsum(lengths)
    passed = ends[None, :] <= positions[:, None]
    segment = jnp.sum(passed.astype(jnp.int32), axis=1)
    device_places = positions - jnp.sum(jnp.where(passed, lengths[None, :], 0), axis=1)
    return (segment, device_places)


def conv_mix(extended, ext_segment, conv_weight, conv_bias):
    row_count = extended.shape[0] - (CONV - 1)
    summed = conv_bias[None, :]
    for lagged in range(CONV):
        same_seq = (ext_segment[lagged : lagged + row_count] == ext_segment[CONV - 1 :]).astype(
            extended.dtype
        )
        summed = (
            summed
            + conv_weight[lagged][None, :]
            * extended[lagged : lagged + row_count]
            * same_seq[:, None]
        )
    return jax.nn.silu(summed)


TILE = 128
PAIRS = QUERY_HEADS // 2
CHUNK = 256


def dot(left, right):
    return jnp.dot(left, right, preferred_element_type=jnp.float32)


def dot_nt(left, right):
    return lax.dot_general(
        left, right, (((1,), (1,)), ((), ())), preferred_element_type=jnp.float32
    )


def dot_tn(left, right):
    return lax.dot_general(
        left, right, (((0,), (0,)), ((), ())), preferred_element_type=jnp.float32
    )


def exact(left, right):
    return jnp.dot(left, right, precision=HIGHEST, preferred_element_type=jnp.float32)


def two_part(left, right):
    high = left.astype(jnp.bfloat16)
    low = (left - high.astype(jnp.float32)).astype(jnp.bfloat16)
    return dot(high, right) + dot(low, right)


def seg_start(where_at, info):
    start = jnp.zeros_like(where_at)
    for k in range(1, 4):
        start = jnp.where(where_at >= info[k], jnp.maximum(start, info[k]), start)
    return start


def big_call(kernel, outs, *args, scratch=(), flops=0, smem=0, limit=48):
    specs = [pl.BlockSpec(memory_space=pltpu.SMEM)] * smem
    specs += [pl.BlockSpec(memory_space=pltpu.VMEM)] * (len(args) - smem)
    moved = sum(a.size * a.dtype.itemsize for a in args)
    moved += sum(o.size * o.dtype.itemsize for o in outs)
    return pl.pallas_call(
        kernel,
        out_shape=list(outs),
        in_specs=specs,
        out_specs=[pl.BlockSpec(memory_space=pltpu.VMEM)] * len(outs),
        scratch_shapes=list(scratch),
        cost_estimate=pl.CostEstimate(flops=flops, bytes_accessed=moved, transcendentals=0),
        compiler_params=pltpu.CompilerParams(vmem_limit_bytes=limit * 1024 * 1024),
    )(*args)


def shape_of(shape, dtype):
    return jax.ShapeDtypeStruct(shape, dtype)


def turn(value, cosine, sine):
    lane = lax.broadcasted_iota(jnp.int32, value.shape, 1) % HEAD_SIZE
    mixed = jnp.where(
        lane < HEAD_SIZE // 2,
        -pltpu.roll(value, TILE - HEAD_SIZE // 2, 1),
        pltpu.roll(value, HEAD_SIZE // 2, 1),
    )
    return value * cosine + mixed * sine


def rope_kernel(proj, cosine, sine, q_out, kv_out):
    cos, sin = cosine[...], sine[...]
    for i in range(PAIRS):
        cols = pl.ds(i * TILE, TILE)
        turned = turn(proj[:, cols], cos, sin).astype(jnp.bfloat16)
        q_out[:, cols] = (turned.astype(jnp.float32) * HEAD_SIZE**-0.5).astype(jnp.bfloat16)
    base = PAIRS * TILE
    kv_out[:, :TILE] = turn(proj[:, base : base + TILE], cos, sin).astype(jnp.bfloat16)
    kv_out[:, TILE:] = proj[:, base + TILE : base + 2 * TILE].astype(jnp.bfloat16)


def halves_of(value):
    lane = lax.broadcasted_iota(jnp.int32, value.shape, 1)
    wide = value.astype(jnp.float32)
    first = jnp.where(lane < HEAD_SIZE, wide, 0.0).astype(value.dtype)
    return first, jnp.where(lane < HEAD_SIZE, 0.0, wide).astype(value.dtype)


def block_range(info):
    first = info[0]
    low = seg_start(first, info) // CHUNK
    return low, first // CHUNK - low + 1


def attn_mask(info, block):
    rows = lax.broadcasted_iota(jnp.int32, (CHUNK, CHUNK), 0) + block * CHUNK
    at = lax.broadcasted_iota(jnp.int32, (1, CHUNK), 1) + info[0]
    return (rows <= at) & (rows >= seg_start(at, info))


def attend_start(q, heads, acc, top, total):
    for i in range(PAIRS):
        heads[2 * i], heads[2 * i + 1] = halves_of(q[:, i * TILE : (i + 1) * TILE])
    acc[...] = jnp.zeros_like(acc)
    total[...] = jnp.zeros_like(total)
    top[...] = jnp.full(top.shape, NEGATIVE_FILL, jnp.float32)


def attend_block(info, block, keys, values_t, heads, acc, top, total):
    allowed = attn_mask(info, block)
    for h in range(QUERY_HEADS):
        scores = jnp.where(allowed, dot_nt(keys, heads[h]), NEGATIVE_FILL)
        old = top[h : h + 1]
        new = jnp.maximum(old, jnp.max(scores, axis=0, keepdims=True))
        probs = jnp.where(allowed, jnp.exp(scores - new), 0.0)
        shrink = jnp.exp(old - new)
        top[h : h + 1] = new
        total[h : h + 1] = total[h : h + 1] * shrink + jnp.sum(probs, axis=0, keepdims=True)
        side = (h % 2) * HEAD_SIZE
        acc[h] = acc[h] * shrink + dot(
            values_t[side : side + HEAD_SIZE], probs.astype(jnp.bfloat16)
        )


def attend_write(acc, total, out, out_t):
    for i in range(PAIRS):
        pair = jnp.concatenate(
            [acc[2 * i] / total[2 * i : 2 * i + 1], acc[2 * i + 1] / total[2 * i + 1 : 2 * i + 2]],
            axis=0,
        )
        out_t[i * TILE : (i + 1) * TILE] = pair
        out[:, i * TILE : (i + 1) * TILE] = pair.T.astype(jnp.bfloat16)


def attn_forward_kernel(info, q, kv, out, out_t, lse, heads, acc, top, total):
    attend_start(q, heads, acc, top, total)
    low, count = block_range(info)

    def step(j, carry):
        block = low + j
        place = pl.ds(pl.multiple_of(block * CHUNK, CHUNK), CHUNK)
        keys = kv[place, :TILE]
        values_t = kv[place, TILE:].astype(jnp.float32).T.astype(jnp.bfloat16)
        attend_block(info, block, keys, values_t, heads, acc, top, total)
        return carry

    lax.fori_loop(0, count, step, 0)
    lse[...] = top[...] + jnp.log(total[...])
    attend_write(acc, total, out, out_t)


def attn_forward(info, q, kv):
    rows = q.shape[0]
    f32 = jnp.float32
    return big_call(
        attn_forward_kernel,
        (
            shape_of(q.shape, jnp.bfloat16),
            shape_of(q.shape[::-1], f32),
            shape_of((QUERY_HEADS, rows), f32),
        ),
        info,
        q,
        kv,
        smem=1,
        scratch=(
            pltpu.VMEM((QUERY_HEADS, rows, TILE), jnp.bfloat16),
            pltpu.VMEM((QUERY_HEADS, HEAD_SIZE, rows), f32),
            pltpu.VMEM((QUERY_HEADS, rows), f32),
            pltpu.VMEM((QUERY_HEADS, rows), f32),
        ),
        flops=4 * rows * kv.shape[0] * q.shape[1],
    )


def attend_back_start(q, grad, out_t, heads, grads, delta, acc):
    for i in range(PAIRS):
        cols = slice(i * TILE, (i + 1) * TILE)
        heads[2 * i], heads[2 * i + 1] = halves_of(q[:, cols])
        grads[2 * i], grads[2 * i + 1] = halves_of(grad[:, cols])
        both = grad[:, cols].astype(jnp.float32).T * out_t[cols]
        delta[2 * i : 2 * i + 1] = jnp.sum(both[:HEAD_SIZE], axis=0, keepdims=True)
        delta[2 * i + 1 : 2 * i + 2] = jnp.sum(both[HEAD_SIZE:], axis=0, keepdims=True)
    acc[...] = jnp.zeros_like(acc)


def attend_back_block(info, block, keys, values, lse, target, heads, grads, delta, acc):
    keys_t = keys.astype(jnp.float32).T.astype(jnp.bfloat16)
    allowed = attn_mask(info, block)
    d_keys = jnp.zeros((CHUNK, TILE), jnp.float32)
    d_values = jnp.zeros((CHUNK, TILE), jnp.float32)
    for h in range(QUERY_HEADS):
        scores = dot_nt(keys, heads[h])
        probs = jnp.where(allowed, jnp.exp(scores - lse[h : h + 1]), 0.0)
        d_probs = dot_nt(values, grads[h])
        d_scores = (probs * (d_probs - delta[h : h + 1])).astype(jnp.bfloat16)
        d_values = d_values + dot(probs.astype(jnp.bfloat16), grads[h])
        d_keys = d_keys + dot(d_scores, heads[h])
        side = (h % 2) * HEAD_SIZE
        acc[h] = acc[h] + dot(keys_t[side : side + HEAD_SIZE], d_scores)
    target[:, :TILE] = d_keys.astype(jnp.bfloat16)
    target[:, TILE:] = d_values.astype(jnp.bfloat16)


def attend_back_write(acc, dq):
    for i in range(PAIRS):
        pair = jnp.concatenate([acc[2 * i], acc[2 * i + 1]], axis=0)
        dq[:, i * TILE : (i + 1) * TILE] = pair.T * HEAD_SIZE**-0.5


def attn_backward_kernel(info, q, kv, grad, out_t, lse, dq, dkv, heads, grads, delta, acc):
    attend_back_start(q, grad, out_t, heads, grads, delta, acc)
    dkv[...] = jnp.zeros_like(dkv)
    low, count = block_range(info)

    def step(j, carry):
        block = low + j
        place = pl.ds(pl.multiple_of(block * CHUNK, CHUNK), CHUNK)
        attend_back_block(
            info, block, kv[place, :TILE], kv[place, TILE:], lse, dkv.at[place], heads, grads,
            delta, acc,
        )
        return carry

    lax.fori_loop(0, count, step, 0)
    attend_back_write(acc, dq)


def attn_backward(info, q, kv, grad, out_t, lse):
    rows = q.shape[0]
    f32 = jnp.float32
    return big_call(
        attn_backward_kernel,
        (shape_of(q.shape, f32), shape_of(kv.shape, jnp.bfloat16)),
        info,
        q,
        kv,
        grad,
        out_t,
        lse,
        smem=1,
        scratch=(
            pltpu.VMEM((QUERY_HEADS, rows, TILE), jnp.bfloat16),
            pltpu.VMEM((QUERY_HEADS, rows, TILE), jnp.bfloat16),
            pltpu.VMEM((QUERY_HEADS, rows), f32),
            pltpu.VMEM((QUERY_HEADS, HEAD_SIZE, rows), f32),
        ),
        flops=10 * rows * kv.shape[0] * q.shape[1],
    )


def rope_back_kernel(dq, dkv, cosine, sine, out):
    cos, sin = cosine[...], -sine[...]
    for i in range(PAIRS):
        cols = slice(i * TILE, (i + 1) * TILE)
        out[:, cols] = turn(dq[:, cols], cos, sin).astype(jnp.bfloat16)
    base = PAIRS * TILE
    out[:, base : base + TILE] = turn(dkv[:, :TILE], cos, sin).astype(jnp.bfloat16)
    out[:, base + TILE :] = dkv[:, TILE:].astype(jnp.bfloat16)


STATE_ROWS = NS + 16


def lane_pick(value, first):
    rows = value.shape[0]
    lane = lax.broadcasted_iota(jnp.int32, (rows, TILE), 1)
    return jnp.where(lane < MP, value[:, first : first + 1], value[:, first + 1 : first + 2])


def spread_heads(width):
    head = lax.broadcasted_iota(jnp.int32, (TILE, width), 0)
    col = lax.broadcasted_iota(jnp.int32, (TILE, width), 1)
    return jnp.where(head == col // MP, 1.0, 0.0).astype(jnp.bfloat16)


def gather_heads(width):
    head = lax.broadcasted_iota(jnp.int32, (width, TILE), 1)
    col = lax.broadcasted_iota(jnp.int32, (width, TILE), 0)
    return jnp.where(head == col // MP, 1.0, 0.0).astype(jnp.bfloat16)


def head_lanes(rows):
    return lax.broadcasted_iota(jnp.int32, (rows, TILE), 1) < MH


def chunk_places(info, rows):
    at = lax.broadcasted_iota(jnp.int32, (rows, 1), 0) + info[0]
    return seg_start(at, info) - info[0]


def ssm_states(info, x, bc, step_in, head_params, state, dt_out, cum_out, dt_t, cum_t):
    rows = x.shape[0]
    bias, rate = head_params[0:1], head_params[1:2]
    raw = step_in[...] + bias
    dt = jnp.maximum(raw, 0.0) + jnp.log1p(jnp.exp(-jnp.abs(raw)))
    dt = jnp.where(head_lanes(rows), dt, 0.0)
    row = lax.broadcasted_iota(jnp.int32, (rows, rows), 0)
    col = lax.broadcasted_iota(jnp.int32, (rows, rows), 1)
    lower = jnp.where(row >= col, 1.0, 0.0)
    cum = exact(lower, -dt * rate)
    dt_out[...] = dt
    cum_out[...] = cum
    dt_t[...] = dt.T
    cum_t[...] = cum.T
    last_start = seg_start(info[0] + rows - 1, info) - info[0]
    place = lax.broadcasted_iota(jnp.int32, (rows, 1), 0)
    end = cum[rows - 1 : rows]
    leave = jnp.where(place >= last_start, jnp.exp(jnp.minimum(end - cum, 0.0)) * dt, 0.0)
    b_t = bc[:, :NS].astype(jnp.float32).T.astype(jnp.bfloat16)
    through = jnp.where(last_start < 0, jnp.exp(end), 0.0)
    high = through.astype(jnp.bfloat16).astype(jnp.float32)
    line = lax.broadcasted_iota(jnp.int32, (16, TILE), 0)
    both = jnp.where(line == 0, high, jnp.where(line == 1, through - high, 0.0))
    spread = spread_heads(x.shape[1])
    state[NS:] = dot(both.astype(jnp.bfloat16), spread).astype(jnp.bfloat16)
    for i in range(MH // 2):
        cols = slice(i * TILE, (i + 1) * TILE)
        weighed = x[:, cols].astype(jnp.float32) * lane_pick(leave, 2 * i)
        state[:NS, cols] = dot(b_t, weighed.astype(jnp.bfloat16)).astype(jnp.bfloat16)


def ssm_local(info, x, bc, head_params, y, cum, dt_t, cum_t):
    rows = x.shape[0]
    row = lax.broadcasted_iota(jnp.int32, (rows, rows), 0)
    col = lax.broadcasted_iota(jnp.int32, (rows, rows), 1)
    starts = chunk_places(info, rows)
    products = dot_nt(bc[:, NS:], bc[:, :NS])
    skips = jnp.broadcast_to(head_params[2:3], (8, TILE))
    skip_row = two_part(skips, spread_heads(x.shape[1]))[:1]
    lane = lax.broadcasted_iota(jnp.int32, (SPAN, TILE), 1)
    for i in range(MH // 2):
        cols = slice(i * TILE, (i + 1) * TILE)
        tile = x[:, cols]
        for part in range(rows // SPAN):
            here = slice(part * SPAN, (part + 1) * SPAN)
            upto = (part + 1) * SPAN
            allowed = (row[here, :upto] >= col[here, :upto]) & (col[here, :upto] >= starts[here])
            sides = []
            for h in (2 * i, 2 * i + 1):
                spread_log = cum[here, h : h + 1] - cum_t[h : h + 1, :upto]
                decay = jnp.exp(jnp.where(allowed, spread_log, NEGATIVE_FILL))
                mixing = products[here, :upto] * decay * dt_t[h : h + 1, :upto]
                sides.append(dot(mixing.astype(jnp.bfloat16), tile[:upto]))
            own = skip_row[:, cols] * tile[here].astype(jnp.float32)
            y[here, cols] = jnp.where(lane < MP, sides[0], sides[1]) + own


def ssm_forward_kernel(info, x, bc, step_in, head_params, y, state, dt_out, cum_out, dt_t, cum_t):
    ssm_states(info, x, bc, step_in, head_params, state, dt_out, cum_out, dt_t, cum_t)
    ssm_local(info, x, bc, head_params, y, cum_out, dt_t, cum_t)


def ssm_forward(info, x, bc, step_in, head_params):
    rows, width = x.shape
    f32 = jnp.float32
    return big_call(
        ssm_forward_kernel,
        (
            shape_of((rows, width), f32),
            shape_of((STATE_ROWS, width), jnp.bfloat16),
            shape_of((rows, TILE), f32),
            shape_of((rows, TILE), f32),
        ),
        info,
        x,
        bc,
        step_in,
        head_params,
        smem=1,
        scratch=(pltpu.VMEM((TILE, rows), f32), pltpu.VMEM((TILE, rows), f32)),
        flops=4 * rows * rows * width,
    )


def entering_of(info, cum):
    rows = cum.shape[0]
    return jnp.where(chunk_places(info, rows) < 0, jnp.exp(jnp.minimum(cum, 0.0)), 0.0)


def ssm_finish_kernel(info, y, bc, cum, state_in, z, gain, ssm_out, normed, scale):
    rows = y.shape[0]
    enter = entering_of(info, cum[...])
    narrow_c = bc[:, NS:]
    squares = jnp.zeros((rows, TILE), jnp.float32)
    tiles = MH // 2
    for i in range(tiles):
        cols = slice(i * TILE, (i + 1) * TILE)
        out = y[:, cols] + lane_pick(enter, 2 * i) * dot(narrow_c, state_in[:, cols])
        ssm_out[:, cols] = out
        gate = z[:, cols]
        gated = out * (gate * jax.nn.sigmoid(gate))
        squares = squares + gated * gated
    mean = jnp.sum(squares, axis=1, keepdims=True) * (1.0 / (tiles * TILE))
    r = lax.rsqrt(mean + NORM_EPS)
    scale[...] = jnp.broadcast_to(r, scale.shape)
    for i in range(tiles):
        cols = slice(i * TILE, (i + 1) * TILE)
        gate = z[:, cols]
        gated = ssm_out[:, cols] * (gate * jax.nn.sigmoid(gate))
        normed[:, cols] = (gated * r * gain[i : i + 1]).astype(jnp.bfloat16)


def ssm_finish(info, y, bc, cum, state_in, z, gain):
    rows, width = y.shape
    return big_call(
        ssm_finish_kernel,
        (
            shape_of((rows, width), jnp.float32),
            shape_of((rows, width), jnp.bfloat16),
            shape_of((rows, TILE), jnp.float32),
        ),
        info,
        y,
        bc,
        cum,
        state_in,
        z,
        gain,
        smem=1,
        flops=2 * rows * NS * width,
    )


def gate_back_kernel(info, dy, ssm_out, z, scale, gain, cum, bc, d_out, d_z, pull, g_gain):
    rows = dy.shape[0]
    tiles = MH // 2
    r = scale[:, :1]
    enter = entering_of(info, cum[...])
    c_t = bc[:, NS:].astype(jnp.float32).T.astype(jnp.bfloat16)
    inner = jnp.zeros((rows, TILE), jnp.float32)
    for i in range(tiles):
        cols = slice(i * TILE, (i + 1) * TILE)
        gate = z[:, cols]
        gated = ssm_out[:, cols] * (gate * jax.nn.sigmoid(gate))
        product = dy[:, cols] * gated
        g_gain[i : i + 1] = jnp.sum(product * r, axis=0, keepdims=True)
        inner = inner + product * gain[i : i + 1]
    coeff = jnp.sum(inner, axis=1, keepdims=True) * (1.0 / (tiles * TILE))
    for i in range(tiles):
        cols = slice(i * TILE, (i + 1) * TILE)
        gate = z[:, cols]
        sig = jax.nn.sigmoid(gate)
        silu = gate * sig
        out = ssm_out[:, cols]
        d_gated = r * (dy[:, cols] * gain[i : i + 1] - out * silu * (r * r * coeff))
        d_ssm = d_gated * silu
        d_out[:, cols] = d_ssm
        d_z[:, cols] = (d_gated * out * (sig * (1.0 + gate * (1.0 - sig)))).astype(jnp.bfloat16)
        pull[:, cols] = dot(c_t, (d_ssm * lane_pick(enter, 2 * i)).astype(jnp.bfloat16)).astype(
            jnp.bfloat16
        )


def gate_back(info, dy, ssm_out, z, scale, gain, cum, bc):
    rows, width = dy.shape
    return big_call(
        gate_back_kernel,
        (
            shape_of((rows, width), jnp.float32),
            shape_of((rows, width), jnp.bfloat16),
            shape_of((NS, width), jnp.bfloat16),
            shape_of(gain.shape, jnp.float32),
        ),
        info,
        dy,
        ssm_out,
        z,
        scale,
        gain,
        cum,
        bc,
        smem=1,
        flops=2 * rows * NS * width,
    )


def ssm_back_kernel(info, x, bc, dt, cum, grad, head_params, dx, d_bc, d_cum, d_dt, g_skip, cols_t, d_rows, between=None):
    rows, width = x.shape
    skip = head_params[2:3]
    cols_t[...] = cum[...].T
    row = lax.broadcasted_iota(jnp.int32, (rows, rows), 0)
    col = lax.broadcasted_iota(jnp.int32, (rows, rows), 1)
    at = lax.broadcasted_iota(jnp.int32, (1, rows), 1) + info[0]
    starts = seg_start(at, info) - info[0]
    narrow_b, narrow_c = bc[:, :NS], bc[:, NS:]
    products = dot_nt(narrow_b, narrow_c)
    skip_row = two_part(jnp.broadcast_to(skip, (8, TILE)), spread_heads(width))[:1]
    lane = lax.broadcasted_iota(jnp.int32, (SPAN, TILE), 1)
    parts = rows // SPAN
    d_products = [jnp.zeros((SPAN, rows - p * SPAN), jnp.float32) for p in range(parts)]
    d_rows[...] = jnp.zeros_like(d_rows)
    step_sums = [jnp.zeros((SPAN, TILE), jnp.float32) for p in range(parts)]
    skip_sums = []
    for i in range(MH // 2):
        cols = slice(i * TILE, (i + 1) * TILE)
        tile = x[:, cols]
        wide = grad[:, cols]
        narrow = wide.astype(jnp.bfloat16)
        skip_sums.append(jnp.sum(wide * tile.astype(jnp.float32), axis=0, keepdims=True))
        tile_sides = halves_of(tile)
        for part in range(parts):
            here = slice(part * SPAN, (part + 1) * SPAN)
            since = part * SPAN
            allowed = (row[here, since:] <= col[here, since:]) & (
                row[here, since:] >= starts[:, since:]
            )
            sides = []
            for side in range(2):
                h = 2 * i + side
                spread_log = cols_t[h : h + 1, since:] - cum[here, h : h + 1]
                decay = jnp.exp(jnp.where(allowed, spread_log, NEGATIVE_FILL))
                decay_dt = decay * dt[here, h : h + 1]
                mixing = products[here, since:] * decay_dt
                sides.append(dot(mixing.astype(jnp.bfloat16), narrow[since:]))
                d_mixing = dot_nt(tile_sides[side][here], narrow[since:])
                d_products[part] = d_products[part] + d_mixing * decay_dt
                whole = d_mixing * mixing
                d_rows[h : h + 1, since:] += jnp.sum(whole, axis=0, keepdims=True)
                weighed = d_mixing * (products[here, since:] * decay)
                step_sums[part] = jnp.where(
                    lane == h, jnp.sum(weighed, axis=1, keepdims=True), step_sums[part]
                )
            dx[here, cols] = (
                jnp.where(lane < MP, sides[0], sides[1]) + skip_row[:, cols] * wide[here]
            )
        if between is not None:
            between(i)
    all_steps = jnp.concatenate(step_sums, axis=0)
    d_dt[...] = all_steps
    d_cum[...] = d_rows[...].T - all_steps * dt[...]
    g_skip[...] = jnp.broadcast_to(
        two_part(
            jnp.broadcast_to(jnp.concatenate(skip_sums, axis=1), (8, width)), gather_heads(width)
        ),
        g_skip.shape,
    )
    full = jnp.concatenate(
        [
            d
            if p == 0
            else jnp.concatenate([jnp.zeros((SPAN, p * SPAN), jnp.float32), d], axis=1)
            for p, d in enumerate(d_products)
        ],
        axis=0,
    ).astype(jnp.bfloat16)
    d_bc[:, :NS] = dot(full, narrow_c)
    d_bc[:, NS:] = dot_tn(full, narrow_b)


def ssm_back(info, x, bc, dt, cum, grad, head_params):
    rows, width = x.shape
    f32 = jnp.float32
    return big_call(
        ssm_back_kernel,
        (
            shape_of((rows, width), f32),
            shape_of((rows, 2 * NS), f32),
            shape_of((rows, TILE), f32),
            shape_of((rows, TILE), f32),
            shape_of((8, TILE), f32),
        ),
        info,
        x,
        bc,
        dt,
        cum,
        grad,
        head_params,
        smem=1,
        scratch=(pltpu.VMEM((TILE, rows), f32), pltpu.VMEM((TILE, rows), f32)),
        flops=8 * rows * rows * width,
    )


def state_back_kernel(
    info, x, bc, dt, cum, grad, head_params, step_in, state_in, d_state, dx_in, d_bc_in, d_cum_in,
    d_dt_in, dx, d_bc, d_step, sums,
):
    rows, width = x.shape
    bias, rate = head_params[0:1], head_params[1:2]
    cums, steps = cum[...], dt[...]
    enter = entering_of(info, cums)
    last_start = seg_start(info[0] + rows - 1, info) - info[0]
    place = lax.broadcasted_iota(jnp.int32, (rows, 1), 0)
    end = cums[rows - 1 : rows]
    fade = jnp.where(place >= last_start, jnp.exp(jnp.minimum(end - cums, 0.0)), 0.0)
    leave = fade * steps
    through = jnp.where(last_start < 0, jnp.exp(end), 0.0)
    narrow_b, narrow_c = bc[:, :NS], bc[:, NS:]
    pick = gather_heads(width)
    d_leave = jnp.zeros((rows, TILE), jnp.float32)
    d_enter = jnp.zeros((rows, TILE), jnp.float32)
    d_b = d_bc_in[:, :NS]
    d_c = d_bc_in[:, NS:]
    link = jnp.zeros((8, TILE), jnp.float32)
    for i in range(MH // 2):
        cols = slice(i * TILE, (i + 1) * TILE)
        tile = x[:, cols].astype(jnp.float32)
        wide = grad[:, cols]
        pulled = d_state[:, cols]
        held = state_in[:, cols]
        from_b = dot(narrow_b, pulled)
        leave_tile = lane_pick(leave, 2 * i)
        dx[:, cols] = dx_in[:, cols] + leave_tile * from_b
        d_leave = d_leave + two_part(tile * from_b, pick[cols])
        d_enter = d_enter + two_part(wide * dot(narrow_c, held), pick[cols])
        d_b = d_b + dot_nt((tile * leave_tile).astype(jnp.bfloat16), pulled)
        d_c = d_c + dot_nt((wide * lane_pick(enter, 2 * i)).astype(jnp.bfloat16), held)
        meet = jnp.sum(
            pulled.astype(jnp.float32) * held.astype(jnp.float32), axis=0, keepdims=True
        )
        link = link + two_part(jnp.broadcast_to(meet, (8, TILE)), pick[cols])
    d_bc[:, :NS] = d_b
    d_bc[:, NS:] = d_c
    left = leave * d_leave
    d_cum = d_cum_in[...] + enter * d_enter - left
    at_end = jnp.sum(left, axis=0, keepdims=True) + through * link[:1]
    d_cum = d_cum + jnp.where(place == rows - 1, at_end, 0.0)
    row = lax.broadcasted_iota(jnp.int32, (rows, rows), 0)
    col = lax.broadcasted_iota(jnp.int32, (rows, rows), 1)
    d_log = exact(jnp.where(row <= col, 1.0, 0.0), d_cum)
    d_steps = d_dt_in[...] + fade * d_leave - d_log * rate
    d_pre = d_steps * jax.nn.sigmoid(step_in[...] + bias)
    d_pre = jnp.where(head_lanes(rows), d_pre, 0.0)
    d_step[...] = d_pre.astype(jnp.bfloat16)
    g_rate = jnp.sum(d_log * (-steps * rate), axis=0, keepdims=True)
    g_bias = jnp.sum(d_pre, axis=0, keepdims=True)
    line = lax.broadcasted_iota(jnp.int32, (8, TILE), 0)
    sums[...] = jnp.where(line == 0, g_rate, jnp.where(line == 1, g_bias, 0.0))


def state_back(info, *args):
    rows, width = args[0].shape
    f32 = jnp.float32
    return big_call(
        state_back_kernel,
        (
            shape_of((rows, width), f32),
            shape_of((rows, 2 * NS), f32),
            shape_of((rows, TILE), jnp.bfloat16),
            shape_of((8, TILE), f32),
        ),
        info,
        *args,
        smem=1,
        flops=12 * rows * NS * width,
    )


def join_states(earlier, later):
    decay = later[NS : NS + 1].astype(jnp.float32) + later[NS + 1 : NS + 2].astype(jnp.float32)
    before = earlier[NS : NS + 1].astype(jnp.float32) + earlier[NS + 1 : NS + 2].astype(jnp.float32)
    state = decay * earlier[:NS].astype(jnp.float32) + later[:NS].astype(jnp.float32)
    both = decay * before
    high = both.astype(jnp.bfloat16)
    low = (both - high.astype(jnp.float32)).astype(jnp.bfloat16)
    rest = jnp.zeros((STATE_ROWS - NS - 2, state.shape[1]), jnp.bfloat16)
    return jnp.concatenate([state.astype(jnp.bfloat16), high, low, rest], axis=0)


def scan_states(own, forward):
    place = lax.axis_index("seq")
    count = lax.axis_size("seq")
    nothing = jnp.concatenate(
        [
            jnp.zeros((NS, own.shape[1]), own.dtype),
            jnp.ones((1, own.shape[1]), own.dtype),
            jnp.zeros((STATE_ROWS - NS - 1, own.shape[1]), own.dtype),
        ],
        axis=0,
    )
    everything = lax.all_gather(own, "seq")

    def step(k, before):
        index = k if forward else count - 1 - k
        reached = index < place if forward else index > place
        part = lax.dynamic_index_in_dim(everything, index, 0, False)
        return jnp.where(reached, join_states(before, part), before)

    return lax.fori_loop(0, count, step, nothing)[:NS]


MESH = pl.DeviceIdType.MESH
ANY = pl.BlockSpec(memory_space=pl.ANY)
INTO_VMEM = pl.BlockSpec(memory_space=pltpu.VMEM)


def partners():
    seq, batch = lax.axis_index("seq"), lax.axis_index("batch")
    return {
        "far": (seq + 4 - 8 * (seq // 4), batch),
        "near": (seq + 2 - 4 * (seq // 2 % 2), batch),
        "x": (seq + 1 - 2 * (seq % 2), batch),
        "y": (seq, batch + 2 - 4 * (batch // 2)),
        "core": (seq, batch + 1 - 2 * (batch % 2)),
    }


def greet(others):
    barrier = pltpu.get_barrier_semaphore()
    for other in others:
        pl.semaphore_signal(barrier, inc=1, device_id=other, device_id_type=MESH)
    pl.semaphore_wait(barrier, len(others))


def remote(src, dst, send, recv, other):
    return pltpu.make_async_remote_copy(
        src_ref=src, dst_ref=dst, send_sem=send, recv_sem=recv, device_id=other, device_id_type=MESH
    )


def comm_call(kernel, outs, out_specs, args, in_specs, scratch, number, moved, limit=56):
    return pl.pallas_call(
        kernel,
        out_shape=list(outs),
        in_specs=in_specs,
        out_specs=out_specs,
        scratch_shapes=list(scratch),
        cost_estimate=pl.CostEstimate(flops=0, bytes_accessed=moved, transcendentals=0),
        compiler_params=pltpu.CompilerParams(
            collective_id=number, has_side_effects=True, vmem_limit_bytes=limit * 1024 * 1024
        ),
    )(*args)


def column_chunks(widths, aim=512, lean=0, z_last=None):
    pairs, late = [], []
    for p, width in enumerate(widths):
        tiles, first = width // TILE, 0
        orders, to = (("xyz", "yxz"), late) if p == z_last else (("xy", "yx"), pairs)
        count = max(1, (width + aim // 2) // (2 * aim)) if p != z_last else max(1, width // 512)
        for i in range(count):
            both = tiles // count + (1 if i < tiles % count else 0)
            one = (both + (0 if p == z_last else lean) + 1) // 2
            pair = []
            for cols, order in ((one * TILE, orders[0]), ((both - one) * TILE, orders[1])):
                pair.append((p, first, cols, order))
                first += cols
            to.append(tuple(pair))
    return pairs + late


def pairs_of(pairs, array):
    return [n for n, (one, other) in enumerate(pairs) if one[0] == array]


BITS = {"far": 1, "near": 2, "x": 4, "y": 8, "core": 16}
ORDERS = {
    "xy": ("far", "near", "x", "y"),
    "yx": ("far", "near", "y", "x"),
    "xyz": ("x", "y", "far", "near"),
    "yxz": ("y", "x", "far", "near"),
}


def runs(places):
    out = []
    for place in places:
        if out and out[-1][0] + out[-1][1] == place:
            out[-1] = (out[-1][0], out[-1][1] + 1)
        else:
            out.append((place, 1))
    return out


def gather_plan(order):
    held, plan = [0], []
    for name in ORDERS[order] + ("core",):
        plan.append((name, [(f, k, f + BITS[name]) for f, k in runs(held)]))
        held = sorted(held + [block + BITS[name] for block in held])
    return plan


def scatter_plan(order):
    held, plan = list(range(16)), []
    for name in reversed(ORDERS[order]):
        bit = BITS[name]
        sent = [i for i, block in enumerate(held) if block & bit]
        kept = [i for i, block in enumerate(held) if not block & bit]
        plan.append((name, runs(sent), runs(kept)))
        held = [held[i] for i in kept]
    return plan


def bit_apart(r):
    me = lax.axis_index("seq")
    far = (r // 4 + me // 4) % 2
    near = (r // 2 % 2 + me // 2 % 2) % 2
    side = (r % 2 + me % 2) % 2
    return 4 * far + 2 * near + side


def join_into(target, earlier, later):
    decay = later[NS : NS + 1].astype(jnp.float32) + later[NS + 1 : NS + 2].astype(jnp.float32)
    before = earlier[NS : NS + 1].astype(jnp.float32) + earlier[NS + 1 : NS + 2].astype(jnp.float32)
    both = decay * before
    high = both.astype(jnp.bfloat16).astype(jnp.float32)
    line = lax.broadcasted_iota(jnp.int32, (STATE_ROWS - NS, both.shape[1]), 0)
    tail = jnp.where(line == 0, high, jnp.where(line == 1, both - high, 0.0))
    for first in range(0, NS, 32):
        rows = slice(first, first + 32)
        target[rows] = (
            decay * earlier[rows].astype(jnp.float32) + later[rows].astype(jnp.float32)
        ).astype(jnp.bfloat16)
    target[NS:] = tail.astype(jnp.bfloat16)


SCAN_PARTS = 2


class StateScan:
    def __init__(self, forward, own, result, arrived, sent, before, send, recv, others):
        me = lax.axis_index("seq")
        self.seconds = []
        for bit in (me % 2, me // 2 % 2, me // 4):
            self.seconds.append(bit == 1 if forward else bit == 0)
        route = (others["x"], others["near"], others["far"])
        width = own.shape[1] // SCAN_PARTS
        self.parts = []
        for part in range(SCAN_PARTS):
            cols = pl.ds(part * width, width)
            here = (slice(None), cols)
            sources = (own.at[here], sent.at[0].at[here], sent.at[1].at[here])
            targets = [arrived.at[k].at[here] for k in range(3)]
            copies = [
                remote(sources[k], targets[k], send.at[k, part], recv.at[k, part], route[k])
                for k in range(3)
            ]
            befores = [before.at[k].at[here] for k in range(2)]
            self.parts.append((sources, targets, copies, befores, result.at[here]))

    def step(self, k):
        for part in self.parts:
            self.part_step(k, *part)

    def part_step(self, k, sources, targets, copies, before, result):
        if k == 0:
            copies[0].start()
            return
        copies[k - 1].wait_recv()
        other, mine = targets[k - 1], sources[k - 1]
        second = self.seconds[k - 1]

        @pl.when(second)
        def _():
            if k < 3:
                join_into(sources[k], other, mine)
            if k == 1:
                before[0][...] = other[...]
            elif k == 2:
                join_into(before[1], other, before[0])
            else:
                last = before[1]
                decay = last[NS : NS + 1].astype(jnp.float32) + last[NS + 1 : NS + 2].astype(
                    jnp.float32
                )
                result[...] = (
                    decay * other[:NS].astype(jnp.float32) + last[:NS].astype(jnp.float32)
                ).astype(jnp.bfloat16)

        @pl.when(jnp.logical_not(second))
        def _():
            if k < 3:
                join_into(sources[k], mine, other)
            if k == 1:
                line = lax.broadcasted_iota(jnp.int32, before[0].shape, 0)
                before[0][...] = jnp.where(line == NS, 1.0, 0.0).astype(jnp.bfloat16)
            elif k == 2:
                before[1][...] = before[0][...]
            else:
                result[...] = before[1][:NS]

        if k < 3:
            copies[k].start()

    def finish(self):
        for part in self.parts:
            for copy in part[2]:
                copy.wait_send()


def scan_scratch(width):
    rows = STATE_ROWS
    dma = pltpu.SemaphoreType.DMA
    narrow = jnp.bfloat16
    return [
        pltpu.VMEM((3, rows, width), narrow),
        pltpu.VMEM((2, rows, width), narrow),
        pltpu.VMEM((2, rows, width), narrow),
        dma((3, SCAN_PARTS)),
        dma((3, SCAN_PARTS)),
    ]


RIM = 8
COLS = 384


def own_order_into(target):
    width = target.shape[0]
    per = width // 32
    me = lax.axis_index("seq") * 4 + lax.axis_index("batch")
    step = 128

    def fill(i, carry):
        first = pl.multiple_of(i * step, step)
        row = lax.broadcasted_iota(jnp.int32, (step, width), 0) + first
        col = lax.broadcasted_iota(jnp.int32, (step, width), 1)
        j = col // per
        flipped = (j & 1) * 16 + (j & 2) * 4 + (j & 4) + (j & 8) // 4 + (j & 16) // 16
        source = (flipped ^ me) * per + col % per
        target[pl.ds(first, step)] = jnp.where(row == source, 1.0, 0.0).astype(target.dtype)
        return carry

    lax.fori_loop(0, width // step, fill, 0)


def three_part(left, right):
    high = left.astype(jnp.bfloat16)
    rest = left - high.astype(jnp.float32)
    mid = rest.astype(jnp.bfloat16)
    low = (rest - mid.astype(jnp.float32)).astype(jnp.bfloat16)
    return dot(high, right) + dot(mid, right) + dot(low, right)


def places_of(lens, rows):
    one, two, three = lens[0, 0], lens[0, 1], lens[0, 2]
    return [lax.axis_index("seq") * rows, one, one + two, one + two + three]


def head_rows(bias, rate_log, skip, target):
    lane = lax.broadcasted_iota(jnp.int32, (1, TILE), 1)
    for k, source in enumerate((bias, rate_log, skip)):
        row = jnp.zeros((1, TILE), jnp.float32)
        for h in range(MH):
            row = jnp.where(lane == h, source[h], row)
        if k == 1:
            row = jnp.where(lane < MH, jnp.exp(row), 0.0)
        target[k : k + 1] = row


def pair_columns(value, back):
    tiles = [value[:, i * TILE : (i + 1) * TILE] for i in range(PAIRS)]
    turned = [pltpu.roll(tile, HEAD_SIZE, 1) for tile in tiles]
    lane = lax.broadcasted_iota(jnp.int32, tiles[0].shape, 1)

    def head(i, side):
        return tiles[i // 2] if i % 2 == side else turned[i // 2]

    out = []
    for i in range(PAIRS):
        if back:
            first, second = 2 * i, 2 * i + 1
            group = QUERY_HEADS // KEY_VALUE_HEADS
            first, second = [2 * (h % group) + h // group for h in (first, second)]
        else:
            first, second = i, i + PAIRS
        out.append(jnp.where(lane < HEAD_SIZE, head(first, 0), head(second, 1)))
    return jnp.concatenate(out, axis=1)


def shards_into(w_attn, w_ssm_in, w_dt, w_out, conv, mix, out):
    f32, narrow = jnp.float32, jnp.bfloat16
    ssm_width = MH * MP
    xbc = w_ssm_in.shape[1] - ssm_width
    query = QUERY_HEADS * HEAD_SIZE
    attn = w_attn.shape[1]
    conv[:, :xbc] = w_ssm_in[:, ssm_width:]
    conv[:, xbc:] = jnp.zeros((conv.shape[0], TILE), narrow)
    block = conv.shape[0]
    row = lax.broadcasted_iota(jnp.int32, (block, block), 0)
    same = row == lax.broadcasted_iota(jnp.int32, (block, block), 1)
    conv[:, xbc : xbc + MH] = dot_nt(jnp.where(same, 1.0, 0.0).astype(narrow), w_dt[...]).astype(
        narrow
    )
    mix[:, :query] = pair_columns(w_attn[:, :query].astype(f32), False).astype(narrow)
    mix[:, query:attn] = w_attn[:, query:]
    mix[:, attn:] = w_ssm_in[:, :ssm_width]
    out[:, :query] = pair_columns(w_out[:, :query].astype(f32), False).astype(narrow)
    out[:, query:] = w_out[:, query:]


class Stage:
    def __init__(self, sources, targets, sems):
        self.copies = [
            pltpu.make_async_copy(source, target, sems.at[k])
            for k, (source, target) in enumerate(zip(sources, targets))
        ]
        self.open = {}

    def start(self, *which):
        for k in which:
            self.copies[k].start()
            self.open[k] = True

    def need(self, *which):
        for k in which:
            if self.open.pop(k, False):
                self.copies[k].wait()

    def finish(self):
        self.need(*list(self.open))


class Gather:
    def __init__(self, ins, outs, pairs, send, recv, local, others):
        self.ins, self.outs, self.pairs = ins, outs, pairs
        self.send, self.recv, self.local, self.others = send, recv, local, others
        self.started = {}
        self.block = ins[0].shape[0]

    def own(self):
        copies = []
        for p in range(len(self.ins)):
            copy = pltpu.make_async_copy(
                self.ins[p], self.outs[p].at[pl.ds(0, self.block)], self.local.at[p]
            )
            copy.start()
            copies.append(copy)
        for copy in copies:
            copy.wait()

    def step(self, n, stage):
        for side in range(2):
            p, column, cols, order = self.pairs[n][side]
            if stage > 0:
                for copy in self.started[n, side, stage - 1]:
                    copy.wait_recv()
            if stage == 5:
                continue
            name, moves = gather_plan(order)[stage]
            copies = []
            for k, (first, rows, there) in enumerate(moves):
                block = self.block
                copy = remote(
                    self.outs[p].at[pl.ds(first * block, rows * block), pl.ds(column, cols)],
                    self.outs[p].at[pl.ds(there * block, rows * block), pl.ds(column, cols)],
                    self.send.at[2 * n + side, stage, k],
                    self.recv.at[2 * n + side, stage, k],
                    self.others[name],
                )
                copy.start()
                copies.append(copy)
            self.started[n, side, stage] = copies

    def finish(self):
        for copies in self.started.values():
            for copy in copies:
                copy.wait_send()


def around():
    seq, batch = lax.axis_index("seq"), lax.axis_index("batch")
    return ((seq + 7) % 8, batch), ((seq + 1) % 8, batch)


def conv_masks(info, rows):
    at = lax.broadcasted_iota(jnp.int32, (rows, 1), 0) + info[0]
    start = seg_start(at, info)
    return [jnp.where(at - (CONV - 1) + i >= start, 1.0, 0.0) for i in range(CONV)]


def conv_forward(info, raw, conv_w, conv_b, pre, x, bc):
    rows = x.shape[0]
    masks = conv_masks(info, rows)
    tiles = pre.shape[1] // TILE
    split = x.shape[1] // TILE
    for i in range(tiles):
        cols = slice(i * TILE, (i + 1) * TILE)
        total = jnp.broadcast_to(conv_b[i : i + 1], (rows, TILE))
        for k in range(CONV):
            first = RIM - (CONV - 1) + k
            shifted_rows = jnp.where(masks[k] > 0.0, raw[first : first + rows, cols], 0.0)
            total = total + conv_w[k : k + 1, cols] * shifted_rows
        pre[:, cols] = total
        out = (total * jax.nn.sigmoid(total)).astype(jnp.bfloat16)
        if i < split:
            x[:, cols] = out
        else:
            bc[:, (i - split) * TILE : (i - split + 1) * TILE] = out


def front_kernel(
    count, pairs, lens, bias, rate_log, skip, layer_x, layer_g, norm_gain, mlp_gain, freqs, conv_w,
    conv_b, w_attn, w_ssm_in, w_dt, w_out, w_gate_up, w_down, *refs
):
    fulls, made, refs = refs[:count], refs[count : count + 23], refs[count + 23 :]
    near, refs = refs[:25], refs[25:]
    writes = Stage((*near,), (*fulls[:2], *made), refs[-1])
    fulls = (*near[:2], *fulls[2:])
    (
        x_own, g_own, gains_own, normed, q, kv, gate_z, raw, pre, x, bc, y, state, dt, cum,
        out, out_t, lse, state_in, order, cosine, sine, head_params,
    ) = near[2:]
    (
        s_conv, s_mix, s_out, gains,
        attn_proj, dt_t, cum_t, heads, acc, top, total, arrived, sent, before,
        scan_send, scan_recv, send, recv, w_send, w_recv, w_local, rim_send, rim_recv,
    ) = refs[:-1]
    ins = (s_conv, s_mix, s_out, w_gate_up, w_down)
    others = partners()
    previous, following = around()
    greet(list(others.values()) + [previous, following])
    me = lax.axis_index("seq")
    rows, width = layer_x.shape
    info = places_of(lens, rows)
    shards_into(w_attn, w_ssm_in, w_dt, w_out, s_conv, s_mix, s_out)
    gather = Gather(ins, fulls, pairs, w_send, w_recv, w_local, others)
    gather.own()

    first = len(pairs_of(pairs, 0)) + len(pairs_of(pairs, 1))
    small = pairs_of(pairs, 2)
    waves = {}
    for n in reversed(range(len(pairs))):
        for stage in range(6):
            late = 1 if n >= first and stage >= 2 else 0
            wave = n - small[0] + 2 * stage if n in small else n + stage + late
            waves.setdefault(wave, []).append((n, stage))

    def pump(*which):
        for wave in which:
            for n, stage in waves.pop(wave, []):
                gather.step(n, stage)

    conv_wave = pairs_of(pairs, 0)[-1] + 5
    mix_wave = pairs_of(pairs, 1)[-1] + 5
    pump(0)
    own_order_into(order)
    head_rows(bias, rate_log, skip, head_params)
    gains[...] = jnp.zeros_like(gains)
    for k, source in enumerate((norm_gain, mlp_gain)):
        for i in range(width // TILE):
            gains[k : k + 1, i * TILE : (i + 1) * TILE] = source[i : i + 1]
    pump(1)
    at = lax.broadcasted_iota(jnp.int32, (rows, 1), 0) + info[0]
    angles = (at - seg_start(at, info)).astype(jnp.float32) * freqs[...]
    cosine[...] = jnp.cos(angles)
    sine[...] = jnp.sin(angles)
    x_own[...] = dot(layer_x[...], order[...]).astype(jnp.bfloat16)
    pump(2)
    gains_own[...] = three_part(gains[...], order[...])
    wide = x_own[...].astype(jnp.float32)
    scale = lax.rsqrt(jnp.mean(wide * wide, axis=-1, keepdims=True) + NORM_EPS)
    normed[...] = (wide * scale * gains_own[0:1]).astype(jnp.bfloat16)
    pump(3)
    g_own[...] = dot(layer_g[...], order[...]).astype(jnp.bfloat16)
    pump(*range(4, conv_wave + 1))

    full_conv, full_mix = fulls[0], fulls[1]
    xbc = pre.shape[1]
    conv_cols = full_conv.shape[1] // COLS
    attn_cols = attn_proj.shape[1] // COLS
    gate_cols = gate_z.shape[1] // COLS

    def project(weights, first, target, row, count_cols):
        def one(j, carry):
            cols = pl.ds(pl.multiple_of(j * COLS, TILE), COLS)
            there = pl.ds(pl.multiple_of(first + j * COLS, TILE), COLS)
            target[row : row + rows, cols] = dot(normed[...], weights[:, there])
            return carry

        lax.fori_loop(0, count_cols, one, 0)

    def at(r):
        return kv.at[pl.ds(r * rows, rows)]

    routes = {4: ("far", 0), 2: ("near", 0), 6: ("near", 4)}
    routes.update({r: ("x", r - 1) for r in (1, 3, 5, 7)})
    copies = {
        r: remote(at(src), at(r), send.at[r], recv.at[r], others[name])
        for r, (name, src) in routes.items()
    }
    project(full_conv, 0, raw, RIM, conv_cols)
    rim = remote(
        raw.at[pl.ds(rows, RIM)], raw.at[pl.ds(0, RIM)], rim_send.at[0], rim_recv.at[0], following
    )
    rim.start()
    pump(*range(conv_wave + 1, mix_wave))
    rim.wait_recv()
    conv_forward(info, raw, conv_w, conv_b, pre, x, bc)
    step_in = raw.at[pl.ds(RIM, rows), pl.ds(xbc, TILE)]
    ssm_states(info, x, bc, step_in, head_params, state, dt, cum, dt_t, cum_t)
    scan = StateScan(True, state, state_in, arrived, sent, before, scan_send, scan_recv, others)
    scan.step(0)
    writes.start(0, 9, 10, 11, 12, 14, 15, 16)
    pump(mix_wave)
    project(full_mix, 0, attn_proj, 0, attn_cols)
    rope_kernel(attn_proj, cosine, sine, q, kv.at[pl.ds(0, rows)])
    copies[4].start()
    copies[2].start()
    copies[1].start()
    pump(mix_wave + 1)
    project(full_mix, attn_proj.shape[1], gate_z, 0, gate_cols)
    writes.start(1, 8, 6, 2, 3, 4, 5, 21, 22, 23, 24)
    attend_start(q, heads, acc, top, total)

    def attend(r):
        block = bit_apart(r)

        @pl.when(block <= me)
        def _():
            place = pl.ds(pl.multiple_of(r * rows, rows), rows)
            keys = kv[place, :TILE]
            values_t = kv[place, TILE:].astype(jnp.float32).T.astype(jnp.bfloat16)
            attend_block(info, block, keys, values_t, heads, acc, top, total)

    def several(first, gap, count_blocks):
        def body(j, carry):
            attend(first + j * gap)
            return carry

        lax.fori_loop(0, count_blocks, body, 0)

    scan.step(1)
    copies[4].wait_recv()
    copies[6].start()
    copies[5].start()
    copies[2].wait_recv()
    copies[3].start()
    copies[6].wait_recv()
    copies[7].start()
    pump(mix_wave + 2)
    several(0, 4, 2)
    pump(mix_wave + 3)
    ssm_local(info, x, bc, head_params, y, cum, dt_t, cum_t)
    writes.start(13)
    scan.step(2)
    pump(mix_wave + 4)
    several(2, 4, 2)
    pump(mix_wave + 5)
    for r in (1, 3, 5, 7):
        copies[r].wait_recv()
    writes.start(7)
    several(1, 2, 2)
    pump(mix_wave + 6)
    several(5, 2, 2)
    pump(mix_wave + 7)
    lse[...] = top[...] + jnp.log(total[...])
    attend_write(acc, total, out, out_t)
    scan.step(3)
    writes.start(17, 18, 19, 20)
    pump(*sorted(waves))
    gather.finish()
    writes.finish()
    scan.finish()
    rim.wait_send()
    for copy in copies.values():
        copy.wait_send()


def front(lens, bias, rate_log, skip, layer_x, layer_g, norm_gain, mlp_gain, freqs, conv_w, conv_b, weights):
    w_attn, w_ssm_in, w_dt, w_out, w_gate_up, w_down = weights
    rows, width = layer_x.shape
    f32, narrow = jnp.float32, jnp.bfloat16
    block = w_attn.shape[0]
    query_width = QUERY_HEADS * HEAD_SIZE
    pair_width = 2 * KEY_VALUE_HEADS * HEAD_SIZE
    ssm_width = MH * MP
    xbc = conv_w.shape[1]
    widths = [
        xbc + TILE, w_attn.shape[1] + ssm_width, w_out.shape[1], w_gate_up.shape[1],
        w_down.shape[1],
    ]
    count = len(widths)
    pairs = column_chunks(widths, z_last=2)
    fulls = [shape_of((width, w), narrow) for w in widths]
    outs = fulls + [
        shape_of((rows, width), narrow),
        shape_of((rows, width), narrow),
        shape_of((8, width), f32),
        shape_of((rows, width), narrow),
        shape_of((rows, query_width), narrow),
        shape_of((8 * rows, pair_width), narrow),
        shape_of((rows, ssm_width), f32),
        shape_of((rows + RIM, widths[0]), f32),
        shape_of((rows, xbc), f32),
        shape_of((rows, ssm_width), narrow),
        shape_of((rows, 2 * NS), narrow),
        shape_of((rows, ssm_width), f32),
        shape_of((STATE_ROWS, ssm_width), narrow),
        shape_of((rows, TILE), f32),
        shape_of((rows, TILE), f32),
        shape_of((rows, query_width), narrow),
        shape_of((query_width, rows), f32),
        shape_of((QUERY_HEADS, rows), f32),
        shape_of((NS, ssm_width), narrow),
        shape_of((width, width), narrow),
        shape_of((rows, TILE), f32),
        shape_of((rows, TILE), f32),
        shape_of((8, TILE), f32),
    ]
    dma = pltpu.SemaphoreType.DMA
    scratch = [pltpu.VMEM(o.shape, o.dtype) for o in (*outs[:2], *outs[count:])]
    scratch += [
        *(pltpu.VMEM((block, widths[k]), narrow) for k in (0, 1, 2)),
        pltpu.VMEM((8, width), f32),
        pltpu.VMEM((rows, query_width + pair_width), f32),
        pltpu.VMEM((TILE, rows), f32),
        pltpu.VMEM((TILE, rows), f32),
        pltpu.VMEM((QUERY_HEADS, rows, TILE), narrow),
        pltpu.VMEM((QUERY_HEADS, HEAD_SIZE, rows), f32),
        pltpu.VMEM((QUERY_HEADS, rows), f32),
        pltpu.VMEM((QUERY_HEADS, rows), f32),
        *scan_scratch(ssm_width),
        dma((8,)),
        dma((8,)),
        dma((2 * len(pairs), 5, 4)),
        dma((2 * len(pairs), 5, 4)),
        dma((count,)),
        dma((1,)),
        dma((1,)),
        dma((25,)),
    ]
    result = comm_call(
        lambda *refs: front_kernel(count, pairs, *refs),
        outs,
        [ANY] * len(outs),
        (
            lens, bias, rate_log, skip, layer_x, layer_g, norm_gain, mlp_gain, freqs, conv_w,
            conv_b, *weights,
        ),
        [pl.BlockSpec(memory_space=pltpu.SMEM)] * 4 + [INTO_VMEM] * 13,
        scratch,
        0,
        200_000_000,
    )
    return result[:count], result[count:]


def middle_kernel(
    lens, y, bc, cum, state_in, state_own, z, ssm_gain, attended, x_own, g_own, gains, order,
    hbm_out, hbm_gu, hbm_down,
    layer_out, joined, hidden, d_gu, normed_two, d_mixer, d_middle, d_ssm, d_z, pull, att_grad,
    g_ssm, g_mlp,
    w_out, w_gu, w_down, ssm_out, scale, middle, gate_up, d_normed, dy, narrow, sems,
):
    rows, width = x_own.shape
    info = places_of(lens, rows)
    copies = [
        pltpu.make_async_copy(src, dst, sems.at[k])
        for k, (src, dst) in enumerate(((hbm_out, w_out), (hbm_gu, w_gu), (hbm_down, w_down)))
    ]
    for copy in copies:
        copy.start()
    attn = attended.shape[1]
    ff = hidden.shape[1]
    step = 512

    def tiles(count, body):
        def one(j, carry):
            body(pl.ds(pl.multiple_of(j * step, step), step), j * step)
            return carry

        lax.fori_loop(0, count // step, one, 0)

    joined[:, :attn] = attended[...]
    ssm_finish_kernel(
        info, y, bc, cum, state_in, z, ssm_gain, ssm_out,
        joined.at[:, pl.ds(attn, joined.shape[1] - attn)], scale,
    )
    copies[0].wait()

    def add_mixers(here, first):
        middle[:, here] = x_own[:, here].astype(jnp.float32) + dot_nt(joined[...], w_out[here])

    tiles(width, add_mixers)
    wide = middle[...]
    r = lax.rsqrt(jnp.mean(wide * wide, axis=-1, keepdims=True) + NORM_EPS)
    normed_two[...] = (wide * r * gains[1:2]).astype(jnp.bfloat16)
    copies[1].wait()

    def up_project(here, first):
        there = pl.ds(pl.multiple_of(ff + first, step), step)
        gate = dot(normed_two[...], w_gu[:, here])
        up = dot(normed_two[...], w_gu[:, there])
        gate_up[:, here] = gate
        gate_up[:, there] = up
        hidden[:, here] = (gate * jax.nn.sigmoid(gate) * up).astype(jnp.bfloat16)

    tiles(ff, up_project)
    copies[2].wait()

    def down_project(here, first):
        narrow[:, here] = (middle[:, here] + dot_nt(hidden[...], w_down[here])).astype(jnp.bfloat16)

    tiles(width, down_project)

    def plain(here, first):
        layer_out[:, here] = dot_nt(narrow[...], order[here]).astype(jnp.bfloat16)

    tiles(width, plain)

    def down_back(here, first):
        there = pl.ds(pl.multiple_of(ff + first, step), step)
        d_hidden = dot(g_own[...], w_down[:, here])
        gate, up = gate_up[:, here], gate_up[:, there]
        sig = jax.nn.sigmoid(gate)
        d_gate = d_hidden * up * (sig * (1.0 + gate * (1.0 - sig)))
        d_gu[:, here] = d_gate.astype(jnp.bfloat16)
        d_gu[:, there] = (d_hidden * gate * sig).astype(jnp.bfloat16)

    tiles(ff, down_back)

    def up_back(here, first):
        d_normed[:, here] = dot_nt(d_gu[...], w_gu[here])

    tiles(width, up_back)
    grads = d_normed[...]
    wide = middle[...]
    g_mlp[...] = jnp.sum(grads * wide * r, axis=0, keepdims=True)
    inner = grads * gains[1:2]
    coeff = jnp.mean(inner * wide, axis=-1, keepdims=True)
    total = g_own[...].astype(jnp.float32) + r * (inner - wide * (r * r * coeff))
    d_middle[...] = total
    d_mixer[...] = total.astype(jnp.bfloat16)

    def att_back(here, first):
        att_grad[:, here] = dot(d_mixer[...], w_out[:, here]).astype(jnp.bfloat16)

    tiles(attn, att_back)

    def ssm_part(here, first):
        there = pl.ds(pl.multiple_of(attn + first, step), step)
        dy[:, here] = dot(d_mixer[...], w_out[:, there])

    tiles(dy.shape[1], ssm_part)
    gate_back_kernel(
        info, dy, ssm_out, z, scale, ssm_gain, cum, bc, d_ssm, d_z, pull.at[pl.ds(0, NS)], g_ssm
    )
    pull[NS:] = state_own[NS:]


def middle_part(lens, y, bc, cum, state_in, state_own, z, ssm_gain, attended, x_own, g_own, gains, order, w_out, w_gu, w_down):
    rows, width = x_own.shape
    ssm_width, attn = y.shape[1], attended.shape[1]
    ff = w_down.shape[1]
    f32, narrow = jnp.float32, jnp.bfloat16
    outs = [
        shape_of((rows, width), narrow),
        shape_of((rows, attn + ssm_width), narrow),
        shape_of((rows, ff), narrow),
        shape_of((rows, 2 * ff), narrow),
        shape_of((rows, width), narrow),
        shape_of((rows, width), narrow),
        shape_of((rows, width), f32),
        shape_of((rows, ssm_width), f32),
        shape_of((rows, ssm_width), narrow),
        shape_of((STATE_ROWS, ssm_width), narrow),
        shape_of((rows, attn), narrow),
        shape_of(ssm_gain.shape, f32),
        shape_of((1, width), f32),
    ]
    args = (
        lens, y, bc, cum, state_in, state_own, z, ssm_gain, attended, x_own, g_own, gains, order,
        w_out, w_gu, w_down,
    )
    return pl.pallas_call(
        middle_kernel,
        out_shape=outs,
        in_specs=[pl.BlockSpec(memory_space=pltpu.SMEM)] + [INTO_VMEM] * 12 + [ANY] * 3,
        out_specs=[INTO_VMEM] * len(outs),
        scratch_shapes=[
            pltpu.VMEM(w_out.shape, narrow),
            pltpu.VMEM(w_gu.shape, narrow),
            pltpu.VMEM(w_down.shape, narrow),
            pltpu.VMEM((rows, ssm_width), f32),
            pltpu.VMEM((rows, TILE), f32),
            pltpu.VMEM((rows, width), f32),
            pltpu.VMEM((rows, 2 * ff), f32),
            pltpu.VMEM((rows, width), f32),
            pltpu.VMEM((rows, ssm_width), f32),
            pltpu.VMEM((rows, width), narrow),
            pltpu.SemaphoreType.DMA((3,)),
        ],
        compiler_params=pltpu.CompilerParams(vmem_limit_bytes=60 * 1024 * 1024),
    )(*args)


def turn_over(value):
    return value.astype(jnp.float32).T.astype(jnp.bfloat16)


class Scatter:
    def __init__(self, ins, outs, arrived, pairs, send, recv, others):
        self.ins, self.outs, self.arrived, self.pairs = ins, outs, arrived, pairs
        self.send, self.recv, self.others = send, recv, others
        self.block = ins[0].shape[0] // 16
        self.started = {}

    def source(self, p, stage):
        return self.ins[p] if stage == 0 else self.arrived[4 * p + stage - 1]

    def step(self, n, stage):
        for side in range(2):
            if stage > 0:
                self.take(n, side, stage - 1)
            if stage < 4:
                self.begin(n, side, stage)

    def begin(self, n, side, stage):
        p, column, width, order = self.pairs[n][side]
        cols = pl.ds(column, width)
        name, sent, unused_kept = scatter_plan(order)[stage]
        copies, row, block = [], 0, self.block
        for k, (first, count) in enumerate(sent):
            copy = remote(
                self.source(p, stage).at[pl.ds(first * block, count * block), cols],
                self.arrived[4 * p + stage].at[pl.ds(row * block, count * block), cols],
                self.send.at[2 * n + side, stage, k],
                self.recv.at[2 * n + side, stage, k],
                self.others[name],
            )
            copy.start()
            copies.append(copy)
            row += count
        self.started[n, side, stage] = copies

    def take(self, n, side, stage):
        p, column, width, order = self.pairs[n][side]
        cols = slice(column, column + width)
        source, got = self.source(p, stage), self.arrived[4 * p + stage]
        target = self.outs[p] if stage == 3 else got
        unused_name, unused_sent, kept = scatter_plan(order)[stage]
        row, block = 0, self.block
        for k, (first, count) in enumerate(kept):
            self.started[n, side, stage][k].wait_recv()

            def add(i, carry):
                at = pl.multiple_of(i * block, block)
                there = pl.ds(row * block + at, block)
                total = source[pl.ds(first * block + at, block), cols].astype(jnp.float32) + got[
                    there, cols
                ].astype(jnp.float32)
                target[there, cols] = total.astype(target.dtype)
                return carry

            lax.fori_loop(0, count, add, 0)
            row += count

    def finish(self):
        for copies in self.started.values():
            for copy in copies:
                copy.wait_send()


def scatter_scratch(widths, size):
    scratch = []
    for width in widths:
        scratch += [pltpu.VMEM((size >> (s + 1), width), jnp.bfloat16) for s in range(4)]
    return scratch


def weight_products(left_t, right, theirs, target):
    rows = right.shape[0]
    step = 256 if right.shape[1] % 256 == 0 else TILE

    def one(j, carry):
        cols = pl.ds(pl.multiple_of(j * step, step), step)
        product = dot(left_t[:, :rows], right[:, cols]) + dot(left_t[:, rows:], theirs[:, cols])
        target[:, cols] = product.astype(target.dtype)
        return carry

    lax.fori_loop(0, right.shape[1] // step, one, 0)


def conv_back_start(info, dx, d_bc, pre, raw, d_pre, g_conv):
    rows, split = dx.shape[0], dx.shape[1] // TILE
    masks = conv_masks(info, rows)
    g_conv[...] = jnp.zeros_like(g_conv)
    for i in range(pre.shape[1] // TILE):
        cols = slice(i * TILE, (i + 1) * TILE)
        if i < split:
            grad = dx[:, cols]
        else:
            grad = d_bc[:, (i - split) * TILE : (i - split + 1) * TILE]
        value = pre[:, cols]
        sig = jax.nn.sigmoid(value)
        grad = grad * (sig * (1.0 + value * (1.0 - sig)))
        d_pre[:rows, cols] = grad
        for k in range(CONV):
            first = RIM - (CONV - 1) + k
            term = jnp.where(masks[k] > 0.0, raw[first : first + rows, cols], 0.0)
            g_conv[k : k + 1, cols] = jnp.sum(grad * term, axis=0, keepdims=True)
        g_conv[CONV : CONV + 1, cols] = jnp.sum(grad, axis=0, keepdims=True)


def conv_back_end(info, d_pre, conv_w, d_raw):
    rows = d_raw.shape[0]
    at = lax.broadcasted_iota(jnp.int32, (rows, 1), 0) + info[0]
    masks = [
        jnp.where(seg_start(at + (CONV - 1) - k, info) <= at, 1.0, 0.0) for k in range(CONV)
    ]
    for i in range(d_pre.shape[1] // TILE):
        cols = slice(i * TILE, (i + 1) * TILE)
        total = jnp.zeros((rows, TILE), jnp.float32)
        for k in range(CONV):
            first = CONV - 1 - k
            part = jnp.where(masks[k] > 0.0, d_pre[first : first + rows, cols], 0.0)
            total = total + conv_w[k : k + 1, cols] * part
        d_raw[:, cols] = total.astype(jnp.bfloat16)


def back_kernel(pairs, *refs):
    (
        lens, head_params, conv_w, cosine, sine, q, kv, grad, out_t, lse, pull, x, bc, dt, cum,
        d_ssm, raw, state_in, pre, normed, normed_two, d_mixer, grad_rows, hidden, joined, d_gu,
        d_z,
    ) = refs[:27]
    (
        d_conv, d_attn, g_conv, head_sums, g_skip, p_conv, p_attn, out_down, out_gu, out_out, out_z,
    ) = refs[27:38]
    refs = refs[38:]
    partials, refs = refs[:4], refs[4:]
    arrived_w, refs = refs[:16], refs[16:]
    (
        half_grad, half_two, half_mixer, their_hidden, their_joined, their_gu, their_z, their_normed,
        their_conv, their_attn, left_t, heads, grads, delta, acc, dkv, from_x, from_far, from_near, dq, d_pair,
        d_cum, d_dt, cols_t, d_rows, d_pre,
        arrived, sent, before, scan_send, scan_recv, send, recv, swap_send, swap_recv,
        w_send, w_recv, rim_send, rim_recv,
    ) = refs
    others = partners()
    previous, following = around()
    greet(list(others.values()) + [previous, following])
    me = lax.axis_index("seq")
    rows = q.shape[0]
    info = places_of(lens, rows)
    half = normed.shape[1] // 2
    xbc = pre.shape[1]
    dx = d_pre.at[pl.ds(0, rows), pl.ds(0, x.shape[1])]
    d_bc = d_pre.at[pl.ds(0, rows), pl.ds(x.shape[1], 2 * NS)]
    d_state = arrived.at[0, pl.ds(0, NS)]
    scan = StateScan(False, pull, d_state, arrived, sent, before, scan_send, scan_recv, others)
    scan.step(0)
    behind = pl.ds(half, half)
    given = [
        (grad_rows.at[:, behind], half_grad),
        (hidden, their_hidden),
        (d_mixer.at[:, behind], half_mixer),
        (joined, their_joined),
        (normed_two.at[:, behind], half_two),
        (d_gu, their_gu),
        (normed.at[:, behind], their_normed),
        (d_z, their_z),
    ]
    swaps = [
        remote(give, take, swap_send.at[k], swap_recv.at[k], others["core"])
        for k, (give, take) in enumerate(given)
    ]
    for copy in swaps:
        copy.start()
    scatter = Scatter(
        partials, (out_down, out_gu, out_out, out_z), arrived_w, pairs, w_send, w_recv, others
    )

    def weights(k, left, left_half, right, theirs):
        first = 2 * (0, 2, 1, 3)[k]
        swaps[first].wait_recv()
        swaps[first + 1].wait_recv()
        left_t[:, :rows] = turn_over(left[:, :half])
        left_t[:, rows:] = turn_over(left_half[...])
        weight_products(left_t, right, theirs, partials[k])

    small = pairs_of(pairs, 2)
    waves = {}
    for n in range(len(pairs)):
        for stage in range(5):
            begin = 1 + (n - small[0]) // 2 if n in small else n
            waves.setdefault(begin + stage, []).append((n, stage))

    def pump(wave):
        for n, stage in waves.pop(wave):
            scatter.step(n, stage)

    attend_back_start(q, grad, out_t, heads, grads, delta, acc)

    def block_back(r):
        block = bit_apart(r)
        place = pl.ds(pl.multiple_of(r * rows, rows), rows)

        @pl.when(block <= me)
        def _():
            attend_back_block(
                info, block, kv[place, :TILE], kv[place, TILE:], lse, dkv.at[r], heads, grads,
                delta, acc,
            )

        @pl.when(block > me)
        def _():
            dkv[r] = jnp.zeros(dkv.shape[1:], dkv.dtype)

    def several(first, gap, count):
        def body(j, carry):
            block_back(first + j * gap)
            return carry

        lax.fori_loop(0, count, body, 0)

    def add(target, source):
        target[...] = (target[...].astype(jnp.float32) + source[...].astype(jnp.float32)).astype(
            jnp.bfloat16
        )

    weights(0, grad_rows, half_grad, hidden, their_hidden)
    pump(0)
    weights(2, d_mixer, half_mixer, joined, their_joined)
    several(1, 2, 4)
    over_x = [
        remote(dkv.at[2 * k + 1], from_x.at[k], send.at[k], recv.at[k], others["x"])
        for k in range(4)
    ]
    for copy in over_x:
        copy.start()
    scan.step(1)
    weights(1, normed_two, half_two, d_gu, their_gu)
    pump(1)
    several(4, 2, 2)
    over_far = [
        remote(dkv.at[4 + 2 * k], from_far.at[k], send.at[4 + k], recv.at[4 + k], others["far"])
        for k in range(2)
    ]
    for k in range(2):
        over_x[2 + k].wait_recv()
        add(dkv.at[4 + 2 * k], from_x.at[2 + k])
        over_far[k].start()
    scan.step(2)
    pump(2)
    several(0, 2, 2)
    for k in range(2):
        over_x[k].wait_recv()
        add(dkv.at[2 * k], from_x.at[k])
    over_far[1].wait_recv()
    add(dkv.at[2], from_far.at[1])
    over_near = remote(dkv.at[2], from_near, send.at[6], recv.at[6], others["near"])
    over_near.start()
    weights(3, normed, their_normed, d_z, their_z)
    pump(3)
    ssm_back_kernel(
        info, x, bc, dt, cum, d_ssm, head_params, dx, d_bc, d_cum, d_dt, g_skip, cols_t, d_rows
    )
    pump(4)
    scan.step(3)
    d_step = d_conv.at[:, pl.ds(xbc, TILE)]
    step_in = raw.at[pl.ds(RIM, rows), pl.ds(xbc, TILE)]
    state_back_kernel(
        info, x, bc, dt, cum, d_ssm, head_params, step_in, state_in, d_state, dx, d_bc, d_cum,
        d_dt, dx, d_bc, d_step, head_sums,
    )
    conv_back_start(info, dx, d_bc, pre, raw, d_pre, g_conv)
    rim = remote(
        d_pre.at[pl.ds(0, RIM)], d_pre.at[pl.ds(rows, RIM)], rim_send.at[0], rim_recv.at[0],
        previous,
    )
    rim.start()
    pump(5)
    over_far[0].wait_recv()
    over_near.wait_recv()
    attend_back_write(acc, dq)
    d_pair[...] = (
        dkv[0].astype(jnp.float32)
        + from_far[0].astype(jnp.float32)
        + from_near[...].astype(jnp.float32)
    )
    rope_back_kernel(dq, d_pair, cosine, sine, d_attn)
    last_swaps = [
        remote(give, take, swap_send.at[8 + k], swap_recv.at[8 + k], others["core"])
        for k, (give, take) in enumerate(((d_attn, their_attn), (d_conv, their_conv)))
    ]
    last_swaps[0].start()
    rim.wait_recv()
    conv_back_end(info, d_pre, conv_w, d_conv.at[:, pl.ds(0, xbc)])
    last_swaps[1].start()
    pump(6)
    last_swaps[0].wait_recv()
    weight_products(left_t, d_attn, their_attn, p_attn)
    last_swaps[1].wait_recv()
    weight_products(left_t, d_conv, their_conv, p_conv)
    for wave in sorted(waves):
        pump(wave)
    swaps += last_swaps
    scatter.finish()
    scan.finish()
    rim.wait_send()
    for copy in over_x + over_far + [over_near] + swaps:
        copy.wait_send()


def back(lens, *args):
    (
        head_params, conv_w, cosine, sine, q, kv, grad, out_t, lse, pull, x, bc, dt, cum,
        d_ssm, raw, state_in, pre, normed, normed_two, d_mixer, grad_rows, hidden, joined, d_gu,
        d_z,
    ) = args
    rows, query_width = q.shape
    width = normed.shape[1]
    half = width // 2
    pair = kv.shape[1]
    ssm_width, xbc = x.shape[1], pre.shape[1]
    f32, narrow = jnp.float32, jnp.bfloat16
    dma = pltpu.SemaphoreType.DMA
    widths = [hidden.shape[1], d_gu.shape[1], joined.shape[1], d_z.shape[1]]
    pairs = column_chunks(widths, 1024, 4, 2)
    own = half // 16
    outs = [
        shape_of((rows, xbc + TILE), narrow),
        shape_of((rows, query_width + pair), narrow),
        shape_of((8, xbc), f32),
        shape_of((8, TILE), f32),
        shape_of((8, TILE), f32),
        shape_of((half, xbc + TILE), narrow),
        shape_of((half, query_width + pair), narrow),
    ] + [shape_of((own, w), f32) for w in widths]
    scratch = [pltpu.VMEM((half, w), narrow) for w in widths]
    scratch += scatter_scratch(widths, half)
    scratch += [pltpu.VMEM((rows, half), narrow)] * 3
    scratch += [pltpu.VMEM(a.shape, narrow) for a in (hidden, joined, d_gu, d_z)]
    scratch += [
        pltpu.VMEM((rows, half), narrow),
        pltpu.VMEM((rows, xbc + TILE), narrow),
        pltpu.VMEM((rows, query_width + pair), narrow),
        pltpu.VMEM((half, 2 * rows), narrow),
        pltpu.VMEM((QUERY_HEADS, rows, TILE), narrow),
        pltpu.VMEM((QUERY_HEADS, rows, TILE), narrow),
        pltpu.VMEM((QUERY_HEADS, rows), f32),
        pltpu.VMEM((QUERY_HEADS, HEAD_SIZE, rows), f32),
        pltpu.VMEM((8, rows, pair), narrow),
        pltpu.VMEM((4, rows, pair), narrow),
        pltpu.VMEM((2, rows, pair), narrow),
        pltpu.VMEM((rows, pair), narrow),
        pltpu.VMEM((rows, query_width), f32),
        pltpu.VMEM((rows, pair), f32),
        pltpu.VMEM((rows, TILE), f32),
        pltpu.VMEM((rows, TILE), f32),
        pltpu.VMEM((TILE, rows), f32),
        pltpu.VMEM((TILE, rows), f32),
        pltpu.VMEM((rows + RIM, xbc), f32),
        *scan_scratch(ssm_width),
        dma((7,)),
        dma((7,)),
        dma((10,)),
        dma((10,)),
        dma((2 * len(pairs), 4, 4)),
        dma((2 * len(pairs), 4, 4)),
        dma((1,)),
        dma((1,)),
    ]
    return comm_call(
        lambda *refs: back_kernel(pairs, *refs),
        outs,
        [INTO_VMEM] * len(outs),
        (lens, *args),
        [pl.BlockSpec(memory_space=pltpu.SMEM)] + [INTO_VMEM] * len(args),
        scratch,
        2,
        200_000_000,
        limit=62,
    )


def dot_nt_two(left, right):
    high = left.astype(jnp.bfloat16)
    low = (left - high.astype(jnp.float32)).astype(jnp.bfloat16)
    return dot_nt(high, right) + dot_nt(low, right)


def last_kernel(pairs, *refs):
    (
        p_conv, p_attn, d_conv, d_attn, d_z, gains, g_mlp, g_ssm, g_conv, head_sums, g_skip,
        sum_out, sum_z, *far_in,
    ) = refs[:18]
    (
        input_grad, g_attn_out, g_in_out, g_dt_out, g_out_out,
        norm_total, mlp_total, ssm_total, conv_total, conv_b_total, head_total,
    ) = refs[18:29]
    refs = refs[29:]
    arrived_w, near_in, refs = refs[:8], refs[8:13], refs[13:]
    full_conv, full_mix, x_own, order, d_middle = near_in
    (
        out_conv, out_attn, d_normed, small_own, small_in, small_mid, small_out, in_sems,
        w_send, w_recv, small_send, small_recv,
    ) = refs
    stage = Stage(far_in, near_in, in_sems)
    stage.start(*range(5))
    others = partners()
    greet(list(others.values()))
    rows, width = d_normed.shape
    scatter = Scatter((p_conv, p_attn), (out_conv, out_attn), arrived_w, pairs, w_send, w_recv, others)
    scatter.step(0, 0)
    scatter.step(1, 0)
    scatter.step(2, 0)
    stage.need(0, 1)
    step = 256
    attn = d_attn.shape[1]

    def back_out(j, carry):
        here = pl.ds(pl.multiple_of(j * step, step), step)
        d_normed[:, here] = (
            dot_nt(d_conv[...], full_conv[here])
            + dot_nt(d_attn[...], full_mix[here, :attn])
            + dot_nt(d_z[...], full_mix[here, attn:])
        )
        return carry

    lax.fori_loop(0, width // step, back_out, 0)
    stage.need(2, 3, 4)
    scatter.step(0, 1)
    scatter.step(1, 1)
    wide = x_own[...].astype(jnp.float32)
    r = lax.rsqrt(jnp.mean(wide * wide, axis=-1, keepdims=True) + NORM_EPS)
    grads = d_normed[...]
    g_norm = jnp.sum(grads * wide * r, axis=0, keepdims=True)
    line = lax.broadcasted_iota(jnp.int32, (8, width), 0)
    both = jnp.where(line == 0, g_norm, jnp.where(line == 1, g_mlp[...], 0.0))
    both = dot_nt_two(both, order[...])
    small_own[16:] = jnp.zeros((small_own.shape[0] - 16, TILE), jnp.float32)
    small_own[16:28] = g_ssm[...]
    small_own[28:30] = head_sums[0:2]
    small_own[30:31] = g_skip[0:1]
    conv_tiles = g_conv.shape[1] // TILE
    for k in range(CONV + 1):
        for i in range(conv_tiles):
            place = 32 + 16 * k + i
            small_own[place : place + 1] = g_conv[k : k + 1, i * TILE : (i + 1) * TILE]
    for k in range(width // TILE):
        for which in range(2):
            small_own[8 * which + k : 8 * which + k + 1] = both[
                which : which + 1, k * TILE : (k + 1) * TILE
            ]
    names = ("core", "y", "x", "near", "far")
    small_copies = []

    def small_step(k):
        if k > 0:
            small_copies[k - 1].wait_recv()
            was = small_own if k == 1 else small_mid.at[k - 2]
            now = small_out if k == 5 else small_mid.at[k - 1]
            now[...] = was[...] + small_in[k - 1]
        if k < 5:
            source = small_own if k == 0 else small_mid.at[k - 1]
            copy = remote(
                source, small_in.at[k], small_send.at[k], small_recv.at[k], others[names[k]]
            )
            copy.start()
            small_copies.append(copy)

    scatter.step(2, 1)
    scatter.step(0, 2)
    small_step(0)
    inner = grads * gains[0:1]
    coeff = jnp.mean(inner * wide, axis=-1, keepdims=True)
    d_normed[...] = d_middle[...] + r * (inner - wide * (r * r * coeff))
    scatter.step(1, 2)
    small_step(1)
    scatter.step(0, 3)
    scatter.step(2, 2)

    def plain(j, carry):
        here = pl.ds(pl.multiple_of(j * step, step), step)
        input_grad[:, here] = dot_nt_two(d_normed[...], order[here])
        return carry

    lax.fori_loop(0, width // step, plain, 0)
    small_step(2)
    query = QUERY_HEADS * HEAD_SIZE
    g_in_out[:, : sum_z.shape[1]] = sum_z[...]
    g_out_out[:, :query] = pair_columns(sum_out[:, :query], True)
    g_out_out[:, query:] = sum_out[:, query:]
    scatter.step(1, 3)
    scatter.step(2, 3)
    small_step(3)
    scatter.step(0, 4)
    small_step(4)
    scatter.step(1, 4)
    scatter.step(2, 4)
    small_step(5)
    norm_total[...] = small_out[:8]
    mlp_total[...] = small_out[8:16]
    ssm_total[...] = small_out[16:28]
    head_total[...] = small_out[24:32]
    for k in range(CONV):
        for i in range(conv_tiles):
            place = 32 + 16 * k + i
            conv_total[k : k + 1, i * TILE : (i + 1) * TILE] = small_out[place : place + 1]
    conv_b_total[...] = small_out[32 + 16 * CONV : 32 + 16 * CONV + conv_tiles]
    g_in_out[:, g_in_out.shape[1] - g_conv.shape[1] :] = out_conv[:, : g_conv.shape[1]]
    g_dt_out[...] = out_conv[:, g_conv.shape[1] : g_conv.shape[1] + MH]
    query = QUERY_HEADS * HEAD_SIZE
    g_attn_out[:, :query] = pair_columns(out_attn[:, :query], True)
    g_attn_out[:, query:] = out_attn[:, query:]
    scatter.finish()
    for copy in small_copies:
        copy.wait_send()


def last(near, far):
    p_conv, p_attn, d_z, g_conv, sum_out = near[0], near[1], near[4], near[8], near[11]
    rows, width = far[2].shape
    half = p_conv.shape[0]
    f32, narrow = jnp.float32, jnp.bfloat16
    dma = pltpu.SemaphoreType.DMA
    widths = [p_conv.shape[1], p_attn.shape[1]]
    pairs = column_chunks(widths)
    total = (32 + 16 * (CONV + 1), TILE)
    block = half // 16
    xbc = g_conv.shape[1]
    joined = sum_out.shape[1]
    outs = [
        shape_of((rows, width), f32),
        shape_of((block, widths[1]), f32),
        shape_of((block, d_z.shape[1] + xbc), f32),
        shape_of((block, MH), f32),
        shape_of((block, joined), f32),
        shape_of((8, TILE), f32),
        shape_of((8, TILE), f32),
        shape_of((12, TILE), f32),
        shape_of((CONV, xbc), f32),
        shape_of((xbc // TILE, TILE), f32),
        shape_of((8, TILE), f32),
    ]
    scratch = scatter_scratch(widths, half)
    scratch += [pltpu.VMEM(a.shape, a.dtype) for a in far]
    scratch += [pltpu.VMEM((block, w), f32) for w in widths]
    scratch += [
        pltpu.VMEM((rows, width), f32),
        pltpu.VMEM(total, f32),
        pltpu.VMEM((5, *total), f32),
        pltpu.VMEM((4, *total), f32),
        pltpu.VMEM(total, f32),
        dma((5,)),
        dma((2 * len(pairs), 4, 4)),
        dma((2 * len(pairs), 4, 4)),
        dma((5,)),
        dma((5,)),
    ]
    return comm_call(
        lambda *refs: last_kernel(pairs, *refs),
        outs,
        [INTO_VMEM] * len(outs),
        (*near, *far),
        [INTO_VMEM] * len(near) + [ANY] * len(far),
        scratch,
        4,
        100_000_000,
    )


def settle_kernel(*refs):
    count = len(refs) // 2
    sems = refs[2 * count]
    copies = [
        pltpu.make_async_copy(refs[k], refs[count + k], sems.at[k]) for k in range(count)
    ]
    for copy in copies:
        copy.start()
    for copy in copies:
        copy.wait()


def settle(*arrays):
    count = len(arrays)
    return pl.pallas_call(
        settle_kernel,
        out_shape=[shape_of(a.shape, a.dtype) for a in arrays],
        in_specs=[ANY] * count,
        out_specs=[INTO_VMEM] * count,
        scratch_shapes=[pltpu.SemaphoreType.DMA((count,))],
        compiler_params=pltpu.CompilerParams(vmem_limit_bytes=60 * 1024 * 1024),
    )(*arrays)


def pair_heads(value, back=False):
    rows = value.shape[0]
    group = QUERY_HEADS // KEY_VALUE_HEADS
    width = QUERY_HEADS * HEAD_SIZE
    shape = (group, KEY_VALUE_HEADS) if back else (KEY_VALUE_HEADS, group)
    moved = value[:, :width].reshape(rows, *shape, HEAD_SIZE).transpose(0, 2, 1, 3)
    return jnp.concatenate([moved.reshape(rows, width), value[:, width:]], axis=1)


def plain_layer(
    layer_input,
    seq_lengths,
    w_attn,
    w_ssm_in,
    w_dt,
    w_out,
    w_gate_up,
    w_down,
    norm_gain,
    mlp_gain,
    ssm_gain,
    conv_w,
    conv_b,
    a_log,
    dt_bias,
    d_skip,
    out_grad,
):
    token_rows = layer_input.shape[1]
    query_width = QUERY_HEADS * HEAD_SIZE
    key_value_width = KEY_VALUE_HEADS * HEAD_SIZE
    attn_width = query_width + 2 * key_value_width
    ssm_width = MH * MP
    xbc_width = ssm_width + 2 * NS
    seq_lens = seq_lengths[0]
    first_pos = lax.axis_index("seq") * token_rows
    positions = first_pos + jnp.arange(token_rows, dtype=jnp.int32)
    segment, device_places = segments(seq_lens, positions)
    ends = jnp.cumsum(seq_lens)
    info = jnp.stack([first_pos, ends[0], ends[1], ends[2]]).astype(jnp.int32)
    half = HEAD_SIZE // 2
    freqs = ROPE_BASE ** (-jnp.arange(half, dtype=jnp.float32) / half)
    angles = device_places.astype(jnp.float32)[:, None] * jnp.tile(freqs, TILE // half)[None, :]
    cosine, sine = jnp.cos(angles), jnp.sin(angles)
    head_params = jnp.pad(
        jnp.stack([dt_bias, jnp.exp(a_log), d_skip]), ((0, 5), (0, TILE - MH))
    )
    step_pad = jnp.pad(w_dt, ((0, 0), (0, TILE - MH)))
    shards = (
        jnp.concatenate([w_ssm_in[:, ssm_width:], step_pad], axis=1),
        jnp.concatenate([pair_heads(w_attn), w_ssm_in[:, :ssm_width]], axis=1),
        pair_heads(w_out.T),
        w_gate_up,
        w_down.T,
    )
    ext_pos = first_pos - (CONV - 1) + jnp.arange(token_rows + CONV - 1, dtype=jnp.int32)
    ext_segment = segments(seq_lens, ext_pos)[0]

    def conv_local(ext_rows, conv_weight, conv_bias):
        return conv_mix(ext_rows, ext_segment, conv_weight, conv_bias)

    full = [lax.all_gather(p, ("seq", "batch"), axis=0, tiled=True) for p in shards]
    full_conv, full_mix, full_out, full_gu, full_down = full
    x_rows = layer_input[0].astype(jnp.float32)
    grad_rows = out_grad[0]
    scale_one = rms_scale(x_rows)
    normed = (x_rows * scale_one * norm_gain).astype(jnp.bfloat16)
    conv_proj = jnp.dot(normed, full_conv, preferred_element_type=jnp.float32)
    mix_proj = jnp.dot(normed, full_mix, preferred_element_type=jnp.float32)
    queries, own_pairs = big_call(
        rope_kernel,
        (
            shape_of((token_rows, query_width), jnp.bfloat16),
            shape_of((token_rows, 2 * key_value_width), jnp.bfloat16),
        ),
        mix_proj[:, :attn_width],
        cosine,
        sine,
    )
    gate_z = mix_proj[:, attn_width:]
    raw_xbc = conv_proj[:, :xbc_width]
    step_proj = conv_proj[:, xbc_width:]
    rim_rows = shifted(raw_xbc[token_rows - (CONV - 1) :], "seq", 1)
    extended = jnp.concatenate([rim_rows, raw_xbc], axis=0)
    conv_out, conv_pullback = jax.vjp(conv_local, extended, conv_w, conv_b)
    conv_narrow = conv_out.astype(jnp.bfloat16)
    inputs_x, inputs_bc = conv_narrow[:, :ssm_width], conv_narrow[:, ssm_width:]
    ssm_own, state_own, steps_dt, running_decay = ssm_forward(
        info, inputs_x, inputs_bc, step_proj, head_params
    )
    all_pairs = lax.all_gather(own_pairs, "seq", axis=0, tiled=True)
    state_in = scan_states(state_own, True)
    attended, attended_t, log_total = attn_forward(info, queries, all_pairs)

    ssm_flat, ssm_normed, scale_gated = ssm_finish(
        info, ssm_own, inputs_bc, running_decay, state_in, gate_z, ssm_gain.reshape(-1, TILE)
    )
    joined = jnp.concatenate([attended, ssm_normed], axis=1)

    def into_width(left, weight):
        return jnp.einsum("tc,dc->td", left, weight, preferred_element_type=jnp.float32)

    def out_of_width(left, weight):
        return jnp.dot(left, weight, preferred_element_type=jnp.float32)

    middle = x_rows + into_width(joined, full_out)
    scale_two = rms_scale(middle)
    normed_two = (middle * scale_two * mlp_gain).astype(jnp.bfloat16)
    gate_up = out_of_width(normed_two, full_gu)
    gate_part, up_part = gate_up[:, :FF], gate_up[:, FF:]
    sig_gate = jax.nn.sigmoid(gate_part)
    hidden = (gate_part * sig_gate * up_part).astype(jnp.bfloat16)
    layer_out = middle + into_width(hidden, full_down)
    d_hidden = out_of_width(grad_rows, full_down)
    d_gate = d_hidden * up_part * (sig_gate * (1.0 + gate_part * (1.0 - sig_gate)))
    d_up = d_hidden * gate_part * sig_gate
    d_gate_up = jnp.concatenate([d_gate, d_up], axis=1).astype(jnp.bfloat16)
    d_normed_two = into_width(d_gate_up, full_gu)
    d_middle_norm, g_mlp_gain = norm_back(middle, scale_two, mlp_gain, d_normed_two)
    d_middle = grad_rows.astype(jnp.float32) + d_middle_norm
    d_mixer = d_middle.astype(jnp.bfloat16)
    d_joined = out_of_width(d_mixer, full_out)
    attended_gradient = d_joined[:, :query_width].astype(jnp.bfloat16)
    d_ssm_out, d_gate_z, pull, g_ssm_gain = gate_back(
        info,
        d_joined[:, query_width:],
        ssm_flat,
        gate_z,
        scale_gated,
        ssm_gain.reshape(-1, TILE),
        running_decay,
        inputs_bc,
    )
    pull = jnp.concatenate([pull, state_own[NS:]], axis=0)
    d_state = scan_states(pull, False)
    d_queries, d_pairs = attn_backward(
        info, queries, all_pairs, attended_gradient, attended_t, log_total
    )
    own_d_pairs = lax.psum_scatter(
        d_pairs.astype(jnp.float32), "seq", scatter_dimension=0, tiled=True
    )
    dx_part, d_bc_part, d_cum_part, d_dt_part, g_skip_rows = ssm_back(
        info, inputs_x, inputs_bc, steps_dt, running_decay, d_ssm_out, head_params
    )
    g_inputs_x, g_inputs_bc, d_step_pad, head_sums = state_back(
        info,
        inputs_x,
        inputs_bc,
        steps_dt,
        running_decay,
        d_ssm_out,
        head_params,
        step_proj,
        state_in,
        d_state,
        dx_part,
        d_bc_part,
        d_cum_part,
        d_dt_part,
    )
    g_extended, g_conv_w, g_conv_b = conv_pullback(
        jnp.concatenate([g_inputs_x, g_inputs_bc], axis=1)
    )
    back_rim = shifted(g_extended[: CONV - 1], "seq", -1)
    d_raw = g_extended[CONV - 1 :] + jnp.concatenate(
        [jnp.zeros((token_rows - (CONV - 1), xbc_width), jnp.float32), back_rim], axis=0
    )
    d_conv_proj = jnp.concatenate([d_raw.astype(jnp.bfloat16), d_step_pad], axis=1)
    (d_attn_proj,) = big_call(
        rope_back_kernel,
        (shape_of((token_rows, attn_width), jnp.bfloat16),),
        d_queries,
        own_d_pairs,
        cosine,
        sine,
    )
    d_mix_proj = jnp.concatenate([d_attn_proj, d_gate_z], axis=1)
    d_normed = into_width(d_conv_proj, full_conv) + into_width(d_mix_proj, full_mix)
    d_input_norm, g_norm_gain = norm_back(x_rows, scale_one, norm_gain, d_normed)
    input_grad = d_middle + d_input_norm
    axes = ("seq", "batch")

    def summed(left, right):
        grad = jnp.einsum("td,tc->dc", left, right, preferred_element_type=jnp.float32)
        return lax.psum_scatter(grad, axes, scatter_dimension=0, tiled=True)

    sum_down, sum_gu = summed(grad_rows, hidden), summed(normed_two, d_gate_up)
    sum_out, sum_conv = summed(d_mixer, joined), summed(normed, d_conv_proj)
    sum_mix = summed(normed, d_mix_proj)
    sum_attn, sum_z = sum_mix[:, :attn_width], sum_mix[:, attn_width:]
    small = (
        g_norm_gain,
        g_mlp_gain,
        g_ssm_gain.reshape(-1),
        g_conv_w,
        g_conv_b,
        head_sums[0, :MH],
        head_sums[1, :MH],
        g_skip_rows[0, :MH],
    )
    small_sums = unpack_small(lax.psum(pack_small(small), axes), small)
    grad_attn = pair_heads(sum_attn, True)
    grad_ssm_in = jnp.concatenate([sum_z, sum_conv[:, :xbc_width]], axis=1)
    grad_dt = sum_conv[:, xbc_width : xbc_width + MH]
    grad_out = pair_heads(sum_out, True).T
    grad_gate_up = sum_gu
    grad_down = sum_down.T
    return (
        layer_out.astype(jnp.bfloat16)[None],
        input_grad[None],
        grad_attn,
        grad_ssm_in,
        grad_dt,
        grad_out,
        grad_gate_up,
        grad_down,
        *small_sums,
    )


def on_device(
    layer_input,
    seq_lengths,
    w_attn,
    w_ssm_in,
    w_dt,
    w_out,
    w_gate_up,
    w_down,
    norm_gain,
    mlp_gain,
    ssm_gain,
    conv_w,
    conv_b,
    a_log,
    dt_bias,
    d_skip,
    out_grad,
):
    if not is_fast(layer_input.shape[2]):
        return plain_layer(
            layer_input, seq_lengths, w_attn, w_ssm_in, w_dt, w_out, w_gate_up, w_down, norm_gain,
            mlp_gain, ssm_gain, conv_w, conv_b, a_log, dt_bias, d_skip, out_grad,
        )
    half = HEAD_SIZE // 2
    freqs = np.float32(ROPE_BASE) ** (-np.arange(half, dtype=np.float32) / np.float32(half))
    freqs = jnp.asarray(np.tile(freqs.astype(np.float32), TILE // half)[None])
    full, made = front(
        seq_lengths,
        dt_bias,
        a_log,
        d_skip,
        layer_input[0],
        out_grad[0],
        norm_gain.reshape(-1, TILE),
        mlp_gain.reshape(-1, TILE),
        freqs,
        conv_w,
        conv_b.reshape(-1, TILE),
        (w_attn, w_ssm_in, w_dt.T, w_out.T, w_gate_up, w_down.T),
    )
    full_conv, full_mix, full_out, full_gu, full_down = full
    (
        x_own, g_own, gains, normed, queries, all_pairs, gate_z, raw_rows, pre_conv, inputs_x,
        inputs_bc, ssm_own, state_own, steps_dt, running_decay, attended, attended_t, log_total,
        state_in, order, cosine, sine, head_params,
    ) = made
    (
        layer_out, joined, hidden, d_gate_up, normed_two, d_mixer, d_middle, d_ssm_out, d_gate_z,
        pull, attended_gradient, g_ssm_gain, g_mlp_gain,
    ) = middle_part(
        seq_lengths, ssm_own, inputs_bc, running_decay, state_in, state_own, gate_z,
        ssm_gain.reshape(-1, TILE), attended, x_own, g_own, gains, order, full_out, full_gu,
        full_down,
    )
    (
        d_conv_proj, d_attn_proj, g_conv, head_sums, g_skip_rows, part_conv, part_attn, sum_down,
        sum_gu, sum_out, sum_z,
    ) = back(
        seq_lengths, head_params, conv_w, cosine, sine, queries, all_pairs, attended_gradient,
        attended_t, log_total, pull, inputs_x, inputs_bc, steps_dt, running_decay, d_ssm_out,
        raw_rows, state_in, pre_conv, normed, normed_two, d_mixer, g_own, hidden, joined,
        d_gate_up, d_gate_z,
    )
    (
        input_grad, grad_attn, grad_ssm_in, grad_dt, grad_out, g_norm, g_mlp, g_ssm, g_conv_w,
        g_conv_b, heads,
    ) = last(
        (
            part_conv, part_attn, d_conv_proj, d_attn_proj, d_gate_z, gains, g_mlp_gain,
            g_ssm_gain, g_conv, head_sums, g_skip_rows, sum_out, sum_z,
        ),
        (full_conv, full_mix, x_own, order, d_middle),
    )
    (
        input_grad, grad_attn, grad_ssm_in, grad_dt, grad_out, sum_gu, sum_down, g_norm, g_mlp,
        g_ssm, g_conv_w, g_conv_b, heads,
    ) = settle(
        input_grad, grad_attn, grad_ssm_in, grad_dt, grad_out, sum_gu, sum_down, g_norm, g_mlp,
        g_ssm, g_conv_w, g_conv_b, heads,
    )
    return (
        layer_out[None],
        input_grad[None],
        grad_attn,
        grad_ssm_in,
        grad_dt,
        grad_out.T,
        sum_gu,
        sum_down.T,
        g_norm.reshape(-1),
        g_mlp.reshape(-1),
        g_ssm.reshape(-1),
        g_conv_w,
        g_conv_b.reshape(-1),
        heads[4, :MH],
        heads[5, :MH],
        heads[6, :MH],
    )


def solution(mesh):
    return jax.shard_map(
        on_device,
        mesh=mesh,
        in_specs=(
            P("batch", "seq", None),
            P("batch", None),
            P(("seq", "batch"), None),
            P(("seq", "batch"), None),
            P(("seq", "batch"), None),
            P(None, ("seq", "batch")),
            P(("seq", "batch"), None),
            P(None, ("seq", "batch")),
            P(),
            P(),
            P(),
            P(),
            P(),
            P(),
            P(),
            P(),
            P("batch", "seq", None),
        ),
        out_specs=(
            P("batch", "seq", None),
            P("batch", "seq", None),
            P(("seq", "batch"), None),
            P(("seq", "batch"), None),
            P(("seq", "batch"), None),
            P(None, ("seq", "batch")),
            P(("seq", "batch"), None),
            P(None, ("seq", "batch")),
            P(),
            P(),
            P(),
            P(),
            P(),
            P(),
            P(),
            P(),
        ),
        check_vma=False,
    )
```

```python
import jax
import jax.numpy as jnp
import numpy as np
from jax import lax
from jax.experimental import pallas as pl
from jax.experimental.pallas import tpu as pltpu
from jax.sharding import PartitionSpec as P

QUERY_HEADS = 8
KEY_VALUE_HEADS = 2
HEAD_SIZE = 64
MH = 24
MP = 64
NS = 128
FF = 2048
CONV = 4
SPAN = 128


HIGHEST = lax.Precision.HIGHEST
NEGATIVE_FILL = -1e30
ROPE_BASE = 10000.0
NORM_EPS = 1e-06


def shifted(block, axis, distance):
    devices = range(lax.axis_size(axis))
    route = [(i - distance, i) for i in devices if i - distance in devices]
    return lax.ppermute(block, axis, route)


def is_fast(width):
    return lax.axis_size("seq") == 8 and lax.axis_size("batch") == 4 and width % (32 * 32) == 0


def pack_small(arrays):
    flat = jnp.concatenate([a.reshape(-1) for a in arrays])
    return jnp.pad(flat, (0, -flat.shape[0] % 1024)).reshape(-1, 128)


def unpack_small(flat, arrays):
    flat = flat.reshape(-1)
    out, start = [], 0
    for a in arrays:
        out.append(flat[start : start + a.size].reshape(a.shape))
        start += a.size
    return out


def rms_scale(value_rows):
    return lax.rsqrt(jnp.mean(value_rows * value_rows, axis=-1, keepdims=True) + NORM_EPS)


def norm_back(value_rows, scales, gains, grads):
    gain_grad = jnp.sum(grads * value_rows * scales, axis=0)
    inner = grads * gains
    coeff = jnp.mean(inner * value_rows, axis=-1, keepdims=True)
    return (scales * (inner - value_rows * scales * scales * coeff), gain_grad)


def segments(lengths, positions):
    ends = jnp.cumsum(lengths)
    passed = ends[None, :] <= positions[:, None]
    segment = jnp.sum(passed.astype(jnp.int32), axis=1)
    device_places = positions - jnp.sum(jnp.where(passed, lengths[None, :], 0), axis=1)
    return (segment, device_places)


def conv_mix(extended, ext_segment, conv_weight, conv_bias):
    row_count = extended.shape[0] - (CONV - 1)
    summed = conv_bias[None, :]
    for lagged in range(CONV):
        same_seq = (ext_segment[lagged : lagged + row_count] == ext_segment[CONV - 1 :]).astype(
            extended.dtype
        )
        summed = (
            summed
            + conv_weight[lagged][None, :]
            * extended[lagged : lagged + row_count]
            * same_seq[:, None]
        )
    return jax.nn.silu(summed)


TILE = 128
PAIRS = QUERY_HEADS // 2
CHUNK = 256


def dot(left, right):
    return jnp.dot(left, right, preferred_element_type=jnp.float32)


def dot_nt(left, right):
    return lax.dot_general(
        left, right, (((1,), (1,)), ((), ())), preferred_element_type=jnp.float32
    )


def dot_tn(left, right):
    return lax.dot_general(
        left, right, (((0,), (0,)), ((), ())), preferred_element_type=jnp.float32
    )


def exact(left, right):
    return jnp.dot(left, right, precision=HIGHEST, preferred_element_type=jnp.float32)


def two_part(left, right):
    high = left.astype(jnp.bfloat16)
    low = (left - high.astype(jnp.float32)).astype(jnp.bfloat16)
    return dot(high, right) + dot(low, right)


def seg_start(where_at, info):
    start = jnp.zeros_like(where_at)
    for k in range(1, 4):
        start = jnp.where(where_at >= info[k], jnp.maximum(start, info[k]), start)
    return start


def big_call(kernel, outs, *args, scratch=(), flops=0, smem=0, limit=48):
    specs = [pl.BlockSpec(memory_space=pltpu.SMEM)] * smem
    specs += [pl.BlockSpec(memory_space=pltpu.VMEM)] * (len(args) - smem)
    moved = sum(a.size * a.dtype.itemsize for a in args)
    moved += sum(o.size * o.dtype.itemsize for o in outs)
    return pl.pallas_call(
        kernel,
        out_shape=list(outs),
        in_specs=specs,
        out_specs=[pl.BlockSpec(memory_space=pltpu.VMEM)] * len(outs),
        scratch_shapes=list(scratch),
        cost_estimate=pl.CostEstimate(flops=flops, bytes_accessed=moved, transcendentals=0),
        compiler_params=pltpu.CompilerParams(vmem_limit_bytes=limit * 1024 * 1024),
    )(*args)


def shape_of(shape, dtype):
    return jax.ShapeDtypeStruct(shape, dtype)


def turn(value, cosine, sine):
    lane = lax.broadcasted_iota(jnp.int32, value.shape, 1) % HEAD_SIZE
    mixed = jnp.where(
        lane < HEAD_SIZE // 2,
        -pltpu.roll(value, TILE - HEAD_SIZE // 2, 1),
        pltpu.roll(value, HEAD_SIZE // 2, 1),
    )
    return value * cosine + mixed * sine


def rope_kernel(proj, cosine, sine, q_out, kv_out):
    cos, sin = cosine[...], sine[...]
    for i in range(PAIRS):
        cols = pl.ds(i * TILE, TILE)
        turned = turn(proj[:, cols], cos, sin).astype(jnp.bfloat16)
        q_out[:, cols] = (turned.astype(jnp.float32) * HEAD_SIZE**-0.5).astype(jnp.bfloat16)
    base = PAIRS * TILE
    kv_out[:, :TILE] = turn(proj[:, base : base + TILE], cos, sin).astype(jnp.bfloat16)
    kv_out[:, TILE:] = proj[:, base + TILE : base + 2 * TILE].astype(jnp.bfloat16)


def halves_of(value):
    lane = lax.broadcasted_iota(jnp.int32, value.shape, 1)
    wide = value.astype(jnp.float32)
    first = jnp.where(lane < HEAD_SIZE, wide, 0.0).astype(value.dtype)
    return first, jnp.where(lane < HEAD_SIZE, 0.0, wide).astype(value.dtype)


def block_range(info):
    first = info[0]
    low = seg_start(first, info) // CHUNK
    return low, first // CHUNK - low + 1


def attn_mask(info, block):
    rows = lax.broadcasted_iota(jnp.int32, (CHUNK, CHUNK), 0) + block * CHUNK
    at = lax.broadcasted_iota(jnp.int32, (1, CHUNK), 1) + info[0]
    return (rows <= at) & (rows >= seg_start(at, info))


def attend_start(q, heads, acc, top, total):
    for i in range(PAIRS):
        heads[2 * i], heads[2 * i + 1] = halves_of(q[:, i * TILE : (i + 1) * TILE])
    acc[...] = jnp.zeros_like(acc)
    total[...] = jnp.zeros_like(total)
    top[...] = jnp.full(top.shape, NEGATIVE_FILL, jnp.float32)


def attend_block(info, block, keys, values_t, heads, acc, top, total):
    allowed = attn_mask(info, block)
    for h in range(QUERY_HEADS):
        scores = jnp.where(allowed, dot_nt(keys, heads[h]), NEGATIVE_FILL)
        old = top[h : h + 1]
        new = jnp.maximum(old, jnp.max(scores, axis=0, keepdims=True))
        probs = jnp.where(allowed, jnp.exp(scores - new), 0.0)
        shrink = jnp.exp(old - new)
        top[h : h + 1] = new
        total[h : h + 1] = total[h : h + 1] * shrink + jnp.sum(probs, axis=0, keepdims=True)
        side = (h % 2) * HEAD_SIZE
        acc[h] = acc[h] * shrink + dot(
            values_t[side : side + HEAD_SIZE], probs.astype(jnp.bfloat16)
        )


def attend_write(acc, total, out, out_t):
    for i in range(PAIRS):
        pair = jnp.concatenate(
            [acc[2 * i] / total[2 * i : 2 * i + 1], acc[2 * i + 1] / total[2 * i + 1 : 2 * i + 2]],
            axis=0,
        )
        out_t[i * TILE : (i + 1) * TILE] = pair
        out[:, i * TILE : (i + 1) * TILE] = pair.T.astype(jnp.bfloat16)


def attn_forward_kernel(info, q, kv, out, out_t, lse, heads, acc, top, total):
    attend_start(q, heads, acc, top, total)
    low, count = block_range(info)

    def step(j, carry):
        block = low + j
        place = pl.ds(pl.multiple_of(block * CHUNK, CHUNK), CHUNK)
        keys = kv[place, :TILE]
        values_t = kv[place, TILE:].astype(jnp.float32).T.astype(jnp.bfloat16)
        attend_block(info, block, keys, values_t, heads, acc, top, total)
        return carry

    lax.fori_loop(0, count, step, 0)
    lse[...] = top[...] + jnp.log(total[...])
    attend_write(acc, total, out, out_t)


def attn_forward(info, q, kv):
    rows = q.shape[0]
    f32 = jnp.float32
    return big_call(
        attn_forward_kernel,
        (
            shape_of(q.shape, jnp.bfloat16),
            shape_of(q.shape[::-1], f32),
            shape_of((QUERY_HEADS, rows), f32),
        ),
        info,
        q,
        kv,
        smem=1,
        scratch=(
            pltpu.VMEM((QUERY_HEADS, rows, TILE), jnp.bfloat16),
            pltpu.VMEM((QUERY_HEADS, HEAD_SIZE, rows), f32),
            pltpu.VMEM((QUERY_HEADS, rows), f32),
            pltpu.VMEM((QUERY_HEADS, rows), f32),
        ),
        flops=4 * rows * kv.shape[0] * q.shape[1],
    )


def attend_back_start(q, grad, out_t, heads, grads, delta, acc):
    for i in range(PAIRS):
        cols = slice(i * TILE, (i + 1) * TILE)
        heads[2 * i], heads[2 * i + 1] = halves_of(q[:, cols])
        grads[2 * i], grads[2 * i + 1] = halves_of(grad[:, cols])
        both = grad[:, cols].astype(jnp.float32).T * out_t[cols]
        delta[2 * i : 2 * i + 1] = jnp.sum(both[:HEAD_SIZE], axis=0, keepdims=True)
        delta[2 * i + 1 : 2 * i + 2] = jnp.sum(both[HEAD_SIZE:], axis=0, keepdims=True)
    acc[...] = jnp.zeros_like(acc)


def attend_back_block(info, block, keys, values, lse, target, heads, grads, delta, acc):
    keys_t = keys.astype(jnp.float32).T.astype(jnp.bfloat16)
    allowed = attn_mask(info, block)
    d_keys = jnp.zeros((CHUNK, TILE), jnp.float32)
    d_values = jnp.zeros((CHUNK, TILE), jnp.float32)
    for h in range(QUERY_HEADS):
        scores = dot_nt(keys, heads[h])
        probs = jnp.where(allowed, jnp.exp(scores - lse[h : h + 1]), 0.0)
        d_probs = dot_nt(values, grads[h])
        d_scores = (probs * (d_probs - delta[h : h + 1])).astype(jnp.bfloat16)
        d_values = d_values + dot(probs.astype(jnp.bfloat16), grads[h])
        d_keys = d_keys + dot(d_scores, heads[h])
        side = (h % 2) * HEAD_SIZE
        acc[h] = acc[h] + dot(keys_t[side : side + HEAD_SIZE], d_scores)
    target[:, :TILE] = d_keys.astype(jnp.bfloat16)
    target[:, TILE:] = d_values.astype(jnp.bfloat16)


def attend_back_write(acc, dq):
    for i in range(PAIRS):
        pair = jnp.concatenate([acc[2 * i], acc[2 * i + 1]], axis=0)
        dq[:, i * TILE : (i + 1) * TILE] = pair.T * HEAD_SIZE**-0.5


def attn_backward_kernel(info, q, kv, grad, out_t, lse, dq, dkv, heads, grads, delta, acc):
    attend_back_start(q, grad, out_t, heads, grads, delta, acc)
    dkv[...] = jnp.zeros_like(dkv)
    low, count = block_range(info)

    def step(j, carry):
        block = low + j
        place = pl.ds(pl.multiple_of(block * CHUNK, CHUNK), CHUNK)
        attend_back_block(
            info, block, kv[place, :TILE], kv[place, TILE:], lse, dkv.at[place], heads, grads,
            delta, acc,
        )
        return carry

    lax.fori_loop(0, count, step, 0)
    attend_back_write(acc, dq)


def attn_backward(info, q, kv, grad, out_t, lse):
    rows = q.shape[0]
    f32 = jnp.float32
    return big_call(
        attn_backward_kernel,
        (shape_of(q.shape, f32), shape_of(kv.shape, jnp.bfloat16)),
        info,
        q,
        kv,
        grad,
        out_t,
        lse,
        smem=1,
        scratch=(
            pltpu.VMEM((QUERY_HEADS, rows, TILE), jnp.bfloat16),
            pltpu.VMEM((QUERY_HEADS, rows, TILE), jnp.bfloat16),
            pltpu.VMEM((QUERY_HEADS, rows), f32),
            pltpu.VMEM((QUERY_HEADS, HEAD_SIZE, rows), f32),
        ),
        flops=10 * rows * kv.shape[0] * q.shape[1],
    )


def rope_back_kernel(dq, dkv, cosine, sine, out):
    cos, sin = cosine[...], -sine[...]
    for i in range(PAIRS):
        cols = slice(i * TILE, (i + 1) * TILE)
        out[:, cols] = turn(dq[:, cols], cos, sin).astype(jnp.bfloat16)
    base = PAIRS * TILE
    out[:, base : base + TILE] = turn(dkv[:, :TILE], cos, sin).astype(jnp.bfloat16)
    out[:, base + TILE :] = dkv[:, TILE:].astype(jnp.bfloat16)


STATE_ROWS = NS + 16


def lane_pick(value, first):
    rows = value.shape[0]
    lane = lax.broadcasted_iota(jnp.int32, (rows, TILE), 1)
    return jnp.where(lane < MP, value[:, first : first + 1], value[:, first + 1 : first + 2])


def spread_heads(width):
    head = lax.broadcasted_iota(jnp.int32, (TILE, width), 0)
    col = lax.broadcasted_iota(jnp.int32, (TILE, width), 1)
    return jnp.where(head == col // MP, 1.0, 0.0).astype(jnp.bfloat16)


def gather_heads(width):
    head = lax.broadcasted_iota(jnp.int32, (width, TILE), 1)
    col = lax.broadcasted_iota(jnp.int32, (width, TILE), 0)
    return jnp.where(head == col // MP, 1.0, 0.0).astype(jnp.bfloat16)


def head_lanes(rows):
    return lax.broadcasted_iota(jnp.int32, (rows, TILE), 1) < MH


def chunk_places(info, rows):
    at = lax.broadcasted_iota(jnp.int32, (rows, 1), 0) + info[0]
    return seg_start(at, info) - info[0]


def ssm_states(info, x, bc, step_in, head_params, state, dt_out, cum_out, dt_t, cum_t):
    rows = x.shape[0]
    bias, rate = head_params[0:1], head_params[1:2]
    raw = step_in[...] + bias
    dt = jnp.maximum(raw, 0.0) + jnp.log1p(jnp.exp(-jnp.abs(raw)))
    dt = jnp.where(head_lanes(rows), dt, 0.0)
    row = lax.broadcasted_iota(jnp.int32, (rows, rows), 0)
    col = lax.broadcasted_iota(jnp.int32, (rows, rows), 1)
    lower = jnp.where(row >= col, 1.0, 0.0)
    cum = exact(lower, -dt * rate)
    dt_out[...] = dt
    cum_out[...] = cum
    dt_t[...] = dt.T
    cum_t[...] = cum.T
    last_start = seg_start(info[0] + rows - 1, info) - info[0]
    place = lax.broadcasted_iota(jnp.int32, (rows, 1), 0)
    end = cum[rows - 1 : rows]
    leave = jnp.where(place >= last_start, jnp.exp(jnp.minimum(end - cum, 0.0)) * dt, 0.0)
    b_t = bc[:, :NS].astype(jnp.float32).T.astype(jnp.bfloat16)
    through = jnp.where(last_start < 0, jnp.exp(end), 0.0)
    high = through.astype(jnp.bfloat16).astype(jnp.float32)
    line = lax.broadcasted_iota(jnp.int32, (16, TILE), 0)
    both = jnp.where(line == 0, high, jnp.where(line == 1, through - high, 0.0))
    spread = spread_heads(x.shape[1])
    state[NS:] = dot(both.astype(jnp.bfloat16), spread).astype(jnp.bfloat16)
    for i in range(MH // 2):
        cols = slice(i * TILE, (i + 1) * TILE)
        weighed = x[:, cols].astype(jnp.float32) * lane_pick(leave, 2 * i)
        state[:NS, cols] = dot(b_t, weighed.astype(jnp.bfloat16)).astype(jnp.bfloat16)


def ssm_local(info, x, bc, head_params, y, cum, dt_t, cum_t):
    rows = x.shape[0]
    row = lax.broadcasted_iota(jnp.int32, (rows, rows), 0)
    col = lax.broadcasted_iota(jnp.int32, (rows, rows), 1)
    starts = chunk_places(info, rows)
    products = dot_nt(bc[:, NS:], bc[:, :NS])
    skips = jnp.broadcast_to(head_params[2:3], (8, TILE))
    skip_row = two_part(skips, spread_heads(x.shape[1]))[:1]
    lane = lax.broadcasted_iota(jnp.int32, (SPAN, TILE), 1)
    for i in range(MH // 2):
        cols = slice(i * TILE, (i + 1) * TILE)
        tile = x[:, cols]
        for part in range(rows // SPAN):
            here = slice(part * SPAN, (part + 1) * SPAN)
            upto = (part + 1) * SPAN
            allowed = (row[here, :upto] >= col[here, :upto]) & (col[here, :upto] >= starts[here])
            sides = []
            for h in (2 * i, 2 * i + 1):
                spread_log = cum[here, h : h + 1] - cum_t[h : h + 1, :upto]
                decay = jnp.exp(jnp.where(allowed, spread_log, NEGATIVE_FILL))
                mixing = products[here, :upto] * decay * dt_t[h : h + 1, :upto]
                sides.append(dot(mixing.astype(jnp.bfloat16), tile[:upto]))
            own = skip_row[:, cols] * tile[here].astype(jnp.float32)
            y[here, cols] = jnp.where(lane < MP, sides[0], sides[1]) + own


def ssm_forward_kernel(info, x, bc, step_in, head_params, y, state, dt_out, cum_out, dt_t, cum_t):
    ssm_states(info, x, bc, step_in, head_params, state, dt_out, cum_out, dt_t, cum_t)
    ssm_local(info, x, bc, head_params, y, cum_out, dt_t, cum_t)


def ssm_forward(info, x, bc, step_in, head_params):
    rows, width = x.shape
    f32 = jnp.float32
    return big_call(
        ssm_forward_kernel,
        (
            shape_of((rows, width), f32),
            shape_of((STATE_ROWS, width), jnp.bfloat16),
            shape_of((rows, TILE), f32),
            shape_of((rows, TILE), f32),
        ),
        info,
        x,
        bc,
        step_in,
        head_params,
        smem=1,
        scratch=(pltpu.VMEM((TILE, rows), f32), pltpu.VMEM((TILE, rows), f32)),
        flops=4 * rows * rows * width,
    )


def entering_of(info, cum):
    rows = cum.shape[0]
    return jnp.where(chunk_places(info, rows) < 0, jnp.exp(jnp.minimum(cum, 0.0)), 0.0)


def ssm_finish_kernel(info, y, bc, cum, state_in, z, gain, ssm_out, normed, scale):
    rows = y.shape[0]
    enter = entering_of(info, cum[...])
    narrow_c = bc[:, NS:]
    squares = jnp.zeros((rows, TILE), jnp.float32)
    tiles = MH // 2
    for i in range(tiles):
        cols = slice(i * TILE, (i + 1) * TILE)
        out = y[:, cols] + lane_pick(enter, 2 * i) * dot(narrow_c, state_in[:, cols])
        ssm_out[:, cols] = out
        gate = z[:, cols]
        gated = out * (gate * jax.nn.sigmoid(gate))
        squares = squares + gated * gated
    mean = jnp.sum(squares, axis=1, keepdims=True) * (1.0 / (tiles * TILE))
    r = lax.rsqrt(mean + NORM_EPS)
    scale[...] = jnp.broadcast_to(r, scale.shape)
    for i in range(tiles):
        cols = slice(i * TILE, (i + 1) * TILE)
        gate = z[:, cols]
        gated = ssm_out[:, cols] * (gate * jax.nn.sigmoid(gate))
        normed[:, cols] = (gated * r * gain[i : i + 1]).astype(jnp.bfloat16)


def ssm_finish(info, y, bc, cum, state_in, z, gain):
    rows, width = y.shape
    return big_call(
        ssm_finish_kernel,
        (
            shape_of((rows, width), jnp.float32),
            shape_of((rows, width), jnp.bfloat16),
            shape_of((rows, TILE), jnp.float32),
        ),
        info,
        y,
        bc,
        cum,
        state_in,
        z,
        gain,
        smem=1,
        flops=2 * rows * NS * width,
    )


def gate_back_kernel(info, dy, ssm_out, z, scale, gain, cum, bc, d_out, d_z, pull, g_gain):
    rows = dy.shape[0]
    tiles = MH // 2
    r = scale[:, :1]
    enter = entering_of(info, cum[...])
    c_t = bc[:, NS:].astype(jnp.float32).T.astype(jnp.bfloat16)
    inner = jnp.zeros((rows, TILE), jnp.float32)
    for i in range(tiles):
        cols = slice(i * TILE, (i + 1) * TILE)
        gate = z[:, cols]
        gated = ssm_out[:, cols] * (gate * jax.nn.sigmoid(gate))
        product = dy[:, cols] * gated
        g_gain[i : i + 1] = jnp.sum(product * r, axis=0, keepdims=True)
        inner = inner + product * gain[i : i + 1]
    coeff = jnp.sum(inner, axis=1, keepdims=True) * (1.0 / (tiles * TILE))
    for i in range(tiles):
        cols = slice(i * TILE, (i + 1) * TILE)
        gate = z[:, cols]
        sig = jax.nn.sigmoid(gate)
        silu = gate * sig
        out = ssm_out[:, cols]
        d_gated = r * (dy[:, cols] * gain[i : i + 1] - out * silu * (r * r * coeff))
        d_ssm = d_gated * silu
        d_out[:, cols] = d_ssm
        d_z[:, cols] = (d_gated * out * (sig * (1.0 + gate * (1.0 - sig)))).astype(jnp.bfloat16)
        pull[:, cols] = dot(c_t, (d_ssm * lane_pick(enter, 2 * i)).astype(jnp.bfloat16)).astype(
            jnp.bfloat16
        )


def gate_back(info, dy, ssm_out, z, scale, gain, cum, bc):
    rows, width = dy.shape
    return big_call(
        gate_back_kernel,
        (
            shape_of((rows, width), jnp.float32),
            shape_of((rows, width), jnp.bfloat16),
            shape_of((NS, width), jnp.bfloat16),
            shape_of(gain.shape, jnp.float32),
        ),
        info,
        dy,
        ssm_out,
        z,
        scale,
        gain,
        cum,
        bc,
        smem=1,
        flops=2 * rows * NS * width,
    )


def ssm_back_kernel(info, x, bc, dt, cum, grad, head_params, dx, d_bc, d_cum, d_dt, g_skip, cols_t, d_rows, between=None):
    rows, width = x.shape
    skip = head_params[2:3]
    cols_t[...] = cum[...].T
    row = lax.broadcasted_iota(jnp.int32, (rows, rows), 0)
    col = lax.broadcasted_iota(jnp.int32, (rows, rows), 1)
    at = lax.broadcasted_iota(jnp.int32, (1, rows), 1) + info[0]
    starts = seg_start(at, info) - info[0]
    narrow_b, narrow_c = bc[:, :NS], bc[:, NS:]
    products = dot_nt(narrow_b, narrow_c)
    skip_row = two_part(jnp.broadcast_to(skip, (8, TILE)), spread_heads(width))[:1]
    lane = lax.broadcasted_iota(jnp.int32, (SPAN, TILE), 1)
    parts = rows // SPAN
    d_products = [jnp.zeros((SPAN, rows - p * SPAN), jnp.float32) for p in range(parts)]
    d_rows[...] = jnp.zeros_like(d_rows)
    step_sums = [jnp.zeros((SPAN, TILE), jnp.float32) for p in range(parts)]
    skip_sums = []
    for i in range(MH // 2):
        cols = slice(i * TILE, (i + 1) * TILE)
        tile = x[:, cols]
        wide = grad[:, cols]
        narrow = wide.astype(jnp.bfloat16)
        skip_sums.append(jnp.sum(wide * tile.astype(jnp.float32), axis=0, keepdims=True))
        tile_sides = halves_of(tile)
        for part in range(parts):
            here = slice(part * SPAN, (part + 1) * SPAN)
            since = part * SPAN
            allowed = (row[here, since:] <= col[here, since:]) & (
                row[here, since:] >= starts[:, since:]
            )
            sides = []
            for side in range(2):
                h = 2 * i + side
                spread_log = cols_t[h : h + 1, since:] - cum[here, h : h + 1]
                decay = jnp.exp(jnp.where(allowed, spread_log, NEGATIVE_FILL))
                decay_dt = decay * dt[here, h : h + 1]
                mixing = products[here, since:] * decay_dt
                sides.append(dot(mixing.astype(jnp.bfloat16), narrow[since:]))
                d_mixing = dot_nt(tile_sides[side][here], narrow[since:])
                d_products[part] = d_products[part] + d_mixing * decay_dt
                whole = d_mixing * mixing
                d_rows[h : h + 1, since:] += jnp.sum(whole, axis=0, keepdims=True)
                weighed = d_mixing * (products[here, since:] * decay)
                step_sums[part] = jnp.where(
                    lane == h, jnp.sum(weighed, axis=1, keepdims=True), step_sums[part]
                )
            dx[here, cols] = (
                jnp.where(lane < MP, sides[0], sides[1]) + skip_row[:, cols] * wide[here]
            )
        if between is not None:
            between(i)
    all_steps = jnp.concatenate(step_sums, axis=0)
    d_dt[...] = all_steps
    d_cum[...] = d_rows[...].T - all_steps * dt[...]
    g_skip[...] = jnp.broadcast_to(
        two_part(
            jnp.broadcast_to(jnp.concatenate(skip_sums, axis=1), (8, width)), gather_heads(width)
        ),
        g_skip.shape,
    )
    full = jnp.concatenate(
        [
            d
            if p == 0
            else jnp.concatenate([jnp.zeros((SPAN, p * SPAN), jnp.float32), d], axis=1)
            for p, d in enumerate(d_products)
        ],
        axis=0,
    ).astype(jnp.bfloat16)
    d_bc[:, :NS] = dot(full, narrow_c)
    d_bc[:, NS:] = dot_tn(full, narrow_b)


def ssm_back(info, x, bc, dt, cum, grad, head_params):
    rows, width = x.shape
    f32 = jnp.float32
    return big_call(
        ssm_back_kernel,
        (
            shape_of((rows, width), f32),
            shape_of((rows, 2 * NS), f32),
            shape_of((rows, TILE), f32),
            shape_of((rows, TILE), f32),
            shape_of((8, TILE), f32),
        ),
        info,
        x,
        bc,
        dt,
        cum,
        grad,
        head_params,
        smem=1,
        scratch=(pltpu.VMEM((TILE, rows), f32), pltpu.VMEM((TILE, rows), f32)),
        flops=8 * rows * rows * width,
    )


def state_back_kernel(
    info, x, bc, dt, cum, grad, head_params, step_in, state_in, d_state, dx_in, d_bc_in, d_cum_in,
    d_dt_in, dx, d_bc, d_step, sums,
):
    rows, width = x.shape
    bias, rate = head_params[0:1], head_params[1:2]
    cums, steps = cum[...], dt[...]
    enter = entering_of(info, cums)
    last_start = seg_start(info[0] + rows - 1, info) - info[0]
    place = lax.broadcasted_iota(jnp.int32, (rows, 1), 0)
    end = cums[rows - 1 : rows]
    fade = jnp.where(place >= last_start, jnp.exp(jnp.minimum(end - cums, 0.0)), 0.0)
    leave = fade * steps
    through = jnp.where(last_start < 0, jnp.exp(end), 0.0)
    narrow_b, narrow_c = bc[:, :NS], bc[:, NS:]
    pick = gather_heads(width)
    d_leave = jnp.zeros((rows, TILE), jnp.float32)
    d_enter = jnp.zeros((rows, TILE), jnp.float32)
    d_b = d_bc_in[:, :NS]
    d_c = d_bc_in[:, NS:]
    link = jnp.zeros((8, TILE), jnp.float32)
    for i in range(MH // 2):
        cols = slice(i * TILE, (i + 1) * TILE)
        tile = x[:, cols].astype(jnp.float32)
        wide = grad[:, cols]
        pulled = d_state[:, cols]
        held = state_in[:, cols]
        from_b = dot(narrow_b, pulled)
        leave_tile = lane_pick(leave, 2 * i)
        dx[:, cols] = dx_in[:, cols] + leave_tile * from_b
        d_leave = d_leave + two_part(tile * from_b, pick[cols])
        d_enter = d_enter + two_part(wide * dot(narrow_c, held), pick[cols])
        d_b = d_b + dot_nt((tile * leave_tile).astype(jnp.bfloat16), pulled)
        d_c = d_c + dot_nt((wide * lane_pick(enter, 2 * i)).astype(jnp.bfloat16), held)
        meet = jnp.sum(
            pulled.astype(jnp.float32) * held.astype(jnp.float32), axis=0, keepdims=True
        )
        link = link + two_part(jnp.broadcast_to(meet, (8, TILE)), pick[cols])
    d_bc[:, :NS] = d_b
    d_bc[:, NS:] = d_c
    left = leave * d_leave
    d_cum = d_cum_in[...] + enter * d_enter - left
    at_end = jnp.sum(left, axis=0, keepdims=True) + through * link[:1]
    d_cum = d_cum + jnp.where(place == rows - 1, at_end, 0.0)
    row = lax.broadcasted_iota(jnp.int32, (rows, rows), 0)
    col = lax.broadcasted_iota(jnp.int32, (rows, rows), 1)
    d_log = exact(jnp.where(row <= col, 1.0, 0.0), d_cum)
    d_steps = d_dt_in[...] + fade * d_leave - d_log * rate
    d_pre = d_steps * jax.nn.sigmoid(step_in[...] + bias)
    d_pre = jnp.where(head_lanes(rows), d_pre, 0.0)
    d_step[...] = d_pre.astype(jnp.bfloat16)
    g_rate = jnp.sum(d_log * (-steps * rate), axis=0, keepdims=True)
    g_bias = jnp.sum(d_pre, axis=0, keepdims=True)
    line = lax.broadcasted_iota(jnp.int32, (8, TILE), 0)
    sums[...] = jnp.where(line == 0, g_rate, jnp.where(line == 1, g_bias, 0.0))


def state_back(info, *args):
    rows, width = args[0].shape
    f32 = jnp.float32
    return big_call(
        state_back_kernel,
        (
            shape_of((rows, width), f32),
            shape_of((rows, 2 * NS), f32),
            shape_of((rows, TILE), jnp.bfloat16),
            shape_of((8, TILE), f32),
        ),
        info,
        *args,
        smem=1,
        flops=12 * rows * NS * width,
    )


def join_states(earlier, later):
    decay = later[NS : NS + 1].astype(jnp.float32) + later[NS + 1 : NS + 2].astype(jnp.float32)
    before = earlier[NS : NS + 1].astype(jnp.float32) + earlier[NS + 1 : NS + 2].astype(jnp.float32)
    state = decay * earlier[:NS].astype(jnp.float32) + later[:NS].astype(jnp.float32)
    both = decay * before
    high = both.astype(jnp.bfloat16)
    low = (both - high.astype(jnp.float32)).astype(jnp.bfloat16)
    rest = jnp.zeros((STATE_ROWS - NS - 2, state.shape[1]), jnp.bfloat16)
    return jnp.concatenate([state.astype(jnp.bfloat16), high, low, rest], axis=0)


def scan_states(own, forward):
    place = lax.axis_index("seq")
    count = lax.axis_size("seq")
    nothing = jnp.concatenate(
        [
            jnp.zeros((NS, own.shape[1]), own.dtype),
            jnp.ones((1, own.shape[1]), own.dtype),
            jnp.zeros((STATE_ROWS - NS - 1, own.shape[1]), own.dtype),
        ],
        axis=0,
    )
    everything = lax.all_gather(own, "seq")

    def step(k, before):
        index = k if forward else count - 1 - k
        reached = index < place if forward else index > place
        part = lax.dynamic_index_in_dim(everything, index, 0, False)
        return jnp.where(reached, join_states(before, part), before)

    return lax.fori_loop(0, count, step, nothing)[:NS]


MESH = pl.DeviceIdType.MESH
ANY = pl.BlockSpec(memory_space=pl.ANY)
INTO_VMEM = pl.BlockSpec(memory_space=pltpu.VMEM)


def partners():
    seq, batch = lax.axis_index("seq"), lax.axis_index("batch")
    return {
        "far": (seq + 4 - 8 * (seq // 4), batch),
        "near": (seq + 2 - 4 * (seq // 2 % 2), batch),
        "x": (seq + 1 - 2 * (seq % 2), batch),
        "y": (seq, batch + 2 - 4 * (batch // 2)),
        "core": (seq, batch + 1 - 2 * (batch % 2)),
    }


def greet(others):
    barrier = pltpu.get_barrier_semaphore()
    for other in others:
        pl.semaphore_signal(barrier, inc=1, device_id=other, device_id_type=MESH)
    pl.semaphore_wait(barrier, len(others))


def remote(src, dst, send, recv, other):
    return pltpu.make_async_remote_copy(
        src_ref=src, dst_ref=dst, send_sem=send, recv_sem=recv, device_id=other, device_id_type=MESH
    )


def comm_call(kernel, outs, out_specs, args, in_specs, scratch, number, moved, limit=56):
    return pl.pallas_call(
        kernel,
        out_shape=list(outs),
        in_specs=in_specs,
        out_specs=out_specs,
        scratch_shapes=list(scratch),
        cost_estimate=pl.CostEstimate(flops=0, bytes_accessed=moved, transcendentals=0),
        compiler_params=pltpu.CompilerParams(
            collective_id=number, has_side_effects=True, vmem_limit_bytes=limit * 1024 * 1024
        ),
    )(*args)


def column_chunks(widths, aim=512, lean=0, z_last=None):
    pairs, late = [], []
    for p, width in enumerate(widths):
        tiles, first = width // TILE, 0
        orders, to = (("xyz", "yxz"), late) if p == z_last else (("xy", "yx"), pairs)
        count = max(1, (width + aim // 2) // (2 * aim)) if p != z_last else max(1, width // 512)
        for i in range(count):
            both = tiles // count + (1 if i < tiles % count else 0)
            one = (both + (0 if p == z_last else lean) + 1) // 2
            pair = []
            for cols, order in ((one * TILE, orders[0]), ((both - one) * TILE, orders[1])):
                pair.append((p, first, cols, order))
                first += cols
            to.append(tuple(pair))
    return pairs + late


def pairs_of(pairs, array):
    return [n for n, (one, other) in enumerate(pairs) if one[0] == array]


BITS = {"far": 1, "near": 2, "x": 4, "y": 8, "core": 16}
ORDERS = {
    "xy": ("far", "near", "x", "y"),
    "yx": ("far", "near", "y", "x"),
    "xyz": ("x", "y", "far", "near"),
    "yxz": ("y", "x", "far", "near"),
}


def runs(places):
    out = []
    for place in places:
        if out and out[-1][0] + out[-1][1] == place:
            out[-1] = (out[-1][0], out[-1][1] + 1)
        else:
            out.append((place, 1))
    return out


def gather_plan(order):
    held, plan = [0], []
    for name in ORDERS[order] + ("core",):
        plan.append((name, [(f, k, f + BITS[name]) for f, k in runs(held)]))
        held = sorted(held + [block + BITS[name] for block in held])
    return plan


def scatter_plan(order):
    held, plan = list(range(16)), []
    for name in reversed(ORDERS[order]):
        bit = BITS[name]
        sent = [i for i, block in enumerate(held) if block & bit]
        kept = [i for i, block in enumerate(held) if not block & bit]
        plan.append((name, runs(sent), runs(kept)))
        held = [held[i] for i in kept]
    return plan


def bit_apart(r):
    me = lax.axis_index("seq")
    far = (r // 4 + me // 4) % 2
    near = (r // 2 % 2 + me // 2 % 2) % 2
    side = (r % 2 + me % 2) % 2
    return 4 * far + 2 * near + side


def join_into(target, earlier, later):
    decay = later[NS : NS + 1].astype(jnp.float32) + later[NS + 1 : NS + 2].astype(jnp.float32)
    before = earlier[NS : NS + 1].astype(jnp.float32) + earlier[NS + 1 : NS + 2].astype(jnp.float32)
    both = decay * before
    high = both.astype(jnp.bfloat16).astype(jnp.float32)
    line = lax.broadcasted_iota(jnp.int32, (STATE_ROWS - NS, both.shape[1]), 0)
    tail = jnp.where(line == 0, high, jnp.where(line == 1, both - high, 0.0))
    for first in range(0, NS, 32):
        rows = slice(first, first + 32)
        target[rows] = (
            decay * earlier[rows].astype(jnp.float32) + later[rows].astype(jnp.float32)
        ).astype(jnp.bfloat16)
    target[NS:] = tail.astype(jnp.bfloat16)


SCAN_PARTS = 2


class StateScan:
    def __init__(self, forward, own, result, arrived, sent, before, send, recv, others):
        me = lax.axis_index("seq")
        self.seconds = []
        for bit in (me % 2, me // 2 % 2, me // 4):
            self.seconds.append(bit == 1 if forward else bit == 0)
        route = (others["x"], others["near"], others["far"])
        width = own.shape[1] // SCAN_PARTS
        self.parts = []
        for part in range(SCAN_PARTS):
            cols = pl.ds(part * width, width)
            here = (slice(None), cols)
            sources = (own.at[here], sent.at[0].at[here], sent.at[1].at[here])
            targets = [arrived.at[k].at[here] for k in range(3)]
            copies = [
                remote(sources[k], targets[k], send.at[k, part], recv.at[k, part], route[k])
                for k in range(3)
            ]
            befores = [before.at[k].at[here] for k in range(2)]
            self.parts.append((sources, targets, copies, befores, result.at[here]))

    def step(self, k):
        for part in self.parts:
            self.part_step(k, *part)

    def part_step(self, k, sources, targets, copies, before, result):
        if k == 0:
            copies[0].start()
            return
        copies[k - 1].wait_recv()
        other, mine = targets[k - 1], sources[k - 1]
        second = self.seconds[k - 1]

        @pl.when(second)
        def _():
            if k < 3:
                join_into(sources[k], other, mine)
            if k == 1:
                before[0][...] = other[...]
            elif k == 2:
                join_into(before[1], other, before[0])
            else:
                last = before[1]
                decay = last[NS : NS + 1].astype(jnp.float32) + last[NS + 1 : NS + 2].astype(
                    jnp.float32
                )
                result[...] = (
                    decay * other[:NS].astype(jnp.float32) + last[:NS].astype(jnp.float32)
                ).astype(jnp.bfloat16)

        @pl.when(jnp.logical_not(second))
        def _():
            if k < 3:
                join_into(sources[k], mine, other)
            if k == 1:
                line = lax.broadcasted_iota(jnp.int32, before[0].shape, 0)
                before[0][...] = jnp.where(line == NS, 1.0, 0.0).astype(jnp.bfloat16)
            elif k == 2:
                before[1][...] = before[0][...]
            else:
                result[...] = before[1][:NS]

        if k < 3:
            copies[k].start()

    def finish(self):
        for part in self.parts:
            for copy in part[2]:
                copy.wait_send()


def scan_scratch(width):
    rows = STATE_ROWS
    dma = pltpu.SemaphoreType.DMA
    narrow = jnp.bfloat16
    return [
        pltpu.VMEM((3, rows, width), narrow),
        pltpu.VMEM((2, rows, width), narrow),
        pltpu.VMEM((2, rows, width), narrow),
        dma((3, SCAN_PARTS)),
        dma((3, SCAN_PARTS)),
    ]


RIM = 8
COLS = 384


def own_order_into(target):
    width = target.shape[0]
    per = width // 32
    me = lax.axis_index("seq") * 4 + lax.axis_index("batch")
    step = 128

    def fill(i, carry):
        first = pl.multiple_of(i * step, step)
        row = lax.broadcasted_iota(jnp.int32, (step, width), 0) + first
        col = lax.broadcasted_iota(jnp.int32, (step, width), 1)
        j = col // per
        flipped = (j & 1) * 16 + (j & 2) * 4 + (j & 4) + (j & 8) // 4 + (j & 16) // 16
        source = (flipped ^ me) * per + col % per
        target[pl.ds(first, step)] = jnp.where(row == source, 1.0, 0.0).astype(target.dtype)
        return carry

    lax.fori_loop(0, width // step, fill, 0)


def three_part(left, right):
    high = left.astype(jnp.bfloat16)
    rest = left - high.astype(jnp.float32)
    mid = rest.astype(jnp.bfloat16)
    low = (rest - mid.astype(jnp.float32)).astype(jnp.bfloat16)
    return dot(high, right) + dot(mid, right) + dot(low, right)


def places_of(lens, rows):
    one, two, three = lens[0, 0], lens[0, 1], lens[0, 2]
    return [lax.axis_index("seq") * rows, one, one + two, one + two + three]


def head_rows(bias, rate_log, skip, target):
    lane = lax.broadcasted_iota(jnp.int32, (1, TILE), 1)
    for k, source in enumerate((bias, rate_log, skip)):
        row = jnp.zeros((1, TILE), jnp.float32)
        for h in range(MH):
            row = jnp.where(lane == h, source[h], row)
        if k == 1:
            row = jnp.where(lane < MH, jnp.exp(row), 0.0)
        target[k : k + 1] = row


def pair_columns(value, back):
    tiles = [value[:, i * TILE : (i + 1) * TILE] for i in range(PAIRS)]
    turned = [pltpu.roll(tile, HEAD_SIZE, 1) for tile in tiles]
    lane = lax.broadcasted_iota(jnp.int32, tiles[0].shape, 1)

    def head(i, side):
        return tiles[i // 2] if i % 2 == side else turned[i // 2]

    out = []
    for i in range(PAIRS):
        if back:
            first, second = 2 * i, 2 * i + 1
            group = QUERY_HEADS // KEY_VALUE_HEADS
            first, second = [2 * (h % group) + h // group for h in (first, second)]
        else:
            first, second = i, i + PAIRS
        out.append(jnp.where(lane < HEAD_SIZE, head(first, 0), head(second, 1)))
    return jnp.concatenate(out, axis=1)


def shards_into(w_attn, w_ssm_in, w_dt, w_out, conv, mix, out):
    f32, narrow = jnp.float32, jnp.bfloat16
    ssm_width = MH * MP
    xbc = w_ssm_in.shape[1] - ssm_width
    query = QUERY_HEADS * HEAD_SIZE
    attn = w_attn.shape[1]
    conv[:, :xbc] = w_ssm_in[:, ssm_width:]
    conv[:, xbc:] = jnp.zeros((conv.shape[0], TILE), narrow)
    block = conv.shape[0]
    row = lax.broadcasted_iota(jnp.int32, (block, block), 0)
    same = row == lax.broadcasted_iota(jnp.int32, (block, block), 1)
    conv[:, xbc : xbc + MH] = dot_nt(jnp.where(same, 1.0, 0.0).astype(narrow), w_dt[...]).astype(
        narrow
    )
    mix[:, :query] = pair_columns(w_attn[:, :query].astype(f32), False).astype(narrow)
    mix[:, query:attn] = w_attn[:, query:]
    mix[:, attn:] = w_ssm_in[:, :ssm_width]
    out[:, :query] = pair_columns(w_out[:, :query].astype(f32), False).astype(narrow)
    out[:, query:] = w_out[:, query:]


class Stage:
    def __init__(self, sources, targets, sems):
        self.copies = [
            pltpu.make_async_copy(source, target, sems.at[k])
            for k, (source, target) in enumerate(zip(sources, targets))
        ]
        self.open = {}

    def start(self, *which):
        for k in which:
            self.copies[k].start()
            self.open[k] = True

    def need(self, *which):
        for k in which:
            if self.open.pop(k, False):
                self.copies[k].wait()

    def finish(self):
        self.need(*list(self.open))


class Gather:
    def __init__(self, ins, outs, pairs, send, recv, local, others):
        self.ins, self.outs, self.pairs = ins, outs, pairs
        self.send, self.recv, self.local, self.others = send, recv, local, others
        self.started = {}
        self.block = ins[0].shape[0]

    def own(self):
        copies = []
        for p in range(len(self.ins)):
            copy = pltpu.make_async_copy(
                self.ins[p], self.outs[p].at[pl.ds(0, self.block)], self.local.at[p]
            )
            copy.start()
            copies.append(copy)
        for copy in copies:
            copy.wait()

    def step(self, n, stage):
        for side in range(2):
            p, column, cols, order = self.pairs[n][side]
            if stage > 0:
                for copy in self.started[n, side, stage - 1]:
                    copy.wait_recv()
            if stage == 5:
                continue
            name, moves = gather_plan(order)[stage]
            copies = []
            for k, (first, rows, there) in enumerate(moves):
                block = self.block
                copy = remote(
                    self.outs[p].at[pl.ds(first * block, rows * block), pl.ds(column, cols)],
                    self.outs[p].at[pl.ds(there * block, rows * block), pl.ds(column, cols)],
                    self.send.at[2 * n + side, stage, k],
                    self.recv.at[2 * n + side, stage, k],
                    self.others[name],
                )
                copy.start()
                copies.append(copy)
            self.started[n, side, stage] = copies

    def finish(self):
        for copies in self.started.values():
            for copy in copies:
                copy.wait_send()


def around():
    seq, batch = lax.axis_index("seq"), lax.axis_index("batch")
    return ((seq + 7) % 8, batch), ((seq + 1) % 8, batch)


def conv_masks(info, rows):
    at = lax.broadcasted_iota(jnp.int32, (rows, 1), 0) + info[0]
    start = seg_start(at, info)
    return [jnp.where(at - (CONV - 1) + i >= start, 1.0, 0.0) for i in range(CONV)]


def conv_forward(info, raw, conv_w, conv_b, pre, x, bc):
    rows = x.shape[0]
    masks = conv_masks(info, rows)
    tiles = pre.shape[1] // TILE
    split = x.shape[1] // TILE
    for i in range(tiles):
        cols = slice(i * TILE, (i + 1) * TILE)
        total = jnp.broadcast_to(conv_b[i : i + 1], (rows, TILE))
        for k in range(CONV):
            first = RIM - (CONV - 1) + k
            shifted_rows = jnp.where(masks[k] > 0.0, raw[first : first + rows, cols], 0.0)
            total = total + conv_w[k : k + 1, cols] * shifted_rows
        pre[:, cols] = total
        out = (total * jax.nn.sigmoid(total)).astype(jnp.bfloat16)
        if i < split:
            x[:, cols] = out
        else:
            bc[:, (i - split) * TILE : (i - split + 1) * TILE] = out


def front_kernel(
    count, pairs, lens, bias, rate_log, skip, layer_x, layer_g, norm_gain, mlp_gain, freqs, conv_w,
    conv_b, w_attn, w_ssm_in, w_dt, w_out, w_gate_up, w_down, *refs
):
    fulls, made, refs = refs[:count], refs[count : count + 23], refs[count + 23 :]
    near, refs = refs[:25], refs[25:]
    writes = Stage((*near,), (*fulls[:2], *made), refs[-1])
    fulls = (*near[:2], *fulls[2:])
    (
        x_own, g_own, gains_own, normed, q, kv, gate_z, raw, pre, x, bc, y, state, dt, cum,
        out, out_t, lse, state_in, order, cosine, sine, head_params,
    ) = near[2:]
    (
        s_conv, s_mix, s_out, gains,
        attn_proj, dt_t, cum_t, heads, acc, top, total, arrived, sent, before,
        scan_send, scan_recv, send, recv, w_send, w_recv, w_local, rim_send, rim_recv,
    ) = refs[:-1]
    ins = (s_conv, s_mix, s_out, w_gate_up, w_down)
    others = partners()
    previous, following = around()
    greet(list(others.values()) + [previous, following])
    me = lax.axis_index("seq")
    rows, width = layer_x.shape
    info = places_of(lens, rows)
    shards_into(w_attn, w_ssm_in, w_dt, w_out, s_conv, s_mix, s_out)
    gather = Gather(ins, fulls, pairs, w_send, w_recv, w_local, others)
    gather.own()

    first = len(pairs_of(pairs, 0)) + len(pairs_of(pairs, 1))
    small = pairs_of(pairs, 2)
    waves = {}
    for n in reversed(range(len(pairs))):
        for stage in range(6):
            late = 1 if n >= first and stage >= 2 else 0
            wave = n - small[0] + 2 * stage if n in small else n + stage + late
            waves.setdefault(wave, []).append((n, stage))

    def pump(*which):
        for wave in which:
            for n, stage in waves.pop(wave, []):
                gather.step(n, stage)

    conv_wave = pairs_of(pairs, 0)[-1] + 5
    mix_wave = pairs_of(pairs, 1)[-1] + 5
    pump(0)
    own_order_into(order)
    head_rows(bias, rate_log, skip, head_params)
    gains[...] = jnp.zeros_like(gains)
    for k, source in enumerate((norm_gain, mlp_gain)):
        for i in range(width // TILE):
            gains[k : k + 1, i * TILE : (i + 1) * TILE] = source[i : i + 1]
    pump(1)
    at = lax.broadcasted_iota(jnp.int32, (rows, 1), 0) + info[0]
    angles = (at - seg_start(at, info)).astype(jnp.float32) * freqs[...]
    cosine[...] = jnp.cos(angles)
    sine[...] = jnp.sin(angles)
    x_own[...] = dot(layer_x[...], order[...]).astype(jnp.bfloat16)
    pump(2)
    gains_own[...] = three_part(gains[...], order[...])
    wide = x_own[...].astype(jnp.float32)
    scale = lax.rsqrt(jnp.mean(wide * wide, axis=-1, keepdims=True) + NORM_EPS)
    normed[...] = (wide * scale * gains_own[0:1]).astype(jnp.bfloat16)
    pump(3)
    g_own[...] = dot(layer_g[...], order[...]).astype(jnp.bfloat16)
    pump(*range(4, conv_wave + 1))

    full_conv, full_mix = fulls[0], fulls[1]
    xbc = pre.shape[1]
    conv_cols = full_conv.shape[1] // COLS
    attn_cols = attn_proj.shape[1] // COLS
    gate_cols = gate_z.shape[1] // COLS

    def project(weights, first, target, row, count_cols):
        def one(j, carry):
            cols = pl.ds(pl.multiple_of(j * COLS, TILE), COLS)
            there = pl.ds(pl.multiple_of(first + j * COLS, TILE), COLS)
            target[row : row + rows, cols] = dot(normed[...], weights[:, there])
            return carry

        lax.fori_loop(0, count_cols, one, 0)

    def at(r):
        return kv.at[pl.ds(r * rows, rows)]

    routes = {4: ("far", 0), 2: ("near", 0), 6: ("near", 4)}
    routes.update({r: ("x", r - 1) for r in (1, 3, 5, 7)})
    copies = {
        r: remote(at(src), at(r), send.at[r], recv.at[r], others[name])
        for r, (name, src) in routes.items()
    }
    project(full_conv, 0, raw, RIM, conv_cols)
    rim = remote(
        raw.at[pl.ds(rows, RIM)], raw.at[pl.ds(0, RIM)], rim_send.at[0], rim_recv.at[0], following
    )
    rim.start()
    pump(*range(conv_wave + 1, mix_wave))
    rim.wait_recv()
    conv_forward(info, raw, conv_w, conv_b, pre, x, bc)
    step_in = raw.at[pl.ds(RIM, rows), pl.ds(xbc, TILE)]
    ssm_states(info, x, bc, step_in, head_params, state, dt, cum, dt_t, cum_t)
    scan = StateScan(True, state, state_in, arrived, sent, before, scan_send, scan_recv, others)
    scan.step(0)
    writes.start(0, 9, 10, 11, 12, 14, 15, 16)
    pump(mix_wave)
    project(full_mix, 0, attn_proj, 0, attn_cols)
    rope_kernel(attn_proj, cosine, sine, q, kv.at[pl.ds(0, rows)])
    copies[4].start()
    copies[2].start()
    copies[1].start()
    pump(mix_wave + 1)
    project(full_mix, attn_proj.shape[1], gate_z, 0, gate_cols)
    writes.start(1, 8, 6, 2, 3, 4, 5, 21, 22, 23, 24)
    attend_start(q, heads, acc, top, total)

    def attend(r):
        block = bit_apart(r)

        @pl.when(block <= me)
        def _():
            place = pl.ds(pl.multiple_of(r * rows, rows), rows)
            keys = kv[place, :TILE]
            values_t = kv[place, TILE:].astype(jnp.float32).T.astype(jnp.bfloat16)
            attend_block(info, block, keys, values_t, heads, acc, top, total)

    def several(first, gap, count_blocks):
        def body(j, carry):
            attend(first + j * gap)
            return carry

        lax.fori_loop(0, count_blocks, body, 0)

    scan.step(1)
    copies[4].wait_recv()
    copies[6].start()
    copies[5].start()
    copies[2].wait_recv()
    copies[3].start()
    copies[6].wait_recv()
    copies[7].start()
    pump(mix_wave + 2)
    several(0, 4, 2)
    pump(mix_wave + 3)
    ssm_local(info, x, bc, head_params, y, cum, dt_t, cum_t)
    writes.start(13)
    scan.step(2)
    pump(mix_wave + 4)
    several(2, 4, 2)
    pump(mix_wave + 5)
    for r in (1, 3, 5, 7):
        copies[r].wait_recv()
    writes.start(7)
    several(1, 2, 2)
    pump(mix_wave + 6)
    several(5, 2, 2)
    pump(mix_wave + 7)
    lse[...] = top[...] + jnp.log(total[...])
    attend_write(acc, total, out, out_t)
    scan.step(3)
    writes.start(17, 18, 19, 20)
    pump(*sorted(waves))
    gather.finish()
    writes.finish()
    scan.finish()
    rim.wait_send()
    for copy in copies.values():
        copy.wait_send()


def front(lens, bias, rate_log, skip, layer_x, layer_g, norm_gain, mlp_gain, freqs, conv_w, conv_b, weights):
    w_attn, w_ssm_in, w_dt, w_out, w_gate_up, w_down = weights
    rows, width = layer_x.shape
    f32, narrow = jnp.float32, jnp.bfloat16
    block = w_attn.shape[0]
    query_width = QUERY_HEADS * HEAD_SIZE
    pair_width = 2 * KEY_VALUE_HEADS * HEAD_SIZE
    ssm_width = MH * MP
    xbc = conv_w.shape[1]
    widths = [
        xbc + TILE, w_attn.shape[1] + ssm_width, w_out.shape[1], w_gate_up.shape[1],
        w_down.shape[1],
    ]
    count = len(widths)
    pairs = column_chunks(widths, z_last=2)
    fulls = [shape_of((width, w), narrow) for w in widths]
    outs = fulls + [
        shape_of((rows, width), narrow),
        shape_of((rows, width), narrow),
        shape_of((8, width), f32),
        shape_of((rows, width), narrow),
        shape_of((rows, query_width), narrow),
        shape_of((8 * rows, pair_width), narrow),
        shape_of((rows, ssm_width), f32),
        shape_of((rows + RIM, widths[0]), f32),
        shape_of((rows, xbc), f32),
        shape_of((rows, ssm_width), narrow),
        shape_of((rows, 2 * NS), narrow),
        shape_of((rows, ssm_width), f32),
        shape_of((STATE_ROWS, ssm_width), narrow),
        shape_of((rows, TILE), f32),
        shape_of((rows, TILE), f32),
        shape_of((rows, query_width), narrow),
        shape_of((query_width, rows), f32),
        shape_of((QUERY_HEADS, rows), f32),
        shape_of((NS, ssm_width), narrow),
        shape_of((width, width), narrow),
        shape_of((rows, TILE), f32),
        shape_of((rows, TILE), f32),
        shape_of((8, TILE), f32),
    ]
    dma = pltpu.SemaphoreType.DMA
    scratch = [pltpu.VMEM(o.shape, o.dtype) for o in (*outs[:2], *outs[count:])]
    scratch += [
        *(pltpu.VMEM((block, widths[k]), narrow) for k in (0, 1, 2)),
        pltpu.VMEM((8, width), f32),
        pltpu.VMEM((rows, query_width + pair_width), f32),
        pltpu.VMEM((TILE, rows), f32),
        pltpu.VMEM((TILE, rows), f32),
        pltpu.VMEM((QUERY_HEADS, rows, TILE), narrow),
        pltpu.VMEM((QUERY_HEADS, HEAD_SIZE, rows), f32),
        pltpu.VMEM((QUERY_HEADS, rows), f32),
        pltpu.VMEM((QUERY_HEADS, rows), f32),
        *scan_scratch(ssm_width),
        dma((8,)),
        dma((8,)),
        dma((2 * len(pairs), 5, 4)),
        dma((2 * len(pairs), 5, 4)),
        dma((count,)),
        dma((1,)),
        dma((1,)),
        dma((25,)),
    ]
    result = comm_call(
        lambda *refs: front_kernel(count, pairs, *refs),
        outs,
        [ANY] * len(outs),
        (
            lens, bias, rate_log, skip, layer_x, layer_g, norm_gain, mlp_gain, freqs, conv_w,
            conv_b, *weights,
        ),
        [pl.BlockSpec(memory_space=pltpu.SMEM)] * 4 + [INTO_VMEM] * 13,
        scratch,
        0,
        200_000_000,
    )
    return result[:count], result[count:]


def middle_kernel(
    lens, y, bc, cum, state_in, state_own, z, ssm_gain, attended, x_own, g_own, gains, order,
    hbm_out, hbm_gu, hbm_down,
    far_layer, far_joined, far_hidden, far_gu, far_two, far_mixer, far_middle, d_ssm, d_z, pull, att_grad,
    g_ssm, g_mlp,
    w_out, w_gu, w_down, ssm_out, scale, middle, gate_up, d_normed, dy, narrow, layer_out,
    joined, hidden, d_gu, normed_two, d_mixer, d_middle, sems, out_sems,
):
    writes = Stage(
        (layer_out, joined, hidden, d_gu, normed_two, d_mixer, d_middle),
        (far_layer, far_joined, far_hidden, far_gu, far_two, far_mixer, far_middle),
        out_sems,
    )
    rows, width = x_own.shape
    info = places_of(lens, rows)
    copies = [
        pltpu.make_async_copy(src, dst, sems.at[k])
        for k, (src, dst) in enumerate(((hbm_out, w_out), (hbm_gu, w_gu), (hbm_down, w_down)))
    ]
    for copy in copies:
        copy.start()
    attn = attended.shape[1]
    ff = hidden.shape[1]
    step = 512

    def tiles(count, body):
        def one(j, carry):
            body(pl.ds(pl.multiple_of(j * step, step), step), j * step)
            return carry

        lax.fori_loop(0, count // step, one, 0)

    joined[:, :attn] = attended[...]
    ssm_finish_kernel(
        info, y, bc, cum, state_in, z, ssm_gain, ssm_out,
        joined.at[:, pl.ds(attn, joined.shape[1] - attn)], scale,
    )
    writes.start(1)
    copies[0].wait()

    def add_mixers(here, first):
        middle[:, here] = x_own[:, here].astype(jnp.float32) + dot_nt(joined[...], w_out[here])

    tiles(width, add_mixers)
    wide = middle[...]
    r = lax.rsqrt(jnp.mean(wide * wide, axis=-1, keepdims=True) + NORM_EPS)
    normed_two[...] = (wide * r * gains[1:2]).astype(jnp.bfloat16)
    writes.start(4)
    copies[1].wait()

    def up_project(here, first):
        there = pl.ds(pl.multiple_of(ff + first, step), step)
        gate = dot(normed_two[...], w_gu[:, here])
        up = dot(normed_two[...], w_gu[:, there])
        gate_up[:, here] = gate
        gate_up[:, there] = up
        hidden[:, here] = (gate * jax.nn.sigmoid(gate) * up).astype(jnp.bfloat16)

    tiles(ff, up_project)
    writes.start(2)
    copies[2].wait()

    def down_project(here, first):
        narrow[:, here] = (middle[:, here] + dot_nt(hidden[...], w_down[here])).astype(jnp.bfloat16)

    tiles(width, down_project)

    def plain(here, first):
        layer_out[:, here] = dot_nt(narrow[...], order[here]).astype(jnp.bfloat16)

    tiles(width, plain)
    writes.start(0)

    def down_back(here, first):
        there = pl.ds(pl.multiple_of(ff + first, step), step)
        d_hidden = dot(g_own[...], w_down[:, here])
        gate, up = gate_up[:, here], gate_up[:, there]
        sig = jax.nn.sigmoid(gate)
        d_gate = d_hidden * up * (sig * (1.0 + gate * (1.0 - sig)))
        d_gu[:, here] = d_gate.astype(jnp.bfloat16)
        d_gu[:, there] = (d_hidden * gate * sig).astype(jnp.bfloat16)

    tiles(ff, down_back)
    writes.start(3)

    def up_back(here, first):
        d_normed[:, here] = dot_nt(d_gu[...], w_gu[here])

    tiles(width, up_back)
    grads = d_normed[...]
    wide = middle[...]
    g_mlp[...] = jnp.sum(grads * wide * r, axis=0, keepdims=True)
    inner = grads * gains[1:2]
    coeff = jnp.mean(inner * wide, axis=-1, keepdims=True)
    total = g_own[...].astype(jnp.float32) + r * (inner - wide * (r * r * coeff))
    d_middle[...] = total
    d_mixer[...] = total.astype(jnp.bfloat16)
    writes.start(5, 6)

    def att_back(here, first):
        att_grad[:, here] = dot(d_mixer[...], w_out[:, here]).astype(jnp.bfloat16)

    tiles(attn, att_back)

    def ssm_part(here, first):
        there = pl.ds(pl.multiple_of(attn + first, step), step)
        dy[:, here] = dot(d_mixer[...], w_out[:, there])

    tiles(dy.shape[1], ssm_part)
    gate_back_kernel(
        info, dy, ssm_out, z, scale, ssm_gain, cum, bc, d_ssm, d_z, pull.at[pl.ds(0, NS)], g_ssm
    )
    pull[NS:] = state_own[NS:]
    writes.finish()


def middle_part(lens, y, bc, cum, state_in, state_own, z, ssm_gain, attended, x_own, g_own, gains, order, w_out, w_gu, w_down):
    rows, width = x_own.shape
    ssm_width, attn = y.shape[1], attended.shape[1]
    ff = w_down.shape[1]
    f32, narrow = jnp.float32, jnp.bfloat16
    outs = [
        shape_of((rows, width), narrow),
        shape_of((rows, attn + ssm_width), narrow),
        shape_of((rows, ff), narrow),
        shape_of((rows, 2 * ff), narrow),
        shape_of((rows, width), narrow),
        shape_of((rows, width), narrow),
        shape_of((rows, width), f32),
        shape_of((rows, ssm_width), f32),
        shape_of((rows, ssm_width), narrow),
        shape_of((STATE_ROWS, ssm_width), narrow),
        shape_of((rows, attn), narrow),
        shape_of(ssm_gain.shape, f32),
        shape_of((1, width), f32),
    ]
    args = (
        lens, y, bc, cum, state_in, state_own, z, ssm_gain, attended, x_own, g_own, gains, order,
        w_out, w_gu, w_down,
    )
    return pl.pallas_call(
        middle_kernel,
        out_shape=outs,
        in_specs=[pl.BlockSpec(memory_space=pltpu.SMEM)] + [INTO_VMEM] * 12 + [ANY] * 3,
        out_specs=[ANY] * 7 + [INTO_VMEM] * (len(outs) - 7),
        scratch_shapes=[
            pltpu.VMEM(w_out.shape, narrow),
            pltpu.VMEM(w_gu.shape, narrow),
            pltpu.VMEM(w_down.shape, narrow),
            pltpu.VMEM((rows, ssm_width), f32),
            pltpu.VMEM((rows, TILE), f32),
            pltpu.VMEM((rows, width), f32),
            pltpu.VMEM((rows, 2 * ff), f32),
            pltpu.VMEM((rows, width), f32),
            pltpu.VMEM((rows, ssm_width), f32),
            pltpu.VMEM((rows, width), narrow),
            *(pltpu.VMEM(o.shape, o.dtype) for o in outs[:7]),
            pltpu.SemaphoreType.DMA((3,)),
            pltpu.SemaphoreType.DMA((7,)),
        ],
        compiler_params=pltpu.CompilerParams(vmem_limit_bytes=60 * 1024 * 1024),
    )(*args)


def turn_over(value):
    return value.astype(jnp.float32).T.astype(jnp.bfloat16)


class Scatter:
    def __init__(self, ins, outs, arrived, pairs, send, recv, others):
        self.ins, self.outs, self.arrived, self.pairs = ins, outs, arrived, pairs
        self.send, self.recv, self.others = send, recv, others
        self.block = ins[0].shape[0] // 16
        self.started = {}

    def source(self, p, stage):
        return self.ins[p] if stage == 0 else self.arrived[4 * p + stage - 1]

    def step(self, n, stage):
        for side in range(2):
            if stage > 0:
                self.take(n, side, stage - 1)
            if stage < 4:
                self.begin(n, side, stage)

    def begin(self, n, side, stage):
        p, column, width, order = self.pairs[n][side]
        cols = pl.ds(column, width)
        name, sent, unused_kept = scatter_plan(order)[stage]
        copies, row, block = [], 0, self.block
        for k, (first, count) in enumerate(sent):
            copy = remote(
                self.source(p, stage).at[pl.ds(first * block, count * block), cols],
                self.arrived[4 * p + stage].at[pl.ds(row * block, count * block), cols],
                self.send.at[2 * n + side, stage, k],
                self.recv.at[2 * n + side, stage, k],
                self.others[name],
            )
            copy.start()
            copies.append(copy)
            row += count
        self.started[n, side, stage] = copies

    def take(self, n, side, stage):
        p, column, width, order = self.pairs[n][side]
        cols = slice(column, column + width)
        source, got = self.source(p, stage), self.arrived[4 * p + stage]
        target = self.outs[p] if stage == 3 else got
        unused_name, unused_sent, kept = scatter_plan(order)[stage]
        row, block = 0, self.block
        for k, (first, count) in enumerate(kept):
            self.started[n, side, stage][k].wait_recv()

            def add(i, carry):
                at = pl.multiple_of(i * block, block)
                there = pl.ds(row * block + at, block)
                total = source[pl.ds(first * block + at, block), cols].astype(jnp.float32) + got[
                    there, cols
                ].astype(jnp.float32)
                target[there, cols] = total.astype(target.dtype)
                return carry

            lax.fori_loop(0, count, add, 0)
            row += count

    def finish(self):
        for copies in self.started.values():
            for copy in copies:
                copy.wait_send()


def scatter_scratch(widths, size):
    scratch = []
    for width in widths:
        scratch += [pltpu.VMEM((size >> (s + 1), width), jnp.bfloat16) for s in range(4)]
    return scratch


def weight_products(left_t, right, theirs, target):
    rows = right.shape[0]
    step = 256 if right.shape[1] % 256 == 0 else TILE

    def one(j, carry):
        cols = pl.ds(pl.multiple_of(j * step, step), step)
        product = dot(left_t[:, :rows], right[:, cols]) + dot(left_t[:, rows:], theirs[:, cols])
        target[:, cols] = product.astype(target.dtype)
        return carry

    lax.fori_loop(0, right.shape[1] // step, one, 0)


def conv_back_start(info, dx, d_bc, pre, raw, d_pre, g_conv):
    rows, split = dx.shape[0], dx.shape[1] // TILE
    masks = conv_masks(info, rows)
    g_conv[...] = jnp.zeros_like(g_conv)
    for i in range(pre.shape[1] // TILE):
        cols = slice(i * TILE, (i + 1) * TILE)
        if i < split:
            grad = dx[:, cols]
        else:
            grad = d_bc[:, (i - split) * TILE : (i - split + 1) * TILE]
        value = pre[:, cols]
        sig = jax.nn.sigmoid(value)
        grad = grad * (sig * (1.0 + value * (1.0 - sig)))
        d_pre[:rows, cols] = grad
        for k in range(CONV):
            first = RIM - (CONV - 1) + k
            term = jnp.where(masks[k] > 0.0, raw[first : first + rows, cols], 0.0)
            g_conv[k : k + 1, cols] = jnp.sum(grad * term, axis=0, keepdims=True)
        g_conv[CONV : CONV + 1, cols] = jnp.sum(grad, axis=0, keepdims=True)


def conv_back_end(info, d_pre, conv_w, d_raw):
    rows = d_raw.shape[0]
    at = lax.broadcasted_iota(jnp.int32, (rows, 1), 0) + info[0]
    masks = [
        jnp.where(seg_start(at + (CONV - 1) - k, info) <= at, 1.0, 0.0) for k in range(CONV)
    ]
    for i in range(d_pre.shape[1] // TILE):
        cols = slice(i * TILE, (i + 1) * TILE)
        total = jnp.zeros((rows, TILE), jnp.float32)
        for k in range(CONV):
            first = CONV - 1 - k
            part = jnp.where(masks[k] > 0.0, d_pre[first : first + rows, cols], 0.0)
            total = total + conv_w[k : k + 1, cols] * part
        d_raw[:, cols] = total.astype(jnp.bfloat16)


def back_kernel(pairs, *refs):
    lens, far, refs = refs[0], refs[1:27], refs[27:]
    outs, near, refs = refs[:11], refs[11:37], refs[37:]
    loads = Stage(far, near, refs[-1])
    loads.start(21, 22, 9, 20, 23, 4, 5, 6, 7, 8, 19, 24, 18, 25, *range(10, 18), *range(4))
    (
        head_params, conv_w, cosine, sine, q, kv, grad, out_t, lse, pull, x, bc, dt, cum,
        d_ssm, raw, state_in, pre, normed, normed_two, d_mixer, grad_rows, hidden, joined, d_gu,
        d_z,
    ) = near
    (
        d_conv, d_attn, g_conv, head_sums, g_skip, p_conv, p_attn, out_down, out_gu, out_out, out_z,
    ) = outs
    refs = refs[:-1]
    partials, refs = refs[:4], refs[4:]
    arrived_w, refs = refs[:16], refs[16:]
    (
        half_grad, half_two, half_mixer, their_hidden, their_joined, their_gu, their_z, their_normed,
        their_conv, their_attn, left_t, heads, grads, delta, acc, dkv, from_x, from_far, from_near, dq, d_pair,
        d_cum, d_dt, cols_t, d_rows, d_pre,
        arrived, sent, before, scan_send, scan_recv, send, recv, swap_send, swap_recv,
        w_send, w_recv, rim_send, rim_recv,
    ) = refs
    others = partners()
    previous, following = around()
    greet(list(others.values()) + [previous, following])
    me = lax.axis_index("seq")
    rows = q.shape[0]
    info = places_of(lens, rows)
    half = normed.shape[1] // 2
    xbc = pre.shape[1]
    dx = d_pre.at[pl.ds(0, rows), pl.ds(0, x.shape[1])]
    d_bc = d_pre.at[pl.ds(0, rows), pl.ds(x.shape[1], 2 * NS)]
    d_state = arrived.at[0, pl.ds(0, NS)]
    scan = StateScan(False, pull, d_state, arrived, sent, before, scan_send, scan_recv, others)
    loads.need(9)
    scan.step(0)
    behind = pl.ds(half, half)
    given = [
        (far[21].at[:, behind], half_grad),
        (far[22], their_hidden),
        (far[20].at[:, behind], half_mixer),
        (far[23], their_joined),
        (far[19].at[:, behind], half_two),
        (far[24], their_gu),
        (far[18].at[:, behind], their_normed),
        (far[25], their_z),
    ]
    swaps = [
        remote(give, take, swap_send.at[k], swap_recv.at[k], others["core"])
        for k, (give, take) in enumerate(given)
    ]
    for copy in swaps:
        copy.start()
    scatter = Scatter(
        partials, (out_down, out_gu, out_out, out_z), arrived_w, pairs, w_send, w_recv, others
    )

    def weights(k, left, left_half, right, theirs):
        first = 2 * (0, 2, 1, 3)[k]
        loads.need(*((21, 22), (19, 24), (20, 23), (18, 25))[k])
        swaps[first].wait_recv()
        swaps[first + 1].wait_recv()
        left_t[:, :rows] = turn_over(left[:, :half])
        left_t[:, rows:] = turn_over(left_half[...])
        weight_products(left_t, right, theirs, partials[k])

    small = pairs_of(pairs, 2)
    waves = {}
    for n in range(len(pairs)):
        for stage in range(5):
            begin = 1 + (n - small[0]) // 2 if n in small else n
            waves.setdefault(begin + stage, []).append((n, stage))

    def pump(wave):
        for n, stage in waves.pop(wave):
            scatter.step(n, stage)

    loads.need(4, 5, 6, 7, 8)
    attend_back_start(q, grad, out_t, heads, grads, delta, acc)

    def block_back(r):
        block = bit_apart(r)
        place = pl.ds(pl.multiple_of(r * rows, rows), rows)

        @pl.when(block <= me)
        def _():
            attend_back_block(
                info, block, kv[place, :TILE], kv[place, TILE:], lse, dkv.at[r], heads, grads,
                delta, acc,
            )

        @pl.when(block > me)
        def _():
            dkv[r] = jnp.zeros(dkv.shape[1:], dkv.dtype)

    def several(first, gap, count):
        def body(j, carry):
            block_back(first + j * gap)
            return carry

        lax.fori_loop(0, count, body, 0)

    def add(target, source):
        target[...] = (target[...].astype(jnp.float32) + source[...].astype(jnp.float32)).astype(
            jnp.bfloat16
        )

    weights(0, grad_rows, half_grad, hidden, their_hidden)
    pump(0)
    weights(2, d_mixer, half_mixer, joined, their_joined)
    several(1, 2, 4)
    over_x = [
        remote(dkv.at[2 * k + 1], from_x.at[k], send.at[k], recv.at[k], others["x"])
        for k in range(4)
    ]
    for copy in over_x:
        copy.start()
    scan.step(1)
    weights(1, normed_two, half_two, d_gu, their_gu)
    pump(1)
    several(4, 2, 2)
    over_far = [
        remote(dkv.at[4 + 2 * k], from_far.at[k], send.at[4 + k], recv.at[4 + k], others["far"])
        for k in range(2)
    ]
    for k in range(2):
        over_x[2 + k].wait_recv()
        add(dkv.at[4 + 2 * k], from_x.at[2 + k])
        over_far[k].start()
    scan.step(2)
    pump(2)
    several(0, 2, 2)
    for k in range(2):
        over_x[k].wait_recv()
        add(dkv.at[2 * k], from_x.at[k])
    over_far[1].wait_recv()
    add(dkv.at[2], from_far.at[1])
    over_near = remote(dkv.at[2], from_near, send.at[6], recv.at[6], others["near"])
    over_near.start()
    weights(3, normed, their_normed, d_z, their_z)
    pump(3)
    loads.need(*range(10, 18), *range(4))
    ssm_back_kernel(
        info, x, bc, dt, cum, d_ssm, head_params, dx, d_bc, d_cum, d_dt, g_skip, cols_t, d_rows
    )
    pump(4)
    scan.step(3)
    d_step = d_conv.at[:, pl.ds(xbc, TILE)]
    step_in = raw.at[pl.ds(RIM, rows), pl.ds(xbc, TILE)]
    state_back_kernel(
        info, x, bc, dt, cum, d_ssm, head_params, step_in, state_in, d_state, dx, d_bc, d_cum,
        d_dt, dx, d_bc, d_step, head_sums,
    )
    conv_back_start(info, dx, d_bc, pre, raw, d_pre, g_conv)
    rim = remote(
        d_pre.at[pl.ds(0, RIM)], d_pre.at[pl.ds(rows, RIM)], rim_send.at[0], rim_recv.at[0],
        previous,
    )
    rim.start()
    pump(5)
    over_far[0].wait_recv()
    over_near.wait_recv()
    attend_back_write(acc, dq)
    d_pair[...] = (
        dkv[0].astype(jnp.float32)
        + from_far[0].astype(jnp.float32)
        + from_near[...].astype(jnp.float32)
    )
    rope_back_kernel(dq, d_pair, cosine, sine, d_attn)
    last_swaps = [
        remote(give, take, swap_send.at[8 + k], swap_recv.at[8 + k], others["core"])
        for k, (give, take) in enumerate(((d_attn, their_attn), (d_conv, their_conv)))
    ]
    last_swaps[0].start()
    rim.wait_recv()
    conv_back_end(info, d_pre, conv_w, d_conv.at[:, pl.ds(0, xbc)])
    last_swaps[1].start()
    pump(6)
    last_swaps[0].wait_recv()
    weight_products(left_t, d_attn, their_attn, p_attn)
    last_swaps[1].wait_recv()
    weight_products(left_t, d_conv, their_conv, p_conv)
    for wave in sorted(waves):
        pump(wave)
    swaps += last_swaps
    loads.finish()
    scatter.finish()
    scan.finish()
    rim.wait_send()
    for copy in over_x + over_far + [over_near] + swaps:
        copy.wait_send()


def back(lens, *args):
    (
        head_params, conv_w, cosine, sine, q, kv, grad, out_t, lse, pull, x, bc, dt, cum,
        d_ssm, raw, state_in, pre, normed, normed_two, d_mixer, grad_rows, hidden, joined, d_gu,
        d_z,
    ) = args
    rows, query_width = q.shape
    width = normed.shape[1]
    half = width // 2
    pair = kv.shape[1]
    ssm_width, xbc = x.shape[1], pre.shape[1]
    f32, narrow = jnp.float32, jnp.bfloat16
    dma = pltpu.SemaphoreType.DMA
    widths = [hidden.shape[1], d_gu.shape[1], joined.shape[1], d_z.shape[1]]
    pairs = column_chunks(widths, 1024, 4, 2)
    own = half // 16
    outs = [
        shape_of((rows, xbc + TILE), narrow),
        shape_of((rows, query_width + pair), narrow),
        shape_of((8, xbc), f32),
        shape_of((8, TILE), f32),
        shape_of((8, TILE), f32),
        shape_of((half, xbc + TILE), narrow),
        shape_of((half, query_width + pair), narrow),
    ] + [shape_of((own, w), f32) for w in widths]
    scratch = [pltpu.VMEM(a.shape, a.dtype) for a in args]
    scratch += [pltpu.VMEM((half, w), narrow) for w in widths]
    scratch += scatter_scratch(widths, half)
    scratch += [pltpu.VMEM((rows, half), narrow)] * 3
    scratch += [pltpu.VMEM(a.shape, narrow) for a in (hidden, joined, d_gu, d_z)]
    scratch += [
        pltpu.VMEM((rows, half), narrow),
        pltpu.VMEM((rows, xbc + TILE), narrow),
        pltpu.VMEM((rows, query_width + pair), narrow),
        pltpu.VMEM((half, 2 * rows), narrow),
        pltpu.VMEM((QUERY_HEADS, rows, TILE), narrow),
        pltpu.VMEM((QUERY_HEADS, rows, TILE), narrow),
        pltpu.VMEM((QUERY_HEADS, rows), f32),
        pltpu.VMEM((QUERY_HEADS, HEAD_SIZE, rows), f32),
        pltpu.VMEM((8, rows, pair), narrow),
        pltpu.VMEM((4, rows, pair), narrow),
        pltpu.VMEM((2, rows, pair), narrow),
        pltpu.VMEM((rows, pair), narrow),
        pltpu.VMEM((rows, query_width), f32),
        pltpu.VMEM((rows, pair), f32),
        pltpu.VMEM((rows, TILE), f32),
        pltpu.VMEM((rows, TILE), f32),
        pltpu.VMEM((TILE, rows), f32),
        pltpu.VMEM((TILE, rows), f32),
        pltpu.VMEM((rows + RIM, xbc), f32),
        *scan_scratch(ssm_width),
        dma((7,)),
        dma((7,)),
        dma((10,)),
        dma((10,)),
        dma((2 * len(pairs), 4, 4)),
        dma((2 * len(pairs), 4, 4)),
        dma((1,)),
        dma((1,)),
        dma((len(args),)),
    ]
    return comm_call(
        lambda *refs: back_kernel(pairs, *refs),
        outs,
        [INTO_VMEM] * len(outs),
        (lens, *args),
        [pl.BlockSpec(memory_space=pltpu.SMEM)] + [ANY] * len(args),
        scratch,
        2,
        200_000_000,
        limit=62,
    )


def dot_nt_two(left, right):
    high = left.astype(jnp.bfloat16)
    low = (left - high.astype(jnp.float32)).astype(jnp.bfloat16)
    return dot_nt(high, right) + dot_nt(low, right)


def last_kernel(pairs, *refs):
    (
        p_conv, p_attn, d_conv, d_attn, d_z, gains, g_mlp, g_ssm, g_conv, head_sums, g_skip,
        sum_out, sum_z, *far_in,
    ) = refs[:18]
    (
        input_grad, g_attn_out, g_in_out, g_dt_out, g_out_out,
        norm_total, mlp_total, ssm_total, conv_total, conv_b_total, head_total,
    ) = refs[18:29]
    refs = refs[29:]
    arrived_w, near_in, refs = refs[:8], refs[8:13], refs[13:]
    full_conv, full_mix, x_own, order, d_middle = near_in
    (
        out_conv, out_attn, d_normed, small_own, small_in, small_mid, small_out, in_sems,
        w_send, w_recv, small_send, small_recv,
    ) = refs
    stage = Stage(far_in, near_in, in_sems)
    stage.start(*range(5))
    others = partners()
    greet(list(others.values()))
    rows, width = d_normed.shape
    scatter = Scatter((p_conv, p_attn), (out_conv, out_attn), arrived_w, pairs, w_send, w_recv, others)
    scatter.step(0, 0)
    scatter.step(1, 0)
    scatter.step(2, 0)
    stage.need(0, 1)
    step = 256
    attn = d_attn.shape[1]

    def back_out(j, carry):
        here = pl.ds(pl.multiple_of(j * step, step), step)
        d_normed[:, here] = (
            dot_nt(d_conv[...], full_conv[here])
            + dot_nt(d_attn[...], full_mix[here, :attn])
            + dot_nt(d_z[...], full_mix[here, attn:])
        )
        return carry

    lax.fori_loop(0, width // step, back_out, 0)
    stage.need(2, 3, 4)
    scatter.step(0, 1)
    scatter.step(1, 1)
    wide = x_own[...].astype(jnp.float32)
    r = lax.rsqrt(jnp.mean(wide * wide, axis=-1, keepdims=True) + NORM_EPS)
    grads = d_normed[...]
    g_norm = jnp.sum(grads * wide * r, axis=0, keepdims=True)
    line = lax.broadcasted_iota(jnp.int32, (8, width), 0)
    both = jnp.where(line == 0, g_norm, jnp.where(line == 1, g_mlp[...], 0.0))
    both = dot_nt_two(both, order[...])
    small_own[16:] = jnp.zeros((small_own.shape[0] - 16, TILE), jnp.float32)
    small_own[16:28] = g_ssm[...]
    small_own[28:30] = head_sums[0:2]
    small_own[30:31] = g_skip[0:1]
    conv_tiles = g_conv.shape[1] // TILE
    for k in range(CONV + 1):
        for i in range(conv_tiles):
            place = 32 + 16 * k + i
            small_own[place : place + 1] = g_conv[k : k + 1, i * TILE : (i + 1) * TILE]
    for k in range(width // TILE):
        for which in range(2):
            small_own[8 * which + k : 8 * which + k + 1] = both[
                which : which + 1, k * TILE : (k + 1) * TILE
            ]
    names = ("core", "y", "x", "near", "far")
    small_copies = []

    def small_step(k):
        if k > 0:
            small_copies[k - 1].wait_recv()
            was = small_own if k == 1 else small_mid.at[k - 2]
            now = small_out if k == 5 else small_mid.at[k - 1]
            now[...] = was[...] + small_in[k - 1]
        if k < 5:
            source = small_own if k == 0 else small_mid.at[k - 1]
            copy = remote(
                source, small_in.at[k], small_send.at[k], small_recv.at[k], others[names[k]]
            )
            copy.start()
            small_copies.append(copy)

    scatter.step(2, 1)
    scatter.step(0, 2)
    small_step(0)
    inner = grads * gains[0:1]
    coeff = jnp.mean(inner * wide, axis=-1, keepdims=True)
    d_normed[...] = d_middle[...] + r * (inner - wide * (r * r * coeff))
    scatter.step(1, 2)
    small_step(1)
    scatter.step(0, 3)
    scatter.step(2, 2)

    def plain(j, carry):
        here = pl.ds(pl.multiple_of(j * step, step), step)
        input_grad[:, here] = dot_nt_two(d_normed[...], order[here])
        return carry

    lax.fori_loop(0, width // step, plain, 0)
    small_step(2)
    query = QUERY_HEADS * HEAD_SIZE
    g_in_out[:, : sum_z.shape[1]] = sum_z[...]
    g_out_out[:, :query] = pair_columns(sum_out[:, :query], True)
    g_out_out[:, query:] = sum_out[:, query:]
    scatter.step(1, 3)
    scatter.step(2, 3)
    small_step(3)
    scatter.step(0, 4)
    small_step(4)
    scatter.step(1, 4)
    scatter.step(2, 4)
    small_step(5)
    norm_total[...] = small_out[:8]
    mlp_total[...] = small_out[8:16]
    ssm_total[...] = small_out[16:28]
    head_total[...] = small_out[24:32]
    for k in range(CONV):
        for i in range(conv_tiles):
            place = 32 + 16 * k + i
            conv_total[k : k + 1, i * TILE : (i + 1) * TILE] = small_out[place : place + 1]
    conv_b_total[...] = small_out[32 + 16 * CONV : 32 + 16 * CONV + conv_tiles]
    g_in_out[:, g_in_out.shape[1] - g_conv.shape[1] :] = out_conv[:, : g_conv.shape[1]]
    g_dt_out[...] = out_conv[:, g_conv.shape[1] : g_conv.shape[1] + MH]
    query = QUERY_HEADS * HEAD_SIZE
    g_attn_out[:, :query] = pair_columns(out_attn[:, :query], True)
    g_attn_out[:, query:] = out_attn[:, query:]
    scatter.finish()
    for copy in small_copies:
        copy.wait_send()


def last(near, far):
    p_conv, p_attn, d_z, g_conv, sum_out = near[0], near[1], near[4], near[8], near[11]
    rows, width = far[2].shape
    half = p_conv.shape[0]
    f32, narrow = jnp.float32, jnp.bfloat16
    dma = pltpu.SemaphoreType.DMA
    widths = [p_conv.shape[1], p_attn.shape[1]]
    pairs = column_chunks(widths)
    total = (32 + 16 * (CONV + 1), TILE)
    block = half // 16
    xbc = g_conv.shape[1]
    joined = sum_out.shape[1]
    outs = [
        shape_of((rows, width), f32),
        shape_of((block, widths[1]), f32),
        shape_of((block, d_z.shape[1] + xbc), f32),
        shape_of((block, MH), f32),
        shape_of((block, joined), f32),
        shape_of((8, TILE), f32),
        shape_of((8, TILE), f32),
        shape_of((12, TILE), f32),
        shape_of((CONV, xbc), f32),
        shape_of((xbc // TILE, TILE), f32),
        shape_of((8, TILE), f32),
    ]
    scratch = scatter_scratch(widths, half)
    scratch += [pltpu.VMEM(a.shape, a.dtype) for a in far]
    scratch += [pltpu.VMEM((block, w), f32) for w in widths]
    scratch += [
        pltpu.VMEM((rows, width), f32),
        pltpu.VMEM(total, f32),
        pltpu.VMEM((5, *total), f32),
        pltpu.VMEM((4, *total), f32),
        pltpu.VMEM(total, f32),
        dma((5,)),
        dma((2 * len(pairs), 4, 4)),
        dma((2 * len(pairs), 4, 4)),
        dma((5,)),
        dma((5,)),
    ]
    return comm_call(
        lambda *refs: last_kernel(pairs, *refs),
        outs,
        [INTO_VMEM] * len(outs),
        (*near, *far),
        [INTO_VMEM] * len(near) + [ANY] * len(far),
        scratch,
        4,
        100_000_000,
    )


def settle_kernel(*refs):
    count = len(refs) // 2
    sems = refs[2 * count]
    copies = [
        pltpu.make_async_copy(refs[k], refs[count + k], sems.at[k]) for k in range(count)
    ]
    for copy in copies:
        copy.start()
    for copy in copies:
        copy.wait()


def settle(*arrays):
    count = len(arrays)
    return pl.pallas_call(
        settle_kernel,
        out_shape=[shape_of(a.shape, a.dtype) for a in arrays],
        in_specs=[ANY] * count,
        out_specs=[INTO_VMEM] * count,
        scratch_shapes=[pltpu.SemaphoreType.DMA((count,))],
        compiler_params=pltpu.CompilerParams(vmem_limit_bytes=60 * 1024 * 1024),
    )(*arrays)


def pair_heads(value, back=False):
    rows = value.shape[0]
    group = QUERY_HEADS // KEY_VALUE_HEADS
    width = QUERY_HEADS * HEAD_SIZE
    shape = (group, KEY_VALUE_HEADS) if back else (KEY_VALUE_HEADS, group)
    moved = value[:, :width].reshape(rows, *shape, HEAD_SIZE).transpose(0, 2, 1, 3)
    return jnp.concatenate([moved.reshape(rows, width), value[:, width:]], axis=1)


def plain_layer(
    layer_input,
    seq_lengths,
    w_attn,
    w_ssm_in,
    w_dt,
    w_out,
    w_gate_up,
    w_down,
    norm_gain,
    mlp_gain,
    ssm_gain,
    conv_w,
    conv_b,
    a_log,
    dt_bias,
    d_skip,
    out_grad,
):
    token_rows = layer_input.shape[1]
    query_width = QUERY_HEADS * HEAD_SIZE
    key_value_width = KEY_VALUE_HEADS * HEAD_SIZE
    attn_width = query_width + 2 * key_value_width
    ssm_width = MH * MP
    xbc_width = ssm_width + 2 * NS
    seq_lens = seq_lengths[0]
    first_pos = lax.axis_index("seq") * token_rows
    positions = first_pos + jnp.arange(token_rows, dtype=jnp.int32)
    segment, device_places = segments(seq_lens, positions)
    ends = jnp.cumsum(seq_lens)
    info = jnp.stack([first_pos, ends[0], ends[1], ends[2]]).astype(jnp.int32)
    half = HEAD_SIZE // 2
    freqs = ROPE_BASE ** (-jnp.arange(half, dtype=jnp.float32) / half)
    angles = device_places.astype(jnp.float32)[:, None] * jnp.tile(freqs, TILE // half)[None, :]
    cosine, sine = jnp.cos(angles), jnp.sin(angles)
    head_params = jnp.pad(
        jnp.stack([dt_bias, jnp.exp(a_log), d_skip]), ((0, 5), (0, TILE - MH))
    )
    step_pad = jnp.pad(w_dt, ((0, 0), (0, TILE - MH)))
    shards = (
        jnp.concatenate([w_ssm_in[:, ssm_width:], step_pad], axis=1),
        jnp.concatenate([pair_heads(w_attn), w_ssm_in[:, :ssm_width]], axis=1),
        pair_heads(w_out.T),
        w_gate_up,
        w_down.T,
    )
    ext_pos = first_pos - (CONV - 1) + jnp.arange(token_rows + CONV - 1, dtype=jnp.int32)
    ext_segment = segments(seq_lens, ext_pos)[0]

    def conv_local(ext_rows, conv_weight, conv_bias):
        return conv_mix(ext_rows, ext_segment, conv_weight, conv_bias)

    full = [lax.all_gather(p, ("seq", "batch"), axis=0, tiled=True) for p in shards]
    full_conv, full_mix, full_out, full_gu, full_down = full
    x_rows = layer_input[0].astype(jnp.float32)
    grad_rows = out_grad[0]
    scale_one = rms_scale(x_rows)
    normed = (x_rows * scale_one * norm_gain).astype(jnp.bfloat16)
    conv_proj = jnp.dot(normed, full_conv, preferred_element_type=jnp.float32)
    mix_proj = jnp.dot(normed, full_mix, preferred_element_type=jnp.float32)
    queries, own_pairs = big_call(
        rope_kernel,
        (
            shape_of((token_rows, query_width), jnp.bfloat16),
            shape_of((token_rows, 2 * key_value_width), jnp.bfloat16),
        ),
        mix_proj[:, :attn_width],
        cosine,
        sine,
    )
    gate_z = mix_proj[:, attn_width:]
    raw_xbc = conv_proj[:, :xbc_width]
    step_proj = conv_proj[:, xbc_width:]
    rim_rows = shifted(raw_xbc[token_rows - (CONV - 1) :], "seq", 1)
    extended = jnp.concatenate([rim_rows, raw_xbc], axis=0)
    conv_out, conv_pullback = jax.vjp(conv_local, extended, conv_w, conv_b)
    conv_narrow = conv_out.astype(jnp.bfloat16)
    inputs_x, inputs_bc = conv_narrow[:, :ssm_width], conv_narrow[:, ssm_width:]
    ssm_own, state_own, steps_dt, running_decay = ssm_forward(
        info, inputs_x, inputs_bc, step_proj, head_params
    )
    all_pairs = lax.all_gather(own_pairs, "seq", axis=0, tiled=True)
    state_in = scan_states(state_own, True)
    attended, attended_t, log_total = attn_forward(info, queries, all_pairs)

    ssm_flat, ssm_normed, scale_gated = ssm_finish(
        info, ssm_own, inputs_bc, running_decay, state_in, gate_z, ssm_gain.reshape(-1, TILE)
    )
    joined = jnp.concatenate([attended, ssm_normed], axis=1)

    def into_width(left, weight):
        return jnp.einsum("tc,dc->td", left, weight, preferred_element_type=jnp.float32)

    def out_of_width(left, weight):
        return jnp.dot(left, weight, preferred_element_type=jnp.float32)

    middle = x_rows + into_width(joined, full_out)
    scale_two = rms_scale(middle)
    normed_two = (middle * scale_two * mlp_gain).astype(jnp.bfloat16)
    gate_up = out_of_width(normed_two, full_gu)
    gate_part, up_part = gate_up[:, :FF], gate_up[:, FF:]
    sig_gate = jax.nn.sigmoid(gate_part)
    hidden = (gate_part * sig_gate * up_part).astype(jnp.bfloat16)
    layer_out = middle + into_width(hidden, full_down)
    d_hidden = out_of_width(grad_rows, full_down)
    d_gate = d_hidden * up_part * (sig_gate * (1.0 + gate_part * (1.0 - sig_gate)))
    d_up = d_hidden * gate_part * sig_gate
    d_gate_up = jnp.concatenate([d_gate, d_up], axis=1).astype(jnp.bfloat16)
    d_normed_two = into_width(d_gate_up, full_gu)
    d_middle_norm, g_mlp_gain = norm_back(middle, scale_two, mlp_gain, d_normed_two)
    d_middle = grad_rows.astype(jnp.float32) + d_middle_norm
    d_mixer = d_middle.astype(jnp.bfloat16)
    d_joined = out_of_width(d_mixer, full_out)
    attended_gradient = d_joined[:, :query_width].astype(jnp.bfloat16)
    d_ssm_out, d_gate_z, pull, g_ssm_gain = gate_back(
        info,
        d_joined[:, query_width:],
        ssm_flat,
        gate_z,
        scale_gated,
        ssm_gain.reshape(-1, TILE),
        running_decay,
        inputs_bc,
    )
    pull = jnp.concatenate([pull, state_own[NS:]], axis=0)
    d_state = scan_states(pull, False)
    d_queries, d_pairs = attn_backward(
        info, queries, all_pairs, attended_gradient, attended_t, log_total
    )
    own_d_pairs = lax.psum_scatter(
        d_pairs.astype(jnp.float32), "seq", scatter_dimension=0, tiled=True
    )
    dx_part, d_bc_part, d_cum_part, d_dt_part, g_skip_rows = ssm_back(
        info, inputs_x, inputs_bc, steps_dt, running_decay, d_ssm_out, head_params
    )
    g_inputs_x, g_inputs_bc, d_step_pad, head_sums = state_back(
        info,
        inputs_x,
        inputs_bc,
        steps_dt,
        running_decay,
        d_ssm_out,
        head_params,
        step_proj,
        state_in,
        d_state,
        dx_part,
        d_bc_part,
        d_cum_part,
        d_dt_part,
    )
    g_extended, g_conv_w, g_conv_b = conv_pullback(
        jnp.concatenate([g_inputs_x, g_inputs_bc], axis=1)
    )
    back_rim = shifted(g_extended[: CONV - 1], "seq", -1)
    d_raw = g_extended[CONV - 1 :] + jnp.concatenate(
        [jnp.zeros((token_rows - (CONV - 1), xbc_width), jnp.float32), back_rim], axis=0
    )
    d_conv_proj = jnp.concatenate([d_raw.astype(jnp.bfloat16), d_step_pad], axis=1)
    (d_attn_proj,) = big_call(
        rope_back_kernel,
        (shape_of((token_rows, attn_width), jnp.bfloat16),),
        d_queries,
        own_d_pairs,
        cosine,
        sine,
    )
    d_mix_proj = jnp.concatenate([d_attn_proj, d_gate_z], axis=1)
    d_normed = into_width(d_conv_proj, full_conv) + into_width(d_mix_proj, full_mix)
    d_input_norm, g_norm_gain = norm_back(x_rows, scale_one, norm_gain, d_normed)
    input_grad = d_middle + d_input_norm
    axes = ("seq", "batch")

    def summed(left, right):
        grad = jnp.einsum("td,tc->dc", left, right, preferred_element_type=jnp.float32)
        return lax.psum_scatter(grad, axes, scatter_dimension=0, tiled=True)

    sum_down, sum_gu = summed(grad_rows, hidden), summed(normed_two, d_gate_up)
    sum_out, sum_conv = summed(d_mixer, joined), summed(normed, d_conv_proj)
    sum_mix = summed(normed, d_mix_proj)
    sum_attn, sum_z = sum_mix[:, :attn_width], sum_mix[:, attn_width:]
    small = (
        g_norm_gain,
        g_mlp_gain,
        g_ssm_gain.reshape(-1),
        g_conv_w,
        g_conv_b,
        head_sums[0, :MH],
        head_sums[1, :MH],
        g_skip_rows[0, :MH],
    )
    small_sums = unpack_small(lax.psum(pack_small(small), axes), small)
    grad_attn = pair_heads(sum_attn, True)
    grad_ssm_in = jnp.concatenate([sum_z, sum_conv[:, :xbc_width]], axis=1)
    grad_dt = sum_conv[:, xbc_width : xbc_width + MH]
    grad_out = pair_heads(sum_out, True).T
    grad_gate_up = sum_gu
    grad_down = sum_down.T
    return (
        layer_out.astype(jnp.bfloat16)[None],
        input_grad[None],
        grad_attn,
        grad_ssm_in,
        grad_dt,
        grad_out,
        grad_gate_up,
        grad_down,
        *small_sums,
    )


def on_device(
    layer_input,
    seq_lengths,
    w_attn,
    w_ssm_in,
    w_dt,
    w_out,
    w_gate_up,
    w_down,
    norm_gain,
    mlp_gain,
    ssm_gain,
    conv_w,
    conv_b,
    a_log,
    dt_bias,
    d_skip,
    out_grad,
):
    if not is_fast(layer_input.shape[2]):
        return plain_layer(
            layer_input, seq_lengths, w_attn, w_ssm_in, w_dt, w_out, w_gate_up, w_down, norm_gain,
            mlp_gain, ssm_gain, conv_w, conv_b, a_log, dt_bias, d_skip, out_grad,
        )
    half = HEAD_SIZE // 2
    freqs = np.float32(ROPE_BASE) ** (-np.arange(half, dtype=np.float32) / np.float32(half))
    freqs = jnp.asarray(np.tile(freqs.astype(np.float32), TILE // half)[None])
    full, made = front(
        seq_lengths,
        dt_bias,
        a_log,
        d_skip,
        layer_input[0],
        out_grad[0],
        norm_gain.reshape(-1, TILE),
        mlp_gain.reshape(-1, TILE),
        freqs,
        conv_w,
        conv_b.reshape(-1, TILE),
        (w_attn, w_ssm_in, w_dt.T, w_out.T, w_gate_up, w_down.T),
    )
    full_conv, full_mix, full_out, full_gu, full_down = full
    (
        x_own, g_own, gains, normed, queries, all_pairs, gate_z, raw_rows, pre_conv, inputs_x,
        inputs_bc, ssm_own, state_own, steps_dt, running_decay, attended, attended_t, log_total,
        state_in, order, cosine, sine, head_params,
    ) = made
    (
        layer_out, joined, hidden, d_gate_up, normed_two, d_mixer, d_middle, d_ssm_out, d_gate_z,
        pull, attended_gradient, g_ssm_gain, g_mlp_gain,
    ) = middle_part(
        seq_lengths, ssm_own, inputs_bc, running_decay, state_in, state_own, gate_z,
        ssm_gain.reshape(-1, TILE), attended, x_own, g_own, gains, order, full_out, full_gu,
        full_down,
    )
    (
        d_conv_proj, d_attn_proj, g_conv, head_sums, g_skip_rows, part_conv, part_attn, sum_down,
        sum_gu, sum_out, sum_z,
    ) = back(
        seq_lengths, head_params, conv_w, cosine, sine, queries, all_pairs, attended_gradient,
        attended_t, log_total, pull, inputs_x, inputs_bc, steps_dt, running_decay, d_ssm_out,
        raw_rows, state_in, pre_conv, normed, normed_two, d_mixer, g_own, hidden, joined,
        d_gate_up, d_gate_z,
    )
    (
        input_grad, grad_attn, grad_ssm_in, grad_dt, grad_out, g_norm, g_mlp, g_ssm, g_conv_w,
        g_conv_b, heads,
    ) = last(
        (
            part_conv, part_attn, d_conv_proj, d_attn_proj, d_gate_z, gains, g_mlp_gain,
            g_ssm_gain, g_conv, head_sums, g_skip_rows, sum_out, sum_z,
        ),
        (full_conv, full_mix, x_own, order, d_middle),
    )
    (
        input_grad, grad_attn, grad_ssm_in, grad_dt, grad_out, sum_gu, sum_down, g_norm, g_mlp,
        g_ssm, g_conv_w, g_conv_b, heads,
    ) = settle(
        input_grad, grad_attn, grad_ssm_in, grad_dt, grad_out, sum_gu, sum_down, g_norm, g_mlp,
        g_ssm, g_conv_w, g_conv_b, heads,
    )
    return (
        layer_out[None],
        input_grad[None],
        grad_attn,
        grad_ssm_in,
        grad_dt,
        grad_out.T,
        sum_gu,
        sum_down.T,
        g_norm.reshape(-1),
        g_mlp.reshape(-1),
        g_ssm.reshape(-1),
        g_conv_w,
        g_conv_b.reshape(-1),
        heads[4, :MH],
        heads[5, :MH],
        heads[6, :MH],
    )


def solution(mesh):
    return jax.shard_map(
        on_device,
        mesh=mesh,
        in_specs=(
            P("batch", "seq", None),
            P("batch", None),
            P(("seq", "batch"), None),
            P(("seq", "batch"), None),
            P(("seq", "batch"), None),
            P(None, ("seq", "batch")),
            P(("seq", "batch"), None),
            P(None, ("seq", "batch")),
            P(),
            P(),
            P(),
            P(),
            P(),
            P(),
            P(),
            P(),
            P("batch", "seq", None),
        ),
        out_specs=(
            P("batch", "seq", None),
            P("batch", "seq", None),
            P(("seq", "batch"), None),
            P(("seq", "batch"), None),
            P(("seq", "batch"), None),
            P(None, ("seq", "batch")),
            P(("seq", "batch"), None),
            P(None, ("seq", "batch")),
            P(),
            P(),
            P(),
            P(),
            P(),
            P(),
            P(),
            P(),
        ),
        check_vma=False,
    )
```

```python
import jax
import jax.numpy as jnp
import numpy as np
from jax import lax
from jax.experimental import pallas as pl
from jax.experimental.pallas import tpu as pltpu
from jax.sharding import PartitionSpec as P

QUERY_HEADS = 8
KEY_VALUE_HEADS = 2
HEAD_SIZE = 64
MH = 24
MP = 64
NS = 128
FF = 2048
CONV = 4
SPAN = 128


HIGHEST = lax.Precision.HIGHEST
NEGATIVE_FILL = -1e30
ROPE_BASE = 10000.0
NORM_EPS = 1e-06


def shifted(block, axis, distance):
    devices = range(lax.axis_size(axis))
    route = [(i - distance, i) for i in devices if i - distance in devices]
    return lax.ppermute(block, axis, route)


def is_fast(width):
    return lax.axis_size("seq") == 8 and lax.axis_size("batch") == 4 and width % (32 * 32) == 0


def pack_small(arrays):
    flat = jnp.concatenate([a.reshape(-1) for a in arrays])
    return jnp.pad(flat, (0, -flat.shape[0] % 1024)).reshape(-1, 128)


def unpack_small(flat, arrays):
    flat = flat.reshape(-1)
    out, start = [], 0
    for a in arrays:
        out.append(flat[start : start + a.size].reshape(a.shape))
        start += a.size
    return out


def rms_scale(value_rows):
    return lax.rsqrt(jnp.mean(value_rows * value_rows, axis=-1, keepdims=True) + NORM_EPS)


def norm_back(value_rows, scales, gains, grads):
    gain_grad = jnp.sum(grads * value_rows * scales, axis=0)
    inner = grads * gains
    coeff = jnp.mean(inner * value_rows, axis=-1, keepdims=True)
    return (scales * (inner - value_rows * scales * scales * coeff), gain_grad)


def segments(lengths, positions):
    ends = jnp.cumsum(lengths)
    passed = ends[None, :] <= positions[:, None]
    segment = jnp.sum(passed.astype(jnp.int32), axis=1)
    device_places = positions - jnp.sum(jnp.where(passed, lengths[None, :], 0), axis=1)
    return (segment, device_places)


def conv_mix(extended, ext_segment, conv_weight, conv_bias):
    row_count = extended.shape[0] - (CONV - 1)
    summed = conv_bias[None, :]
    for lagged in range(CONV):
        same_seq = (ext_segment[lagged : lagged + row_count] == ext_segment[CONV - 1 :]).astype(
            extended.dtype
        )
        summed = (
            summed
            + conv_weight[lagged][None, :]
            * extended[lagged : lagged + row_count]
            * same_seq[:, None]
        )
    return jax.nn.silu(summed)


TILE = 128
PAIRS = QUERY_HEADS // 2
CHUNK = 256


def dot(left, right):
    return jnp.dot(left, right, preferred_element_type=jnp.float32)


def dot_nt(left, right):
    return lax.dot_general(
        left, right, (((1,), (1,)), ((), ())), preferred_element_type=jnp.float32
    )


def dot_tn(left, right):
    return lax.dot_general(
        left, right, (((0,), (0,)), ((), ())), preferred_element_type=jnp.float32
    )


def exact(left, right):
    return jnp.dot(left, right, precision=HIGHEST, preferred_element_type=jnp.float32)


def two_part(left, right):
    high = left.astype(jnp.bfloat16)
    low = (left - high.astype(jnp.float32)).astype(jnp.bfloat16)
    return dot(high, right) + dot(low, right)


def seg_start(where_at, info):
    start = jnp.zeros_like(where_at)
    for k in range(1, 4):
        start = jnp.where(where_at >= info[k], jnp.maximum(start, info[k]), start)
    return start


def big_call(kernel, outs, *args, scratch=(), flops=0, smem=0, limit=48):
    specs = [pl.BlockSpec(memory_space=pltpu.SMEM)] * smem
    specs += [pl.BlockSpec(memory_space=pltpu.VMEM)] * (len(args) - smem)
    moved = sum(a.size * a.dtype.itemsize for a in args)
    moved += sum(o.size * o.dtype.itemsize for o in outs)
    return pl.pallas_call(
        kernel,
        out_shape=list(outs),
        in_specs=specs,
        out_specs=[pl.BlockSpec(memory_space=pltpu.VMEM)] * len(outs),
        scratch_shapes=list(scratch),
        cost_estimate=pl.CostEstimate(flops=flops, bytes_accessed=moved, transcendentals=0),
        compiler_params=pltpu.CompilerParams(vmem_limit_bytes=limit * 1024 * 1024),
    )(*args)


def shape_of(shape, dtype):
    return jax.ShapeDtypeStruct(shape, dtype)


def turn(value, cosine, sine):
    lane = lax.broadcasted_iota(jnp.int32, value.shape, 1) % HEAD_SIZE
    mixed = jnp.where(
        lane < HEAD_SIZE // 2,
        -pltpu.roll(value, TILE - HEAD_SIZE // 2, 1),
        pltpu.roll(value, HEAD_SIZE // 2, 1),
    )
    return value * cosine + mixed * sine


def rope_kernel(proj, cosine, sine, q_out, kv_out):
    cos, sin = cosine[...], sine[...]
    for i in range(PAIRS):
        cols = pl.ds(i * TILE, TILE)
        turned = turn(proj[:, cols], cos, sin).astype(jnp.bfloat16)
        q_out[:, cols] = (turned.astype(jnp.float32) * HEAD_SIZE**-0.5).astype(jnp.bfloat16)
    base = PAIRS * TILE
    kv_out[:, :TILE] = turn(proj[:, base : base + TILE], cos, sin).astype(jnp.bfloat16)
    kv_out[:, TILE:] = proj[:, base + TILE : base + 2 * TILE].astype(jnp.bfloat16)


def halves_of(value):
    lane = lax.broadcasted_iota(jnp.int32, value.shape, 1)
    wide = value.astype(jnp.float32)
    first = jnp.where(lane < HEAD_SIZE, wide, 0.0).astype(value.dtype)
    return first, jnp.where(lane < HEAD_SIZE, 0.0, wide).astype(value.dtype)


def block_range(info):
    first = info[0]
    low = seg_start(first, info) // CHUNK
    return low, first // CHUNK - low + 1


def attn_mask(info, block):
    rows = lax.broadcasted_iota(jnp.int32, (CHUNK, CHUNK), 0) + block * CHUNK
    at = lax.broadcasted_iota(jnp.int32, (1, CHUNK), 1) + info[0]
    return (rows <= at) & (rows >= seg_start(at, info))


def attend_start(q, heads, acc, top, total):
    for i in range(PAIRS):
        heads[2 * i], heads[2 * i + 1] = halves_of(q[:, i * TILE : (i + 1) * TILE])
    acc[...] = jnp.zeros_like(acc)
    total[...] = jnp.zeros_like(total)
    top[...] = jnp.full(top.shape, NEGATIVE_FILL, jnp.float32)


def attend_block(info, block, keys, values_t, heads, acc, top, total):
    allowed = attn_mask(info, block)
    for h in range(QUERY_HEADS):
        scores = jnp.where(allowed, dot_nt(keys, heads[h]), NEGATIVE_FILL)
        old = top[h : h + 1]
        new = jnp.maximum(old, jnp.max(scores, axis=0, keepdims=True))
        probs = jnp.where(allowed, jnp.exp(scores - new), 0.0)
        shrink = jnp.exp(old - new)
        top[h : h + 1] = new
        total[h : h + 1] = total[h : h + 1] * shrink + jnp.sum(probs, axis=0, keepdims=True)
        side = (h % 2) * HEAD_SIZE
        acc[h] = acc[h] * shrink + dot(
            values_t[side : side + HEAD_SIZE], probs.astype(jnp.bfloat16)
        )


def attend_write(acc, total, out, out_t):
    for i in range(PAIRS):
        pair = jnp.concatenate(
            [acc[2 * i] / total[2 * i : 2 * i + 1], acc[2 * i + 1] / total[2 * i + 1 : 2 * i + 2]],
            axis=0,
        )
        out_t[i * TILE : (i + 1) * TILE] = pair
        out[:, i * TILE : (i + 1) * TILE] = pair.T.astype(jnp.bfloat16)


def attn_forward_kernel(info, q, kv, out, out_t, lse, heads, acc, top, total):
    attend_start(q, heads, acc, top, total)
    low, count = block_range(info)

    def step(j, carry):
        block = low + j
        place = pl.ds(pl.multiple_of(block * CHUNK, CHUNK), CHUNK)
        keys = kv[place, :TILE]
        values_t = kv[place, TILE:].astype(jnp.float32).T.astype(jnp.bfloat16)
        attend_block(info, block, keys, values_t, heads, acc, top, total)
        return carry

    lax.fori_loop(0, count, step, 0)
    lse[...] = top[...] + jnp.log(total[...])
    attend_write(acc, total, out, out_t)


def attn_forward(info, q, kv):
    rows = q.shape[0]
    f32 = jnp.float32
    return big_call(
        attn_forward_kernel,
        (
            shape_of(q.shape, jnp.bfloat16),
            shape_of(q.shape[::-1], f32),
            shape_of((QUERY_HEADS, rows), f32),
        ),
        info,
        q,
        kv,
        smem=1,
        scratch=(
            pltpu.VMEM((QUERY_HEADS, rows, TILE), jnp.bfloat16),
            pltpu.VMEM((QUERY_HEADS, HEAD_SIZE, rows), f32),
            pltpu.VMEM((QUERY_HEADS, rows), f32),
            pltpu.VMEM((QUERY_HEADS, rows), f32),
        ),
        flops=4 * rows * kv.shape[0] * q.shape[1],
    )


def attend_back_start(q, grad, out_t, heads, grads, delta, acc):
    for i in range(PAIRS):
        cols = slice(i * TILE, (i + 1) * TILE)
        heads[2 * i], heads[2 * i + 1] = halves_of(q[:, cols])
        grads[2 * i], grads[2 * i + 1] = halves_of(grad[:, cols])
        both = grad[:, cols].astype(jnp.float32).T * out_t[cols]
        delta[2 * i : 2 * i + 1] = jnp.sum(both[:HEAD_SIZE], axis=0, keepdims=True)
        delta[2 * i + 1 : 2 * i + 2] = jnp.sum(both[HEAD_SIZE:], axis=0, keepdims=True)
    acc[...] = jnp.zeros_like(acc)


def attend_back_block(info, block, keys, values, lse, target, heads, grads, delta, acc):
    keys_t = keys.astype(jnp.float32).T.astype(jnp.bfloat16)
    allowed = attn_mask(info, block)
    d_keys = jnp.zeros((CHUNK, TILE), jnp.float32)
    d_values = jnp.zeros((CHUNK, TILE), jnp.float32)
    for h in range(QUERY_HEADS):
        scores = dot_nt(keys, heads[h])
        probs = jnp.where(allowed, jnp.exp(scores - lse[h : h + 1]), 0.0)
        d_probs = dot_nt(values, grads[h])
        d_scores = (probs * (d_probs - delta[h : h + 1])).astype(jnp.bfloat16)
        d_values = d_values + dot(probs.astype(jnp.bfloat16), grads[h])
        d_keys = d_keys + dot(d_scores, heads[h])
        side = (h % 2) * HEAD_SIZE
        acc[h] = acc[h] + dot(keys_t[side : side + HEAD_SIZE], d_scores)
    target[:, :TILE] = d_keys.astype(jnp.bfloat16)
    target[:, TILE:] = d_values.astype(jnp.bfloat16)


def attend_back_write(acc, dq):
    for i in range(PAIRS):
        pair = jnp.concatenate([acc[2 * i], acc[2 * i + 1]], axis=0)
        dq[:, i * TILE : (i + 1) * TILE] = pair.T * HEAD_SIZE**-0.5


def attn_backward_kernel(info, q, kv, grad, out_t, lse, dq, dkv, heads, grads, delta, acc):
    attend_back_start(q, grad, out_t, heads, grads, delta, acc)
    dkv[...] = jnp.zeros_like(dkv)
    low, count = block_range(info)

    def step(j, carry):
        block = low + j
        place = pl.ds(pl.multiple_of(block * CHUNK, CHUNK), CHUNK)
        attend_back_block(
            info, block, kv[place, :TILE], kv[place, TILE:], lse, dkv.at[place], heads, grads,
            delta, acc,
        )
        return carry

    lax.fori_loop(0, count, step, 0)
    attend_back_write(acc, dq)


def attn_backward(info, q, kv, grad, out_t, lse):
    rows = q.shape[0]
    f32 = jnp.float32
    return big_call(
        attn_backward_kernel,
        (shape_of(q.shape, f32), shape_of(kv.shape, jnp.bfloat16)),
        info,
        q,
        kv,
        grad,
        out_t,
        lse,
        smem=1,
        scratch=(
            pltpu.VMEM((QUERY_HEADS, rows, TILE), jnp.bfloat16),
            pltpu.VMEM((QUERY_HEADS, rows, TILE), jnp.bfloat16),
            pltpu.VMEM((QUERY_HEADS, rows), f32),
            pltpu.VMEM((QUERY_HEADS, HEAD_SIZE, rows), f32),
        ),
        flops=10 * rows * kv.shape[0] * q.shape[1],
    )


def rope_back_kernel(dq, dkv, cosine, sine, out):
    cos, sin = cosine[...], -sine[...]
    for i in range(PAIRS):
        cols = slice(i * TILE, (i + 1) * TILE)
        out[:, cols] = turn(dq[:, cols], cos, sin).astype(jnp.bfloat16)
    base = PAIRS * TILE
    out[:, base : base + TILE] = turn(dkv[:, :TILE], cos, sin).astype(jnp.bfloat16)
    out[:, base + TILE :] = dkv[:, TILE:].astype(jnp.bfloat16)


STATE_ROWS = NS + 16


def lane_pick(value, first):
    rows = value.shape[0]
    lane = lax.broadcasted_iota(jnp.int32, (rows, TILE), 1)
    return jnp.where(lane < MP, value[:, first : first + 1], value[:, first + 1 : first + 2])


def spread_heads(width):
    head = lax.broadcasted_iota(jnp.int32, (TILE, width), 0)
    col = lax.broadcasted_iota(jnp.int32, (TILE, width), 1)
    return jnp.where(head == col // MP, 1.0, 0.0).astype(jnp.bfloat16)


def gather_heads(width):
    head = lax.broadcasted_iota(jnp.int32, (width, TILE), 1)
    col = lax.broadcasted_iota(jnp.int32, (width, TILE), 0)
    return jnp.where(head == col // MP, 1.0, 0.0).astype(jnp.bfloat16)


def head_lanes(rows):
    return lax.broadcasted_iota(jnp.int32, (rows, TILE), 1) < MH


def chunk_places(info, rows):
    at = lax.broadcasted_iota(jnp.int32, (rows, 1), 0) + info[0]
    return seg_start(at, info) - info[0]


def ssm_states(info, x, bc, step_in, head_params, state, dt_out, cum_out, dt_t, cum_t):
    rows = x.shape[0]
    bias, rate = head_params[0:1], head_params[1:2]
    raw = step_in[...] + bias
    dt = jnp.maximum(raw, 0.0) + jnp.log1p(jnp.exp(-jnp.abs(raw)))
    dt = jnp.where(head_lanes(rows), dt, 0.0)
    row = lax.broadcasted_iota(jnp.int32, (rows, rows), 0)
    col = lax.broadcasted_iota(jnp.int32, (rows, rows), 1)
    lower = jnp.where(row >= col, 1.0, 0.0)
    cum = exact(lower, -dt * rate)
    dt_out[...] = dt
    cum_out[...] = cum
    dt_t[...] = dt.T
    cum_t[...] = cum.T
    last_start = seg_start(info[0] + rows - 1, info) - info[0]
    place = lax.broadcasted_iota(jnp.int32, (rows, 1), 0)
    end = cum[rows - 1 : rows]
    leave = jnp.where(place >= last_start, jnp.exp(jnp.minimum(end - cum, 0.0)) * dt, 0.0)
    b_t = bc[:, :NS].astype(jnp.float32).T.astype(jnp.bfloat16)
    through = jnp.where(last_start < 0, jnp.exp(end), 0.0)
    high = through.astype(jnp.bfloat16).astype(jnp.float32)
    line = lax.broadcasted_iota(jnp.int32, (16, TILE), 0)
    both = jnp.where(line == 0, high, jnp.where(line == 1, through - high, 0.0))
    spread = spread_heads(x.shape[1])
    state[NS:] = dot(both.astype(jnp.bfloat16), spread).astype(jnp.bfloat16)
    for i in range(MH // 2):
        cols = slice(i * TILE, (i + 1) * TILE)
        weighed = x[:, cols].astype(jnp.float32) * lane_pick(leave, 2 * i)
        state[:NS, cols] = dot(b_t, weighed.astype(jnp.bfloat16)).astype(jnp.bfloat16)


def ssm_local(info, x, bc, head_params, y, cum, dt_t, cum_t):
    rows = x.shape[0]
    row = lax.broadcasted_iota(jnp.int32, (rows, rows), 0)
    col = lax.broadcasted_iota(jnp.int32, (rows, rows), 1)
    starts = chunk_places(info, rows)
    products = dot_nt(bc[:, NS:], bc[:, :NS])
    skips = jnp.broadcast_to(head_params[2:3], (8, TILE))
    skip_row = two_part(skips, spread_heads(x.shape[1]))[:1]
    lane = lax.broadcasted_iota(jnp.int32, (SPAN, TILE), 1)
    for i in range(MH // 2):
        cols = slice(i * TILE, (i + 1) * TILE)
        tile = x[:, cols]
        for part in range(rows // SPAN):
            here = slice(part * SPAN, (part + 1) * SPAN)
            upto = (part + 1) * SPAN
            allowed = (row[here, :upto] >= col[here, :upto]) & (col[here, :upto] >= starts[here])
            sides = []
            for h in (2 * i, 2 * i + 1):
                spread_log = cum[here, h : h + 1] - cum_t[h : h + 1, :upto]
                decay = jnp.exp(jnp.where(allowed, spread_log, NEGATIVE_FILL))
                mixing = products[here, :upto] * decay * dt_t[h : h + 1, :upto]
                sides.append(dot(mixing.astype(jnp.bfloat16), tile[:upto]))
            own = skip_row[:, cols] * tile[here].astype(jnp.float32)
            y[here, cols] = jnp.where(lane < MP, sides[0], sides[1]) + own


def ssm_forward_kernel(info, x, bc, step_in, head_params, y, state, dt_out, cum_out, dt_t, cum_t):
    ssm_states(info, x, bc, step_in, head_params, state, dt_out, cum_out, dt_t, cum_t)
    ssm_local(info, x, bc, head_params, y, cum_out, dt_t, cum_t)


def ssm_forward(info, x, bc, step_in, head_params):
    rows, width = x.shape
    f32 = jnp.float32
    return big_call(
        ssm_forward_kernel,
        (
            shape_of((rows, width), f32),
            shape_of((STATE_ROWS, width), jnp.bfloat16),
            shape_of((rows, TILE), f32),
            shape_of((rows, TILE), f32),
        ),
        info,
        x,
        bc,
        step_in,
        head_params,
        smem=1,
        scratch=(pltpu.VMEM((TILE, rows), f32), pltpu.VMEM((TILE, rows), f32)),
        flops=4 * rows * rows * width,
    )


def entering_of(info, cum):
    rows = cum.shape[0]
    return jnp.where(chunk_places(info, rows) < 0, jnp.exp(jnp.minimum(cum, 0.0)), 0.0)


def ssm_finish_kernel(info, y, bc, cum, state_in, z, gain, ssm_out, normed, scale):
    rows = y.shape[0]
    enter = entering_of(info, cum[...])
    narrow_c = bc[:, NS:]
    squares = jnp.zeros((rows, TILE), jnp.float32)
    tiles = MH // 2
    for i in range(tiles):
        cols = slice(i * TILE, (i + 1) * TILE)
        out = y[:, cols] + lane_pick(enter, 2 * i) * dot(narrow_c, state_in[:, cols])
        ssm_out[:, cols] = out
        gate = z[:, cols]
        gated = out * (gate * jax.nn.sigmoid(gate))
        squares = squares + gated * gated
    mean = jnp.sum(squares, axis=1, keepdims=True) * (1.0 / (tiles * TILE))
    r = lax.rsqrt(mean + NORM_EPS)
    scale[...] = jnp.broadcast_to(r, scale.shape)
    for i in range(tiles):
        cols = slice(i * TILE, (i + 1) * TILE)
        gate = z[:, cols]
        gated = ssm_out[:, cols] * (gate * jax.nn.sigmoid(gate))
        normed[:, cols] = (gated * r * gain[i : i + 1]).astype(jnp.bfloat16)


def ssm_finish(info, y, bc, cum, state_in, z, gain):
    rows, width = y.shape
    return big_call(
        ssm_finish_kernel,
        (
            shape_of((rows, width), jnp.float32),
            shape_of((rows, width), jnp.bfloat16),
            shape_of((rows, TILE), jnp.float32),
        ),
        info,
        y,
        bc,
        cum,
        state_in,
        z,
        gain,
        smem=1,
        flops=2 * rows * NS * width,
    )


def gate_back_kernel(info, dy, ssm_out, z, scale, gain, cum, bc, d_out, d_z, pull, g_gain):
    rows = dy.shape[0]
    tiles = MH // 2
    r = scale[:, :1]
    enter = entering_of(info, cum[...])
    c_t = bc[:, NS:].astype(jnp.float32).T.astype(jnp.bfloat16)
    inner = jnp.zeros((rows, TILE), jnp.float32)
    for i in range(tiles):
        cols = slice(i * TILE, (i + 1) * TILE)
        gate = z[:, cols]
        gated = ssm_out[:, cols] * (gate * jax.nn.sigmoid(gate))
        product = dy[:, cols] * gated
        g_gain[i : i + 1] = jnp.sum(product * r, axis=0, keepdims=True)
        inner = inner + product * gain[i : i + 1]
    coeff = jnp.sum(inner, axis=1, keepdims=True) * (1.0 / (tiles * TILE))
    for i in range(tiles):
        cols = slice(i * TILE, (i + 1) * TILE)
        gate = z[:, cols]
        sig = jax.nn.sigmoid(gate)
        silu = gate * sig
        out = ssm_out[:, cols]
        d_gated = r * (dy[:, cols] * gain[i : i + 1] - out * silu * (r * r * coeff))
        d_ssm = d_gated * silu
        d_out[:, cols] = d_ssm
        d_z[:, cols] = (d_gated * out * (sig * (1.0 + gate * (1.0 - sig)))).astype(jnp.bfloat16)
        pull[:, cols] = dot(c_t, (d_ssm * lane_pick(enter, 2 * i)).astype(jnp.bfloat16)).astype(
            jnp.bfloat16
        )


def gate_back(info, dy, ssm_out, z, scale, gain, cum, bc):
    rows, width = dy.shape
    return big_call(
        gate_back_kernel,
        (
            shape_of((rows, width), jnp.float32),
            shape_of((rows, width), jnp.bfloat16),
            shape_of((NS, width), jnp.bfloat16),
            shape_of(gain.shape, jnp.float32),
        ),
        info,
        dy,
        ssm_out,
        z,
        scale,
        gain,
        cum,
        bc,
        smem=1,
        flops=2 * rows * NS * width,
    )


def ssm_back_kernel(info, x, bc, dt, cum, grad, head_params, dx, d_bc, d_cum, d_dt, g_skip, cols_t, d_rows, between=None):
    rows, width = x.shape
    skip = head_params[2:3]
    cols_t[...] = cum[...].T
    row = lax.broadcasted_iota(jnp.int32, (rows, rows), 0)
    col = lax.broadcasted_iota(jnp.int32, (rows, rows), 1)
    at = lax.broadcasted_iota(jnp.int32, (1, rows), 1) + info[0]
    starts = seg_start(at, info) - info[0]
    narrow_b, narrow_c = bc[:, :NS], bc[:, NS:]
    products = dot_nt(narrow_b, narrow_c)
    skip_row = two_part(jnp.broadcast_to(skip, (8, TILE)), spread_heads(width))[:1]
    lane = lax.broadcasted_iota(jnp.int32, (SPAN, TILE), 1)
    parts = rows // SPAN
    d_products = [jnp.zeros((SPAN, rows - p * SPAN), jnp.float32) for p in range(parts)]
    d_rows[...] = jnp.zeros_like(d_rows)
    step_sums = [jnp.zeros((SPAN, TILE), jnp.float32) for p in range(parts)]
    skip_sums = []
    for i in range(MH // 2):
        cols = slice(i * TILE, (i + 1) * TILE)
        tile = x[:, cols]
        wide = grad[:, cols]
        narrow = wide.astype(jnp.bfloat16)
        skip_sums.append(jnp.sum(wide * tile.astype(jnp.float32), axis=0, keepdims=True))
        tile_sides = halves_of(tile)
        for part in range(parts):
            here = slice(part * SPAN, (part + 1) * SPAN)
            since = part * SPAN
            allowed = (row[here, since:] <= col[here, since:]) & (
                row[here, since:] >= starts[:, since:]
            )
            sides = []
            for side in range(2):
                h = 2 * i + side
                spread_log = cols_t[h : h + 1, since:] - cum[here, h : h + 1]
                decay = jnp.exp(jnp.where(allowed, spread_log, NEGATIVE_FILL))
                decay_dt = decay * dt[here, h : h + 1]
                mixing = products[here, since:] * decay_dt
                sides.append(dot(mixing.astype(jnp.bfloat16), narrow[since:]))
                d_mixing = dot_nt(tile_sides[side][here], narrow[since:])
                d_products[part] = d_products[part] + d_mixing * decay_dt
                whole = d_mixing * mixing
                d_rows[h : h + 1, since:] += jnp.sum(whole, axis=0, keepdims=True)
                weighed = d_mixing * (products[here, since:] * decay)
                step_sums[part] = jnp.where(
                    lane == h, jnp.sum(weighed, axis=1, keepdims=True), step_sums[part]
                )
            dx[here, cols] = (
                jnp.where(lane < MP, sides[0], sides[1]) + skip_row[:, cols] * wide[here]
            )
        if between is not None:
            between(i)
    all_steps = jnp.concatenate(step_sums, axis=0)
    d_dt[...] = all_steps
    d_cum[...] = d_rows[...].T - all_steps * dt[...]
    g_skip[...] = jnp.broadcast_to(
        two_part(
            jnp.broadcast_to(jnp.concatenate(skip_sums, axis=1), (8, width)), gather_heads(width)
        ),
        g_skip.shape,
    )
    full = jnp.concatenate(
        [
            d
            if p == 0
            else jnp.concatenate([jnp.zeros((SPAN, p * SPAN), jnp.float32), d], axis=1)
            for p, d in enumerate(d_products)
        ],
        axis=0,
    ).astype(jnp.bfloat16)
    d_bc[:, :NS] = dot(full, narrow_c)
    d_bc[:, NS:] = dot_tn(full, narrow_b)


def ssm_back(info, x, bc, dt, cum, grad, head_params):
    rows, width = x.shape
    f32 = jnp.float32
    return big_call(
        ssm_back_kernel,
        (
            shape_of((rows, width), f32),
            shape_of((rows, 2 * NS), f32),
            shape_of((rows, TILE), f32),
            shape_of((rows, TILE), f32),
            shape_of((8, TILE), f32),
        ),
        info,
        x,
        bc,
        dt,
        cum,
        grad,
        head_params,
        smem=1,
        scratch=(pltpu.VMEM((TILE, rows), f32), pltpu.VMEM((TILE, rows), f32)),
        flops=8 * rows * rows * width,
    )


def state_back_kernel(
    info, x, bc, dt, cum, grad, head_params, step_in, state_in, d_state, dx_in, d_bc_in, d_cum_in,
    d_dt_in, dx, d_bc, d_step, sums,
):
    rows, width = x.shape
    bias, rate = head_params[0:1], head_params[1:2]
    cums, steps = cum[...], dt[...]
    enter = entering_of(info, cums)
    last_start = seg_start(info[0] + rows - 1, info) - info[0]
    place = lax.broadcasted_iota(jnp.int32, (rows, 1), 0)
    end = cums[rows - 1 : rows]
    fade = jnp.where(place >= last_start, jnp.exp(jnp.minimum(end - cums, 0.0)), 0.0)
    leave = fade * steps
    through = jnp.where(last_start < 0, jnp.exp(end), 0.0)
    narrow_b, narrow_c = bc[:, :NS], bc[:, NS:]
    pick = gather_heads(width)
    d_leave = jnp.zeros((rows, TILE), jnp.float32)
    d_enter = jnp.zeros((rows, TILE), jnp.float32)
    d_b = d_bc_in[:, :NS]
    d_c = d_bc_in[:, NS:]
    link = jnp.zeros((8, TILE), jnp.float32)
    for i in range(MH // 2):
        cols = slice(i * TILE, (i + 1) * TILE)
        tile = x[:, cols].astype(jnp.float32)
        wide = grad[:, cols]
        pulled = d_state[:, cols]
        held = state_in[:, cols]
        from_b = dot(narrow_b, pulled)
        leave_tile = lane_pick(leave, 2 * i)
        dx[:, cols] = dx_in[:, cols] + leave_tile * from_b
        d_leave = d_leave + two_part(tile * from_b, pick[cols])
        d_enter = d_enter + two_part(wide * dot(narrow_c, held), pick[cols])
        d_b = d_b + dot_nt((tile * leave_tile).astype(jnp.bfloat16), pulled)
        d_c = d_c + dot_nt((wide * lane_pick(enter, 2 * i)).astype(jnp.bfloat16), held)
        meet = jnp.sum(
            pulled.astype(jnp.float32) * held.astype(jnp.float32), axis=0, keepdims=True
        )
        link = link + two_part(jnp.broadcast_to(meet, (8, TILE)), pick[cols])
    d_bc[:, :NS] = d_b
    d_bc[:, NS:] = d_c
    left = leave * d_leave
    d_cum = d_cum_in[...] + enter * d_enter - left
    at_end = jnp.sum(left, axis=0, keepdims=True) + through * link[:1]
    d_cum = d_cum + jnp.where(place == rows - 1, at_end, 0.0)
    row = lax.broadcasted_iota(jnp.int32, (rows, rows), 0)
    col = lax.broadcasted_iota(jnp.int32, (rows, rows), 1)
    d_log = exact(jnp.where(row <= col, 1.0, 0.0), d_cum)
    d_steps = d_dt_in[...] + fade * d_leave - d_log * rate
    d_pre = d_steps * jax.nn.sigmoid(step_in[...] + bias)
    d_pre = jnp.where(head_lanes(rows), d_pre, 0.0)
    d_step[...] = d_pre.astype(jnp.bfloat16)
    g_rate = jnp.sum(d_log * (-steps * rate), axis=0, keepdims=True)
    g_bias = jnp.sum(d_pre, axis=0, keepdims=True)
    line = lax.broadcasted_iota(jnp.int32, (8, TILE), 0)
    sums[...] = jnp.where(line == 0, g_rate, jnp.where(line == 1, g_bias, 0.0))


def state_back(info, *args):
    rows, width = args[0].shape
    f32 = jnp.float32
    return big_call(
        state_back_kernel,
        (
            shape_of((rows, width), f32),
            shape_of((rows, 2 * NS), f32),
            shape_of((rows, TILE), jnp.bfloat16),
            shape_of((8, TILE), f32),
        ),
        info,
        *args,
        smem=1,
        flops=12 * rows * NS * width,
    )


def join_states(earlier, later):
    decay = later[NS : NS + 1].astype(jnp.float32) + later[NS + 1 : NS + 2].astype(jnp.float32)
    before = earlier[NS : NS + 1].astype(jnp.float32) + earlier[NS + 1 : NS + 2].astype(jnp.float32)
    state = decay * earlier[:NS].astype(jnp.float32) + later[:NS].astype(jnp.float32)
    both = decay * before
    high = both.astype(jnp.bfloat16)
    low = (both - high.astype(jnp.float32)).astype(jnp.bfloat16)
    rest = jnp.zeros((STATE_ROWS - NS - 2, state.shape[1]), jnp.bfloat16)
    return jnp.concatenate([state.astype(jnp.bfloat16), high, low, rest], axis=0)


def scan_states(own, forward):
    place = lax.axis_index("seq")
    count = lax.axis_size("seq")
    nothing = jnp.concatenate(
        [
            jnp.zeros((NS, own.shape[1]), own.dtype),
            jnp.ones((1, own.shape[1]), own.dtype),
            jnp.zeros((STATE_ROWS - NS - 1, own.shape[1]), own.dtype),
        ],
        axis=0,
    )
    everything = lax.all_gather(own, "seq")

    def step(k, before):
        index = k if forward else count - 1 - k
        reached = index < place if forward else index > place
        part = lax.dynamic_index_in_dim(everything, index, 0, False)
        return jnp.where(reached, join_states(before, part), before)

    return lax.fori_loop(0, count, step, nothing)[:NS]


MESH = pl.DeviceIdType.MESH
ANY = pl.BlockSpec(memory_space=pl.ANY)
INTO_VMEM = pl.BlockSpec(memory_space=pltpu.VMEM)


def partners():
    seq, batch = lax.axis_index("seq"), lax.axis_index("batch")
    return {
        "far": (seq + 4 - 8 * (seq // 4), batch),
        "near": (seq + 2 - 4 * (seq // 2 % 2), batch),
        "x": (seq + 1 - 2 * (seq % 2), batch),
        "y": (seq, batch + 2 - 4 * (batch // 2)),
        "core": (seq, batch + 1 - 2 * (batch % 2)),
    }


def greet(others):
    barrier = pltpu.get_barrier_semaphore()
    for other in others:
        pl.semaphore_signal(barrier, inc=1, device_id=other, device_id_type=MESH)
    pl.semaphore_wait(barrier, len(others))


def remote(src, dst, send, recv, other):
    return pltpu.make_async_remote_copy(
        src_ref=src, dst_ref=dst, send_sem=send, recv_sem=recv, device_id=other, device_id_type=MESH
    )


def comm_call(kernel, outs, out_specs, args, in_specs, scratch, number, moved, limit=56):
    return pl.pallas_call(
        kernel,
        out_shape=list(outs),
        in_specs=in_specs,
        out_specs=out_specs,
        scratch_shapes=list(scratch),
        cost_estimate=pl.CostEstimate(flops=0, bytes_accessed=moved, transcendentals=0),
        compiler_params=pltpu.CompilerParams(
            collective_id=number, has_side_effects=True, vmem_limit_bytes=limit * 1024 * 1024
        ),
    )(*args)


def column_chunks(widths, aim=512, lean=0, z_last=None):
    pairs, late = [], []
    for p, width in enumerate(widths):
        tiles, first = width // TILE, 0
        orders, to = (("xyz", "yxz"), late) if p == z_last else (("xy", "yx"), pairs)
        count = max(1, (width + aim // 2) // (2 * aim)) if p != z_last else max(1, width // 512)
        for i in range(count):
            both = tiles // count + (1 if i < tiles % count else 0)
            one = (both + (0 if p == z_last else lean) + 1) // 2
            pair = []
            for cols, order in ((one * TILE, orders[0]), ((both - one) * TILE, orders[1])):
                pair.append((p, first, cols, order))
                first += cols
            to.append(tuple(pair))
    return pairs + late


def pairs_of(pairs, array):
    return [n for n, (one, other) in enumerate(pairs) if one[0] == array]


BITS = {"far": 1, "near": 2, "x": 4, "y": 8, "core": 16}
ORDERS = {
    "xy": ("far", "near", "x", "y"),
    "yx": ("far", "near", "y", "x"),
    "xyz": ("x", "y", "far", "near"),
    "yxz": ("y", "x", "far", "near"),
}


def runs(places):
    out = []
    for place in places:
        if out and out[-1][0] + out[-1][1] == place:
            out[-1] = (out[-1][0], out[-1][1] + 1)
        else:
            out.append((place, 1))
    return out


def gather_plan(order):
    held, plan = [0], []
    for name in ORDERS[order] + ("core",):
        plan.append((name, [(f, k, f + BITS[name]) for f, k in runs(held)]))
        held = sorted(held + [block + BITS[name] for block in held])
    return plan


def scatter_plan(order):
    held, plan = list(range(16)), []
    for name in reversed(ORDERS[order]):
        bit = BITS[name]
        sent = [i for i, block in enumerate(held) if block & bit]
        kept = [i for i, block in enumerate(held) if not block & bit]
        plan.append((name, runs(sent), runs(kept)))
        held = [held[i] for i in kept]
    return plan


def bit_apart(r):
    me = lax.axis_index("seq")
    far = (r // 4 + me // 4) % 2
    near = (r // 2 % 2 + me // 2 % 2) % 2
    side = (r % 2 + me % 2) % 2
    return 4 * far + 2 * near + side


def join_into(target, earlier, later):
    decay = later[NS : NS + 1].astype(jnp.float32) + later[NS + 1 : NS + 2].astype(jnp.float32)
    before = earlier[NS : NS + 1].astype(jnp.float32) + earlier[NS + 1 : NS + 2].astype(jnp.float32)
    both = decay * before
    high = both.astype(jnp.bfloat16).astype(jnp.float32)
    line = lax.broadcasted_iota(jnp.int32, (STATE_ROWS - NS, both.shape[1]), 0)
    tail = jnp.where(line == 0, high, jnp.where(line == 1, both - high, 0.0))
    for first in range(0, NS, 32):
        rows = slice(first, first + 32)
        target[rows] = (
            decay * earlier[rows].astype(jnp.float32) + later[rows].astype(jnp.float32)
        ).astype(jnp.bfloat16)
    target[NS:] = tail.astype(jnp.bfloat16)


SCAN_PARTS = 2


class StateScan:
    def __init__(self, forward, own, result, arrived, sent, before, send, recv, others):
        me = lax.axis_index("seq")
        self.seconds = []
        for bit in (me % 2, me // 2 % 2, me // 4):
            self.seconds.append(bit == 1 if forward else bit == 0)
        route = (others["x"], others["near"], others["far"])
        width = own.shape[1] // SCAN_PARTS
        self.parts = []
        for part in range(SCAN_PARTS):
            cols = pl.ds(part * width, width)
            here = (slice(None), cols)
            sources = (own.at[here], sent.at[0].at[here], sent.at[1].at[here])
            targets = [arrived.at[k].at[here] for k in range(3)]
            copies = [
                remote(sources[k], targets[k], send.at[k, part], recv.at[k, part], route[k])
                for k in range(3)
            ]
            befores = [before.at[k].at[here] for k in range(2)]
            self.parts.append((sources, targets, copies, befores, result.at[here]))

    def step(self, k):
        for part in self.parts:
            self.part_step(k, *part)

    def part_step(self, k, sources, targets, copies, before, result):
        if k == 0:
            copies[0].start()
            return
        copies[k - 1].wait_recv()
        other, mine = targets[k - 1], sources[k - 1]
        second = self.seconds[k - 1]

        @pl.when(second)
        def _():
            if k < 3:
                join_into(sources[k], other, mine)
            if k == 1:
                before[0][...] = other[...]
            elif k == 2:
                join_into(before[1], other, before[0])
            else:
                last = before[1]
                decay = last[NS : NS + 1].astype(jnp.float32) + last[NS + 1 : NS + 2].astype(
                    jnp.float32
                )
                result[...] = (
                    decay * other[:NS].astype(jnp.float32) + last[:NS].astype(jnp.float32)
                ).astype(jnp.bfloat16)

        @pl.when(jnp.logical_not(second))
        def _():
            if k < 3:
                join_into(sources[k], mine, other)
            if k == 1:
                line = lax.broadcasted_iota(jnp.int32, before[0].shape, 0)
                before[0][...] = jnp.where(line == NS, 1.0, 0.0).astype(jnp.bfloat16)
            elif k == 2:
                before[1][...] = before[0][...]
            else:
                result[...] = before[1][:NS]

        if k < 3:
            copies[k].start()

    def finish(self):
        for part in self.parts:
            for copy in part[2]:
                copy.wait_send()


def scan_scratch(width):
    rows = STATE_ROWS
    dma = pltpu.SemaphoreType.DMA
    narrow = jnp.bfloat16
    return [
        pltpu.VMEM((3, rows, width), narrow),
        pltpu.VMEM((2, rows, width), narrow),
        pltpu.VMEM((2, rows, width), narrow),
        dma((3, SCAN_PARTS)),
        dma((3, SCAN_PARTS)),
    ]


RIM = 8
COLS = 384


def own_order_into(target):
    width = target.shape[0]
    per = width // 32
    me = lax.axis_index("seq") * 4 + lax.axis_index("batch")
    step = 128

    def fill(i, carry):
        first = pl.multiple_of(i * step, step)
        row = lax.broadcasted_iota(jnp.int32, (step, width), 0) + first
        col = lax.broadcasted_iota(jnp.int32, (step, width), 1)
        j = col // per
        flipped = (j & 1) * 16 + (j & 2) * 4 + (j & 4) + (j & 8) // 4 + (j & 16) // 16
        source = (flipped ^ me) * per + col % per
        target[pl.ds(first, step)] = jnp.where(row == source, 1.0, 0.0).astype(target.dtype)
        return carry

    lax.fori_loop(0, width // step, fill, 0)


def three_part(left, right):
    high = left.astype(jnp.bfloat16)
    rest = left - high.astype(jnp.float32)
    mid = rest.astype(jnp.bfloat16)
    low = (rest - mid.astype(jnp.float32)).astype(jnp.bfloat16)
    return dot(high, right) + dot(mid, right) + dot(low, right)


def places_of(lens, rows):
    one, two, three = lens[0, 0], lens[0, 1], lens[0, 2]
    return [lax.axis_index("seq") * rows, one, one + two, one + two + three]


def head_rows(bias, rate_log, skip, target):
    lane = lax.broadcasted_iota(jnp.int32, (1, TILE), 1)
    for k, source in enumerate((bias, rate_log, skip)):
        row = jnp.zeros((1, TILE), jnp.float32)
        for h in range(MH):
            row = jnp.where(lane == h, source[h], row)
        if k == 1:
            row = jnp.where(lane < MH, jnp.exp(row), 0.0)
        target[k : k + 1] = row


def pair_columns(value, back):
    tiles = [value[:, i * TILE : (i + 1) * TILE] for i in range(PAIRS)]
    turned = [pltpu.roll(tile, HEAD_SIZE, 1) for tile in tiles]
    lane = lax.broadcasted_iota(jnp.int32, tiles[0].shape, 1)

    def head(i, side):
        return tiles[i // 2] if i % 2 == side else turned[i // 2]

    out = []
    for i in range(PAIRS):
        if back:
            first, second = 2 * i, 2 * i + 1
            group = QUERY_HEADS // KEY_VALUE_HEADS
            first, second = [2 * (h % group) + h // group for h in (first, second)]
        else:
            first, second = i, i + PAIRS
        out.append(jnp.where(lane < HEAD_SIZE, head(first, 0), head(second, 1)))
    return jnp.concatenate(out, axis=1)


def shards_into(w_attn, w_ssm_in, w_dt, w_out, conv, mix, out):
    f32, narrow = jnp.float32, jnp.bfloat16
    ssm_width = MH * MP
    xbc = w_ssm_in.shape[1] - ssm_width
    query = QUERY_HEADS * HEAD_SIZE
    attn = w_attn.shape[1]
    conv[:, :xbc] = w_ssm_in[:, ssm_width:]
    conv[:, xbc:] = jnp.zeros((conv.shape[0], TILE), narrow)
    block = conv.shape[0]
    row = lax.broadcasted_iota(jnp.int32, (block, block), 0)
    same = row == lax.broadcasted_iota(jnp.int32, (block, block), 1)
    conv[:, xbc : xbc + MH] = dot_nt(jnp.where(same, 1.0, 0.0).astype(narrow), w_dt[...]).astype(
        narrow
    )
    mix[:, :query] = pair_columns(w_attn[:, :query].astype(f32), False).astype(narrow)
    mix[:, query:attn] = w_attn[:, query:]
    mix[:, attn:] = w_ssm_in[:, :ssm_width]
    out[:, :query] = pair_columns(w_out[:, :query].astype(f32), False).astype(narrow)
    out[:, query:] = w_out[:, query:]


class Stage:
    def __init__(self, sources, targets, sems):
        self.copies = [
            pltpu.make_async_copy(source, target, sems.at[k])
            for k, (source, target) in enumerate(zip(sources, targets))
        ]
        self.open = {}

    def start(self, *which):
        for k in which:
            self.copies[k].start()
            self.open[k] = True

    def need(self, *which):
        for k in which:
            if self.open.pop(k, False):
                self.copies[k].wait()

    def finish(self):
        self.need(*list(self.open))


class Gather:
    def __init__(self, ins, outs, pairs, send, recv, local, others):
        self.ins, self.outs, self.pairs = ins, outs, pairs
        self.send, self.recv, self.local, self.others = send, recv, local, others
        self.started = {}
        self.block = ins[0].shape[0]

    def own(self):
        copies = []
        for p in range(len(self.ins)):
            copy = pltpu.make_async_copy(
                self.ins[p], self.outs[p].at[pl.ds(0, self.block)], self.local.at[p]
            )
            copy.start()
            copies.append(copy)
        for copy in copies:
            copy.wait()

    def step(self, n, stage):
        for side in range(2):
            p, column, cols, order = self.pairs[n][side]
            if stage > 0:
                for copy in self.started[n, side, stage - 1]:
                    copy.wait_recv()
            if stage == 5:
                continue
            name, moves = gather_plan(order)[stage]
            copies = []
            for k, (first, rows, there) in enumerate(moves):
                block = self.block
                copy = remote(
                    self.outs[p].at[pl.ds(first * block, rows * block), pl.ds(column, cols)],
                    self.outs[p].at[pl.ds(there * block, rows * block), pl.ds(column, cols)],
                    self.send.at[2 * n + side, stage, k],
                    self.recv.at[2 * n + side, stage, k],
                    self.others[name],
                )
                copy.start()
                copies.append(copy)
            self.started[n, side, stage] = copies

    def finish(self):
        for copies in self.started.values():
            for copy in copies:
                copy.wait_send()


def around():
    seq, batch = lax.axis_index("seq"), lax.axis_index("batch")
    return ((seq + 7) % 8, batch), ((seq + 1) % 8, batch)


def conv_masks(info, rows):
    at = lax.broadcasted_iota(jnp.int32, (rows, 1), 0) + info[0]
    start = seg_start(at, info)
    return [jnp.where(at - (CONV - 1) + i >= start, 1.0, 0.0) for i in range(CONV)]


def conv_forward(info, raw, conv_w, conv_b, pre, x, bc):
    rows = x.shape[0]
    masks = conv_masks(info, rows)
    tiles = pre.shape[1] // TILE
    split = x.shape[1] // TILE
    for i in range(tiles):
        cols = slice(i * TILE, (i + 1) * TILE)
        total = jnp.broadcast_to(conv_b[i : i + 1], (rows, TILE))
        for k in range(CONV):
            first = RIM - (CONV - 1) + k
            shifted_rows = jnp.where(masks[k] > 0.0, raw[first : first + rows, cols], 0.0)
            total = total + conv_w[k : k + 1, cols] * shifted_rows
        pre[:, cols] = total
        out = (total * jax.nn.sigmoid(total)).astype(jnp.bfloat16)
        if i < split:
            x[:, cols] = out
        else:
            bc[:, (i - split) * TILE : (i - split + 1) * TILE] = out


def front_kernel(
    count, pairs, lens, bias, rate_log, skip, layer_x, layer_g, norm_gain, mlp_gain, freqs, conv_w,
    conv_b, w_attn, w_ssm_in, w_dt, w_out, w_gate_up, w_down, *refs
):
    fulls, made, refs = refs[:count], refs[count : count + 23], refs[count + 23 :]
    near, refs = refs[:25], refs[25:]
    writes = Stage((*near,), (*fulls[:2], *made), refs[-1])
    fulls = (*near[:2], *fulls[2:])
    (
        x_own, g_own, gains_own, normed, q, kv, gate_z, raw, pre, x, bc, y, state, dt, cum,
        out, out_t, lse, state_in, order, cosine, sine, head_params,
    ) = near[2:]
    (
        s_conv, s_mix, s_out, gains,
        attn_proj, dt_t, cum_t, heads, acc, top, total, arrived, sent, before,
        scan_send, scan_recv, send, recv, w_send, w_recv, w_local, rim_send, rim_recv,
    ) = refs[:-1]
    ins = (s_conv, s_mix, s_out, w_gate_up, w_down)
    others = partners()
    previous, following = around()
    greet(list(others.values()) + [previous, following])
    me = lax.axis_index("seq")
    rows, width = layer_x.shape
    info = places_of(lens, rows)
    shards_into(w_attn, w_ssm_in, w_dt, w_out, s_conv, s_mix, s_out)
    gather = Gather(ins, fulls, pairs, w_send, w_recv, w_local, others)
    gather.own()

    first = len(pairs_of(pairs, 0)) + len(pairs_of(pairs, 1))
    small = pairs_of(pairs, 2)
    waves = {}
    for n in reversed(range(len(pairs))):
        for stage in range(6):
            late = 1 if n >= first and stage >= 2 else 0
            wave = n - small[0] + 2 * stage if n in small else n + stage + late
            waves.setdefault(wave, []).append((n, stage))

    def pump(*which):
        for wave in which:
            for n, stage in waves.pop(wave, []):
                gather.step(n, stage)

    conv_wave = pairs_of(pairs, 0)[-1] + 5
    mix_wave = pairs_of(pairs, 1)[-1] + 5
    pump(0)
    own_order_into(order)
    head_rows(bias, rate_log, skip, head_params)
    gains[...] = jnp.zeros_like(gains)
    for k, source in enumerate((norm_gain, mlp_gain)):
        for i in range(width // TILE):
            gains[k : k + 1, i * TILE : (i + 1) * TILE] = source[i : i + 1]
    pump(1)
    at = lax.broadcasted_iota(jnp.int32, (rows, 1), 0) + info[0]
    angles = (at - seg_start(at, info)).astype(jnp.float32) * freqs[...]
    cosine[...] = jnp.cos(angles)
    sine[...] = jnp.sin(angles)
    x_own[...] = dot(layer_x[...], order[...]).astype(jnp.bfloat16)
    pump(2)
    gains_own[...] = three_part(gains[...], order[...])
    wide = x_own[...].astype(jnp.float32)
    scale = lax.rsqrt(jnp.mean(wide * wide, axis=-1, keepdims=True) + NORM_EPS)
    normed[...] = (wide * scale * gains_own[0:1]).astype(jnp.bfloat16)
    pump(3)
    g_own[...] = dot(layer_g[...], order[...]).astype(jnp.bfloat16)
    pump(*range(4, conv_wave + 1))

    full_conv, full_mix = fulls[0], fulls[1]
    xbc = pre.shape[1]
    conv_cols = full_conv.shape[1] // COLS
    attn_cols = attn_proj.shape[1] // COLS
    gate_cols = gate_z.shape[1] // COLS

    def project(weights, first, target, row, count_cols):
        def one(j, carry):
            cols = pl.ds(pl.multiple_of(j * COLS, TILE), COLS)
            there = pl.ds(pl.multiple_of(first + j * COLS, TILE), COLS)
            target[row : row + rows, cols] = dot(normed[...], weights[:, there])
            return carry

        lax.fori_loop(0, count_cols, one, 0)

    def at(r):
        return kv.at[pl.ds(r * rows, rows)]

    routes = {4: ("far", 0), 2: ("near", 0), 6: ("near", 4)}
    routes.update({r: ("x", r - 1) for r in (1, 3, 5, 7)})
    copies = {
        r: remote(at(src), at(r), send.at[r], recv.at[r], others[name])
        for r, (name, src) in routes.items()
    }
    project(full_conv, 0, raw, RIM, conv_cols)
    rim = remote(
        raw.at[pl.ds(rows, RIM)], raw.at[pl.ds(0, RIM)], rim_send.at[0], rim_recv.at[0], following
    )
    rim.start()
    pump(*range(conv_wave + 1, mix_wave))
    rim.wait_recv()
    conv_forward(info, raw, conv_w, conv_b, pre, x, bc)
    step_in = raw.at[pl.ds(RIM, rows), pl.ds(xbc, TILE)]
    ssm_states(info, x, bc, step_in, head_params, state, dt, cum, dt_t, cum_t)
    scan = StateScan(True, state, state_in, arrived, sent, before, scan_send, scan_recv, others)
    scan.step(0)
    writes.start(0, 9, 10, 11, 12, 14, 15, 16)
    pump(mix_wave)
    project(full_mix, 0, attn_proj, 0, attn_cols)
    rope_kernel(attn_proj, cosine, sine, q, kv.at[pl.ds(0, rows)])
    copies[4].start()
    copies[2].start()
    copies[1].start()
    pump(mix_wave + 1)
    project(full_mix, attn_proj.shape[1], gate_z, 0, gate_cols)
    writes.start(1, 8, 6, 2, 3, 4, 5, 21, 22, 23, 24)
    attend_start(q, heads, acc, top, total)

    def attend(r):
        block = bit_apart(r)

        @pl.when(block <= me)
        def _():
            place = pl.ds(pl.multiple_of(r * rows, rows), rows)
            keys = kv[place, :TILE]
            values_t = kv[place, TILE:].astype(jnp.float32).T.astype(jnp.bfloat16)
            attend_block(info, block, keys, values_t, heads, acc, top, total)

    def several(first, gap, count_blocks):
        def body(j, carry):
            attend(first + j * gap)
            return carry

        lax.fori_loop(0, count_blocks, body, 0)

    scan.step(1)
    copies[4].wait_recv()
    copies[6].start()
    copies[5].start()
    copies[2].wait_recv()
    copies[3].start()
    copies[6].wait_recv()
    copies[7].start()
    pump(mix_wave + 2)
    several(0, 4, 2)
    pump(mix_wave + 3)
    ssm_local(info, x, bc, head_params, y, cum, dt_t, cum_t)
    writes.start(13)
    scan.step(2)
    pump(mix_wave + 4)
    several(2, 4, 2)
    pump(mix_wave + 5)
    for r in (1, 3, 5, 7):
        copies[r].wait_recv()
    writes.start(7)
    several(1, 2, 2)
    pump(mix_wave + 6)
    several(5, 2, 2)
    pump(mix_wave + 7)
    lse[...] = top[...] + jnp.log(total[...])
    attend_write(acc, total, out, out_t)
    scan.step(3)
    writes.start(17, 18, 19, 20)
    pump(*sorted(waves))
    gather.finish()
    writes.finish()
    scan.finish()
    rim.wait_send()
    for copy in copies.values():
        copy.wait_send()


def front(lens, bias, rate_log, skip, layer_x, layer_g, norm_gain, mlp_gain, freqs, conv_w, conv_b, weights):
    w_attn, w_ssm_in, w_dt, w_out, w_gate_up, w_down = weights
    rows, width = layer_x.shape
    f32, narrow = jnp.float32, jnp.bfloat16
    block = w_attn.shape[0]
    query_width = QUERY_HEADS * HEAD_SIZE
    pair_width = 2 * KEY_VALUE_HEADS * HEAD_SIZE
    ssm_width = MH * MP
    xbc = conv_w.shape[1]
    widths = [
        xbc + TILE, w_attn.shape[1] + ssm_width, w_out.shape[1], w_gate_up.shape[1],
        w_down.shape[1],
    ]
    count = len(widths)
    pairs = column_chunks(widths, z_last=2)
    fulls = [shape_of((width, w), narrow) for w in widths]
    outs = fulls + [
        shape_of((rows, width), narrow),
        shape_of((rows, width), narrow),
        shape_of((8, width), f32),
        shape_of((rows, width), narrow),
        shape_of((rows, query_width), narrow),
        shape_of((8 * rows, pair_width), narrow),
        shape_of((rows, ssm_width), f32),
        shape_of((rows + RIM, widths[0]), f32),
        shape_of((rows, xbc), f32),
        shape_of((rows, ssm_width), narrow),
        shape_of((rows, 2 * NS), narrow),
        shape_of((rows, ssm_width), f32),
        shape_of((STATE_ROWS, ssm_width), narrow),
        shape_of((rows, TILE), f32),
        shape_of((rows, TILE), f32),
        shape_of((rows, query_width), narrow),
        shape_of((query_width, rows), f32),
        shape_of((QUERY_HEADS, rows), f32),
        shape_of((NS, ssm_width), narrow),
        shape_of((width, width), narrow),
        shape_of((rows, TILE), f32),
        shape_of((rows, TILE), f32),
        shape_of((8, TILE), f32),
    ]
    dma = pltpu.SemaphoreType.DMA
    scratch = [pltpu.VMEM(o.shape, o.dtype) for o in (*outs[:2], *outs[count:])]
    scratch += [
        *(pltpu.VMEM((block, widths[k]), narrow) for k in (0, 1, 2)),
        pltpu.VMEM((8, width), f32),
        pltpu.VMEM((rows, query_width + pair_width), f32),
        pltpu.VMEM((TILE, rows), f32),
        pltpu.VMEM((TILE, rows), f32),
        pltpu.VMEM((QUERY_HEADS, rows, TILE), narrow),
        pltpu.VMEM((QUERY_HEADS, HEAD_SIZE, rows), f32),
        pltpu.VMEM((QUERY_HEADS, rows), f32),
        pltpu.VMEM((QUERY_HEADS, rows), f32),
        *scan_scratch(ssm_width),
        dma((8,)),
        dma((8,)),
        dma((2 * len(pairs), 5, 4)),
        dma((2 * len(pairs), 5, 4)),
        dma((count,)),
        dma((1,)),
        dma((1,)),
        dma((25,)),
    ]
    result = comm_call(
        lambda *refs: front_kernel(count, pairs, *refs),
        outs,
        [ANY] * len(outs),
        (
            lens, bias, rate_log, skip, layer_x, layer_g, norm_gain, mlp_gain, freqs, conv_w,
            conv_b, *weights,
        ),
        [pl.BlockSpec(memory_space=pltpu.SMEM)] * 4 + [INTO_VMEM] * 13,
        scratch,
        0,
        200_000_000,
    )
    return result[:count], result[count:]


def middle_kernel(
    lens, y, bc, cum, state_in, state_own, z, ssm_gain, attended, x_own, g_own, gains, order,
    hbm_out, hbm_gu, hbm_down,
    layer_out, joined, hidden, d_gu, normed_two, d_mixer, d_middle, d_ssm, d_z, pull, att_grad,
    g_ssm, g_mlp,
    w_out, w_gu, w_down, ssm_out, scale, middle, gate_up, d_normed, dy, narrow, sems,
):
    rows, width = x_own.shape
    info = places_of(lens, rows)
    copies = [
        pltpu.make_async_copy(src, dst, sems.at[k])
        for k, (src, dst) in enumerate(((hbm_out, w_out), (hbm_gu, w_gu), (hbm_down, w_down)))
    ]
    for copy in copies:
        copy.start()
    attn = attended.shape[1]
    ff = hidden.shape[1]
    step = 512

    def tiles(count, body):
        def one(j, carry):
            body(pl.ds(pl.multiple_of(j * step, step), step), j * step)
            return carry

        lax.fori_loop(0, count // step, one, 0)

    joined[:, :attn] = attended[...]
    ssm_finish_kernel(
        info, y, bc, cum, state_in, z, ssm_gain, ssm_out,
        joined.at[:, pl.ds(attn, joined.shape[1] - attn)], scale,
    )
    copies[0].wait()

    def add_mixers(here, first):
        middle[:, here] = x_own[:, here].astype(jnp.float32) + dot_nt(joined[...], w_out[here])

    tiles(width, add_mixers)
    wide = middle[...]
    r = lax.rsqrt(jnp.mean(wide * wide, axis=-1, keepdims=True) + NORM_EPS)
    normed_two[...] = (wide * r * gains[1:2]).astype(jnp.bfloat16)
    copies[1].wait()

    def up_project(here, first):
        there = pl.ds(pl.multiple_of(ff + first, step), step)
        gate = dot(normed_two[...], w_gu[:, here])
        up = dot(normed_two[...], w_gu[:, there])
        gate_up[:, here] = gate
        gate_up[:, there] = up
        hidden[:, here] = (gate * jax.nn.sigmoid(gate) * up).astype(jnp.bfloat16)

    tiles(ff, up_project)
    copies[2].wait()

    def down_project(here, first):
        narrow[:, here] = (middle[:, here] + dot_nt(hidden[...], w_down[here])).astype(jnp.bfloat16)

    tiles(width, down_project)

    def plain(here, first):
        layer_out[:, here] = dot_nt(narrow[...], order[here]).astype(jnp.bfloat16)

    tiles(width, plain)

    def down_back(here, first):
        there = pl.ds(pl.multiple_of(ff + first, step), step)
        d_hidden = dot(g_own[...], w_down[:, here])
        gate, up = gate_up[:, here], gate_up[:, there]
        sig = jax.nn.sigmoid(gate)
        d_gate = d_hidden * up * (sig * (1.0 + gate * (1.0 - sig)))
        d_gu[:, here] = d_gate.astype(jnp.bfloat16)
        d_gu[:, there] = (d_hidden * gate * sig).astype(jnp.bfloat16)

    tiles(ff, down_back)

    def up_back(here, first):
        d_normed[:, here] = dot_nt(d_gu[...], w_gu[here])

    tiles(width, up_back)
    grads = d_normed[...]
    wide = middle[...]
    g_mlp[...] = jnp.sum(grads * wide * r, axis=0, keepdims=True)
    inner = grads * gains[1:2]
    coeff = jnp.mean(inner * wide, axis=-1, keepdims=True)
    total = g_own[...].astype(jnp.float32) + r * (inner - wide * (r * r * coeff))
    d_middle[...] = total
    d_mixer[...] = total.astype(jnp.bfloat16)

    def att_back(here, first):
        att_grad[:, here] = dot(d_mixer[...], w_out[:, here]).astype(jnp.bfloat16)

    tiles(attn, att_back)

    def ssm_part(here, first):
        there = pl.ds(pl.multiple_of(attn + first, step), step)
        dy[:, here] = dot(d_mixer[...], w_out[:, there])

    tiles(dy.shape[1], ssm_part)
    gate_back_kernel(
        info, dy, ssm_out, z, scale, ssm_gain, cum, bc, d_ssm, d_z, pull.at[pl.ds(0, NS)], g_ssm
    )
    pull[NS:] = state_own[NS:]


def middle_part(lens, y, bc, cum, state_in, state_own, z, ssm_gain, attended, x_own, g_own, gains, order, w_out, w_gu, w_down):
    rows, width = x_own.shape
    ssm_width, attn = y.shape[1], attended.shape[1]
    ff = w_down.shape[1]
    f32, narrow = jnp.float32, jnp.bfloat16
    outs = [
        shape_of((rows, width), narrow),
        shape_of((rows, attn + ssm_width), narrow),
        shape_of((rows, ff), narrow),
        shape_of((rows, 2 * ff), narrow),
        shape_of((rows, width), narrow),
        shape_of((rows, width), narrow),
        shape_of((rows, width), f32),
        shape_of((rows, ssm_width), f32),
        shape_of((rows, ssm_width), narrow),
        shape_of((STATE_ROWS, ssm_width), narrow),
        shape_of((rows, attn), narrow),
        shape_of(ssm_gain.shape, f32),
        shape_of((1, width), f32),
    ]
    args = (
        lens, y, bc, cum, state_in, state_own, z, ssm_gain, attended, x_own, g_own, gains, order,
        w_out, w_gu, w_down,
    )
    return pl.pallas_call(
        middle_kernel,
        out_shape=outs,
        in_specs=[pl.BlockSpec(memory_space=pltpu.SMEM)] + [INTO_VMEM] * 12 + [ANY] * 3,
        out_specs=[INTO_VMEM] * len(outs),
        scratch_shapes=[
            pltpu.VMEM(w_out.shape, narrow),
            pltpu.VMEM(w_gu.shape, narrow),
            pltpu.VMEM(w_down.shape, narrow),
            pltpu.VMEM((rows, ssm_width), f32),
            pltpu.VMEM((rows, TILE), f32),
            pltpu.VMEM((rows, width), f32),
            pltpu.VMEM((rows, 2 * ff), f32),
            pltpu.VMEM((rows, width), f32),
            pltpu.VMEM((rows, ssm_width), f32),
            pltpu.VMEM((rows, width), narrow),
            pltpu.SemaphoreType.DMA((3,)),
        ],
        compiler_params=pltpu.CompilerParams(vmem_limit_bytes=60 * 1024 * 1024),
    )(*args)


def turn_over(value):
    return value.astype(jnp.float32).T.astype(jnp.bfloat16)


class Scatter:
    def __init__(self, ins, outs, arrived, pairs, send, recv, others):
        self.ins, self.outs, self.arrived, self.pairs = ins, outs, arrived, pairs
        self.send, self.recv, self.others = send, recv, others
        self.block = ins[0].shape[0] // 16
        self.started = {}

    def source(self, p, stage):
        return self.ins[p] if stage == 0 else self.arrived[4 * p + stage - 1]

    def step(self, n, stage):
        for side in range(2):
            if stage > 0:
                self.take(n, side, stage - 1)
            if stage < 4:
                self.begin(n, side, stage)

    def begin(self, n, side, stage):
        p, column, width, order = self.pairs[n][side]
        cols = pl.ds(column, width)
        name, sent, unused_kept = scatter_plan(order)[stage]
        copies, row, block = [], 0, self.block
        for k, (first, count) in enumerate(sent):
            copy = remote(
                self.source(p, stage).at[pl.ds(first * block, count * block), cols],
                self.arrived[4 * p + stage].at[pl.ds(row * block, count * block), cols],
                self.send.at[2 * n + side, stage, k],
                self.recv.at[2 * n + side, stage, k],
                self.others[name],
            )
            copy.start()
            copies.append(copy)
            row += count
        self.started[n, side, stage] = copies

    def take(self, n, side, stage):
        p, column, width, order = self.pairs[n][side]
        cols = slice(column, column + width)
        source, got = self.source(p, stage), self.arrived[4 * p + stage]
        target = self.outs[p] if stage == 3 else got
        unused_name, unused_sent, kept = scatter_plan(order)[stage]
        row, block = 0, self.block
        for k, (first, count) in enumerate(kept):
            self.started[n, side, stage][k].wait_recv()

            def add(i, carry):
                at = pl.multiple_of(i * block, block)
                there = pl.ds(row * block + at, block)
                total = source[pl.ds(first * block + at, block), cols].astype(jnp.float32) + got[
                    there, cols
                ].astype(jnp.float32)
                target[there, cols] = total.astype(target.dtype)
                return carry

            lax.fori_loop(0, count, add, 0)
            row += count

    def finish(self):
        for copies in self.started.values():
            for copy in copies:
                copy.wait_send()


def scatter_scratch(widths, size):
    scratch = []
    for width in widths:
        scratch += [pltpu.VMEM((size >> (s + 1), width), jnp.bfloat16) for s in range(4)]
    return scratch


def weight_products(left_t, right, theirs, target):
    rows = right.shape[0]
    step = 256 if right.shape[1] % 256 == 0 else TILE

    def one(j, carry):
        cols = pl.ds(pl.multiple_of(j * step, step), step)
        product = dot(left_t[:, :rows], right[:, cols]) + dot(left_t[:, rows:], theirs[:, cols])
        target[:, cols] = product.astype(target.dtype)
        return carry

    lax.fori_loop(0, right.shape[1] // step, one, 0)


def conv_back_start(info, dx, d_bc, pre, raw, d_pre, g_conv):
    rows, split = dx.shape[0], dx.shape[1] // TILE
    masks = conv_masks(info, rows)
    g_conv[...] = jnp.zeros_like(g_conv)
    for i in range(pre.shape[1] // TILE):
        cols = slice(i * TILE, (i + 1) * TILE)
        if i < split:
            grad = dx[:, cols]
        else:
            grad = d_bc[:, (i - split) * TILE : (i - split + 1) * TILE]
        value = pre[:, cols]
        sig = jax.nn.sigmoid(value)
        grad = grad * (sig * (1.0 + value * (1.0 - sig)))
        d_pre[:rows, cols] = grad
        for k in range(CONV):
            first = RIM - (CONV - 1) + k
            term = jnp.where(masks[k] > 0.0, raw[first : first + rows, cols], 0.0)
            g_conv[k : k + 1, cols] = jnp.sum(grad * term, axis=0, keepdims=True)
        g_conv[CONV : CONV + 1, cols] = jnp.sum(grad, axis=0, keepdims=True)


def conv_back_end(info, d_pre, conv_w, d_raw):
    rows = d_raw.shape[0]
    at = lax.broadcasted_iota(jnp.int32, (rows, 1), 0) + info[0]
    masks = [
        jnp.where(seg_start(at + (CONV - 1) - k, info) <= at, 1.0, 0.0) for k in range(CONV)
    ]
    for i in range(d_pre.shape[1] // TILE):
        cols = slice(i * TILE, (i + 1) * TILE)
        total = jnp.zeros((rows, TILE), jnp.float32)
        for k in range(CONV):
            first = CONV - 1 - k
            part = jnp.where(masks[k] > 0.0, d_pre[first : first + rows, cols], 0.0)
            total = total + conv_w[k : k + 1, cols] * part
        d_raw[:, cols] = total.astype(jnp.bfloat16)


def back_kernel(pairs, *refs):
    lens, far, refs = refs[0], refs[1:27], refs[27:]
    outs, near, refs = refs[:11], refs[11:37], refs[37:]
    loads = Stage(far, near, refs[-1])
    loads.start(21, 22, 9, 20, 23, 4, 5, 6, 7, 8, 19, 24, 18, 25, *range(10, 18), *range(4))
    (
        head_params, conv_w, cosine, sine, q, kv, grad, out_t, lse, pull, x, bc, dt, cum,
        d_ssm, raw, state_in, pre, normed, normed_two, d_mixer, grad_rows, hidden, joined, d_gu,
        d_z,
    ) = near
    (
        d_conv, d_attn, g_conv, head_sums, g_skip, p_conv, p_attn, out_down, out_gu, out_out, out_z,
    ) = outs
    refs = refs[:-1]
    partials, refs = refs[:4], refs[4:]
    arrived_w, refs = refs[:16], refs[16:]
    (
        half_grad, half_two, half_mixer, their_hidden, their_joined, their_gu, their_z, their_normed,
        their_conv, their_attn, left_t, heads, grads, delta, acc, dkv, from_x, from_far, from_near, dq, d_pair,
        d_cum, d_dt, cols_t, d_rows, d_pre,
        arrived, sent, before, scan_send, scan_recv, send, recv, swap_send, swap_recv,
        w_send, w_recv, rim_send, rim_recv,
    ) = refs
    others = partners()
    previous, following = around()
    greet(list(others.values()) + [previous, following])
    me = lax.axis_index("seq")
    rows = q.shape[0]
    info = places_of(lens, rows)
    half = normed.shape[1] // 2
    xbc = pre.shape[1]
    dx = d_pre.at[pl.ds(0, rows), pl.ds(0, x.shape[1])]
    d_bc = d_pre.at[pl.ds(0, rows), pl.ds(x.shape[1], 2 * NS)]
    d_state = arrived.at[0, pl.ds(0, NS)]
    scan = StateScan(False, pull, d_state, arrived, sent, before, scan_send, scan_recv, others)
    loads.need(9)
    scan.step(0)
    behind = pl.ds(half, half)
    given = [
        (far[21].at[:, behind], half_grad),
        (far[22], their_hidden),
        (far[20].at[:, behind], half_mixer),
        (far[23], their_joined),
        (far[19].at[:, behind], half_two),
        (far[24], their_gu),
        (far[18].at[:, behind], their_normed),
        (far[25], their_z),
    ]
    swaps = [
        remote(give, take, swap_send.at[k], swap_recv.at[k], others["core"])
        for k, (give, take) in enumerate(given)
    ]
    for copy in swaps:
        copy.start()
    scatter = Scatter(
        partials, (out_down, out_gu, out_out, out_z), arrived_w, pairs, w_send, w_recv, others
    )

    def weights(k, left, left_half, right, theirs):
        first = 2 * (0, 2, 1, 3)[k]
        loads.need(*((21, 22), (19, 24), (20, 23), (18, 25))[k])
        swaps[first].wait_recv()
        swaps[first + 1].wait_recv()
        left_t[:, :rows] = turn_over(left[:, :half])
        left_t[:, rows:] = turn_over(left_half[...])
        weight_products(left_t, right, theirs, partials[k])

    small = pairs_of(pairs, 2)
    waves = {}
    for n in range(len(pairs)):
        for stage in range(5):
            begin = 1 + (n - small[0]) // 2 if n in small else n
            waves.setdefault(begin + stage, []).append((n, stage))

    def pump(wave):
        for n, stage in waves.pop(wave):
            scatter.step(n, stage)

    loads.need(4, 5, 6, 7, 8)
    attend_back_start(q, grad, out_t, heads, grads, delta, acc)

    def block_back(r):
        block = bit_apart(r)
        place = pl.ds(pl.multiple_of(r * rows, rows), rows)

        @pl.when(block <= me)
        def _():
            attend_back_block(
                info, block, kv[place, :TILE], kv[place, TILE:], lse, dkv.at[r], heads, grads,
                delta, acc,
            )

        @pl.when(block > me)
        def _():
            dkv[r] = jnp.zeros(dkv.shape[1:], dkv.dtype)

    def several(first, gap, count):
        def body(j, carry):
            block_back(first + j * gap)
            return carry

        lax.fori_loop(0, count, body, 0)

    def add(target, source):
        target[...] = (target[...].astype(jnp.float32) + source[...].astype(jnp.float32)).astype(
            jnp.bfloat16
        )

    weights(0, grad_rows, half_grad, hidden, their_hidden)
    pump(0)
    weights(2, d_mixer, half_mixer, joined, their_joined)
    several(1, 2, 4)
    over_x = [
        remote(dkv.at[2 * k + 1], from_x.at[k], send.at[k], recv.at[k], others["x"])
        for k in range(4)
    ]
    for copy in over_x:
        copy.start()
    scan.step(1)
    weights(1, normed_two, half_two, d_gu, their_gu)
    pump(1)
    several(4, 2, 2)
    over_far = [
        remote(dkv.at[4 + 2 * k], from_far.at[k], send.at[4 + k], recv.at[4 + k], others["far"])
        for k in range(2)
    ]
    for k in range(2):
        over_x[2 + k].wait_recv()
        add(dkv.at[4 + 2 * k], from_x.at[2 + k])
        over_far[k].start()
    scan.step(2)
    pump(2)
    several(0, 2, 2)
    for k in range(2):
        over_x[k].wait_recv()
        add(dkv.at[2 * k], from_x.at[k])
    over_far[1].wait_recv()
    add(dkv.at[2], from_far.at[1])
    over_near = remote(dkv.at[2], from_near, send.at[6], recv.at[6], others["near"])
    over_near.start()
    weights(3, normed, their_normed, d_z, their_z)
    pump(3)
    loads.need(*range(10, 18), *range(4))
    ssm_back_kernel(
        info, x, bc, dt, cum, d_ssm, head_params, dx, d_bc, d_cum, d_dt, g_skip, cols_t, d_rows
    )
    pump(4)
    scan.step(3)
    d_step = d_conv.at[:, pl.ds(xbc, TILE)]
    step_in = raw.at[pl.ds(RIM, rows), pl.ds(xbc, TILE)]
    state_back_kernel(
        info, x, bc, dt, cum, d_ssm, head_params, step_in, state_in, d_state, dx, d_bc, d_cum,
        d_dt, dx, d_bc, d_step, head_sums,
    )
    conv_back_start(info, dx, d_bc, pre, raw, d_pre, g_conv)
    rim = remote(
        d_pre.at[pl.ds(0, RIM)], d_pre.at[pl.ds(rows, RIM)], rim_send.at[0], rim_recv.at[0],
        previous,
    )
    rim.start()
    pump(5)
    over_far[0].wait_recv()
    over_near.wait_recv()
    attend_back_write(acc, dq)
    d_pair[...] = (
        dkv[0].astype(jnp.float32)
        + from_far[0].astype(jnp.float32)
        + from_near[...].astype(jnp.float32)
    )
    rope_back_kernel(dq, d_pair, cosine, sine, d_attn)
    last_swaps = [
        remote(give, take, swap_send.at[8 + k], swap_recv.at[8 + k], others["core"])
        for k, (give, take) in enumerate(((d_attn, their_attn), (d_conv, their_conv)))
    ]
    last_swaps[0].start()
    rim.wait_recv()
    conv_back_end(info, d_pre, conv_w, d_conv.at[:, pl.ds(0, xbc)])
    last_swaps[1].start()
    pump(6)
    last_swaps[0].wait_recv()
    weight_products(left_t, d_attn, their_attn, p_attn)
    last_swaps[1].wait_recv()
    weight_products(left_t, d_conv, their_conv, p_conv)
    for wave in sorted(waves):
        pump(wave)
    swaps += last_swaps
    loads.finish()
    scatter.finish()
    scan.finish()
    rim.wait_send()
    for copy in over_x + over_far + [over_near] + swaps:
        copy.wait_send()


def back(lens, *args):
    (
        head_params, conv_w, cosine, sine, q, kv, grad, out_t, lse, pull, x, bc, dt, cum,
        d_ssm, raw, state_in, pre, normed, normed_two, d_mixer, grad_rows, hidden, joined, d_gu,
        d_z,
    ) = args
    rows, query_width = q.shape
    width = normed.shape[1]
    half = width // 2
    pair = kv.shape[1]
    ssm_width, xbc = x.shape[1], pre.shape[1]
    f32, narrow = jnp.float32, jnp.bfloat16
    dma = pltpu.SemaphoreType.DMA
    widths = [hidden.shape[1], d_gu.shape[1], joined.shape[1], d_z.shape[1]]
    pairs = column_chunks(widths, 1024, 4, 2)
    own = half // 16
    outs = [
        shape_of((rows, xbc + TILE), narrow),
        shape_of((rows, query_width + pair), narrow),
        shape_of((8, xbc), f32),
        shape_of((8, TILE), f32),
        shape_of((8, TILE), f32),
        shape_of((half, xbc + TILE), narrow),
        shape_of((half, query_width + pair), narrow),
    ] + [shape_of((own, w), f32) for w in widths]
    scratch = [pltpu.VMEM(a.shape, a.dtype) for a in args]
    scratch += [pltpu.VMEM((half, w), narrow) for w in widths]
    scratch += scatter_scratch(widths, half)
    scratch += [pltpu.VMEM((rows, half), narrow)] * 3
    scratch += [pltpu.VMEM(a.shape, narrow) for a in (hidden, joined, d_gu, d_z)]
    scratch += [
        pltpu.VMEM((rows, half), narrow),
        pltpu.VMEM((rows, xbc + TILE), narrow),
        pltpu.VMEM((rows, query_width + pair), narrow),
        pltpu.VMEM((half, 2 * rows), narrow),
        pltpu.VMEM((QUERY_HEADS, rows, TILE), narrow),
        pltpu.VMEM((QUERY_HEADS, rows, TILE), narrow),
        pltpu.VMEM((QUERY_HEADS, rows), f32),
        pltpu.VMEM((QUERY_HEADS, HEAD_SIZE, rows), f32),
        pltpu.VMEM((8, rows, pair), narrow),
        pltpu.VMEM((4, rows, pair), narrow),
        pltpu.VMEM((2, rows, pair), narrow),
        pltpu.VMEM((rows, pair), narrow),
        pltpu.VMEM((rows, query_width), f32),
        pltpu.VMEM((rows, pair), f32),
        pltpu.VMEM((rows, TILE), f32),
        pltpu.VMEM((rows, TILE), f32),
        pltpu.VMEM((TILE, rows), f32),
        pltpu.VMEM((TILE, rows), f32),
        pltpu.VMEM((rows + RIM, xbc), f32),
        *scan_scratch(ssm_width),
        dma((7,)),
        dma((7,)),
        dma((10,)),
        dma((10,)),
        dma((2 * len(pairs), 4, 4)),
        dma((2 * len(pairs), 4, 4)),
        dma((1,)),
        dma((1,)),
        dma((len(args),)),
    ]
    return comm_call(
        lambda *refs: back_kernel(pairs, *refs),
        outs,
        [INTO_VMEM] * len(outs),
        (lens, *args),
        [pl.BlockSpec(memory_space=pltpu.SMEM)] + [ANY] * len(args),
        scratch,
        2,
        200_000_000,
        limit=62,
    )


def dot_nt_two(left, right):
    high = left.astype(jnp.bfloat16)
    low = (left - high.astype(jnp.float32)).astype(jnp.bfloat16)
    return dot_nt(high, right) + dot_nt(low, right)


def last_kernel(pairs, *refs):
    (
        p_conv, p_attn, d_conv, d_attn, d_z, gains, g_mlp, g_ssm, g_conv, head_sums, g_skip,
        sum_out, sum_z, *far_in,
    ) = refs[:18]
    (
        input_grad, g_attn_out, g_in_out, g_dt_out, g_out_out,
        norm_total, mlp_total, ssm_total, conv_total, conv_b_total, head_total,
    ) = refs[18:29]
    refs = refs[29:]
    arrived_w, near_in, refs = refs[:8], refs[8:13], refs[13:]
    full_conv, full_mix, x_own, order, d_middle = near_in
    (
        out_conv, out_attn, d_normed, small_own, small_in, small_mid, small_out, in_sems,
        w_send, w_recv, small_send, small_recv,
    ) = refs
    stage = Stage(far_in, near_in, in_sems)
    stage.start(*range(5))
    others = partners()
    greet(list(others.values()))
    rows, width = d_normed.shape
    scatter = Scatter((p_conv, p_attn), (out_conv, out_attn), arrived_w, pairs, w_send, w_recv, others)
    scatter.step(0, 0)
    scatter.step(1, 0)
    scatter.step(2, 0)
    stage.need(0, 1)
    step = 256
    attn = d_attn.shape[1]

    def back_out(j, carry):
        here = pl.ds(pl.multiple_of(j * step, step), step)
        d_normed[:, here] = (
            dot_nt(d_conv[...], full_conv[here])
            + dot_nt(d_attn[...], full_mix[here, :attn])
            + dot_nt(d_z[...], full_mix[here, attn:])
        )
        return carry

    lax.fori_loop(0, width // step, back_out, 0)
    stage.need(2, 3, 4)
    scatter.step(0, 1)
    scatter.step(1, 1)
    wide = x_own[...].astype(jnp.float32)
    r = lax.rsqrt(jnp.mean(wide * wide, axis=-1, keepdims=True) + NORM_EPS)
    grads = d_normed[...]
    g_norm = jnp.sum(grads * wide * r, axis=0, keepdims=True)
    line = lax.broadcasted_iota(jnp.int32, (8, width), 0)
    both = jnp.where(line == 0, g_norm, jnp.where(line == 1, g_mlp[...], 0.0))
    both = dot_nt_two(both, order[...])
    small_own[16:] = jnp.zeros((small_own.shape[0] - 16, TILE), jnp.float32)
    small_own[16:28] = g_ssm[...]
    small_own[28:30] = head_sums[0:2]
    small_own[30:31] = g_skip[0:1]
    conv_tiles = g_conv.shape[1] // TILE
    for k in range(CONV + 1):
        for i in range(conv_tiles):
            place = 32 + 16 * k + i
            small_own[place : place + 1] = g_conv[k : k + 1, i * TILE : (i + 1) * TILE]
    for k in range(width // TILE):
        for which in range(2):
            small_own[8 * which + k : 8 * which + k + 1] = both[
                which : which + 1, k * TILE : (k + 1) * TILE
            ]
    names = ("core", "y", "x", "near", "far")
    small_copies = []

    def small_step(k):
        if k > 0:
            small_copies[k - 1].wait_recv()
            was = small_own if k == 1 else small_mid.at[k - 2]
            now = small_out if k == 5 else small_mid.at[k - 1]
            now[...] = was[...] + small_in[k - 1]
        if k < 5:
            source = small_own if k == 0 else small_mid.at[k - 1]
            copy = remote(
                source, small_in.at[k], small_send.at[k], small_recv.at[k], others[names[k]]
            )
            copy.start()
            small_copies.append(copy)

    scatter.step(2, 1)
    scatter.step(0, 2)
    small_step(0)
    inner = grads * gains[0:1]
    coeff = jnp.mean(inner * wide, axis=-1, keepdims=True)
    d_normed[...] = d_middle[...] + r * (inner - wide * (r * r * coeff))
    scatter.step(1, 2)
    small_step(1)
    scatter.step(0, 3)
    scatter.step(2, 2)

    def plain(j, carry):
        here = pl.ds(pl.multiple_of(j * step, step), step)
        input_grad[:, here] = dot_nt_two(d_normed[...], order[here])
        return carry

    lax.fori_loop(0, width // step, plain, 0)
    small_step(2)
    query = QUERY_HEADS * HEAD_SIZE
    g_in_out[:, : sum_z.shape[1]] = sum_z[...]
    g_out_out[:, :query] = pair_columns(sum_out[:, :query], True)
    g_out_out[:, query:] = sum_out[:, query:]
    scatter.step(1, 3)
    scatter.step(2, 3)
    small_step(3)
    scatter.step(0, 4)
    small_step(4)
    scatter.step(1, 4)
    scatter.step(2, 4)
    small_step(5)
    norm_total[...] = small_out[:8]
    mlp_total[...] = small_out[8:16]
    ssm_total[...] = small_out[16:28]
    head_total[...] = small_out[24:32]
    for k in range(CONV):
        for i in range(conv_tiles):
            place = 32 + 16 * k + i
            conv_total[k : k + 1, i * TILE : (i + 1) * TILE] = small_out[place : place + 1]
    conv_b_total[...] = small_out[32 + 16 * CONV : 32 + 16 * CONV + conv_tiles]
    g_in_out[:, g_in_out.shape[1] - g_conv.shape[1] :] = out_conv[:, : g_conv.shape[1]]
    g_dt_out[...] = out_conv[:, g_conv.shape[1] :].T[:MH]
    query = QUERY_HEADS * HEAD_SIZE
    g_attn_out[:, :query] = pair_columns(out_attn[:, :query], True)
    g_attn_out[:, query:] = out_attn[:, query:]
    scatter.finish()
    for copy in small_copies:
        copy.wait_send()


def last(near, far):
    p_conv, p_attn, d_z, g_conv, sum_out = near[0], near[1], near[4], near[8], near[11]
    rows, width = far[2].shape
    half = p_conv.shape[0]
    f32, narrow = jnp.float32, jnp.bfloat16
    dma = pltpu.SemaphoreType.DMA
    widths = [p_conv.shape[1], p_attn.shape[1]]
    pairs = column_chunks(widths)
    total = (32 + 16 * (CONV + 1), TILE)
    block = half // 16
    xbc = g_conv.shape[1]
    joined = sum_out.shape[1]
    outs = [
        shape_of((rows, width), f32),
        shape_of((block, widths[1]), f32),
        shape_of((block, d_z.shape[1] + xbc), f32),
        shape_of((MH, block), f32),
        shape_of((block, joined), f32),
        shape_of((8, TILE), f32),
        shape_of((8, TILE), f32),
        shape_of((12, TILE), f32),
        shape_of((CONV, xbc), f32),
        shape_of((xbc // TILE, TILE), f32),
        shape_of((8, TILE), f32),
    ]
    scratch = scatter_scratch(widths, half)
    scratch += [pltpu.VMEM(a.shape, a.dtype) for a in far]
    scratch += [pltpu.VMEM((block, w), f32) for w in widths]
    scratch += [
        pltpu.VMEM((rows, width), f32),
        pltpu.VMEM(total, f32),
        pltpu.VMEM((5, *total), f32),
        pltpu.VMEM((4, *total), f32),
        pltpu.VMEM(total, f32),
        dma((5,)),
        dma((2 * len(pairs), 4, 4)),
        dma((2 * len(pairs), 4, 4)),
        dma((5,)),
        dma((5,)),
    ]
    return comm_call(
        lambda *refs: last_kernel(pairs, *refs),
        outs,
        [INTO_VMEM] * len(outs),
        (*near, *far),
        [INTO_VMEM] * len(near) + [ANY] * len(far),
        scratch,
        4,
        100_000_000,
    )


def settle_kernel(*refs):
    count = len(refs) // 2
    sems = refs[2 * count]
    copies = [
        pltpu.make_async_copy(refs[k], refs[count + k], sems.at[k]) for k in range(count)
    ]
    for copy in copies:
        copy.start()
    for copy in copies:
        copy.wait()


def settle(*arrays):
    count = len(arrays)
    return pl.pallas_call(
        settle_kernel,
        out_shape=[shape_of(a.shape, a.dtype) for a in arrays],
        in_specs=[ANY] * count,
        out_specs=[INTO_VMEM] * count,
        scratch_shapes=[pltpu.SemaphoreType.DMA((count,))],
        compiler_params=pltpu.CompilerParams(vmem_limit_bytes=60 * 1024 * 1024),
    )(*arrays)


def pair_heads(value, back=False):
    rows = value.shape[0]
    group = QUERY_HEADS // KEY_VALUE_HEADS
    width = QUERY_HEADS * HEAD_SIZE
    shape = (group, KEY_VALUE_HEADS) if back else (KEY_VALUE_HEADS, group)
    moved = value[:, :width].reshape(rows, *shape, HEAD_SIZE).transpose(0, 2, 1, 3)
    return jnp.concatenate([moved.reshape(rows, width), value[:, width:]], axis=1)


def plain_layer(
    layer_input,
    seq_lengths,
    w_attn,
    w_ssm_in,
    w_dt,
    w_out,
    w_gate_up,
    w_down,
    norm_gain,
    mlp_gain,
    ssm_gain,
    conv_w,
    conv_b,
    a_log,
    dt_bias,
    d_skip,
    out_grad,
):
    token_rows = layer_input.shape[1]
    query_width = QUERY_HEADS * HEAD_SIZE
    key_value_width = KEY_VALUE_HEADS * HEAD_SIZE
    attn_width = query_width + 2 * key_value_width
    ssm_width = MH * MP
    xbc_width = ssm_width + 2 * NS
    seq_lens = seq_lengths[0]
    first_pos = lax.axis_index("seq") * token_rows
    positions = first_pos + jnp.arange(token_rows, dtype=jnp.int32)
    segment, device_places = segments(seq_lens, positions)
    ends = jnp.cumsum(seq_lens)
    info = jnp.stack([first_pos, ends[0], ends[1], ends[2]]).astype(jnp.int32)
    half = HEAD_SIZE // 2
    freqs = ROPE_BASE ** (-jnp.arange(half, dtype=jnp.float32) / half)
    angles = device_places.astype(jnp.float32)[:, None] * jnp.tile(freqs, TILE // half)[None, :]
    cosine, sine = jnp.cos(angles), jnp.sin(angles)
    head_params = jnp.pad(
        jnp.stack([dt_bias, jnp.exp(a_log), d_skip]), ((0, 5), (0, TILE - MH))
    )
    step_pad = jnp.pad(w_dt, ((0, 0), (0, TILE - MH)))
    shards = (
        jnp.concatenate([w_ssm_in[:, ssm_width:], step_pad], axis=1),
        jnp.concatenate([pair_heads(w_attn), w_ssm_in[:, :ssm_width]], axis=1),
        pair_heads(w_out.T),
        w_gate_up,
        w_down.T,
    )
    ext_pos = first_pos - (CONV - 1) + jnp.arange(token_rows + CONV - 1, dtype=jnp.int32)
    ext_segment = segments(seq_lens, ext_pos)[0]

    def conv_local(ext_rows, conv_weight, conv_bias):
        return conv_mix(ext_rows, ext_segment, conv_weight, conv_bias)

    full = [lax.all_gather(p, ("seq", "batch"), axis=0, tiled=True) for p in shards]
    full_conv, full_mix, full_out, full_gu, full_down = full
    x_rows = layer_input[0].astype(jnp.float32)
    grad_rows = out_grad[0]
    scale_one = rms_scale(x_rows)
    normed = (x_rows * scale_one * norm_gain).astype(jnp.bfloat16)
    conv_proj = jnp.dot(normed, full_conv, preferred_element_type=jnp.float32)
    mix_proj = jnp.dot(normed, full_mix, preferred_element_type=jnp.float32)
    queries, own_pairs = big_call(
        rope_kernel,
        (
            shape_of((token_rows, query_width), jnp.bfloat16),
            shape_of((token_rows, 2 * key_value_width), jnp.bfloat16),
        ),
        mix_proj[:, :attn_width],
        cosine,
        sine,
    )
    gate_z = mix_proj[:, attn_width:]
    raw_xbc = conv_proj[:, :xbc_width]
    step_proj = conv_proj[:, xbc_width:]
    rim_rows = shifted(raw_xbc[token_rows - (CONV - 1) :], "seq", 1)
    extended = jnp.concatenate([rim_rows, raw_xbc], axis=0)
    conv_out, conv_pullback = jax.vjp(conv_local, extended, conv_w, conv_b)
    conv_narrow = conv_out.astype(jnp.bfloat16)
    inputs_x, inputs_bc = conv_narrow[:, :ssm_width], conv_narrow[:, ssm_width:]
    ssm_own, state_own, steps_dt, running_decay = ssm_forward(
        info, inputs_x, inputs_bc, step_proj, head_params
    )
    all_pairs = lax.all_gather(own_pairs, "seq", axis=0, tiled=True)
    state_in = scan_states(state_own, True)
    attended, attended_t, log_total = attn_forward(info, queries, all_pairs)

    ssm_flat, ssm_normed, scale_gated = ssm_finish(
        info, ssm_own, inputs_bc, running_decay, state_in, gate_z, ssm_gain.reshape(-1, TILE)
    )
    joined = jnp.concatenate([attended, ssm_normed], axis=1)

    def into_width(left, weight):
        return jnp.einsum("tc,dc->td", left, weight, preferred_element_type=jnp.float32)

    def out_of_width(left, weight):
        return jnp.dot(left, weight, preferred_element_type=jnp.float32)

    middle = x_rows + into_width(joined, full_out)
    scale_two = rms_scale(middle)
    normed_two = (middle * scale_two * mlp_gain).astype(jnp.bfloat16)
    gate_up = out_of_width(normed_two, full_gu)
    gate_part, up_part = gate_up[:, :FF], gate_up[:, FF:]
    sig_gate = jax.nn.sigmoid(gate_part)
    hidden = (gate_part * sig_gate * up_part).astype(jnp.bfloat16)
    layer_out = middle + into_width(hidden, full_down)
    d_hidden = out_of_width(grad_rows, full_down)
    d_gate = d_hidden * up_part * (sig_gate * (1.0 + gate_part * (1.0 - sig_gate)))
    d_up = d_hidden * gate_part * sig_gate
    d_gate_up = jnp.concatenate([d_gate, d_up], axis=1).astype(jnp.bfloat16)
    d_normed_two = into_width(d_gate_up, full_gu)
    d_middle_norm, g_mlp_gain = norm_back(middle, scale_two, mlp_gain, d_normed_two)
    d_middle = grad_rows.astype(jnp.float32) + d_middle_norm
    d_mixer = d_middle.astype(jnp.bfloat16)
    d_joined = out_of_width(d_mixer, full_out)
    attended_gradient = d_joined[:, :query_width].astype(jnp.bfloat16)
    d_ssm_out, d_gate_z, pull, g_ssm_gain = gate_back(
        info,
        d_joined[:, query_width:],
        ssm_flat,
        gate_z,
        scale_gated,
        ssm_gain.reshape(-1, TILE),
        running_decay,
        inputs_bc,
    )
    pull = jnp.concatenate([pull, state_own[NS:]], axis=0)
    d_state = scan_states(pull, False)
    d_queries, d_pairs = attn_backward(
        info, queries, all_pairs, attended_gradient, attended_t, log_total
    )
    own_d_pairs = lax.psum_scatter(
        d_pairs.astype(jnp.float32), "seq", scatter_dimension=0, tiled=True
    )
    dx_part, d_bc_part, d_cum_part, d_dt_part, g_skip_rows = ssm_back(
        info, inputs_x, inputs_bc, steps_dt, running_decay, d_ssm_out, head_params
    )
    g_inputs_x, g_inputs_bc, d_step_pad, head_sums = state_back(
        info,
        inputs_x,
        inputs_bc,
        steps_dt,
        running_decay,
        d_ssm_out,
        head_params,
        step_proj,
        state_in,
        d_state,
        dx_part,
        d_bc_part,
        d_cum_part,
        d_dt_part,
    )
    g_extended, g_conv_w, g_conv_b = conv_pullback(
        jnp.concatenate([g_inputs_x, g_inputs_bc], axis=1)
    )
    back_rim = shifted(g_extended[: CONV - 1], "seq", -1)
    d_raw = g_extended[CONV - 1 :] + jnp.concatenate(
        [jnp.zeros((token_rows - (CONV - 1), xbc_width), jnp.float32), back_rim], axis=0
    )
    d_conv_proj = jnp.concatenate([d_raw.astype(jnp.bfloat16), d_step_pad], axis=1)
    (d_attn_proj,) = big_call(
        rope_back_kernel,
        (shape_of((token_rows, attn_width), jnp.bfloat16),),
        d_queries,
        own_d_pairs,
        cosine,
        sine,
    )
    d_mix_proj = jnp.concatenate([d_attn_proj, d_gate_z], axis=1)
    d_normed = into_width(d_conv_proj, full_conv) + into_width(d_mix_proj, full_mix)
    d_input_norm, g_norm_gain = norm_back(x_rows, scale_one, norm_gain, d_normed)
    input_grad = d_middle + d_input_norm
    axes = ("seq", "batch")

    def summed(left, right):
        grad = jnp.einsum("td,tc->dc", left, right, preferred_element_type=jnp.float32)
        return lax.psum_scatter(grad, axes, scatter_dimension=0, tiled=True)

    sum_down, sum_gu = summed(grad_rows, hidden), summed(normed_two, d_gate_up)
    sum_out, sum_conv = summed(d_mixer, joined), summed(normed, d_conv_proj)
    sum_mix = summed(normed, d_mix_proj)
    sum_attn, sum_z = sum_mix[:, :attn_width], sum_mix[:, attn_width:]
    small = (
        g_norm_gain,
        g_mlp_gain,
        g_ssm_gain.reshape(-1),
        g_conv_w,
        g_conv_b,
        head_sums[0, :MH],
        head_sums[1, :MH],
        g_skip_rows[0, :MH],
    )
    small_sums = unpack_small(lax.psum(pack_small(small), axes), small)
    grad_attn = pair_heads(sum_attn, True)
    grad_ssm_in = jnp.concatenate([sum_z, sum_conv[:, :xbc_width]], axis=1)
    grad_dt = sum_conv[:, xbc_width : xbc_width + MH]
    grad_out = pair_heads(sum_out, True).T
    grad_gate_up = sum_gu
    grad_down = sum_down.T
    return (
        layer_out.astype(jnp.bfloat16)[None],
        input_grad[None],
        grad_attn,
        grad_ssm_in,
        grad_dt,
        grad_out,
        grad_gate_up,
        grad_down,
        *small_sums,
    )


def on_device(
    layer_input,
    seq_lengths,
    w_attn,
    w_ssm_in,
    w_dt,
    w_out,
    w_gate_up,
    w_down,
    norm_gain,
    mlp_gain,
    ssm_gain,
    conv_w,
    conv_b,
    a_log,
    dt_bias,
    d_skip,
    out_grad,
):
    if not is_fast(layer_input.shape[2]):
        return plain_layer(
            layer_input, seq_lengths, w_attn, w_ssm_in, w_dt, w_out, w_gate_up, w_down, norm_gain,
            mlp_gain, ssm_gain, conv_w, conv_b, a_log, dt_bias, d_skip, out_grad,
        )
    half = HEAD_SIZE // 2
    freqs = np.float32(ROPE_BASE) ** (-np.arange(half, dtype=np.float32) / np.float32(half))
    freqs = jnp.asarray(np.tile(freqs.astype(np.float32), TILE // half)[None])
    full, made = front(
        seq_lengths,
        dt_bias,
        a_log,
        d_skip,
        layer_input[0],
        out_grad[0],
        norm_gain.reshape(-1, TILE),
        mlp_gain.reshape(-1, TILE),
        freqs,
        conv_w,
        conv_b.reshape(-1, TILE),
        (w_attn, w_ssm_in, w_dt.T, w_out.T, w_gate_up, w_down.T),
    )
    full_conv, full_mix, full_out, full_gu, full_down = full
    (
        x_own, g_own, gains, normed, queries, all_pairs, gate_z, raw_rows, pre_conv, inputs_x,
        inputs_bc, ssm_own, state_own, steps_dt, running_decay, attended, attended_t, log_total,
        state_in, order, cosine, sine, head_params,
    ) = made
    (
        layer_out, joined, hidden, d_gate_up, normed_two, d_mixer, d_middle, d_ssm_out, d_gate_z,
        pull, attended_gradient, g_ssm_gain, g_mlp_gain,
    ) = middle_part(
        seq_lengths, ssm_own, inputs_bc, running_decay, state_in, state_own, gate_z,
        ssm_gain.reshape(-1, TILE), attended, x_own, g_own, gains, order, full_out, full_gu,
        full_down,
    )
    (
        d_conv_proj, d_attn_proj, g_conv, head_sums, g_skip_rows, part_conv, part_attn, sum_down,
        sum_gu, sum_out, sum_z,
    ) = back(
        seq_lengths, head_params, conv_w, cosine, sine, queries, all_pairs, attended_gradient,
        attended_t, log_total, pull, inputs_x, inputs_bc, steps_dt, running_decay, d_ssm_out,
        raw_rows, state_in, pre_conv, normed, normed_two, d_mixer, g_own, hidden, joined,
        d_gate_up, d_gate_z,
    )
    (
        input_grad, grad_attn, grad_ssm_in, grad_dt, grad_out, g_norm, g_mlp, g_ssm, g_conv_w,
        g_conv_b, heads,
    ) = last(
        (
            part_conv, part_attn, d_conv_proj, d_attn_proj, d_gate_z, gains, g_mlp_gain,
            g_ssm_gain, g_conv, head_sums, g_skip_rows, sum_out, sum_z,
        ),
        (full_conv, full_mix, x_own, order, d_middle),
    )
    (
        input_grad, grad_attn, grad_ssm_in, grad_dt, grad_out, sum_gu, sum_down, g_norm, g_mlp,
        g_ssm, g_conv_w, g_conv_b, heads,
    ) = settle(
        input_grad, grad_attn, grad_ssm_in, grad_dt, grad_out, sum_gu, sum_down, g_norm, g_mlp,
        g_ssm, g_conv_w, g_conv_b, heads,
    )
    return (
        layer_out[None],
        input_grad[None],
        grad_attn,
        grad_ssm_in,
        grad_dt.T,
        grad_out.T,
        sum_gu,
        sum_down.T,
        g_norm.reshape(-1),
        g_mlp.reshape(-1),
        g_ssm.reshape(-1),
        g_conv_w,
        g_conv_b.reshape(-1),
        heads[4, :MH],
        heads[5, :MH],
        heads[6, :MH],
    )


def solution(mesh):
    return jax.shard_map(
        on_device,
        mesh=mesh,
        in_specs=(
            P("batch", "seq", None),
            P("batch", None),
            P(("seq", "batch"), None),
            P(("seq", "batch"), None),
            P(("seq", "batch"), None),
            P(None, ("seq", "batch")),
            P(("seq", "batch"), None),
            P(None, ("seq", "batch")),
            P(),
            P(),
            P(),
            P(),
            P(),
            P(),
            P(),
            P(),
            P("batch", "seq", None),
        ),
        out_specs=(
            P("batch", "seq", None),
            P("batch", "seq", None),
            P(("seq", "batch"), None),
            P(("seq", "batch"), None),
            P(("seq", "batch"), None),
            P(None, ("seq", "batch")),
            P(("seq", "batch"), None),
            P(None, ("seq", "batch")),
            P(),
            P(),
            P(),
            P(),
            P(),
            P(),
            P(),
            P(),
        ),
        check_vma=False,
    )
```
